32 devices in a mesh: lat: 4 (over y, core), lon: 8 (over z, x).
Axes of the slice: x: 2, y: 2, z: 4, core: 2. Of those that a mesh axis runs over, the one named last changes fastest.
Arguments:
- latent: bfloat16 [8, 96, 640], P('lat', 'lon'), may hold values from -6 to 6
- lon_filter: bfloat16 [9, 96], replicated, may hold values from -0.625 to 0.625
- mix_weight: bfloat16 [9, 640, 20], P(None, 'lon'), may hold values from -1.25 to 1.25
- band_weight: bfloat16 [9, 8, 3], P(None, 'lat'), may hold values from -1.25 to 1.25
- offsets: int32 [8], P('lat'), may hold values from -2 to 7, as said below
- w_up: bfloat16 [640, 1280], replicated, may hold values from -0.25 to 0.25
- w_down: bfloat16 [1280, 640], replicated, may hold values from -0.15625 to 0.15625
Outputs:
- result: bfloat16 [8, 96, 640], P('lat', 'lon')
The draws below stay inside these ranges and needn't reach their ends.
Inputs may be any that keep to these rules, and one draw needn't show every extreme that they name: offsets[i] - i lies between -2 and 0, so a band's rows lie within 2 rows of its output row; in every aligned block of 2 rows the first row's band starts 2 rows below it and the last row's band ends 2 rows above it.
All inputs are finite; a program needn't handle non-finite values.
Results may differ from the reference program's by a relative error of at most 0.0095.
Values may be sent and summed in bfloat16 or wider, within the bound.
No kernel may reach another device: no remote copies, remote signals or barrier semaphores. Data moves between devices by JAX's collectives and lax.ppermute only.
A program may use at most 128 MiB of HBM per device.

```python
import jax
import jax.numpy as jnp
from jax import lax

C = 640
HID = 1280
GROUP = 20
NB = 9
BW = 3
REACH = 2
LAT_DEV = 2
LAT = 8
LON = 96


def draw_offsets(key, part):
    top_shift = 2 * REACH - BW + 1
    shifts = jax.random.randint(jax.random.fold_in(key, 17), (LAT,), 0, top_shift + 1).astype(jnp.int32)
    places = jnp.arange(LAT, dtype=jnp.int32)
    within = places % LAT_DEV
    shifts = jnp.where(within == 0, 0, shifts)
    shifts = jnp.where(within == LAT_DEV - 1, top_shift, shifts)
    return (places - REACH + shifts).astype(jnp.int32)


def steps_of(key, shape, split, smallest, top_value):
    def one(position, parts):
        steps = jax.random.uniform(jax.random.fold_in(jax.random.fold_in(key, 6), position), (parts,), jnp.float32, smallest / len(split), top_value / len(split))
        return jnp.repeat(jnp.exp(steps), shape[position] // parts).reshape((-1,) + (1,) * (len(shape) - position - 1))

    level = one(*split[0])
    for cut in split[1:]:
        level = level * one(*cut)
    return level


def scatter_about(own_key, dims, scale, most, cuts=(), kind=jnp.bfloat16):
    drawn = jax.random.normal(own_key, dims, jnp.float32) * scale
    if len(cuts) > 0:
        drawn = steps_of(own_key, dims, cuts, -0.22, 0.18) * drawn
    return jnp.clip(drawn, min=-most, max=most).astype(kind)


def setup_inputs(seed: int = 0) -> dict:
    key_of = jax.random.split(jax.random.key(seed), 8)
    return {
        "latent": scatter_about(key_of[0], (LAT, LON, C), 1.0, 6.0, ((0, 4), (1, 8))),
        "lon_filter": scatter_about(key_of[1], (NB, LON), LON ** -0.5, 0.625),
        "mix_weight": scatter_about(key_of[2], (NB, C, GROUP), GROUP ** -0.5, 1.25, ((1, 8),)),
        "band_weight": scatter_about(key_of[3], (NB, LAT, BW), (NB * BW) ** -0.5, 1.25, ((1, 4),)),
        "offsets": draw_offsets(jax.random.fold_in(key_of[7], 71), 0),
        "w_up": scatter_about(key_of[5], (C, HID), C ** -0.5, 0.25),
        "w_down": scatter_about(key_of[6], (HID, C), HID ** -0.5, 0.15625),
    }


def circulant(lon_filter):
    length = lon_filter.shape[1]
    places = jnp.arange(length, dtype=jnp.int32)
    index_table = (places[:, None] - places[None, :]) % length
    return lon_filter[:, index_table]

def block_mix(mix_weight):
    chan_width = mix_weight.shape[1]
    group_size = mix_weight.shape[2]
    repeated = jnp.tile(mix_weight.astype(jnp.float32), (1, 1, chan_width // group_size))
    member = jnp.arange(chan_width, dtype=jnp.int32) // group_size
    same_group = (member[:, None] == member[None, :]).astype(jnp.float32)
    return repeated * same_group[None]

def feed_forward(summed, w_up, w_down):
    flat_rows = summed.reshape(-1, summed.shape[-1]).astype(jnp.float32)
    row_mean = lax.optimization_barrier(jnp.mean(flat_rows, axis=1, keepdims=True))
    centred = flat_rows - row_mean
    row_var = lax.optimization_barrier(jnp.mean(centred * centred, axis=1, keepdims=True))
    normed = (centred * lax.rsqrt(row_var + 1e-05)).astype(jnp.bfloat16)
    hidden = jax.nn.gelu(jnp.dot(normed, w_up, preferred_element_type=jnp.float32), approximate=False).astype(jnp.bfloat16)
    output = flat_rows + jnp.dot(hidden, w_down, preferred_element_type=jnp.float32)
    return output.astype(jnp.bfloat16).reshape(summed.shape)

def reference(latent, lon_filter, mix_weight, band_weight, offsets, w_up, w_down):
    latent_f = latent.astype(jnp.float32)
    lon_table = circulant(lon_filter).astype(jnp.float32)
    mix_blocks = block_mix(mix_weight)
    band_f = band_weight.astype(jnp.float32)

    def one_basis(running, inputs):
        table_k, block_k, band_k = inputs
        spread = jnp.einsum('ijc,xj->icx', latent_f, table_k, precision=lax.Precision.HIGHEST)
        mixed_rows = jnp.einsum('icx,dc->idx', spread, block_k, precision=lax.Precision.HIGHEST).astype(jnp.bfloat16)
        padded = jnp.pad(mixed_rows, ((REACH, REACH), (0, 0), (0, 0)))
        for band_tap in range(BW):
            picked = (offsets + band_tap + REACH).astype(jnp.int32)
            running = running + band_k[:, band_tap][:, None, None] * padded[picked].astype(jnp.float32)
        return (running, None)
    convolved, unused = lax.scan(one_basis, jnp.zeros((LAT, C, LON), jnp.float32), (lon_table, mix_blocks, band_f))
    convolved = convolved.astype(jnp.bfloat16)
    turned = jnp.transpose(convolved, (0, 2, 1)).astype(jnp.float32)
    summed = (latent_f + turned).astype(jnp.bfloat16)
    return feed_forward(summed, w_up, w_down)
```

```python
import jax
import jax.numpy as jnp
from jax import lax
from jax.sharding import PartitionSpec as P


def feed_forward(flat_rows, w_up, w_down):
    row_mean = jnp.mean(flat_rows, axis=1, keepdims=True)
    centred = flat_rows - row_mean
    row_var = jnp.mean(centred * centred, axis=1, keepdims=True)
    normed = (centred * lax.rsqrt(row_var + 1e-05)).astype(jnp.bfloat16)
    hidden = jax.nn.gelu(
        jnp.dot(normed, w_up, preferred_element_type=jnp.float32), approximate=False
    ).astype(jnp.bfloat16)
    return flat_rows + jnp.dot(hidden, w_down, preferred_element_type=jnp.float32)


def local(latent, lon_filter, mix_weight, band_weight, offsets, w_up, w_down):
    rows, width, chans = latent.shape
    bases, lons = lon_filter.shape
    taps = band_weight.shape[2]
    block, group = mix_weight.shape[1:]
    lats = rows * lax.axis_size("lat")
    field = lax.all_gather(latent, ("lat", "lon"))
    weights = lax.all_gather(mix_weight, "lon")

    own_lon = lax.axis_index("lon") * width + jnp.arange(width, dtype=jnp.int32)
    places = jnp.arange(lons, dtype=jnp.int32)
    distance = (own_lon[:, None] - places[None, :]) % lons
    pick = (distance[None] == places[:, None, None]).astype(jnp.bfloat16)
    table = jnp.einsum("ks,sxj->kxj", lon_filter, pick, preferred_element_type=jnp.float32)
    positions = offsets[:, None] + jnp.arange(taps, dtype=jnp.int32)[None, :]
    reach = (positions[:, :, None] == jnp.arange(lats, dtype=jnp.int32)).astype(jnp.float32)
    band = jnp.sum(band_weight.astype(jnp.float32)[:, :, :, None] * reach[None], axis=2)
    spread_by = (
        band.reshape(bases, rows, 1, lats // rows, 1, rows, 1)
        * table.reshape(bases, 1, width, 1, lons // width, 1, width)
    ).astype(jnp.bfloat16)
    spread_by = spread_by.reshape(bases * rows * width, lats * lons)

    member = jnp.arange(block, dtype=jnp.int32) // group
    same = member[:, None] == member[None, :]
    squares = jnp.where(same[None, None], jnp.tile(weights, (1, 1, 1, block // group)), 0)

    spread = jnp.dot(
        spread_by, field.reshape(lats * lons, chans), preferred_element_type=jnp.float32
    ).astype(jnp.bfloat16)
    spread = spread.reshape(bases, rows * width, chans // block, block)
    convolved = jnp.einsum(
        "knbc,bkdc->nbd", spread, squares, preferred_element_type=jnp.float32
    ).astype(jnp.bfloat16)
    flat = latent.reshape(rows * width, chans).astype(jnp.float32)
    summed = (flat + convolved.reshape(rows * width, chans).astype(jnp.float32)).astype(
        jnp.bfloat16
    )
    result = feed_forward(summed.astype(jnp.float32), w_up, w_down)
    return result.astype(jnp.bfloat16).reshape(latent.shape)


def solution(mesh):
    return jax.shard_map(
        local,
        mesh=mesh,
        in_specs=(
            P("lat", "lon", None),
            P(),
            P(None, "lon", None),
            P(None, "lat", None),
            P("lat"),
            P(),
            P(),
        ),
        out_specs=P("lat", "lon", None),
        check_vma=False,
    )
```

```python
import functools

import jax
import jax.numpy as jnp
from jax import lax
from jax.experimental import pallas as pl
from jax.experimental.pallas import tpu as pltpu
from jax.sharding import PartitionSpec as P

F32 = jnp.float32
BF16 = jnp.bfloat16
LANES = 128
SUBLANES = 16


def up_to(size, step):
    return -(-size // step) * step


def pack_kernel(block, latent_ref, out_ref, wide):
    peers, rows, _, lanes = out_ref.shape
    width, _, chans = latent_ref.shape
    kept = lax.broadcasted_iota(jnp.int32, out_ref.shape[2:], 1) < block
    wide[...] = jnp.zeros_like(wide)
    for row in range(rows):
        wide[:width] = latent_ref[:, row, :].astype(F32)
        points = wide[...]
        for peer in range(peers):
            turned = pltpu.roll(points, (chans - peer * block) % chans, 1)[:, :lanes]
            out_ref[peer, row] = jnp.where(kept, turned, 0.0).astype(BF16)


def tables_kernel(width, filter_ref, mix_ref, table_ref, squares_ref, first, padded):
    bases, lons = filter_ref.shape
    places = table_ref.shape[2]
    step = first.shape[1]
    profile = filter_ref[...]
    source = lax.broadcasted_iota(jnp.int32, (lons, places), 0)
    place = lax.broadcasted_iota(jnp.int32, (lons, places), 1)
    apart = source + (place // step) * width + place % step
    apart = jnp.where(apart >= 2 * lons, apart - 2 * lons, apart)
    apart = jnp.where(apart >= lons, apart - lons, apart)
    first[...] = jnp.zeros_like(first)
    for lon in range(width):
        pick = (apart == lon).astype(F32).astype(BF16)
        first[:, lon, :] = jnp.dot(profile, pick, preferred_element_type=F32)
    for basis in range(bases):
        band = first[basis]
        for peer in range(places // step):
            turned = pltpu.roll(band, peer * step, 1) if peer else band
            table_ref[basis, peer * step : (peer + 1) * step, :] = turned.astype(BF16)

    group, block = mix_ref.shape[1:]
    lanes = squares_ref.shape[1]
    padded[...] = jnp.zeros_like(padded)
    padded[:, :group, :block] = mix_ref[...].astype(F32)
    into = lax.broadcasted_iota(jnp.int32, (lanes, padded.shape[1]), 0)
    member = lax.broadcasted_iota(jnp.int32, (lanes, padded.shape[1]), 1)
    repeat = (into % group == member).astype(F32).astype(BF16)
    row = lax.broadcasted_iota(jnp.int32, (lanes, lanes), 0)
    column = lax.broadcasted_iota(jnp.int32, (lanes, lanes), 1)
    same = (row // group == column // group) & (row < block) & (column < block)
    for basis in range(bases):
        repeated = jnp.dot(repeat, padded[basis].astype(BF16), preferred_element_type=F32)
        squares_ref[basis * lanes : (basis + 1) * lanes] = jnp.where(same, repeated, 0.0).astype(
            BF16
        )


def conv_kernel(
    odd_ref, band_ref, own_ref, even_ref, other_ref, table_ref, squares_ref, out_ref, spread
):
    peers, rows, step, lanes = own_ref.shape
    bases, points, _ = table_ref.shape
    odd = odd_ref[0] == 1

    def flat(ref, row):
        return ref[:, row].astype(F32).reshape(points, lanes)

    inside = [flat(own_ref, row) for row in range(rows)]
    even = [flat(even_ref, row) for row in range(rows)]
    other = [flat(other_ref, row) for row in range(rows)]
    low = [jnp.where(odd, a, b) for a, b in zip(even, other)]
    high = [jnp.where(odd, b, a) for a, b in zip(even, other)]
    read = [low + inside[:1], inside[1:] + high]
    taps = len(read[0])
    for basis in range(bases):
        joined = []
        for row in range(rows):
            at = (basis * rows + row) * taps
            joined.append(sum(band_ref[at + tap] * read[row][tap] for tap in range(taps)))
        joined = jnp.concatenate(joined, axis=1).astype(BF16)
        over = jnp.dot(table_ref[basis], joined, preferred_element_type=F32).astype(BF16)
        for row in range(rows):
            spread[row * points : (row + 1) * points, basis * lanes : (basis + 1) * lanes] = over[
                :, row * lanes : (row + 1) * lanes
            ]
    mixed = jnp.dot(spread[...], squares_ref[...], preferred_element_type=F32).astype(BF16)
    for row in range(rows):
        out_ref[:, row] = mixed[row * points : (row + 1) * points].reshape(peers, step, lanes)


def tail_kernel(
    block, back_ref, latent_ref, up_hbm, down_hbm, out_ref, wide, up_ref, down_ref, sems
):
    copies = [
        pltpu.make_async_copy(up_hbm, up_ref, sems.at[0]),
        pltpu.make_async_copy(down_hbm, down_ref, sems.at[1]),
    ]
    for copy in copies:
        copy.start()
    peers, rows, step, lanes = back_ref.shape
    width, _, chans = latent_ref.shape
    wide[...] = jnp.zeros_like(wide)
    gap = jnp.zeros((rows * step, chans - lanes), F32)
    turned = None
    for peer in range(peers):
        piece = back_ref[peer].astype(F32).reshape(rows * step, lanes)
        piece = jnp.concatenate([piece, gap], axis=1)
        piece = pltpu.roll(piece, peer * block, 1) if peer else piece
        turned = piece if turned is None else turned + piece
    for row in range(rows):
        wide[row * step : row * step + width] = latent_ref[:, row, :].astype(F32)
    summed = (wide[...] + turned).astype(BF16).astype(F32)
    centred = summed - jnp.mean(summed, axis=1, keepdims=True)
    spread = jnp.mean(centred * centred, axis=1, keepdims=True)
    normed = (centred * lax.rsqrt(spread + 1e-05)).astype(BF16)
    copies[0].wait()
    hidden = jnp.dot(normed, up_ref[...], preferred_element_type=F32)
    hidden = (0.5 * hidden * (1.0 + lax.erf(hidden * 0.5**0.5))).astype(BF16)
    copies[1].wait()
    result = summed + jnp.dot(hidden, down_ref[...], preferred_element_type=F32)
    for row in range(rows):
        out_ref[:, row, :] = result[row * step : row * step + width].astype(BF16)


def neighbours(block):
    count = lax.axis_size("lat")
    swaps = []
    for start in (0, 1):
        pairs = [(i, i + 1) for i in range(start, count - 1, 2)]
        swaps.append(lax.ppermute(block, "lat", pairs + [(b, a) for a, b in pairs]))
    return swaps


VMEM = pl.BlockSpec(memory_space=pltpu.VMEM)
SMEM = pl.BlockSpec(memory_space=pltpu.SMEM)
ANY = pl.BlockSpec(memory_space=pl.ANY)


def local(latent, lon_filter, mix_weight, band_weight, offsets, w_up, w_down):
    rows, width, chans = latent.shape
    bases, lons = lon_filter.shape
    block, group = mix_weight.shape[1:]
    peers = lons // width
    assert rows == 2 and band_weight.shape[2] == 3
    step = up_to(width, SUBLANES)
    lanes = up_to(block, LANES)
    places = peers * step
    params = pltpu.CompilerParams(vmem_limit_bytes=24 * 2**20)
    lon_first = jnp.transpose(latent, (1, 0, 2))
    tiles = jax.ShapeDtypeStruct((peers, rows, step, lanes), BF16)

    packed = pl.pallas_call(
        functools.partial(pack_kernel, block),
        out_shape=tiles,
        in_specs=[VMEM],
        out_specs=VMEM,
        scratch_shapes=[pltpu.VMEM((step, chans), F32)],
        compiler_params=params,
        name="pack",
    )(lon_first)
    own = lax.all_to_all(packed, "lon", split_axis=0, concat_axis=0, tiled=True)
    table, squares = pl.pallas_call(
        functools.partial(tables_kernel, width),
        out_shape=(
            jax.ShapeDtypeStruct((bases, places, places), BF16),
            jax.ShapeDtypeStruct((bases * lanes, lanes), BF16),
        ),
        in_specs=[VMEM] * 2,
        out_specs=(VMEM, VMEM),
        scratch_shapes=[
            pltpu.VMEM((bases, step, places), F32),
            pltpu.VMEM((bases, up_to(group, SUBLANES), lanes), F32),
        ],
        compiler_params=params,
        name="tables",
    )(lon_filter, jnp.transpose(mix_weight, (0, 2, 1)))
    even, other = neighbours(own)
    odd = (lax.axis_index("lat") % 2).astype(jnp.int32).reshape(1)
    band = band_weight.astype(F32).reshape(-1)
    mixed = pl.pallas_call(
        conv_kernel,
        out_shape=tiles,
        in_specs=[SMEM] * 2 + [VMEM] * 5,
        out_specs=VMEM,
        scratch_shapes=[pltpu.VMEM((rows * places, bases * lanes), BF16)],
        compiler_params=params,
        name="conv",
    )(odd, band, own, even, other, table, squares)
    back = lax.all_to_all(mixed, "lon", split_axis=0, concat_axis=0, tiled=True)
    result = pl.pallas_call(
        functools.partial(tail_kernel, block),
        out_shape=jax.ShapeDtypeStruct(lon_first.shape, BF16),
        in_specs=[VMEM] * 2 + [ANY] * 2,
        out_specs=VMEM,
        scratch_shapes=[
            pltpu.VMEM((rows * step, chans), F32),
            pltpu.VMEM(w_up.shape, BF16),
            pltpu.VMEM(w_down.shape, BF16),
            pltpu.SemaphoreType.DMA((2,)),
        ],
        compiler_params=params,
        name="tail",
    )(back, lon_first, w_up, w_down)
    return jnp.transpose(result, (1, 0, 2))


def solution(mesh):
    return jax.shard_map(
        local,
        mesh=mesh,
        in_specs=(
            P("lat", "lon", None),
            P(),
            P(None, "lon", None),
            P(None, "lat", None),
            P("lat"),
            P(),
            P(),
        ),
        out_specs=P("lat", "lon", None),
        check_vma=False,
    )
```

```python
import functools

import jax
import jax.numpy as jnp
from jax import lax
from jax.experimental import pallas as pl
from jax.experimental.pallas import tpu as pltpu
from jax.sharding import PartitionSpec as P

F32 = jnp.float32
BF16 = jnp.bfloat16
LANES = 128
SUBLANES = 16


def up_to(size, step):
    return -(-size // step) * step


def pack_kernel(block, latent_ref, out_ref, wide):
    peers, rows, _, lanes = out_ref.shape
    width, _, chans = latent_ref.shape
    kept = lax.broadcasted_iota(jnp.int32, out_ref.shape[2:], 1) < block
    wide[...] = jnp.zeros_like(wide)
    for row in range(rows):
        wide[:width] = latent_ref[:, row, :].astype(F32)
        points = wide[...]
        for peer in range(peers):
            turned = pltpu.roll(points, (chans - peer * block) % chans, 1)[:, :lanes]
            out_ref[peer, row] = jnp.where(kept, turned, 0.0).astype(BF16)


def tables_kernel(width, filter_ref, mix_ref, table_ref, squares_ref, first, padded):
    bases, lons = filter_ref.shape
    places = table_ref.shape[2]
    step = first.shape[1]
    profile = filter_ref[...]
    source = lax.broadcasted_iota(jnp.int32, (lons, places), 0)
    place = lax.broadcasted_iota(jnp.int32, (lons, places), 1)
    apart = source + (place // step) * width + place % step
    apart = jnp.where(apart >= 2 * lons, apart - 2 * lons, apart)
    apart = jnp.where(apart >= lons, apart - lons, apart)
    first[...] = jnp.zeros_like(first)
    for lon in range(width):
        pick = (apart == lon).astype(F32).astype(BF16)
        first[:, lon, :] = jnp.dot(profile, pick, preferred_element_type=F32)
    for basis in range(bases):
        band = first[basis]
        for peer in range(places // step):
            turned = pltpu.roll(band, peer * step, 1) if peer else band
            table_ref[basis, peer * step : (peer + 1) * step, :] = turned.astype(BF16)

    group, block = mix_ref.shape[1:]
    lanes = squares_ref.shape[1]
    padded[...] = jnp.zeros_like(padded)
    padded[:, :group, :block] = mix_ref[...].astype(F32)
    into = lax.broadcasted_iota(jnp.int32, (lanes, padded.shape[1]), 0)
    member = lax.broadcasted_iota(jnp.int32, (lanes, padded.shape[1]), 1)
    repeat = (into % group == member).astype(F32).astype(BF16)
    row = lax.broadcasted_iota(jnp.int32, (lanes, lanes), 0)
    column = lax.broadcasted_iota(jnp.int32, (lanes, lanes), 1)
    same = (row // group == column // group) & (row < block) & (column < block)
    for basis in range(bases):
        repeated = jnp.dot(repeat, padded[basis].astype(BF16), preferred_element_type=F32)
        squares_ref[basis * lanes : (basis + 1) * lanes] = jnp.where(same, repeated, 0.0).astype(
            BF16
        )


def conv_kernel(
    odd_ref, band_ref, own_ref, even_ref, other_ref, table_ref, squares_ref, out_ref, spread
):
    peers, rows, step, lanes = own_ref.shape
    bases, points, _ = table_ref.shape
    odd = odd_ref[0] == 1
    band = band_ref[...].astype(F32)

    def flat(ref, row):
        return ref[:, row].astype(F32).reshape(points, lanes)

    inside = [flat(own_ref, row) for row in range(rows)]
    even = [flat(even_ref, row) for row in range(rows)]
    other = [flat(other_ref, row) for row in range(rows)]
    low = [jnp.where(odd, a, b) for a, b in zip(even, other)]
    high = [jnp.where(odd, b, a) for a, b in zip(even, other)]
    read = [low + inside[:1], inside[1:] + high]
    taps = len(read[0])
    for basis in range(bases):
        joined = []
        for row in range(rows):
            weights = [band[tap, row : row + 1, basis : basis + 1] for tap in range(taps)]
            joined.append(sum(weights[tap] * read[row][tap] for tap in range(taps)))
        joined = jnp.concatenate(joined, axis=1).astype(BF16)
        over = jnp.dot(table_ref[basis], joined, preferred_element_type=F32).astype(BF16)
        for row in range(rows):
            spread[row * points : (row + 1) * points, basis * lanes : (basis + 1) * lanes] = over[
                :, row * lanes : (row + 1) * lanes
            ]
    mixed = jnp.dot(spread[...], squares_ref[...], preferred_element_type=F32).astype(BF16)
    for row in range(rows):
        out_ref[:, row] = mixed[row * points : (row + 1) * points].reshape(peers, step, lanes)


def tail_kernel(
    block, back_ref, latent_ref, up_hbm, down_hbm, out_ref, wide, up_ref, down_ref, sems
):
    copies = [
        pltpu.make_async_copy(up_hbm, up_ref, sems.at[0]),
        pltpu.make_async_copy(down_hbm, down_ref, sems.at[1]),
    ]
    for copy in copies:
        copy.start()
    peers, rows, step, lanes = back_ref.shape
    width, _, chans = latent_ref.shape
    wide[...] = jnp.zeros_like(wide)
    gap = jnp.zeros((rows * step, chans - lanes), F32)
    turned = None
    for peer in range(peers):
        piece = back_ref[peer].astype(F32).reshape(rows * step, lanes)
        piece = jnp.concatenate([piece, gap], axis=1)
        piece = pltpu.roll(piece, peer * block, 1) if peer else piece
        turned = piece if turned is None else turned + piece
    for row in range(rows):
        wide[row * step : row * step + width] = latent_ref[:, row, :].astype(F32)
    summed = (wide[...] + turned).astype(BF16).astype(F32)
    centred = summed - jnp.mean(summed, axis=1, keepdims=True)
    spread = jnp.mean(centred * centred, axis=1, keepdims=True)
    normed = (centred * lax.rsqrt(spread + 1e-05)).astype(BF16)
    copies[0].wait()
    hidden = jnp.dot(normed, up_ref[...], preferred_element_type=F32)
    hidden = (0.5 * hidden * (1.0 + lax.erf(hidden * 0.5**0.5))).astype(BF16)
    copies[1].wait()
    result = summed + jnp.dot(hidden, down_ref[...], preferred_element_type=F32)
    for row in range(rows):
        out_ref[:, row, :] = result[row * step : row * step + width].astype(BF16)


def neighbours(block):
    count = lax.axis_size("lat")
    swaps = []
    for start in (0, 1):
        pairs = [(i, i + 1) for i in range(start, count - 1, 2)]
        swaps.append(lax.ppermute(block, "lat", pairs + [(b, a) for a, b in pairs]))
    return swaps


VMEM = pl.BlockSpec(memory_space=pltpu.VMEM)
SMEM = pl.BlockSpec(memory_space=pltpu.SMEM)
ANY = pl.BlockSpec(memory_space=pl.ANY)


def local(latent, lon_filter, mix_weight, band_weight, offsets, w_up, w_down):
    rows, width, chans = latent.shape
    bases, lons = lon_filter.shape
    block, group = mix_weight.shape[1:]
    peers = lons // width
    assert rows == 2 and band_weight.shape[2] == 3
    step = up_to(width, SUBLANES)
    lanes = up_to(block, LANES)
    places = peers * step
    params = pltpu.CompilerParams(vmem_limit_bytes=24 * 2**20)
    lon_first = jnp.transpose(latent, (1, 0, 2))
    tiles = jax.ShapeDtypeStruct((peers, rows, step, lanes), BF16)

    packed = pl.pallas_call(
        functools.partial(pack_kernel, block),
        out_shape=tiles,
        in_specs=[VMEM],
        out_specs=VMEM,
        scratch_shapes=[pltpu.VMEM((step, chans), F32)],
        compiler_params=params,
        cost_estimate=pl.CostEstimate(flops=10**10, bytes_accessed=10**6, transcendentals=0),
        name="pack",
    )(lon_first)
    own = lax.all_to_all(packed, "lon", split_axis=0, concat_axis=0, tiled=True)
    table, squares = pl.pallas_call(
        functools.partial(tables_kernel, width),
        out_shape=(
            jax.ShapeDtypeStruct((bases, places, places), BF16),
            jax.ShapeDtypeStruct((bases * lanes, lanes), BF16),
        ),
        in_specs=[VMEM] * 2,
        out_specs=(VMEM, VMEM),
        scratch_shapes=[
            pltpu.VMEM((bases, step, places), F32),
            pltpu.VMEM((bases, up_to(group, SUBLANES), lanes), F32),
        ],
        compiler_params=params,
        cost_estimate=pl.CostEstimate(flops=10**9, bytes_accessed=10**6, transcendentals=0),
        name="tables",
    )(lon_filter, jnp.transpose(mix_weight, (0, 2, 1)))
    even, other = neighbours(own)
    odd = (lax.axis_index("lat") % 2).astype(jnp.int32).reshape(1)
    band = jnp.transpose(band_weight, (2, 1, 0))
    mixed = pl.pallas_call(
        conv_kernel,
        out_shape=tiles,
        in_specs=[SMEM] + [VMEM] * 6,
        out_specs=VMEM,
        scratch_shapes=[pltpu.VMEM((rows * places, bases * lanes), BF16)],
        compiler_params=params,
        cost_estimate=pl.CostEstimate(
            flops=2 * 10**10, bytes_accessed=10**7, transcendentals=0
        ),
        name="conv",
    )(odd, band, own, even, other, table, squares)
    back = lax.all_to_all(mixed, "lon", split_axis=0, concat_axis=0, tiled=True)
    result = pl.pallas_call(
        functools.partial(tail_kernel, block),
        out_shape=jax.ShapeDtypeStruct(lon_first.shape, BF16),
        in_specs=[VMEM] * 2 + [ANY] * 2,
        out_specs=VMEM,
        scratch_shapes=[
            pltpu.VMEM((rows * step, chans), F32),
            pltpu.VMEM(w_up.shape, BF16),
            pltpu.VMEM(w_down.shape, BF16),
            pltpu.SemaphoreType.DMA((2,)),
        ],
        compiler_params=params,
        name="tail",
    )(back, lon_first, w_up, w_down)
    return jnp.transpose(result, (1, 0, 2))


def solution(mesh):
    return jax.shard_map(
        local,
        mesh=mesh,
        in_specs=(
            P("lat", "lon", None),
            P(),
            P(None, "lon", None),
            P(None, "lat", None),
            P("lat"),
            P(),
            P(),
        ),
        out_specs=P("lat", "lon", None),
        check_vma=False,
    )
```

```python
import functools

import jax
import jax.numpy as jnp
from jax import lax
from jax.experimental import pallas as pl
from jax.experimental.pallas import tpu as pltpu
from jax.sharding import PartitionSpec as P

F32 = jnp.float32
BF16 = jnp.bfloat16
LANES = 128
SUBLANES = 8


def up_to(size, step):
    return -(-size // step) * step


def column_and_side():
    place = lax.axis_index("lon")
    return place // 2, place % 2


def message_rows(block):
    tiles = block // LANES
    return up_to(3 * SUBLANES * tiles + (SUBLANES if block % LANES else 0), 2 * SUBLANES)


def lanes_of(block):
    return up_to(block, LANES)


def fold(points, block):
    whole, rest = divmod(block, LANES)
    parts = [points[:, tile * LANES : (tile + 1) * LANES] for tile in range(whole)]
    if rest:
        odd = points[:, whole * LANES : (whole + 1) * LANES]
        kept = lax.broadcasted_iota(jnp.int32, (SUBLANES, LANES), 1) < rest
        shared = None
        for third in range(3):
            piece = jnp.where(kept, odd[third * SUBLANES : (third + 1) * SUBLANES], 0.0)
            piece = pltpu.roll(piece, third * rest, 1) if third else piece
            shared = piece if shared is None else shared + piece
        parts.append(shared)
    filled = sum(part.shape[0] for part in parts)
    if message_rows(block) > filled:
        parts.append(jnp.zeros((message_rows(block) - filled, LANES), F32))
    return jnp.concatenate(parts, axis=0).astype(BF16)


def unfold(message, block):
    whole, rest = divmod(block, LANES)
    groups = []
    for third in range(3):
        first = third * SUBLANES
        parts = [
            message[tile * 3 * SUBLANES + first : tile * 3 * SUBLANES + first + SUBLANES]
            for tile in range(whole)
        ]
        if rest:
            odd = message[whole * 3 * SUBLANES : whole * 3 * SUBLANES + SUBLANES]
            parts.append(pltpu.roll(odd, LANES - third * rest, 1) if third else odd)
        groups.append(jnp.concatenate(parts, axis=1) if len(parts) > 1 else parts[0])
    return groups


def group_points(latent_ref, points):
    width, rows, _ = latent_ref.shape
    rest = width - SUBLANES
    for row in range(rows):
        points[row * SUBLANES : (row + 1) * SUBLANES] = latent_ref[:SUBLANES, row, :].astype(F32)
        at = rows * SUBLANES + row * rest
        points[at : at + rest] = latent_ref[SUBLANES:, row, :].astype(F32)


def pack_kernel(latent_ref, *refs):
    *out_refs, points, stage = refs
    columns = len(out_refs)
    chans = latent_ref.shape[2]
    block = chans // columns
    column, _ = column_and_side()
    group_points(latent_ref, points)
    own = points[...]
    for target in range(columns):
        turned = pltpu.roll(own, chans - target * block, 1) if target else own
        stage[target] = fold(turned[:, : lanes_of(block)], block)
    for apart in range(columns):
        out_refs[apart][...] = stage[column ^ apart]


def column_kernel(*refs):
    *in_refs, out_ref = refs
    column, _ = column_and_side()
    for apart, ref in enumerate(in_refs):
        out_ref[column ^ apart] = ref[...]


def sides_kernel(own_ref, mate_ref, out_ref):
    _, side = column_and_side()
    out_ref[:, side] = own_ref[...]
    out_ref[:, 1 - side] = mate_ref[...]


def tables_kernel(width, filter_ref, band_ref, table_ref, first):
    bases, lons = filter_ref.shape
    taps, rows, _ = band_ref.shape
    step, places = first.shape[1:]
    columns = places // (2 * step)
    _, side = column_and_side()
    profile = filter_ref[...]
    band = band_ref[...].astype(F32)
    source = lax.broadcasted_iota(jnp.int32, (lons, places), 0)
    place = lax.broadcasted_iota(jnp.int32, (lons, places), 1)
    within = place % step
    apart = source + (place // step) * width + within + (lons - side * width)
    for _ in range(3):
        apart = jnp.where(apart >= lons, apart - lons, apart)
    apart = jnp.where(within < width, apart, -1)
    first[...] = jnp.zeros_like(first)
    for lon in range(width):
        pick = (apart == lon).astype(F32).astype(BF16)
        first[:, lon, :] = jnp.dot(profile, pick, preferred_element_type=F32)
    for basis in range(bases):
        circle = first[basis]
        for column in range(columns):
            turned = pltpu.roll(circle, column * 2 * step, 1) if column else circle
            at = (basis * columns + column) * step
            for row in range(rows):
                for tap in range(taps):
                    weight = band[tap, row : row + 1, basis : basis + 1]
                    table_ref[row, at : at + step, tap * places : (tap + 1) * places] = (
                        weight * turned
                    ).astype(BF16)


def squares_kernel(own_ref, mate_ref, squares_ref, padded):
    bases, group, half = own_ref.shape
    lanes = squares_ref.shape[1]
    _, side = column_and_side()
    first = side == 0
    own = own_ref[...].astype(F32)
    mate = mate_ref[...].astype(F32)
    padded[...] = jnp.zeros_like(padded)
    padded[0, :, :group, :half] = jnp.where(first, own, mate)
    padded[1, :, :group, :half] = jnp.where(first, mate, own)
    members = padded.shape[2]
    into = lax.broadcasted_iota(jnp.int32, (lanes, members), 0)
    member = lax.broadcasted_iota(jnp.int32, (lanes, members), 1)
    repeat = (into % group == member).astype(F32).astype(BF16)
    row = lax.broadcasted_iota(jnp.int32, (lanes, lanes), 0)
    column = lax.broadcasted_iota(jnp.int32, (lanes, lanes), 1)
    same = (row // group == column // group) & (row < 2 * half) & (column < 2 * half)
    for basis in range(bases):
        weights = padded[0, basis] + pltpu.roll(padded[1, basis], half, 1)
        repeated = jnp.dot(repeat, weights.astype(BF16), preferred_element_type=F32)
        squares_ref[basis * lanes : (basis + 1) * lanes] = jnp.where(same, repeated, 0.0).astype(
            BF16
        )


def conv_kernel(block, width, own_ref, even_ref, other_ref, table_ref, squares_ref, *refs):
    *out_refs, field, spread, stage = refs
    columns = len(out_refs)
    lanes = squares_ref.shape[1]
    bases = squares_ref.shape[0] // lanes
    rows, _, inner = table_ref.shape
    places = inner // 3
    step = places // (2 * columns)
    half = places // 2
    rest = width - SUBLANES
    column, _ = column_and_side()
    odd = lax.axis_index("lat") % 2 == 1
    for at in range(2 * columns):
        own = own_ref[at // 2, at % 2].astype(F32)
        even = even_ref[at // 2, at % 2].astype(F32)
        other = other_ref[at // 2, at % 2].astype(F32)
        low = jnp.where(odd, even, other)
        high = jnp.where(odd, other, even)
        read = []
        for message in (low, own, high):
            groups = unfold(message, block)
            for row in range(rows):
                last = pltpu.roll(groups[2], SUBLANES - row * rest, 0) if row else groups[2]
                read.append(jnp.concatenate([groups[row], last], axis=0).astype(BF16))
        for row in range(rows):
            for tap in range(3):
                first = tap * places + at * step
                field[row, first : first + step] = read[row * 3 + tap]
    for row in range(rows):
        over = jnp.dot(table_ref[row], field[row], preferred_element_type=F32).astype(BF16)
        for basis in range(bases):
            spread[row * half : (row + 1) * half, basis * lanes : (basis + 1) * lanes] = over[
                basis * half : (basis + 1) * half
            ]
    mixed = jnp.dot(spread[...], squares_ref[...], preferred_element_type=F32)
    upper = lax.broadcasted_iota(jnp.int32, (SUBLANES, lanes), 0) < rest
    for target in range(columns):
        top = mixed[target * step : (target + 1) * step]
        bottom = mixed[half + target * step : half + (target + 1) * step]
        last = jnp.where(upper, top[SUBLANES:], pltpu.roll(bottom[SUBLANES:], rest, 0))
        points = jnp.concatenate([top[:SUBLANES], bottom[:SUBLANES], last], axis=0)
        stage[target] = fold(points, block)
    for apart in range(columns):
        out_refs[apart][...] = stage[column ^ apart]


def tail_kernel(columns, *refs):
    back_refs = refs[:columns]
    latent_ref, up_ref, down_ref, out_ref, points, stage = refs[columns:]
    width, rows, chans = latent_ref.shape
    rest = width - SUBLANES
    block = chans // columns
    lanes = lanes_of(block)
    column, _ = column_and_side()
    for apart in range(columns):
        stage[column ^ apart] = back_refs[apart][...]
    group_points(latent_ref, points)
    kept = lax.broadcasted_iota(jnp.int32, (3 * SUBLANES, lanes), 1) < block
    convolved = None
    for target in range(columns):
        piece = jnp.concatenate(unfold(stage[target].astype(F32), block), axis=0)
        piece = jnp.where(kept, piece, 0.0)
        if chans > lanes:
            gap = jnp.zeros((3 * SUBLANES, chans - lanes), F32)
            piece = jnp.concatenate([piece, gap], axis=1)
        piece = pltpu.roll(piece, target * block, 1) if target else piece
        convolved = piece if convolved is None else convolved + piece
    summed = (points[...] + convolved).astype(BF16).astype(F32)
    centred = summed - jnp.mean(summed, axis=1, keepdims=True)
    variance = jnp.mean(centred * centred, axis=1, keepdims=True)
    normed = (centred * lax.rsqrt(variance + 1e-05)).astype(BF16)
    hidden = jnp.dot(normed, up_ref[...], preferred_element_type=F32)
    hidden = (0.5 * hidden * (1.0 + lax.erf(hidden * 0.5**0.5))).astype(BF16)
    result = summed + jnp.dot(hidden, down_ref[...], preferred_element_type=F32)
    for row in range(rows):
        out_ref[:SUBLANES, row, :] = result[row * SUBLANES : (row + 1) * SUBLANES].astype(BF16)
        at = rows * SUBLANES + row * rest
        out_ref[SUBLANES:, row, :] = result[at : at + rest].astype(BF16)


VMEM = pl.BlockSpec(memory_space=pltpu.VMEM)


def call(kernel, name, out_shape, scratch, work, *operands):
    several = isinstance(out_shape, tuple)
    return pl.pallas_call(
        kernel,
        out_shape=out_shape,
        in_specs=[VMEM] * len(operands),
        out_specs=(VMEM,) * len(out_shape) if several else VMEM,
        scratch_shapes=scratch,
        compiler_params=pltpu.CompilerParams(vmem_limit_bytes=24 * 2**20),
        cost_estimate=pl.CostEstimate(flops=work, bytes_accessed=10**6, transcendentals=0),
        name=name,
    )(*operands)


def over_columns(messages, count):
    arrived = []
    for apart in range(1, count // 2):
        pairs = [(i, ((i // 2) ^ apart) * 2 + i % 2) for i in range(count)]
        arrived.append(lax.ppermute(messages[apart], "lon", pairs))
    return [messages[0]] + arrived


def over_sides(block, count):
    return lax.ppermute(block, "lon", [(i, i ^ 1) for i in range(count)])


def over_rows(block):
    count = lax.axis_size("lat")
    swaps = []
    for start in (0, 1):
        pairs = [(i, i + 1) for i in range(start, count - 1, 2)]
        swaps.append(lax.ppermute(block, "lat", pairs + [(b, a) for a, b in pairs]))
    return swaps


def local(latent, lon_filter, mix_weight, band_weight, offsets, w_up, w_down):
    rows, width, chans = latent.shape
    bases, lons = lon_filter.shape
    half, group = mix_weight.shape[1:]
    taps = band_weight.shape[2]
    count = lons // width
    columns = count // 2
    block = 2 * half
    step = up_to(width, 2 * SUBLANES)
    places = count * step
    lanes = lanes_of(block)
    height = message_rows(block)
    assert rows == 2 and taps == 3 and columns & (columns - 1) == 0
    assert SUBLANES < width and rows * (width - SUBLANES) <= SUBLANES
    assert 3 * (block % LANES) <= LANES

    message = jax.ShapeDtypeStruct((height, LANES), BF16)
    messages = (message,) * columns
    stage = pltpu.VMEM((columns, height, LANES), BF16)
    points = pltpu.VMEM((3 * SUBLANES, chans), F32)
    lon_first = jnp.transpose(latent, (1, 0, 2))
    mix_own = jnp.transpose(mix_weight, (0, 2, 1))

    packed = call(pack_kernel, "pack", messages, [points, stage], 10**9, lon_first)
    arrived = over_columns(packed, count)
    mix_mate = over_sides(mix_own, count)
    table = call(
        functools.partial(tables_kernel, width),
        "tables",
        jax.ShapeDtypeStruct((rows, bases * places // 2, taps * places), BF16),
        [pltpu.VMEM((bases, step, places), F32)],
        10**9,
        lon_filter,
        jnp.transpose(band_weight, (2, 1, 0)),
    )
    squares = call(
        squares_kernel,
        "squares",
        jax.ShapeDtypeStruct((bases * lanes, lanes), BF16),
        [pltpu.VMEM((2, bases, up_to(group, 2 * SUBLANES), lanes), F32)],
        10**9,
        mix_own,
        mix_mate,
    )
    gathered = jax.ShapeDtypeStruct((columns, height, LANES), BF16)
    own_side = call(column_kernel, "join_columns", gathered, [], 10**8, *arrived)
    mate_side = over_sides(own_side, count)
    circle = jax.ShapeDtypeStruct((columns, 2, height, LANES), BF16)
    own = call(sides_kernel, "join_sides", circle, [], 10**8, own_side, mate_side)
    even, other = over_rows(own)
    mixed = call(
        functools.partial(conv_kernel, block, width),
        "conv",
        messages,
        [
            pltpu.VMEM((rows, taps * places, lanes), BF16),
            pltpu.VMEM((rows * places // 2, bases * lanes), BF16),
            stage,
        ],
        10**10,
        own,
        even,
        other,
        table,
        squares,
    )
    back = over_columns(mixed, count)
    result = call(
        functools.partial(tail_kernel, columns),
        "tail",
        jax.ShapeDtypeStruct(lon_first.shape, BF16),
        [points, stage],
        10**9,
        *back,
        lon_first,
        w_up,
        w_down,
    )
    return jnp.transpose(result, (1, 0, 2))


def solution(mesh):
    return jax.shard_map(
        local,
        mesh=mesh,
        in_specs=(
            P("lat", "lon", None),
            P(),
            P(None, "lon", None),
            P(None, "lat", None),
            P("lat"),
            P(),
            P(),
        ),
        out_specs=P("lat", "lon", None),
        check_vma=False,
    )
```

```python
import functools

import jax
import jax.numpy as jnp
from jax import lax
from jax.experimental import pallas as pl
from jax.experimental.pallas import tpu as pltpu
from jax.sharding import PartitionSpec as P

F32 = jnp.float32
BF16 = jnp.bfloat16
LANES = 128
SUBLANES = 8


def up_to(size, step):
    return -(-size // step) * step


def column_and_side():
    place = lax.axis_index("lon")
    return place // 2, place % 2


def message_rows(block):
    tiles = block // LANES
    return up_to(3 * SUBLANES * tiles + (SUBLANES if block % LANES else 0), 2 * SUBLANES)


def lanes_of(block):
    return up_to(block, LANES)


def fold(points, block):
    whole, rest = divmod(block, LANES)
    parts = [points[:, tile * LANES : (tile + 1) * LANES] for tile in range(whole)]
    if rest:
        odd = points[:, whole * LANES : (whole + 1) * LANES]
        kept = lax.broadcasted_iota(jnp.int32, (SUBLANES, LANES), 1) < rest
        shared = None
        for third in range(3):
            piece = jnp.where(kept, odd[third * SUBLANES : (third + 1) * SUBLANES], 0.0)
            piece = pltpu.roll(piece, third * rest, 1) if third else piece
            shared = piece if shared is None else shared + piece
        parts.append(shared)
    filled = sum(part.shape[0] for part in parts)
    if message_rows(block) > filled:
        parts.append(jnp.zeros((message_rows(block) - filled, LANES), F32))
    return jnp.concatenate(parts, axis=0).astype(BF16)


def unfold(message, block):
    whole, rest = divmod(block, LANES)
    groups = []
    for third in range(3):
        first = third * SUBLANES
        parts = [
            message[tile * 3 * SUBLANES + first : tile * 3 * SUBLANES + first + SUBLANES]
            for tile in range(whole)
        ]
        if rest:
            odd = message[whole * 3 * SUBLANES : whole * 3 * SUBLANES + SUBLANES]
            parts.append(pltpu.roll(odd, LANES - third * rest, 1) if third else odd)
        groups.append(jnp.concatenate(parts, axis=1) if len(parts) > 1 else parts[0])
    return groups


def group_points(latent_ref, points):
    width, rows, _ = latent_ref.shape
    rest = width - SUBLANES
    for row in range(rows):
        points[row * SUBLANES : (row + 1) * SUBLANES] = latent_ref[:SUBLANES, row, :].astype(F32)
        at = rows * SUBLANES + row * rest
        points[at : at + rest] = latent_ref[SUBLANES:, row, :].astype(F32)


def pack_kernel(latent_ref, *refs):
    *out_refs, points, stage = refs
    columns = len(out_refs)
    chans = latent_ref.shape[2]
    block = chans // columns
    column, _ = column_and_side()
    group_points(latent_ref, points)
    own = points[...]
    for target in range(columns):
        turned = pltpu.roll(own, chans - target * block, 1) if target else own
        stage[target] = fold(turned[:, : lanes_of(block)], block)
    for apart in range(columns):
        out_refs[apart][...] = stage[column ^ apart]


def column_kernel(*refs):
    *in_refs, out_ref = refs
    column, _ = column_and_side()
    for apart, ref in enumerate(in_refs):
        out_ref[column ^ apart] = ref[...]


def tables_kernel(width, filter_ref, band_ref, table_ref, first):
    bases, lons = filter_ref.shape
    taps, rows, _ = band_ref.shape
    step, places = first.shape[1:]
    columns = places // (2 * step)
    _, side = column_and_side()
    lat = lax.axis_index("lat")
    below = (lat > 0).astype(F32)
    above = (lat < lax.axis_size("lat") - 1).astype(F32)
    inside = [[below, below, 1.0], [1.0, above, above]]
    profile = filter_ref[...]
    band = band_ref[...].astype(F32)
    source = lax.broadcasted_iota(jnp.int32, (lons, places), 0)
    place = lax.broadcasted_iota(jnp.int32, (lons, places), 1)
    within = place % step
    apart = source + (place // step) * width + within + (lons - side * width)
    for _ in range(3):
        apart = jnp.where(apart >= lons, apart - lons, apart)
    apart = jnp.where(within < width, apart, -1)
    first[...] = jnp.zeros_like(first)
    for lon in range(width):
        pick = (apart == lon).astype(F32).astype(BF16)
        first[:, lon, :] = jnp.dot(profile, pick, preferred_element_type=F32)
    for basis in range(bases):
        circle = first[basis]
        for column in range(columns):
            turned = pltpu.roll(circle, column * 2 * step, 1) if column else circle
            at = (basis * columns + column) * step
            for row in range(rows):
                for tap in range(taps):
                    weight = band[tap, row : row + 1, basis : basis + 1] * inside[row][tap]
                    table_ref[row, at : at + step, tap * places : (tap + 1) * places] = (
                        weight * turned
                    ).astype(BF16)


def squares_kernel(own_ref, mate_ref, squares_ref, padded):
    bases, group, half = own_ref.shape
    lanes = squares_ref.shape[1]
    _, side = column_and_side()
    first = side == 0
    own = own_ref[...].astype(F32)
    mate = mate_ref[...].astype(F32)
    padded[...] = jnp.zeros_like(padded)
    padded[0, :, :group, :half] = jnp.where(first, own, mate)
    padded[1, :, :group, :half] = jnp.where(first, mate, own)
    members = padded.shape[2]
    into = lax.broadcasted_iota(jnp.int32, (lanes, members), 0)
    member = lax.broadcasted_iota(jnp.int32, (lanes, members), 1)
    repeat = (into % group == member).astype(F32).astype(BF16)
    row = lax.broadcasted_iota(jnp.int32, (lanes, lanes), 0)
    column = lax.broadcasted_iota(jnp.int32, (lanes, lanes), 1)
    same = (row // group == column // group) & (row < 2 * half) & (column < 2 * half)
    for basis in range(bases):
        weights = padded[0, basis] + pltpu.roll(padded[1, basis], half, 1)
        repeated = jnp.dot(repeat, weights.astype(BF16), preferred_element_type=F32)
        squares_ref[basis * lanes : (basis + 1) * lanes] = jnp.where(same, repeated, 0.0).astype(
            BF16
        )


def conv_kernel(block, width, *refs):
    sources, (table_ref, squares_ref), refs = refs[:6], refs[6:8], refs[8:]
    *out_refs, field, spread, stage = refs
    columns = len(out_refs)
    lanes = squares_ref.shape[1]
    bases = squares_ref.shape[0] // lanes
    rows, _, inner = table_ref.shape
    places = inner // 3
    step = places // (2 * columns)
    half = places // 2
    rest = width - SUBLANES
    column, side = column_and_side()
    odd = lax.axis_index("lat") % 2 == 1
    for at in range(2 * columns):
        here = side == at % 2
        own, even, other = (
            jnp.where(here, near[at // 2].astype(F32), far[at // 2].astype(F32))
            for near, far in zip(sources[::2], sources[1::2])
        )
        low = jnp.where(odd, even, other)
        high = jnp.where(odd, other, even)
        read = []
        for message in (low, own, high):
            groups = unfold(message, block)
            for row in range(rows):
                last = pltpu.roll(groups[2], SUBLANES - row * rest, 0) if row else groups[2]
                read.append(jnp.concatenate([groups[row], last], axis=0).astype(BF16))
        for row in range(rows):
            for tap in range(3):
                first = tap * places + at * step
                field[row, first : first + step] = read[row * 3 + tap]
    for row in range(rows):
        over = jnp.dot(table_ref[row], field[row], preferred_element_type=F32).astype(BF16)
        for basis in range(bases):
            spread[row * half : (row + 1) * half, basis * lanes : (basis + 1) * lanes] = over[
                basis * half : (basis + 1) * half
            ]
    mixed = jnp.dot(spread[...], squares_ref[...], preferred_element_type=F32)
    upper = lax.broadcasted_iota(jnp.int32, (SUBLANES, lanes), 0) < rest
    for target in range(columns):
        top = mixed[target * step : (target + 1) * step]
        bottom = mixed[half + target * step : half + (target + 1) * step]
        last = jnp.where(upper, top[SUBLANES:], pltpu.roll(bottom[SUBLANES:], rest, 0))
        points = jnp.concatenate([top[:SUBLANES], bottom[:SUBLANES], last], axis=0)
        stage[target] = fold(points, block)
    for apart in range(columns):
        out_refs[apart][...] = stage[column ^ apart]


def tail_kernel(columns, *refs):
    back_refs = refs[:columns]
    latent_ref, up_ref, down_ref, out_ref, points, stage = refs[columns:]
    width, rows, chans = latent_ref.shape
    rest = width - SUBLANES
    block = chans // columns
    lanes = lanes_of(block)
    column, _ = column_and_side()
    for apart in range(columns):
        stage[column ^ apart] = back_refs[apart][...]
    group_points(latent_ref, points)
    kept = lax.broadcasted_iota(jnp.int32, (3 * SUBLANES, lanes), 1) < block
    convolved = None
    for target in range(columns):
        piece = jnp.concatenate(unfold(stage[target].astype(F32), block), axis=0)
        piece = jnp.where(kept, piece, 0.0)
        if chans > lanes:
            gap = jnp.zeros((3 * SUBLANES, chans - lanes), F32)
            piece = jnp.concatenate([piece, gap], axis=1)
        piece = pltpu.roll(piece, target * block, 1) if target else piece
        convolved = piece if convolved is None else convolved + piece
    summed = (points[...] + convolved).astype(BF16).astype(F32)
    centred = summed - jnp.mean(summed, axis=1, keepdims=True)
    variance = jnp.mean(centred * centred, axis=1, keepdims=True)
    normed = (centred * lax.rsqrt(variance + 1e-05)).astype(BF16)
    hidden = jnp.dot(normed, up_ref[...], preferred_element_type=F32)
    hidden = (0.5 * hidden * (1.0 + lax.erf(hidden * 0.5**0.5))).astype(BF16)
    result = summed + jnp.dot(hidden, down_ref[...], preferred_element_type=F32)
    for row in range(rows):
        out_ref[:SUBLANES, row, :] = result[row * SUBLANES : (row + 1) * SUBLANES].astype(BF16)
        at = rows * SUBLANES + row * rest
        out_ref[SUBLANES:, row, :] = result[at : at + rest].astype(BF16)


VMEM = pl.BlockSpec(memory_space=pltpu.VMEM)


def call(kernel, name, out_shape, scratch, work, *operands):
    several = isinstance(out_shape, tuple)
    return pl.pallas_call(
        kernel,
        out_shape=out_shape,
        in_specs=[VMEM] * len(operands),
        out_specs=(VMEM,) * len(out_shape) if several else VMEM,
        scratch_shapes=scratch,
        compiler_params=pltpu.CompilerParams(vmem_limit_bytes=24 * 2**20),
        cost_estimate=pl.CostEstimate(flops=work, bytes_accessed=10**6, transcendentals=0),
        name=name,
    )(*operands)


def over_columns(messages, count):
    arrived = {0: messages[0]}
    for apart in reversed(range(1, count // 2)):
        pairs = [(i, ((i // 2) ^ apart) * 2 + i % 2) for i in range(count)]
        arrived[apart] = lax.ppermute(messages[apart], "lon", pairs)
    return [arrived[apart] for apart in range(count // 2)]


def over_sides(block, count):
    return lax.ppermute(block, "lon", [(i, i ^ 1) for i in range(count)])


def around(block, count):
    rows = lax.axis_size("lat")
    lat_even = [i ^ 1 for i in range(rows)]
    lat_odd = [((i - 1) ^ 1) + 1 if i else rows - 1 for i in range(rows)]
    lat_odd[rows - 1] = 0
    lat_self = list(range(rows))

    def swap(lat_of, other_side):
        pairs = [
            (lat * count + lon, lat_of[lat] * count + (lon ^ other_side))
            for lat in range(rows)
            for lon in range(count)
        ]
        return lax.ppermute(block, ("lat", "lon"), pairs)

    odd_mate = swap(lat_odd, 1)
    even_mate = swap(lat_even, 1)
    odd_own = swap(lat_odd, 0)
    mate = swap(lat_self, 1)
    even_own = swap(lat_even, 0)
    return mate, even_own, even_mate, odd_own, odd_mate


def local(latent, lon_filter, mix_weight, band_weight, offsets, w_up, w_down):
    rows, width, chans = latent.shape
    bases, lons = lon_filter.shape
    half, group = mix_weight.shape[1:]
    taps = band_weight.shape[2]
    count = lons // width
    columns = count // 2
    block = 2 * half
    step = up_to(width, 2 * SUBLANES)
    places = count * step
    lanes = lanes_of(block)
    height = message_rows(block)
    assert rows == 2 and taps == 3 and columns & (columns - 1) == 0
    assert SUBLANES < width and rows * (width - SUBLANES) <= SUBLANES
    assert 3 * (block % LANES) <= LANES

    message = jax.ShapeDtypeStruct((height, LANES), BF16)
    messages = (message,) * columns
    stage = pltpu.VMEM((columns, height, LANES), BF16)
    points = pltpu.VMEM((3 * SUBLANES, chans), F32)
    lon_first = jnp.transpose(latent, (1, 0, 2))
    mix_own = jnp.transpose(mix_weight, (0, 2, 1))

    packed = call(pack_kernel, "pack", messages, [points, stage], 10**9, lon_first)
    arrived = over_columns(packed, count)
    mix_mate = over_sides(mix_own, count)
    table = call(
        functools.partial(tables_kernel, width),
        "tables",
        jax.ShapeDtypeStruct((rows, bases * places // 2, taps * places), BF16),
        [pltpu.VMEM((bases, step, places), F32)],
        10**9,
        lon_filter,
        jnp.transpose(band_weight, (2, 1, 0)),
    )
    squares = call(
        squares_kernel,
        "squares",
        jax.ShapeDtypeStruct((bases * lanes, lanes), BF16),
        [pltpu.VMEM((2, bases, up_to(group, 2 * SUBLANES), lanes), F32)],
        10**9,
        mix_own,
        mix_mate,
    )
    gathered = jax.ShapeDtypeStruct((columns, height, LANES), BF16)
    own_side = call(column_kernel, "join_columns", gathered, [], 10**8, *arrived)
    sources = around(own_side, count)
    mixed = call(
        functools.partial(conv_kernel, block, width),
        "conv",
        messages,
        [
            pltpu.VMEM((rows, taps * places, lanes), BF16),
            pltpu.VMEM((rows * places // 2, bases * lanes), BF16),
            stage,
        ],
        10**10,
        own_side,
        *sources,
        table,
        squares,
    )
    back = over_columns(mixed, count)
    result = call(
        functools.partial(tail_kernel, columns),
        "tail",
        jax.ShapeDtypeStruct(lon_first.shape, BF16),
        [points, stage],
        10**9,
        *back,
        lon_first,
        w_up,
        w_down,
    )
    return jnp.transpose(result, (1, 0, 2))


def solution(mesh):
    return jax.shard_map(
        local,
        mesh=mesh,
        in_specs=(
            P("lat", "lon", None),
            P(),
            P(None, "lon", None),
            P(None, "lat", None),
            P("lat"),
            P(),
            P(),
        ),
        out_specs=P("lat", "lon", None),
        check_vma=False,
    )
```

```python
import functools

import jax
import jax.numpy as jnp
from jax import lax
from jax.experimental import pallas as pl
from jax.experimental.pallas import tpu as pltpu
from jax.sharding import PartitionSpec as P

F32 = jnp.float32
BF16 = jnp.bfloat16
LANES = 128
SUBLANES = 8


def up_to(size, step):
    return -(-size // step) * step


def message_rows(block):
    tiles = block // LANES
    return up_to(3 * SUBLANES * tiles + (SUBLANES if block % LANES else 0), 2 * SUBLANES)


def lanes_of(block):
    return up_to(block, LANES)


def fold(points, block):
    whole, rest = divmod(block, LANES)
    parts = [points[:, tile * LANES : (tile + 1) * LANES] for tile in range(whole)]
    if rest:
        odd = points[:, whole * LANES : (whole + 1) * LANES]
        kept = lax.broadcasted_iota(jnp.int32, (SUBLANES, LANES), 1) < rest
        shared = None
        for third in range(3):
            piece = jnp.where(kept, odd[third * SUBLANES : (third + 1) * SUBLANES], 0.0)
            piece = pltpu.roll(piece, third * rest, 1) if third else piece
            shared = piece if shared is None else shared + piece
        parts.append(shared)
    filled = sum(part.shape[0] for part in parts)
    if message_rows(block) > filled:
        parts.append(jnp.zeros((message_rows(block) - filled, LANES), F32))
    return jnp.concatenate(parts, axis=0).astype(BF16)


def unfold(message, block):
    whole, rest = divmod(block, LANES)
    groups = []
    for third in range(3):
        first = third * SUBLANES
        parts = [
            message[tile * 3 * SUBLANES + first : tile * 3 * SUBLANES + first + SUBLANES]
            for tile in range(whole)
        ]
        if rest:
            odd = message[whole * 3 * SUBLANES : whole * 3 * SUBLANES + SUBLANES]
            parts.append(pltpu.roll(odd, LANES - third * rest, 1) if third else odd)
        groups.append(jnp.concatenate(parts, axis=1) if len(parts) > 1 else parts[0])
    return groups


def group_points(latent_ref, points):
    width, rows, _ = latent_ref.shape
    rest = width - SUBLANES
    for row in range(rows):
        points[row * SUBLANES : (row + 1) * SUBLANES] = latent_ref[:SUBLANES, row, :].astype(F32)
        at = rows * SUBLANES + row * rest
        points[at : at + rest] = latent_ref[SUBLANES:, row, :].astype(F32)


def pack_kernel(latent_ref, out_ref, points):
    columns = out_ref.shape[0]
    chans = latent_ref.shape[2]
    block = chans // columns
    group_points(latent_ref, points)
    own = points[...]
    for target in range(columns):
        turned = pltpu.roll(own, chans - target * block, 1) if target else own
        out_ref[target] = fold(turned[:, : lanes_of(block)], block)


def tables_kernel(width, filter_ref, band_ref, table_ref, first):
    bases, lons = filter_ref.shape
    taps, rows, _ = band_ref.shape
    step, places = first.shape[1:]
    columns = places // (2 * step)
    side = lax.axis_index("lon") % 2
    lat = lax.axis_index("lat")
    below = (lat > 0).astype(F32)
    above = (lat < lax.axis_size("lat") - 1).astype(F32)
    inside = [[below, below, 1.0], [1.0, above, above]]
    profile = filter_ref[...]
    band = band_ref[...].astype(F32)
    source = lax.broadcasted_iota(jnp.int32, (lons, places), 0)
    place = lax.broadcasted_iota(jnp.int32, (lons, places), 1)
    within = place % step
    apart = source + (place // step) * width + within + (lons - side * width)
    for _ in range(3):
        apart = jnp.where(apart >= lons, apart - lons, apart)
    apart = jnp.where(within < width, apart, -1)
    first[...] = jnp.zeros_like(first)
    for lon in range(width):
        pick = (apart == lon).astype(F32).astype(BF16)
        first[:, lon, :] = jnp.dot(profile, pick, preferred_element_type=F32)
    for basis in range(bases):
        circle = first[basis]
        for column in range(columns):
            turned = pltpu.roll(circle, column * 2 * step, 1) if column else circle
            at = (basis * columns + column) * step
            for row in range(rows):
                for tap in range(taps):
                    weight = band[tap, row : row + 1, basis : basis + 1] * inside[row][tap]
                    table_ref[row, at : at + step, tap * places : (tap + 1) * places] = (
                        weight * turned
                    ).astype(BF16)


def squares_kernel(own_ref, mate_ref, squares_ref, padded):
    bases, group, half = own_ref.shape
    lanes = squares_ref.shape[1]
    side = lax.axis_index("lon") % 2
    first = side == 0
    own = own_ref[...].astype(F32)
    mate = mate_ref[...].astype(F32)
    padded[...] = jnp.zeros_like(padded)
    padded[0, :, :group, :half] = jnp.where(first, own, mate)
    padded[1, :, :group, :half] = jnp.where(first, mate, own)
    members = padded.shape[2]
    into = lax.broadcasted_iota(jnp.int32, (lanes, members), 0)
    member = lax.broadcasted_iota(jnp.int32, (lanes, members), 1)
    repeat = (into % group == member).astype(F32).astype(BF16)
    row = lax.broadcasted_iota(jnp.int32, (lanes, lanes), 0)
    column = lax.broadcasted_iota(jnp.int32, (lanes, lanes), 1)
    same = (row // group == column // group) & (row < 2 * half) & (column < 2 * half)
    for basis in range(bases):
        weights = padded[0, basis] + pltpu.roll(padded[1, basis], half, 1)
        repeated = jnp.dot(repeat, weights.astype(BF16), preferred_element_type=F32)
        squares_ref[basis * lanes : (basis + 1) * lanes] = jnp.where(same, repeated, 0.0).astype(
            BF16
        )


def conv_kernel(block, width, *refs):
    sources, (table_ref, squares_ref), refs = refs[:6], refs[6:8], refs[8:]
    out_ref, field, spread = refs
    columns = out_ref.shape[0]
    lanes = squares_ref.shape[1]
    bases = squares_ref.shape[0] // lanes
    rows, _, inner = table_ref.shape
    places = inner // 3
    step = places // (2 * columns)
    half = places // 2
    rest = width - SUBLANES
    side = lax.axis_index("lon") % 2
    odd = lax.axis_index("lat") % 2 == 1
    for at in range(2 * columns):
        here = side == at % 2
        own, even, other = (
            jnp.where(here, near[at // 2].astype(F32), far[at // 2].astype(F32))
            for near, far in zip(sources[::2], sources[1::2])
        )
        low = jnp.where(odd, even, other)
        high = jnp.where(odd, other, even)
        read = []
        for message in (low, own, high):
            groups = unfold(message, block)
            for row in range(rows):
                last = pltpu.roll(groups[2], SUBLANES - row * rest, 0) if row else groups[2]
                read.append(jnp.concatenate([groups[row], last], axis=0).astype(BF16))
        for row in range(rows):
            for tap in range(3):
                first = tap * places + at * step
                field[row, first : first + step] = read[row * 3 + tap]
    for row in range(rows):
        over = jnp.dot(table_ref[row], field[row], preferred_element_type=F32).astype(BF16)
        for basis in range(bases):
            spread[row * half : (row + 1) * half, basis * lanes : (basis + 1) * lanes] = over[
                basis * half : (basis + 1) * half
            ]
    mixed = jnp.dot(spread[...], squares_ref[...], preferred_element_type=F32)
    upper = lax.broadcasted_iota(jnp.int32, (SUBLANES, lanes), 0) < rest
    for target in range(columns):
        top = mixed[target * step : (target + 1) * step]
        bottom = mixed[half + target * step : half + (target + 1) * step]
        last = jnp.where(upper, top[SUBLANES:], pltpu.roll(bottom[SUBLANES:], rest, 0))
        points = jnp.concatenate([top[:SUBLANES], bottom[:SUBLANES], last], axis=0)
        out_ref[target] = fold(points, block)


def tail_kernel(back_ref, latent_ref, up_ref, down_ref, out_ref, points):
    columns = back_ref.shape[0]
    width, rows, chans = latent_ref.shape
    rest = width - SUBLANES
    block = chans // columns
    lanes = lanes_of(block)
    group_points(latent_ref, points)
    kept = lax.broadcasted_iota(jnp.int32, (3 * SUBLANES, lanes), 1) < block
    convolved = None
    for target in range(columns):
        piece = jnp.concatenate(unfold(back_ref[target].astype(F32), block), axis=0)
        piece = jnp.where(kept, piece, 0.0)
        if chans > lanes:
            gap = jnp.zeros((3 * SUBLANES, chans - lanes), F32)
            piece = jnp.concatenate([piece, gap], axis=1)
        piece = pltpu.roll(piece, target * block, 1) if target else piece
        convolved = piece if convolved is None else convolved + piece
    summed = (points[...] + convolved).astype(BF16).astype(F32)
    centred = summed - jnp.mean(summed, axis=1, keepdims=True)
    variance = jnp.mean(centred * centred, axis=1, keepdims=True)
    normed = (centred * lax.rsqrt(variance + 1e-05)).astype(BF16)
    hidden = jnp.dot(normed, up_ref[...], preferred_element_type=F32)
    hidden = (0.5 * hidden * (1.0 + lax.erf(hidden * 0.5**0.5))).astype(BF16)
    result = summed + jnp.dot(hidden, down_ref[...], preferred_element_type=F32)
    for row in range(rows):
        out_ref[:SUBLANES, row, :] = result[row * SUBLANES : (row + 1) * SUBLANES].astype(BF16)
        at = rows * SUBLANES + row * rest
        out_ref[SUBLANES:, row, :] = result[at : at + rest].astype(BF16)


VMEM = pl.BlockSpec(memory_space=pltpu.VMEM)


def call(kernel, name, out_shape, scratch, work, *operands):
    several = isinstance(out_shape, tuple)
    return pl.pallas_call(
        kernel,
        out_shape=out_shape,
        in_specs=[VMEM] * len(operands),
        out_specs=(VMEM,) * len(out_shape) if several else VMEM,
        scratch_shapes=scratch,
        compiler_params=pltpu.CompilerParams(vmem_limit_bytes=24 * 2**20),
        cost_estimate=pl.CostEstimate(flops=work, bytes_accessed=10**6, transcendentals=0),
        name=name,
    )(*operands)


def over_columns(messages, count):
    groups = [list(range(side, count, 2)) for side in range(2)]
    return lax.all_to_all(
        messages, "lon", split_axis=0, concat_axis=0, axis_index_groups=groups, tiled=True
    )


def over_sides(block, count):
    return lax.ppermute(block, "lon", [(i, i ^ 1) for i in range(count)])


def around(block, count):
    rows = lax.axis_size("lat")
    lat_even = [i ^ 1 for i in range(rows)]
    lat_odd = [((i - 1) ^ 1) + 1 if i else rows - 1 for i in range(rows)]
    lat_odd[rows - 1] = 0
    lat_self = list(range(rows))

    def swap(lat_of, other_side):
        pairs = [
            (lat * count + lon, lat_of[lat] * count + (lon ^ other_side))
            for lat in range(rows)
            for lon in range(count)
        ]
        return lax.ppermute(block, ("lat", "lon"), pairs)

    odd_mate = swap(lat_odd, 1)
    even_mate = swap(lat_even, 1)
    odd_own = swap(lat_odd, 0)
    mate = swap(lat_self, 1)
    even_own = swap(lat_even, 0)
    return mate, even_own, even_mate, odd_own, odd_mate


def local(latent, lon_filter, mix_weight, band_weight, offsets, w_up, w_down):
    rows, width, chans = latent.shape
    bases, lons = lon_filter.shape
    half, group = mix_weight.shape[1:]
    taps = band_weight.shape[2]
    count = lons // width
    columns = count // 2
    block = 2 * half
    step = up_to(width, 2 * SUBLANES)
    places = count * step
    lanes = lanes_of(block)
    height = message_rows(block)
    assert rows == 2 and taps == 3 and count % 2 == 0
    assert SUBLANES < width and rows * (width - SUBLANES) <= SUBLANES
    assert 3 * (block % LANES) <= LANES

    messages = jax.ShapeDtypeStruct((columns, height, LANES), BF16)
    points = pltpu.VMEM((3 * SUBLANES, chans), F32)
    lon_first = jnp.transpose(latent, (1, 0, 2))
    mix_own = jnp.transpose(mix_weight, (0, 2, 1))

    packed = call(pack_kernel, "pack", messages, [points], 10**9, lon_first)
    own_side = over_columns(packed, count)
    mix_mate = over_sides(mix_own, count)
    table = call(
        functools.partial(tables_kernel, width),
        "tables",
        jax.ShapeDtypeStruct((rows, bases * places // 2, taps * places), BF16),
        [pltpu.VMEM((bases, step, places), F32)],
        10**9,
        lon_filter,
        jnp.transpose(band_weight, (2, 1, 0)),
    )
    squares = call(
        squares_kernel,
        "squares",
        jax.ShapeDtypeStruct((bases * lanes, lanes), BF16),
        [pltpu.VMEM((2, bases, up_to(group, 2 * SUBLANES), lanes), F32)],
        10**9,
        mix_own,
        mix_mate,
    )
    sources = around(own_side, count)
    mixed = call(
        functools.partial(conv_kernel, block, width),
        "conv",
        messages,
        [
            pltpu.VMEM((rows, taps * places, lanes), BF16),
            pltpu.VMEM((rows * places // 2, bases * lanes), BF16),
        ],
        10**10,
        own_side,
        *sources,
        table,
        squares,
    )
    back = over_columns(mixed, count)
    result = call(
        tail_kernel,
        "tail",
        jax.ShapeDtypeStruct(lon_first.shape, BF16),
        [points],
        10**9,
        back,
        lon_first,
        w_up,
        w_down,
    )
    return jnp.transpose(result, (1, 0, 2))


def solution(mesh):
    return jax.shard_map(
        local,
        mesh=mesh,
        in_specs=(
            P("lat", "lon", None),
            P(),
            P(None, "lon", None),
            P(None, "lat", None),
            P("lat"),
            P(),
            P(),
        ),
        out_specs=P("lat", "lon", None),
        check_vma=False,
    )
```

```python
import functools

import jax
import jax.numpy as jnp
from jax import lax
from jax.experimental import pallas as pl
from jax.experimental.pallas import tpu as pltpu
from jax.sharding import PartitionSpec as P

F32 = jnp.float32
BF16 = jnp.bfloat16
LANES = 128
SUBLANES = 8


def up_to(size, step):
    return -(-size // step) * step


def column_and_side():
    place = lax.axis_index("lon")
    return place // 2, place % 2


def message_rows(block):
    tiles = block // LANES
    return up_to(3 * SUBLANES * tiles + (SUBLANES if block % LANES else 0), 2 * SUBLANES)


def lanes_of(block):
    return up_to(block, LANES)


def fold(points, block):
    whole, rest = divmod(block, LANES)
    parts = [points[:, tile * LANES : (tile + 1) * LANES] for tile in range(whole)]
    if rest:
        odd = points[:, whole * LANES : (whole + 1) * LANES]
        kept = lax.broadcasted_iota(jnp.int32, (SUBLANES, LANES), 1) < rest
        shared = None
        for third in range(3):
            piece = jnp.where(kept, odd[third * SUBLANES : (third + 1) * SUBLANES], 0.0)
            piece = pltpu.roll(piece, third * rest, 1) if third else piece
            shared = piece if shared is None else shared + piece
        parts.append(shared)
    filled = sum(part.shape[0] for part in parts)
    if message_rows(block) > filled:
        parts.append(jnp.zeros((message_rows(block) - filled, LANES), F32))
    return jnp.concatenate(parts, axis=0).astype(BF16)


def unfold(message, block):
    whole, rest = divmod(block, LANES)
    groups = []
    for third in range(3):
        first = third * SUBLANES
        parts = [
            message[tile * 3 * SUBLANES + first : tile * 3 * SUBLANES + first + SUBLANES]
            for tile in range(whole)
        ]
        if rest:
            odd = message[whole * 3 * SUBLANES : whole * 3 * SUBLANES + SUBLANES]
            parts.append(pltpu.roll(odd, LANES - third * rest, 1) if third else odd)
        groups.append(jnp.concatenate(parts, axis=1) if len(parts) > 1 else parts[0])
    return groups


def group_points(latent_ref, points):
    width, rows, _ = latent_ref.shape
    rest = width - SUBLANES
    for row in range(rows):
        points[row * SUBLANES : (row + 1) * SUBLANES] = latent_ref[:SUBLANES, row, :].astype(F32)
        at = rows * SUBLANES + row * rest
        points[at : at + rest] = latent_ref[SUBLANES:, row, :].astype(F32)


def pack_kernel(latent_ref, *refs):
    *out_refs, points, stage = refs
    columns = len(out_refs)
    chans = latent_ref.shape[2]
    block = chans // columns
    column, _ = column_and_side()
    group_points(latent_ref, points)
    own = points[...]
    for target in range(columns):
        turned = pltpu.roll(own, chans - target * block, 1) if target else own
        stage[target] = fold(turned[:, : lanes_of(block)], block)
    for apart in range(columns):
        out_refs[apart][...] = stage[column ^ apart]


def column_kernel(order, *refs):
    *in_refs, out_ref = refs
    column, _ = column_and_side()
    for apart, ref in zip(order, in_refs):
        out_ref[column ^ apart] = ref[...]


def tables_kernel(width, filter_ref, band_ref, table_ref, first):
    bases, lons = filter_ref.shape
    taps, rows, _ = band_ref.shape
    step, places = first.shape[1:]
    columns = places // (2 * step)
    _, side = column_and_side()
    lat = lax.axis_index("lat")
    below = (lat > 0).astype(F32)
    above = (lat < lax.axis_size("lat") - 1).astype(F32)
    inside = [[below, below, 1.0], [1.0, above, above]]
    profile = filter_ref[...]
    band = band_ref[...].astype(F32)
    source = lax.broadcasted_iota(jnp.int32, (lons, places), 0)
    place = lax.broadcasted_iota(jnp.int32, (lons, places), 1)
    within = place % step
    apart = source + (place // step) * width + within + (lons - side * width)
    for _ in range(3):
        apart = jnp.where(apart >= lons, apart - lons, apart)
    apart = jnp.where(within < width, apart, -1)
    first[...] = jnp.zeros_like(first)
    for lon in range(width):
        pick = (apart == lon).astype(F32).astype(BF16)
        first[:, lon, :] = jnp.dot(profile, pick, preferred_element_type=F32)
    for basis in range(bases):
        circle = first[basis]
        for column in range(columns):
            turned = pltpu.roll(circle, column * 2 * step, 1) if column else circle
            at = (basis * columns + column) * step
            for row in range(rows):
                for tap in range(taps):
                    weight = band[tap, row : row + 1, basis : basis + 1] * inside[row][tap]
                    table_ref[row, at : at + step, tap * places : (tap + 1) * places] = (
                        weight * turned
                    ).astype(BF16)


def squares_kernel(own_ref, mate_ref, squares_ref, padded):
    bases, group, half = own_ref.shape
    lanes = squares_ref.shape[1]
    _, side = column_and_side()
    first = side == 0
    own = own_ref[...].astype(F32)
    mate = mate_ref[...].astype(F32)
    padded[...] = jnp.zeros_like(padded)
    padded[0, :, :group, :half] = jnp.where(first, own, mate)
    padded[1, :, :group, :half] = jnp.where(first, mate, own)
    members = padded.shape[2]
    into = lax.broadcasted_iota(jnp.int32, (lanes, members), 0)
    member = lax.broadcasted_iota(jnp.int32, (lanes, members), 1)
    repeat = (into % group == member).astype(F32).astype(BF16)
    row = lax.broadcasted_iota(jnp.int32, (lanes, lanes), 0)
    column = lax.broadcasted_iota(jnp.int32, (lanes, lanes), 1)
    same = (row // group == column // group) & (row < 2 * half) & (column < 2 * half)
    for basis in range(bases):
        weights = padded[0, basis] + pltpu.roll(padded[1, basis], half, 1)
        repeated = jnp.dot(repeat, weights.astype(BF16), preferred_element_type=F32)
        squares_ref[basis * lanes : (basis + 1) * lanes] = jnp.where(same, repeated, 0.0).astype(
            BF16
        )


def conv_kernel(block, width, *refs):
    odd_mate, odd_own, even_mate, mate, even_own, home = refs[:6]
    (table_ref, squares_ref), refs = refs[6:8], refs[8:]
    sources = ((home, mate), (even_own, even_mate), (odd_own, odd_mate))
    *out_refs, field, spread, stage = refs
    columns = len(out_refs)
    lanes = squares_ref.shape[1]
    bases = squares_ref.shape[0] // lanes
    rows, _, inner = table_ref.shape
    places = inner // 3
    step = places // (2 * columns)
    half = places // 2
    rest = width - SUBLANES
    column, side = column_and_side()
    odd = lax.axis_index("lat") % 2 == 1
    for at in range(2 * columns):
        here = side == at % 2
        own, even, other = (
            jnp.where(here, near[at // 2].astype(F32), far[at // 2].astype(F32))
            for near, far in sources
        )
        low = jnp.where(odd, even, other)
        high = jnp.where(odd, other, even)
        read = []
        for message in (low, own, high):
            groups = unfold(message, block)
            for row in range(rows):
                last = pltpu.roll(groups[2], SUBLANES - row * rest, 0) if row else groups[2]
                read.append(jnp.concatenate([groups[row], last], axis=0).astype(BF16))
        for row in range(rows):
            for tap in range(3):
                first = tap * places + at * step
                field[row, first : first + step] = read[row * 3 + tap]
    for row in range(rows):
        over = jnp.dot(table_ref[row], field[row], preferred_element_type=F32).astype(BF16)
        for basis in range(bases):
            spread[row * half : (row + 1) * half, basis * lanes : (basis + 1) * lanes] = over[
                basis * half : (basis + 1) * half
            ]
    mixed = jnp.dot(spread[...], squares_ref[...], preferred_element_type=F32)
    upper = lax.broadcasted_iota(jnp.int32, (SUBLANES, lanes), 0) < rest
    for target in range(columns):
        top = mixed[target * step : (target + 1) * step]
        bottom = mixed[half + target * step : half + (target + 1) * step]
        last = jnp.where(upper, top[SUBLANES:], pltpu.roll(bottom[SUBLANES:], rest, 0))
        points = jnp.concatenate([top[:SUBLANES], bottom[:SUBLANES], last], axis=0)
        stage[target] = fold(points, block)
    for apart in range(columns):
        out_refs[apart][...] = stage[column ^ apart]


def tail_kernel(order, *refs):
    columns = len(order)
    back_refs = refs[:columns]
    latent_ref, up_ref, down_ref, out_ref, points, stage = refs[columns:]
    width, rows, chans = latent_ref.shape
    rest = width - SUBLANES
    block = chans // columns
    lanes = lanes_of(block)
    column, _ = column_and_side()
    for apart, ref in zip(order, back_refs):
        stage[column ^ apart] = ref[...]
    group_points(latent_ref, points)
    kept = lax.broadcasted_iota(jnp.int32, (3 * SUBLANES, lanes), 1) < block
    convolved = None
    for target in range(columns):
        piece = jnp.concatenate(unfold(stage[target].astype(F32), block), axis=0)
        piece = jnp.where(kept, piece, 0.0)
        if chans > lanes:
            gap = jnp.zeros((3 * SUBLANES, chans - lanes), F32)
            piece = jnp.concatenate([piece, gap], axis=1)
        piece = pltpu.roll(piece, target * block, 1) if target else piece
        convolved = piece if convolved is None else convolved + piece
    summed = (points[...] + convolved).astype(BF16).astype(F32)
    centred = summed - jnp.mean(summed, axis=1, keepdims=True)
    variance = jnp.mean(centred * centred, axis=1, keepdims=True)
    normed = (centred * lax.rsqrt(variance + 1e-05)).astype(BF16)
    hidden = jnp.dot(normed, up_ref[...], preferred_element_type=F32)
    hidden = (0.5 * hidden * (1.0 + lax.erf(hidden * 0.5**0.5))).astype(BF16)
    result = summed + jnp.dot(hidden, down_ref[...], preferred_element_type=F32)
    for row in range(rows):
        out_ref[:SUBLANES, row, :] = result[row * SUBLANES : (row + 1) * SUBLANES].astype(BF16)
        at = rows * SUBLANES + row * rest
        out_ref[SUBLANES:, row, :] = result[at : at + rest].astype(BF16)


VMEM = pl.BlockSpec(memory_space=pltpu.VMEM)


def call(kernel, name, out_shape, scratch, work, *operands):
    several = isinstance(out_shape, tuple)
    return pl.pallas_call(
        kernel,
        out_shape=out_shape,
        in_specs=[VMEM] * len(operands),
        out_specs=(VMEM,) * len(out_shape) if several else VMEM,
        scratch_shapes=scratch,
        compiler_params=pltpu.CompilerParams(vmem_limit_bytes=24 * 2**20),
        cost_estimate=pl.CostEstimate(flops=work, bytes_accessed=10**6, transcendentals=0),
        name=name,
    )(*operands)


def over_columns(messages, count):
    arrived = {0: messages[0]}
    for apart in reversed(range(1, count // 2)):
        pairs = [(i, ((i // 2) ^ apart) * 2 + i % 2) for i in range(count)]
        arrived[apart] = lax.ppermute(messages[apart], "lon", pairs)
    return arrived


def over_sides(block, count):
    return lax.ppermute(block, "lon", [(i, i ^ 1) for i in range(count)])


def around(block, count):
    rows = lax.axis_size("lat")
    lat_even = [i ^ 1 for i in range(rows)]
    lat_odd = [((i - 1) ^ 1) + 1 if i else rows - 1 for i in range(rows)]
    lat_odd[rows - 1] = 0
    lat_self = list(range(rows))

    def swap(lat_of, other_side):
        pairs = [
            (lat * count + lon, lat_of[lat] * count + (lon ^ other_side))
            for lat in range(rows)
            for lon in range(count)
        ]
        return lax.ppermute(block, ("lat", "lon"), pairs)

    odd_mate = swap(lat_odd, 1)
    even_mate = swap(lat_even, 1)
    odd_own = swap(lat_odd, 0)
    mate = swap(lat_self, 1)
    even_own = swap(lat_even, 0)
    return odd_mate, odd_own, even_mate, mate, even_own


def local(latent, lon_filter, mix_weight, band_weight, offsets, w_up, w_down):
    rows, width, chans = latent.shape
    bases, lons = lon_filter.shape
    half, group = mix_weight.shape[1:]
    taps = band_weight.shape[2]
    count = lons // width
    columns = count // 2
    block = 2 * half
    step = up_to(width, 2 * SUBLANES)
    places = count * step
    lanes = lanes_of(block)
    height = message_rows(block)
    assert rows == 2 and taps == 3 and columns & (columns - 1) == 0
    assert SUBLANES < width and rows * (width - SUBLANES) <= SUBLANES
    assert 3 * (block % LANES) <= LANES

    far_first = tuple(reversed(range(columns)))
    near_then_far = (1,) + tuple(reversed(range(2, columns))) + (0,)
    message = jax.ShapeDtypeStruct((height, LANES), BF16)
    messages = (message,) * columns
    stage = pltpu.VMEM((columns, height, LANES), BF16)
    points = pltpu.VMEM((3 * SUBLANES, chans), F32)
    lon_first = jnp.transpose(latent, (1, 0, 2))
    mix_own = jnp.transpose(mix_weight, (0, 2, 1))

    packed = call(pack_kernel, "pack", messages, [points, stage], 10**9, lon_first)
    arrived = over_columns(packed, count)
    mix_mate = over_sides(mix_own, count)
    table = call(
        functools.partial(tables_kernel, width),
        "tables",
        jax.ShapeDtypeStruct((rows, bases * places // 2, taps * places), BF16),
        [pltpu.VMEM((bases, step, places), F32)],
        10**9,
        lon_filter,
        jnp.transpose(band_weight, (2, 1, 0)),
    )
    squares = call(
        squares_kernel,
        "squares",
        jax.ShapeDtypeStruct((bases * lanes, lanes), BF16),
        [pltpu.VMEM((2, bases, up_to(group, 2 * SUBLANES), lanes), F32)],
        10**9,
        mix_own,
        mix_mate,
    )
    gathered = jax.ShapeDtypeStruct((columns, height, LANES), BF16)
    own_side = call(
        functools.partial(column_kernel, far_first),
        "join_columns",
        gathered,
        [],
        10**8,
        *[arrived[apart] for apart in far_first],
    )
    sources = around(own_side, count)
    mixed = call(
        functools.partial(conv_kernel, block, width),
        "conv",
        messages,
        [
            pltpu.VMEM((rows, taps * places, lanes), BF16),
            pltpu.VMEM((rows * places // 2, bases * lanes), BF16),
            stage,
        ],
        10**10,
        *sources,
        own_side,
        table,
        squares,
    )
    back = over_columns(mixed, count)
    result = call(
        functools.partial(tail_kernel, near_then_far),
        "tail",
        jax.ShapeDtypeStruct(lon_first.shape, BF16),
        [points, stage],
        10**9,
        *[back[apart] for apart in near_then_far],
        lon_first,
        w_up,
        w_down,
    )
    return jnp.transpose(result, (1, 0, 2))


def solution(mesh):
    return jax.shard_map(
        local,
        mesh=mesh,
        in_specs=(
            P("lat", "lon", None),
            P(),
            P(None, "lon", None),
            P(None, "lat", None),
            P("lat"),
            P(),
            P(),
        ),
        out_specs=P("lat", "lon", None),
        check_vma=False,
    )
```

```python
import functools

import jax
import jax.numpy as jnp
from jax import lax
from jax.experimental import pallas as pl
from jax.experimental.pallas import tpu as pltpu
from jax.sharding import PartitionSpec as P

F32 = jnp.float32
BF16 = jnp.bfloat16
LANES = 128
SUBLANES = 8


def up_to(size, step):
    return -(-size // step) * step


def column_and_side():
    place = lax.axis_index("lon")
    return place // 2, place % 2


def message_rows(block):
    tiles = block // LANES
    return up_to(3 * SUBLANES * tiles + (SUBLANES if block % LANES else 0), 2 * SUBLANES)


def lanes_of(block):
    return up_to(block, LANES)


def fold(points, block):
    whole, rest = divmod(block, LANES)
    parts = [points[:, tile * LANES : (tile + 1) * LANES] for tile in range(whole)]
    if rest:
        odd = points[:, whole * LANES : (whole + 1) * LANES]
        kept = lax.broadcasted_iota(jnp.int32, (SUBLANES, LANES), 1) < rest
        shared = None
        for third in range(3):
            piece = jnp.where(kept, odd[third * SUBLANES : (third + 1) * SUBLANES], 0.0)
            piece = pltpu.roll(piece, third * rest, 1) if third else piece
            shared = piece if shared is None else shared + piece
        parts.append(shared)
    filled = sum(part.shape[0] for part in parts)
    if message_rows(block) > filled:
        parts.append(jnp.zeros((message_rows(block) - filled, LANES), F32))
    return jnp.concatenate(parts, axis=0).astype(BF16)


def unfold(message, block):
    whole, rest = divmod(block, LANES)
    groups = []
    for third in range(3):
        first = third * SUBLANES
        parts = [
            message[tile * 3 * SUBLANES + first : tile * 3 * SUBLANES + first + SUBLANES]
            for tile in range(whole)
        ]
        if rest:
            odd = message[whole * 3 * SUBLANES : whole * 3 * SUBLANES + SUBLANES]
            parts.append(pltpu.roll(odd, LANES - third * rest, 1) if third else odd)
        groups.append(jnp.concatenate(parts, axis=1) if len(parts) > 1 else parts[0])
    return groups


def group_points(latent_ref, points):
    width, rows, _ = latent_ref.shape
    rest = width - SUBLANES
    for row in range(rows):
        points[row * SUBLANES : (row + 1) * SUBLANES] = latent_ref[:SUBLANES, row, :].astype(F32)
        at = rows * SUBLANES + row * rest
        points[at : at + rest] = latent_ref[SUBLANES:, row, :].astype(F32)


def pack_kernel(latent_ref, *refs):
    *out_refs, points, stage = refs
    columns = len(out_refs)
    chans = latent_ref.shape[2]
    block = chans // columns
    column, _ = column_and_side()
    group_points(latent_ref, points)
    own = points[...]
    for target in range(columns):
        turned = pltpu.roll(own, chans - target * block, 1) if target else own
        stage[target] = fold(turned[:, : lanes_of(block)], block)
    for apart in range(columns):
        out_refs[apart][...] = stage[column ^ apart]


def column_kernel(order, *refs):
    *in_refs, out_ref = refs
    column, _ = column_and_side()
    for apart, ref in zip(order, in_refs):
        out_ref[column ^ apart] = ref[...]


def tables_kernel(width, filter_ref, band_ref, table_ref, first):
    bases, lons = filter_ref.shape
    taps, rows, _ = band_ref.shape
    step, places = first.shape[1:]
    columns = places // (2 * step)
    _, side = column_and_side()
    lat = lax.axis_index("lat")
    below = (lat > 0).astype(F32)
    above = (lat < lax.axis_size("lat") - 1).astype(F32)
    inside = [[below, below, 1.0], [1.0, above, above]]
    slots = [[0, 1, 2], [2, 0, 1]]
    profile = filter_ref[...]
    band = band_ref[...].astype(F32)
    source = lax.broadcasted_iota(jnp.int32, (lons, places), 0)
    place = lax.broadcasted_iota(jnp.int32, (lons, places), 1)
    within = place % step
    apart = source + (place // step) * width + within + (lons - side * width)
    for _ in range(3):
        apart = jnp.where(apart >= lons, apart - lons, apart)
    apart = jnp.where(within < width, apart, -1)
    first[...] = jnp.zeros_like(first)
    for lon in range(width):
        pick = (apart == lon).astype(F32).astype(BF16)
        first[:, lon, :] = jnp.dot(profile, pick, preferred_element_type=F32)
    for basis in range(bases):
        circle = first[basis]
        for column in range(columns):
            turned = pltpu.roll(circle, column * 2 * step, 1) if column else circle
            at = (basis * columns + column) * step
            for row in range(rows):
                for tap in range(taps):
                    weight = band[tap, row : row + 1, basis : basis + 1] * inside[row][tap]
                    to = slots[row][tap] * places
                    table_ref[row, at : at + step, to : to + places] = (weight * turned).astype(
                        BF16
                    )


def squares_kernel(own_ref, mate_ref, squares_ref, padded):
    bases, group, half = own_ref.shape
    lanes = squares_ref.shape[1]
    _, side = column_and_side()
    first = side == 0
    own = own_ref[...].astype(F32)
    mate = mate_ref[...].astype(F32)
    padded[...] = jnp.zeros_like(padded)
    padded[0, :, :group, :half] = jnp.where(first, own, mate)
    padded[1, :, :group, :half] = jnp.where(first, mate, own)
    members = padded.shape[2]
    into = lax.broadcasted_iota(jnp.int32, (lanes, members), 0)
    member = lax.broadcasted_iota(jnp.int32, (lanes, members), 1)
    repeat = (into % group == member).astype(F32).astype(BF16)
    row = lax.broadcasted_iota(jnp.int32, (lanes, lanes), 0)
    column = lax.broadcasted_iota(jnp.int32, (lanes, lanes), 1)
    same = (row // group == column // group) & (row < 2 * half) & (column < 2 * half)
    for basis in range(bases):
        weights = padded[0, basis] + pltpu.roll(padded[1, basis], half, 1)
        repeated = jnp.dot(repeat, weights.astype(BF16), preferred_element_type=F32)
        squares_ref[basis * lanes : (basis + 1) * lanes] = jnp.where(same, repeated, 0.0).astype(
            BF16
        )


def rows_of(message, block, rest):
    groups = unfold(message.astype(F32), block)
    last = (groups[2], pltpu.roll(groups[2], SUBLANES - rest, 0))
    return [jnp.concatenate([groups[row], last[row]], axis=0) for row in range(2)]


def both_sides(near, far, side, at):
    return jnp.where(side == at % 2, near[at // 2].astype(F32), far[at // 2].astype(F32))


def mix(over, squares_ref, spread):
    bases = spread.shape[1] // squares_ref.shape[1]
    lanes = squares_ref.shape[1]
    half = spread.shape[0]
    over = over.astype(BF16)
    for basis in range(bases):
        spread[:, basis * lanes : (basis + 1) * lanes] = over[basis * half : (basis + 1) * half]
    return jnp.dot(spread[...], squares_ref[...], preferred_element_type=F32)


def early_kernel(
    block,
    width,
    even_mate,
    mate,
    even_own,
    home,
    table_ref,
    squares_ref,
    mixed_ref,
    part_ref,
    field,
    own_field,
    spread,
):
    columns = home.shape[0]
    places = table_ref.shape[2] // 3
    step = places // (2 * columns)
    rest = width - SUBLANES
    side = lax.axis_index("lon") % 2
    odd = lax.axis_index("lat") % 2
    for at in range(2 * columns):
        own = rows_of(both_sides(home, mate, side, at), block, rest)
        near = rows_of(both_sides(even_own, even_mate, side, at), block, rest)
        first = jnp.where(odd == 1, own[0], own[1])
        second = jnp.where(odd == 1, own[1], own[0])
        for slot, read in enumerate(near + [first]):
            field[slot * places + at * step : slot * places + (at + 1) * step] = read.astype(BF16)
        own_field[at * step : (at + 1) * step] = second.astype(BF16)
    part_ref[...] = jnp.dot(
        table_ref[odd][:, 2 * places :], own_field[...], preferred_element_type=F32
    )
    over = jnp.dot(table_ref[1 - odd], field[...], preferred_element_type=F32)
    mixed_ref[...] = mix(over, squares_ref, spread)


def late_kernel(
    block, width, odd_mate, odd_own, mixed_ref, part_ref, table_ref, squares_ref, *refs
):
    *out_refs, field, spread, stage = refs
    columns = len(out_refs)
    lanes = squares_ref.shape[1]
    places = table_ref.shape[2] // 3
    step = places // (2 * columns)
    rest = width - SUBLANES
    column, side = column_and_side()
    odd = lax.axis_index("lat") % 2
    for at in range(2 * columns):
        far = rows_of(both_sides(odd_own, odd_mate, side, at), block, rest)
        for slot, read in enumerate(far):
            field[slot * places + at * step : slot * places + (at + 1) * step] = read.astype(BF16)
    over = part_ref[...] + jnp.dot(
        table_ref[odd][:, : 2 * places], field[...], preferred_element_type=F32
    )
    late = mix(over, squares_ref, spread)
    early = mixed_ref[...]
    tops = jnp.where(odd == 1, early, late)
    bottoms = jnp.where(odd == 1, late, early)
    upper = lax.broadcasted_iota(jnp.int32, (SUBLANES, lanes), 0) < rest
    for target in range(columns):
        top = tops[target * step : (target + 1) * step]
        bottom = bottoms[target * step : (target + 1) * step]
        last = jnp.where(upper, top[SUBLANES:], pltpu.roll(bottom[SUBLANES:], rest, 0))
        points = jnp.concatenate([top[:SUBLANES], bottom[:SUBLANES], last], axis=0)
        stage[target] = fold(points, block)
    for apart in range(columns):
        out_refs[apart][...] = stage[column ^ apart]


def tail_kernel(order, *refs):
    columns = len(order)
    back_refs = refs[:columns]
    latent_ref, up_ref, down_ref, out_ref, points, stage = refs[columns:]
    width, rows, chans = latent_ref.shape
    rest = width - SUBLANES
    block = chans // columns
    lanes = lanes_of(block)
    column, _ = column_and_side()
    for apart, ref in zip(order, back_refs):
        stage[column ^ apart] = ref[...]
    group_points(latent_ref, points)
    kept = lax.broadcasted_iota(jnp.int32, (3 * SUBLANES, lanes), 1) < block
    convolved = None
    for target in range(columns):
        piece = jnp.concatenate(unfold(stage[target].astype(F32), block), axis=0)
        piece = jnp.where(kept, piece, 0.0)
        if chans > lanes:
            gap = jnp.zeros((3 * SUBLANES, chans - lanes), F32)
            piece = jnp.concatenate([piece, gap], axis=1)
        piece = pltpu.roll(piece, target * block, 1) if target else piece
        convolved = piece if convolved is None else convolved + piece
    summed = (points[...] + convolved).astype(BF16).astype(F32)
    centred = summed - jnp.mean(summed, axis=1, keepdims=True)
    variance = jnp.mean(centred * centred, axis=1, keepdims=True)
    normed = (centred * lax.rsqrt(variance + 1e-05)).astype(BF16)
    hidden = jnp.dot(normed, up_ref[...], preferred_element_type=F32)
    hidden = (0.5 * hidden * (1.0 + lax.erf(hidden * 0.5**0.5))).astype(BF16)
    result = summed + jnp.dot(hidden, down_ref[...], preferred_element_type=F32)
    for row in range(rows):
        out_ref[:SUBLANES, row, :] = result[row * SUBLANES : (row + 1) * SUBLANES].astype(BF16)
        at = rows * SUBLANES + row * rest
        out_ref[SUBLANES:, row, :] = result[at : at + rest].astype(BF16)


VMEM = pl.BlockSpec(memory_space=pltpu.VMEM)


def call(kernel, name, out_shape, scratch, work, *operands):
    several = isinstance(out_shape, tuple)
    return pl.pallas_call(
        kernel,
        out_shape=out_shape,
        in_specs=[VMEM] * len(operands),
        out_specs=(VMEM,) * len(out_shape) if several else VMEM,
        scratch_shapes=scratch,
        compiler_params=pltpu.CompilerParams(vmem_limit_bytes=24 * 2**20),
        cost_estimate=pl.CostEstimate(flops=work, bytes_accessed=10**6, transcendentals=0),
        name=name,
    )(*operands)


def over_columns(messages, count):
    arrived = {0: messages[0]}
    for apart in reversed(range(1, count // 2)):
        pairs = [(i, ((i // 2) ^ apart) * 2 + i % 2) for i in range(count)]
        arrived[apart] = lax.ppermute(messages[apart], "lon", pairs)
    return arrived


def over_sides(block, count):
    return lax.ppermute(block, "lon", [(i, i ^ 1) for i in range(count)])


def around(block, count):
    rows = lax.axis_size("lat")
    lat_even = [i ^ 1 for i in range(rows)]
    lat_odd = [((i - 1) ^ 1) + 1 if i else rows - 1 for i in range(rows)]
    lat_odd[rows - 1] = 0
    lat_self = list(range(rows))

    def swap(lat_of, other_side):
        pairs = [
            (lat * count + lon, lat_of[lat] * count + (lon ^ other_side))
            for lat in range(rows)
            for lon in range(count)
        ]
        return lax.ppermute(block, ("lat", "lon"), pairs)

    even_mate = swap(lat_even, 1)
    mate = swap(lat_self, 1)
    even_own = swap(lat_even, 0)
    odd_mate = swap(lat_odd, 1)
    odd_own = swap(lat_odd, 0)
    return odd_mate, odd_own, even_mate, mate, even_own


def local(latent, lon_filter, mix_weight, band_weight, offsets, w_up, w_down):
    rows, width, chans = latent.shape
    bases, lons = lon_filter.shape
    half, group = mix_weight.shape[1:]
    taps = band_weight.shape[2]
    count = lons // width
    columns = count // 2
    block = 2 * half
    step = up_to(width, 2 * SUBLANES)
    places = count * step
    lanes = lanes_of(block)
    height = message_rows(block)
    assert rows == 2 and taps == 3 and columns & (columns - 1) == 0
    assert SUBLANES < width and rows * (width - SUBLANES) <= SUBLANES
    assert 3 * (block % LANES) <= LANES

    far_first = tuple(reversed(range(columns)))
    near_then_far = (1,) + tuple(reversed(range(2, columns))) + (0,)
    message = jax.ShapeDtypeStruct((height, LANES), BF16)
    messages = (message,) * columns
    stage = pltpu.VMEM((columns, height, LANES), BF16)
    points = pltpu.VMEM((3 * SUBLANES, chans), F32)
    lon_first = jnp.transpose(latent, (1, 0, 2))
    mix_own = jnp.transpose(mix_weight, (0, 2, 1))

    packed = call(pack_kernel, "pack", messages, [points, stage], 10**9, lon_first)
    arrived = over_columns(packed, count)
    mix_mate = over_sides(mix_own, count)
    table = call(
        functools.partial(tables_kernel, width),
        "tables",
        jax.ShapeDtypeStruct((rows, bases * places // 2, taps * places), BF16),
        [pltpu.VMEM((bases, step, places), F32)],
        10**9,
        lon_filter,
        jnp.transpose(band_weight, (2, 1, 0)),
    )
    squares = call(
        squares_kernel,
        "squares",
        jax.ShapeDtypeStruct((bases * lanes, lanes), BF16),
        [pltpu.VMEM((2, bases, up_to(group, 2 * SUBLANES), lanes), F32)],
        10**9,
        mix_own,
        mix_mate,
    )
    gathered = jax.ShapeDtypeStruct((columns, height, LANES), BF16)
    own_side = call(
        functools.partial(column_kernel, far_first),
        "join_columns",
        gathered,
        [],
        10**8,
        *[arrived[apart] for apart in far_first],
    )
    odd_mate, odd_own, even_mate, mate, even_own = around(own_side, count)
    inner = bases * places // 2
    spread = pltpu.VMEM((places // 2, bases * lanes), BF16)
    early = call(
        functools.partial(early_kernel, block, width),
        "conv_early",
        (
            jax.ShapeDtypeStruct((places // 2, lanes), F32),
            jax.ShapeDtypeStruct((inner, lanes), F32),
        ),
        [pltpu.VMEM((3 * places, lanes), BF16), pltpu.VMEM((places, lanes), BF16), spread],
        10**9,
        even_mate,
        mate,
        even_own,
        own_side,
        table,
        squares,
    )
    mixed = call(
        functools.partial(late_kernel, block, width),
        "conv_late",
        messages,
        [pltpu.VMEM((2 * places, lanes), BF16), spread, stage],
        10**10,
        odd_mate,
        odd_own,
        *early,
        table,
        squares,
    )
    back = over_columns(mixed, count)
    result = call(
        functools.partial(tail_kernel, near_then_far),
        "tail",
        jax.ShapeDtypeStruct(lon_first.shape, BF16),
        [points, stage],
        10**9,
        *[back[apart] for apart in near_then_far],
        lon_first,
        w_up,
        w_down,
    )
    return jnp.transpose(result, (1, 0, 2))


def solution(mesh):
    return jax.shard_map(
        local,
        mesh=mesh,
        in_specs=(
            P("lat", "lon", None),
            P(),
            P(None, "lon", None),
            P(None, "lat", None),
            P("lat"),
            P(),
            P(),
        ),
        out_specs=P("lat", "lon", None),
        check_vma=False,
    )
```

```python
import functools

import jax
import jax.numpy as jnp
from jax import lax
from jax.experimental import pallas as pl
from jax.experimental.pallas import tpu as pltpu
from jax.sharding import PartitionSpec as P

F32 = jnp.float32
BF16 = jnp.bfloat16
LANES = 128
SUBLANES = 8


def up_to(size, step):
    return -(-size // step) * step


def column_and_side():
    place = lax.axis_index("lon")
    return place // 2, place % 2


def message_rows(block):
    tiles = block // LANES
    return up_to(3 * SUBLANES * tiles + (SUBLANES if block % LANES else 0), 2 * SUBLANES)


def lanes_of(block):
    return up_to(block, LANES)


def fold(points, block):
    whole, rest = divmod(block, LANES)
    parts = [points[:, tile * LANES : (tile + 1) * LANES] for tile in range(whole)]
    if rest:
        odd = points[:, whole * LANES : (whole + 1) * LANES]
        kept = lax.broadcasted_iota(jnp.int32, (SUBLANES, LANES), 1) < rest
        shared = None
        for third in range(3):
            piece = jnp.where(kept, odd[third * SUBLANES : (third + 1) * SUBLANES], 0.0)
            piece = pltpu.roll(piece, third * rest, 1) if third else piece
            shared = piece if shared is None else shared + piece
        parts.append(shared)
    filled = sum(part.shape[0] for part in parts)
    if message_rows(block) > filled:
        parts.append(jnp.zeros((message_rows(block) - filled, LANES), F32))
    return jnp.concatenate(parts, axis=0).astype(BF16)


def unfold(message, block):
    whole, rest = divmod(block, LANES)
    groups = []
    for third in range(3):
        first = third * SUBLANES
        parts = [
            message[tile * 3 * SUBLANES + first : tile * 3 * SUBLANES + first + SUBLANES]
            for tile in range(whole)
        ]
        if rest:
            odd = message[whole * 3 * SUBLANES : whole * 3 * SUBLANES + SUBLANES]
            parts.append(pltpu.roll(odd, LANES - third * rest, 1) if third else odd)
        groups.append(jnp.concatenate(parts, axis=1) if len(parts) > 1 else parts[0])
    return groups


def group_points(latent_ref, points):
    width, rows, _ = latent_ref.shape
    rest = width - SUBLANES
    for row in range(rows):
        points[row * SUBLANES : (row + 1) * SUBLANES] = latent_ref[:SUBLANES, row, :].astype(F32)
        at = rows * SUBLANES + row * rest
        points[at : at + rest] = latent_ref[SUBLANES:, row, :].astype(F32)


def pack_kernel(latent_ref, out_ref, points):
    columns = out_ref.shape[0] // 2
    chans = latent_ref.shape[2]
    block = chans // columns
    group_points(latent_ref, points)
    own = points[...]
    for target in range(columns):
        turned = pltpu.roll(own, chans - target * block, 1) if target else own
        message = fold(turned[:, : lanes_of(block)], block)
        out_ref[2 * target] = message
        out_ref[2 * target + 1] = message


def tables_kernel(width, filter_ref, band_ref, table_ref, first):
    bases, lons = filter_ref.shape
    taps, rows, _ = band_ref.shape
    step, places = first.shape[1:]
    columns = places // (2 * step)
    _, side = column_and_side()
    lat = lax.axis_index("lat")
    below = (lat > 0).astype(F32)
    above = (lat < lax.axis_size("lat") - 1).astype(F32)
    inside = [[below, below, 1.0], [1.0, above, above]]
    profile = filter_ref[...]
    band = band_ref[...].astype(F32)
    source = lax.broadcasted_iota(jnp.int32, (lons, places), 0)
    place = lax.broadcasted_iota(jnp.int32, (lons, places), 1)
    within = place % step
    apart = source + (place // step) * width + within + (lons - side * width)
    for _ in range(3):
        apart = jnp.where(apart >= lons, apart - lons, apart)
    apart = jnp.where(within < width, apart, -1)
    first[...] = jnp.zeros_like(first)
    for lon in range(width):
        pick = (apart == lon).astype(F32).astype(BF16)
        first[:, lon, :] = jnp.dot(profile, pick, preferred_element_type=F32)
    for basis in range(bases):
        circle = first[basis]
        for column in range(columns):
            turned = pltpu.roll(circle, column * 2 * step, 1) if column else circle
            at = (basis * columns + column) * step
            for row in range(rows):
                for tap in range(taps):
                    weight = band[tap, row : row + 1, basis : basis + 1] * inside[row][tap]
                    table_ref[row, at : at + step, tap * places : (tap + 1) * places] = (
                        weight * turned
                    ).astype(BF16)


def squares_kernel(own_ref, mate_ref, squares_ref, padded):
    bases, group, half = own_ref.shape
    lanes = squares_ref.shape[1]
    _, side = column_and_side()
    first = side == 0
    own = own_ref[...].astype(F32)
    mate = mate_ref[...].astype(F32)
    padded[...] = jnp.zeros_like(padded)
    padded[0, :, :group, :half] = jnp.where(first, own, mate)
    padded[1, :, :group, :half] = jnp.where(first, mate, own)
    members = padded.shape[2]
    into = lax.broadcasted_iota(jnp.int32, (lanes, members), 0)
    member = lax.broadcasted_iota(jnp.int32, (lanes, members), 1)
    repeat = (into % group == member).astype(F32).astype(BF16)
    row = lax.broadcasted_iota(jnp.int32, (lanes, lanes), 0)
    column = lax.broadcasted_iota(jnp.int32, (lanes, lanes), 1)
    same = (row // group == column // group) & (row < 2 * half) & (column < 2 * half)
    for basis in range(bases):
        weights = padded[0, basis] + pltpu.roll(padded[1, basis], half, 1)
        repeated = jnp.dot(repeat, weights.astype(BF16), preferred_element_type=F32)
        squares_ref[basis * lanes : (basis + 1) * lanes] = jnp.where(same, repeated, 0.0).astype(
            BF16
        )


def conv_kernel(block, width, *refs):
    odd_refs, even_refs, home, table_ref, squares_ref, *refs = refs
    *out_refs, field, spread, stage = refs
    columns = len(out_refs)
    lanes = squares_ref.shape[1]
    bases = squares_ref.shape[0] // lanes
    rows, _, inner = table_ref.shape
    places = inner // 3
    step = places // (2 * columns)
    half = places // 2
    rest = width - SUBLANES
    column, _ = column_and_side()
    odd = lax.axis_index("lat") % 2 == 1
    for at in range(2 * columns):
        own, even, other = (ref[at].astype(F32) for ref in (home, even_refs, odd_refs))
        low = jnp.where(odd, even, other)
        high = jnp.where(odd, other, even)
        read = []
        for message in (low, own, high):
            groups = unfold(message, block)
            for row in range(rows):
                last = pltpu.roll(groups[2], SUBLANES - row * rest, 0) if row else groups[2]
                read.append(jnp.concatenate([groups[row], last], axis=0).astype(BF16))
        for row in range(rows):
            for tap in range(3):
                first = tap * places + at * step
                field[row, first : first + step] = read[row * 3 + tap]
    for row in range(rows):
        over = jnp.dot(table_ref[row], field[row], preferred_element_type=F32).astype(BF16)
        for basis in range(bases):
            spread[row * half : (row + 1) * half, basis * lanes : (basis + 1) * lanes] = over[
                basis * half : (basis + 1) * half
            ]
    mixed = jnp.dot(spread[...], squares_ref[...], preferred_element_type=F32)
    upper = lax.broadcasted_iota(jnp.int32, (SUBLANES, lanes), 0) < rest
    for target in range(columns):
        top = mixed[target * step : (target + 1) * step]
        bottom = mixed[half + target * step : half + (target + 1) * step]
        last = jnp.where(upper, top[SUBLANES:], pltpu.roll(bottom[SUBLANES:], rest, 0))
        points = jnp.concatenate([top[:SUBLANES], bottom[:SUBLANES], last], axis=0)
        stage[target] = fold(points, block)
    for apart in range(columns):
        out_refs[apart][...] = stage[column ^ apart]


def tail_kernel(order, *refs):
    columns = len(order)
    back_refs = refs[:columns]
    latent_ref, up_ref, down_ref, out_ref, points, stage = refs[columns:]
    width, rows, chans = latent_ref.shape
    rest = width - SUBLANES
    block = chans // columns
    lanes = lanes_of(block)
    column, _ = column_and_side()
    for apart, ref in zip(order, back_refs):
        stage[column ^ apart] = ref[...]
    group_points(latent_ref, points)
    kept = lax.broadcasted_iota(jnp.int32, (3 * SUBLANES, lanes), 1) < block
    convolved = None
    for target in range(columns):
        piece = jnp.concatenate(unfold(stage[target].astype(F32), block), axis=0)
        piece = jnp.where(kept, piece, 0.0)
        if chans > lanes:
            gap = jnp.zeros((3 * SUBLANES, chans - lanes), F32)
            piece = jnp.concatenate([piece, gap], axis=1)
        piece = pltpu.roll(piece, target * block, 1) if target else piece
        convolved = piece if convolved is None else convolved + piece
    summed = (points[...] + convolved).astype(BF16).astype(F32)
    centred = summed - jnp.mean(summed, axis=1, keepdims=True)
    variance = jnp.mean(centred * centred, axis=1, keepdims=True)
    normed = (centred * lax.rsqrt(variance + 1e-05)).astype(BF16)
    hidden = jnp.dot(normed, up_ref[...], preferred_element_type=F32)
    hidden = (0.5 * hidden * (1.0 + lax.erf(hidden * 0.5**0.5))).astype(BF16)
    result = summed + jnp.dot(hidden, down_ref[...], preferred_element_type=F32)
    for row in range(rows):
        out_ref[:SUBLANES, row, :] = result[row * SUBLANES : (row + 1) * SUBLANES].astype(BF16)
        at = rows * SUBLANES + row * rest
        out_ref[SUBLANES:, row, :] = result[at : at + rest].astype(BF16)


VMEM = pl.BlockSpec(memory_space=pltpu.VMEM)


def call(kernel, name, out_shape, scratch, work, *operands):
    several = isinstance(out_shape, tuple)
    return pl.pallas_call(
        kernel,
        out_shape=out_shape,
        in_specs=[VMEM] * len(operands),
        out_specs=(VMEM,) * len(out_shape) if several else VMEM,
        scratch_shapes=scratch,
        compiler_params=pltpu.CompilerParams(vmem_limit_bytes=24 * 2**20),
        cost_estimate=pl.CostEstimate(flops=work, bytes_accessed=10**6, transcendentals=0),
        name=name,
    )(*operands)


def over_columns(messages, count):
    arrived = {0: messages[0]}
    for apart in reversed(range(1, count // 2)):
        pairs = [(i, ((i // 2) ^ apart) * 2 + i % 2) for i in range(count)]
        arrived[apart] = lax.ppermute(messages[apart], "lon", pairs)
    return arrived


def over_sides(block, count):
    return lax.ppermute(block, "lon", [(i, i ^ 1) for i in range(count)])


def over_rows(block):
    rows = lax.axis_size("lat")
    odd = [(i, (i + 1 if i % 2 else i - 1) % rows) for i in range(rows)]
    even = [(i, i ^ 1) for i in range(rows)]
    return lax.ppermute(block, "lat", odd), lax.ppermute(block, "lat", even)


def local(latent, lon_filter, mix_weight, band_weight, offsets, w_up, w_down):
    rows, width, chans = latent.shape
    bases, lons = lon_filter.shape
    half, group = mix_weight.shape[1:]
    taps = band_weight.shape[2]
    count = lons // width
    columns = count // 2
    block = 2 * half
    step = up_to(width, 2 * SUBLANES)
    places = count * step
    lanes = lanes_of(block)
    height = message_rows(block)
    assert rows == 2 and taps == 3 and columns & (columns - 1) == 0
    assert lax.axis_size("lat") % 2 == 0
    assert SUBLANES < width and rows * (width - SUBLANES) <= SUBLANES
    assert 3 * (block % LANES) <= LANES

    far_first = tuple(reversed(range(columns)))
    message = jax.ShapeDtypeStruct((height, LANES), BF16)
    messages = (message,) * columns
    stage = pltpu.VMEM((columns, height, LANES), BF16)
    points = pltpu.VMEM((3 * SUBLANES, chans), F32)
    lon_first = jnp.transpose(latent, (1, 0, 2))
    mix_own = jnp.transpose(mix_weight, (0, 2, 1))

    circle = jax.ShapeDtypeStruct((count, height, LANES), BF16)
    packed = call(pack_kernel, "pack", circle, [points], 10**9, lon_first)
    home = lax.all_to_all(packed, "lon", split_axis=0, concat_axis=0, tiled=True)
    mix_mate = over_sides(mix_own, count)
    table = call(
        functools.partial(tables_kernel, width),
        "tables",
        jax.ShapeDtypeStruct((rows, bases * places // 2, taps * places), BF16),
        [pltpu.VMEM((bases, step, places), F32)],
        10**6,
        lon_filter,
        jnp.transpose(band_weight, (2, 1, 0)),
    )
    squares = call(
        squares_kernel,
        "squares",
        jax.ShapeDtypeStruct((bases * lanes, lanes), BF16),
        [pltpu.VMEM((2, bases, up_to(group, 2 * SUBLANES), lanes), F32)],
        2 * 10**10,
        mix_own,
        mix_mate,
    )
    odd, even = over_rows(home)
    mixed = call(
        functools.partial(conv_kernel, block, width),
        "conv",
        messages,
        [
            pltpu.VMEM((rows, taps * places, lanes), BF16),
            pltpu.VMEM((rows * places // 2, bases * lanes), BF16),
            stage,
        ],
        10**10,
        odd,
        even,
        home,
        table,
        squares,
    )
    back = over_columns(mixed, count)
    result = call(
        functools.partial(tail_kernel, far_first),
        "tail",
        jax.ShapeDtypeStruct(lon_first.shape, BF16),
        [points, stage],
        10**9,
        *[back[apart] for apart in far_first],
        lon_first,
        w_up,
        w_down,
    )
    return jnp.transpose(result, (1, 0, 2))


def solution(mesh):
    return jax.shard_map(
        local,
        mesh=mesh,
        in_specs=(
            P("lat", "lon", None),
            P(),
            P(None, "lon", None),
            P(None, "lat", None),
            P("lat"),
            P(),
            P(),
        ),
        out_specs=P("lat", "lon", None),
        check_vma=False,
    )
```

```python
import functools

import jax
import jax.numpy as jnp
from jax import lax
from jax.experimental import pallas as pl
from jax.experimental.pallas import tpu as pltpu
from jax.sharding import PartitionSpec as P

F32 = jnp.float32
BF16 = jnp.bfloat16
LANES = 128
SUBLANES = 8


def up_to(size, step):
    return -(-size // step) * step


def column_and_side():
    place = lax.axis_index("lon")
    return place // 2, place % 2


def message_rows(block):
    tiles = block // LANES
    return up_to(3 * SUBLANES * tiles + (SUBLANES if block % LANES else 0), 2 * SUBLANES)


def lanes_of(block):
    return up_to(block, LANES)


def fold(points, block):
    whole, rest = divmod(block, LANES)
    parts = [points[:, tile * LANES : (tile + 1) * LANES] for tile in range(whole)]
    if rest:
        odd = points[:, whole * LANES : (whole + 1) * LANES]
        kept = lax.broadcasted_iota(jnp.int32, (SUBLANES, LANES), 1) < rest
        shared = None
        for third in range(3):
            piece = jnp.where(kept, odd[third * SUBLANES : (third + 1) * SUBLANES], 0.0)
            piece = pltpu.roll(piece, third * rest, 1) if third else piece
            shared = piece if shared is None else shared + piece
        parts.append(shared)
    filled = sum(part.shape[0] for part in parts)
    if message_rows(block) > filled:
        parts.append(jnp.zeros((message_rows(block) - filled, LANES), F32))
    return jnp.concatenate(parts, axis=0).astype(BF16)


def unfold(message, block):
    whole, rest = divmod(block, LANES)
    groups = []
    for third in range(3):
        first = third * SUBLANES
        parts = [
            message[tile * 3 * SUBLANES + first : tile * 3 * SUBLANES + first + SUBLANES]
            for tile in range(whole)
        ]
        if rest:
            odd = message[whole * 3 * SUBLANES : whole * 3 * SUBLANES + SUBLANES]
            parts.append(pltpu.roll(odd, LANES - third * rest, 1) if third else odd)
        groups.append(jnp.concatenate(parts, axis=1) if len(parts) > 1 else parts[0])
    return groups


def group_points(latent_ref, points):
    width, rows, _ = latent_ref.shape
    rest = width - SUBLANES
    for row in range(rows):
        points[row * SUBLANES : (row + 1) * SUBLANES] = latent_ref[:SUBLANES, row, :].astype(F32)
        at = rows * SUBLANES + row * rest
        points[at : at + rest] = latent_ref[SUBLANES:, row, :].astype(F32)


def pack_kernel(latent_ref, out_ref, points):
    columns = out_ref.shape[0] // 2
    chans = latent_ref.shape[2]
    block = chans // columns
    group_points(latent_ref, points)
    own = points[...]
    for target in range(columns):
        turned = pltpu.roll(own, chans - target * block, 1) if target else own
        message = fold(turned[:, : lanes_of(block)], block)
        out_ref[2 * target] = message
        out_ref[2 * target + 1] = message


def tables_kernel(width, filter_ref, band_ref, table_ref, first):
    bases, lons = filter_ref.shape
    taps, rows, _ = band_ref.shape
    step, places = first.shape[1:]
    columns = places // (2 * step)
    _, side = column_and_side()
    lat = lax.axis_index("lat")
    below = (lat > 0).astype(F32)
    above = (lat < lax.axis_size("lat") - 1).astype(F32)
    inside = [[below, below, 1.0], [1.0, above, above]]
    profile = filter_ref[...]
    band = band_ref[...].astype(F32)
    source = lax.broadcasted_iota(jnp.int32, (lons, places), 0)
    place = lax.broadcasted_iota(jnp.int32, (lons, places), 1)
    within = place % step
    apart = source + (place // step) * width + within + (lons - side * width)
    for _ in range(3):
        apart = jnp.where(apart >= lons, apart - lons, apart)
    apart = jnp.where(within < width, apart, -1)
    first[...] = jnp.zeros_like(first)
    for lon in range(width):
        pick = (apart == lon).astype(F32).astype(BF16)
        first[:, lon, :] = jnp.dot(profile, pick, preferred_element_type=F32)
    for basis in range(bases):
        circle = first[basis]
        for column in range(columns):
            turned = pltpu.roll(circle, column * 2 * step, 1) if column else circle
            at = (basis * columns + column) * step
            for row in range(rows):
                for tap in range(taps):
                    weight = band[tap, row : row + 1, basis : basis + 1] * inside[row][tap]
                    table_ref[row, at : at + step, tap * places : (tap + 1) * places] = (
                        weight * turned
                    ).astype(BF16)


def squares_kernel(own_ref, mate_ref, squares_ref, padded):
    bases, group, half = own_ref.shape
    lanes = squares_ref.shape[1]
    _, side = column_and_side()
    first = side == 0
    own = own_ref[...].astype(F32)
    mate = mate_ref[...].astype(F32)
    padded[...] = jnp.zeros_like(padded)
    padded[0, :, :group, :half] = jnp.where(first, own, mate)
    padded[1, :, :group, :half] = jnp.where(first, mate, own)
    members = padded.shape[2]
    into = lax.broadcasted_iota(jnp.int32, (lanes, members), 0)
    member = lax.broadcasted_iota(jnp.int32, (lanes, members), 1)
    repeat = (into % group == member).astype(F32).astype(BF16)
    row = lax.broadcasted_iota(jnp.int32, (lanes, lanes), 0)
    column = lax.broadcasted_iota(jnp.int32, (lanes, lanes), 1)
    same = (row // group == column // group) & (row < 2 * half) & (column < 2 * half)
    for basis in range(bases):
        weights = padded[0, basis] + pltpu.roll(padded[1, basis], half, 1)
        repeated = jnp.dot(repeat, weights.astype(BF16), preferred_element_type=F32)
        squares_ref[basis * lanes : (basis + 1) * lanes] = jnp.where(same, repeated, 0.0).astype(
            BF16
        )


def conv_kernel(block, width, *refs):
    odd_refs, even_refs, home, table_ref, squares_ref, *refs = refs
    *out_refs, field, spread, stage = refs
    columns = len(out_refs)
    lanes = squares_ref.shape[1]
    bases = squares_ref.shape[0] // lanes
    rows, _, inner = table_ref.shape
    places = inner // 3
    step = places // (2 * columns)
    half = places // 2
    rest = width - SUBLANES
    column, _ = column_and_side()
    odd = lax.axis_index("lat") % 2 == 1
    for at in range(2 * columns):
        own, even, other = (ref[at].astype(F32) for ref in (home, even_refs, odd_refs))
        low = jnp.where(odd, even, other)
        high = jnp.where(odd, other, even)
        read = []
        for message in (low, own, high):
            groups = unfold(message, block)
            for row in range(rows):
                last = pltpu.roll(groups[2], SUBLANES - row * rest, 0) if row else groups[2]
                read.append(jnp.concatenate([groups[row], last], axis=0).astype(BF16))
        for row in range(rows):
            for tap in range(3):
                first = tap * places + at * step
                field[row, first : first + step] = read[row * 3 + tap]
    for row in range(rows):
        over = jnp.dot(table_ref[row], field[row], preferred_element_type=F32).astype(BF16)
        for basis in range(bases):
            spread[row * half : (row + 1) * half, basis * lanes : (basis + 1) * lanes] = over[
                basis * half : (basis + 1) * half
            ]
    mixed = jnp.dot(spread[...], squares_ref[...], preferred_element_type=F32)
    upper = lax.broadcasted_iota(jnp.int32, (SUBLANES, lanes), 0) < rest
    for target in range(columns):
        top = mixed[target * step : (target + 1) * step]
        bottom = mixed[half + target * step : half + (target + 1) * step]
        last = jnp.where(upper, top[SUBLANES:], pltpu.roll(bottom[SUBLANES:], rest, 0))
        points = jnp.concatenate([top[:SUBLANES], bottom[:SUBLANES], last], axis=0)
        stage[target] = fold(points, block)
    for apart in range(columns):
        out_refs[apart][...] = stage[column ^ apart]


def tail_kernel(order, *refs):
    columns = len(order)
    back_refs = refs[:columns]
    latent_ref, up_ref, down_ref, out_ref, points, stage = refs[columns:]
    width, rows, chans = latent_ref.shape
    rest = width - SUBLANES
    block = chans // columns
    lanes = lanes_of(block)
    column, _ = column_and_side()
    for apart, ref in zip(order, back_refs):
        stage[column ^ apart] = ref[...]
    group_points(latent_ref, points)
    kept = lax.broadcasted_iota(jnp.int32, (3 * SUBLANES, lanes), 1) < block
    convolved = None
    for target in range(columns):
        piece = jnp.concatenate(unfold(stage[target].astype(F32), block), axis=0)
        piece = jnp.where(kept, piece, 0.0)
        if chans > lanes:
            gap = jnp.zeros((3 * SUBLANES, chans - lanes), F32)
            piece = jnp.concatenate([piece, gap], axis=1)
        piece = pltpu.roll(piece, target * block, 1) if target else piece
        convolved = piece if convolved is None else convolved + piece
    summed = (points[...] + convolved).astype(BF16).astype(F32)
    centred = summed - jnp.mean(summed, axis=1, keepdims=True)
    variance = jnp.mean(centred * centred, axis=1, keepdims=True)
    normed = (centred * lax.rsqrt(variance + 1e-05)).astype(BF16)
    hidden = jnp.dot(normed, up_ref[...], preferred_element_type=F32)
    hidden = (0.5 * hidden * (1.0 + lax.erf(hidden * 0.5**0.5))).astype(BF16)
    result = summed + jnp.dot(hidden, down_ref[...], preferred_element_type=F32)
    for row in range(rows):
        out_ref[:SUBLANES, row, :] = result[row * SUBLANES : (row + 1) * SUBLANES].astype(BF16)
        at = rows * SUBLANES + row * rest
        out_ref[SUBLANES:, row, :] = result[at : at + rest].astype(BF16)


VMEM = pl.BlockSpec(memory_space=pltpu.VMEM)


def call(kernel, name, out_shape, scratch, work, *operands):
    several = isinstance(out_shape, tuple)
    return pl.pallas_call(
        kernel,
        out_shape=out_shape,
        in_specs=[VMEM] * len(operands),
        out_specs=(VMEM,) * len(out_shape) if several else VMEM,
        scratch_shapes=scratch,
        compiler_params=pltpu.CompilerParams(vmem_limit_bytes=24 * 2**20),
        cost_estimate=pl.CostEstimate(flops=work, bytes_accessed=10**6, transcendentals=0),
        name=name,
    )(*operands)


def over_columns(messages, count):
    arrived = {0: messages[0]}
    for apart in reversed(range(1, count // 2)):
        pairs = [(i, ((i // 2) ^ apart) * 2 + i % 2) for i in range(count)]
        arrived[apart] = lax.ppermute(messages[apart], "lon", pairs)
    return arrived


def around_circle(messages, always):
    def exchange(block):
        return lax.all_to_all(block, "lon", split_axis=0, concat_axis=0, tiled=True)

    def in_rows(block):
        return exchange(block.reshape(block.shape[0], -1)).reshape(block.shape)

    return lax.cond(always, exchange, in_rows, messages)


def over_sides(block, count):
    return lax.ppermute(block, "lon", [(i, i ^ 1) for i in range(count)])


def over_rows(block):
    rows = lax.axis_size("lat")
    odd = [(i, (i + 1 if i % 2 else i - 1) % rows) for i in range(rows)]
    even = [(i, i ^ 1) for i in range(rows)]
    return lax.ppermute(block, "lat", odd), lax.ppermute(block, "lat", even)


def local(latent, lon_filter, mix_weight, band_weight, offsets, w_up, w_down):
    rows, width, chans = latent.shape
    bases, lons = lon_filter.shape
    half, group = mix_weight.shape[1:]
    taps = band_weight.shape[2]
    count = lons // width
    columns = count // 2
    block = 2 * half
    step = up_to(width, 2 * SUBLANES)
    places = count * step
    lanes = lanes_of(block)
    height = message_rows(block)
    assert rows == 2 and taps == 3 and columns & (columns - 1) == 0
    assert lax.axis_size("lat") % 2 == 0
    assert SUBLANES < width and rows * (width - SUBLANES) <= SUBLANES
    assert 3 * (block % LANES) <= LANES

    far_first = tuple(reversed(range(columns)))
    message = jax.ShapeDtypeStruct((height, LANES), BF16)
    messages = (message,) * columns
    stage = pltpu.VMEM((columns, height, LANES), BF16)
    points = pltpu.VMEM((3 * SUBLANES, chans), F32)
    lon_first = jnp.transpose(latent, (1, 0, 2))
    mix_own = jnp.transpose(mix_weight, (0, 2, 1))

    circle = jax.ShapeDtypeStruct((count, height, LANES), BF16)
    packed = call(pack_kernel, "pack", circle, [points], 10**9, lon_first)
    home = around_circle(packed, offsets[0] >= -lons)
    mix_mate = over_sides(mix_own, count)
    table = call(
        functools.partial(tables_kernel, width),
        "tables",
        jax.ShapeDtypeStruct((rows, bases * places // 2, taps * places), BF16),
        [pltpu.VMEM((bases, step, places), F32)],
        10**6,
        lon_filter,
        jnp.transpose(band_weight, (2, 1, 0)),
    )
    squares = call(
        squares_kernel,
        "squares",
        jax.ShapeDtypeStruct((bases * lanes, lanes), BF16),
        [pltpu.VMEM((2, bases, up_to(group, 2 * SUBLANES), lanes), F32)],
        2 * 10**10,
        mix_own,
        mix_mate,
    )
    odd, even = over_rows(home)
    mixed = call(
        functools.partial(conv_kernel, block, width),
        "conv",
        messages,
        [
            pltpu.VMEM((rows, taps * places, lanes), BF16),
            pltpu.VMEM((rows * places // 2, bases * lanes), BF16),
            stage,
        ],
        10**10,
        odd,
        even,
        home,
        table,
        squares,
    )
    back = over_columns(mixed, count)
    result = call(
        functools.partial(tail_kernel, far_first),
        "tail",
        jax.ShapeDtypeStruct(lon_first.shape, BF16),
        [points, stage],
        10**9,
        *[back[apart] for apart in far_first],
        lon_first,
        w_up,
        w_down,
    )
    return jnp.transpose(result, (1, 0, 2))


def solution(mesh):
    return jax.shard_map(
        local,
        mesh=mesh,
        in_specs=(
            P("lat", "lon", None),
            P(),
            P(None, "lon", None),
            P(None, "lat", None),
            P("lat"),
            P(),
            P(),
        ),
        out_specs=P("lat", "lon", None),
        check_vma=False,
    )
```

```python
import functools

import jax
import jax.numpy as jnp
from jax import lax
from jax.experimental import pallas as pl
from jax.experimental.pallas import tpu as pltpu
from jax.sharding import PartitionSpec as P

F32 = jnp.float32
BF16 = jnp.bfloat16
LANES = 128
SUBLANES = 8


def up_to(size, step):
    return -(-size // step) * step


def column_and_side():
    place = lax.axis_index("lon")
    return place // 2, place % 2


def message_rows(block):
    tiles = block // LANES
    return up_to(3 * SUBLANES * tiles + (SUBLANES if block % LANES else 0), 2 * SUBLANES)


def lanes_of(block):
    return up_to(block, LANES)


def fold(points, block):
    whole, rest = divmod(block, LANES)
    parts = [points[:, tile * LANES : (tile + 1) * LANES] for tile in range(whole)]
    if rest:
        odd = points[:, whole * LANES : (whole + 1) * LANES]
        kept = lax.broadcasted_iota(jnp.int32, (SUBLANES, LANES), 1) < rest
        shared = None
        for third in range(3):
            piece = jnp.where(kept, odd[third * SUBLANES : (third + 1) * SUBLANES], 0.0)
            piece = pltpu.roll(piece, third * rest, 1) if third else piece
            shared = piece if shared is None else shared + piece
        parts.append(shared)
    filled = sum(part.shape[0] for part in parts)
    if message_rows(block) > filled:
        parts.append(jnp.zeros((message_rows(block) - filled, LANES), F32))
    return jnp.concatenate(parts, axis=0).astype(BF16)


def unfold(message, block):
    whole, rest = divmod(block, LANES)
    groups = []
    for third in range(3):
        first = third * SUBLANES
        parts = [
            message[tile * 3 * SUBLANES + first : tile * 3 * SUBLANES + first + SUBLANES]
            for tile in range(whole)
        ]
        if rest:
            odd = message[whole * 3 * SUBLANES : whole * 3 * SUBLANES + SUBLANES]
            parts.append(pltpu.roll(odd, LANES - third * rest, 1) if third else odd)
        groups.append(jnp.concatenate(parts, axis=1) if len(parts) > 1 else parts[0])
    return groups


def group_points(latent_ref, points):
    width, rows, _ = latent_ref.shape
    rest = width - SUBLANES
    for row in range(rows):
        points[row * SUBLANES : (row + 1) * SUBLANES] = latent_ref[:SUBLANES, row, :].astype(F32)
        at = rows * SUBLANES + row * rest
        points[at : at + rest] = latent_ref[SUBLANES:, row, :].astype(F32)


def pack_kernel(latent_hbm, *refs):
    *out_refs, points, stage, latent_ref, sem = refs
    copy = pltpu.make_async_copy(latent_hbm, latent_ref, sem)
    copy.start()
    copy.wait()
    columns = len(out_refs)
    chans = latent_ref.shape[2]
    block = chans // columns
    column, _ = column_and_side()
    group_points(latent_ref, points)
    own = points[...]
    for target in range(columns):
        turned = pltpu.roll(own, chans - target * block, 1) if target else own
        stage[target] = fold(turned[:, : lanes_of(block)], block)
    for apart in range(columns):
        out_refs[apart][...] = stage[column ^ apart]


def column_kernel(order, *refs):
    *in_refs, out_ref = refs
    column, _ = column_and_side()
    for apart, ref in zip(order, in_refs):
        out_ref[column ^ apart] = ref[...]


def tables_kernel(width, filter_ref, band_ref, table_ref, first):
    bases, lons = filter_ref.shape
    taps, rows, _ = band_ref.shape
    step, places = first.shape[1:]
    columns = places // (2 * step)
    _, side = column_and_side()
    lat = lax.axis_index("lat")
    below = (lat > 0).astype(F32)
    above = (lat < lax.axis_size("lat") - 1).astype(F32)
    inside = [[below, below, 1.0], [1.0, above, above]]
    slots = [[0, 1, 2], [2, 0, 1]]
    profile = filter_ref[...]
    band = band_ref[...].astype(F32)
    source = lax.broadcasted_iota(jnp.int32, (lons, places), 0)
    place = lax.broadcasted_iota(jnp.int32, (lons, places), 1)
    within = place % step
    apart = source + (place // step) * width + within + (lons - side * width)
    for _ in range(3):
        apart = jnp.where(apart >= lons, apart - lons, apart)
    apart = jnp.where(within < width, apart, -1)
    first[...] = jnp.zeros_like(first)
    for lon in range(width):
        pick = (apart == lon).astype(F32).astype(BF16)
        first[:, lon, :] = jnp.dot(profile, pick, preferred_element_type=F32)
    for basis in range(bases):
        circle = first[basis]
        for column in range(columns):
            turned = pltpu.roll(circle, column * 2 * step, 1) if column else circle
            at = (basis * columns + column) * step
            for row in range(rows):
                for tap in range(taps):
                    weight = band[tap, row : row + 1, basis : basis + 1] * inside[row][tap]
                    to = slots[row][tap] * places
                    table_ref[row, at : at + step, to : to + places] = (weight * turned).astype(
                        BF16
                    )


def squares_kernel(own_ref, mate_ref, squares_ref, padded):
    bases, group, half = own_ref.shape
    lanes = squares_ref.shape[1]
    _, side = column_and_side()
    first = side == 0
    own = own_ref[...].astype(F32)
    mate = mate_ref[...].astype(F32)
    padded[...] = jnp.zeros_like(padded)
    padded[0, :, :group, :half] = jnp.where(first, own, mate)
    padded[1, :, :group, :half] = jnp.where(first, mate, own)
    members = padded.shape[2]
    into = lax.broadcasted_iota(jnp.int32, (lanes, members), 0)
    member = lax.broadcasted_iota(jnp.int32, (lanes, members), 1)
    repeat = (into % group == member).astype(F32).astype(BF16)
    row = lax.broadcasted_iota(jnp.int32, (lanes, lanes), 0)
    column = lax.broadcasted_iota(jnp.int32, (lanes, lanes), 1)
    same = (row // group == column // group) & (row < 2 * half) & (column < 2 * half)
    for basis in range(bases):
        weights = padded[0, basis] + pltpu.roll(padded[1, basis], half, 1)
        repeated = jnp.dot(repeat, weights.astype(BF16), preferred_element_type=F32)
        squares_ref[basis * lanes : (basis + 1) * lanes] = jnp.where(same, repeated, 0.0).astype(
            BF16
        )


def rows_of(message, block, rest):
    groups = unfold(message.astype(F32), block)
    last = (groups[2], pltpu.roll(groups[2], SUBLANES - rest, 0))
    return [jnp.concatenate([groups[row], last[row]], axis=0).astype(BF16) for row in range(2)]


def conv_kernel(block, width, *refs):
    even_mate, mate, odd_mate, odd_own, even_own, home = refs[:6]
    (table_ref, squares_ref), refs = refs[6:8], refs[8:]
    *out_refs, field, spread, stage = refs
    columns = len(out_refs)
    lanes = squares_ref.shape[1]
    bases = squares_ref.shape[0] // lanes
    rows, _, inner = table_ref.shape
    places = inner // 3
    step = places // (2 * columns)
    half = places // 2
    rest = width - SUBLANES
    column, side = column_and_side()
    odd = lax.axis_index("lat") % 2
    for message_side, (own, even, other) in (
        (side, (home, even_own, odd_own)),
        (1 - side, (mate, even_mate, odd_mate)),
    ):
        for at in range(columns):
            first = pl.multiple_of((2 * at + message_side) * step, step)
            for row, read in enumerate(rows_of(own[at], block, rest)):
                field[row, pl.ds(2 * places + first, step)] = read
            for ref, row in ((even, 1 - odd), (other, odd)):
                for slot, read in enumerate(rows_of(ref[at], block, rest)):
                    field[row, pl.ds(slot * places + first, step)] = read
    for row in range(rows):
        over = jnp.dot(table_ref[row], field[row], preferred_element_type=F32).astype(BF16)
        for basis in range(bases):
            spread[row * half : (row + 1) * half, basis * lanes : (basis + 1) * lanes] = over[
                basis * half : (basis + 1) * half
            ]
    mixed = jnp.dot(spread[...], squares_ref[...], preferred_element_type=F32)
    upper = lax.broadcasted_iota(jnp.int32, (SUBLANES, lanes), 0) < rest
    for target in range(columns):
        top = mixed[target * step : (target + 1) * step]
        bottom = mixed[half + target * step : half + (target + 1) * step]
        last = jnp.where(upper, top[SUBLANES:], pltpu.roll(bottom[SUBLANES:], rest, 0))
        points = jnp.concatenate([top[:SUBLANES], bottom[:SUBLANES], last], axis=0)
        stage[target] = fold(points, block)
    for apart in range(columns):
        out_refs[apart][...] = stage[column ^ apart]


def tail_kernel(order, *refs):
    columns = len(order)
    back_refs = refs[:columns]
    latent_ref, up_ref, down_ref, out_ref, points, stage = refs[columns:]
    width, rows, chans = latent_ref.shape
    rest = width - SUBLANES
    block = chans // columns
    lanes = lanes_of(block)
    column, _ = column_and_side()
    for apart, ref in zip(order, back_refs):
        stage[column ^ apart] = ref[...]
    group_points(latent_ref, points)
    kept = lax.broadcasted_iota(jnp.int32, (3 * SUBLANES, lanes), 1) < block
    convolved = None
    for target in range(columns):
        piece = jnp.concatenate(unfold(stage[target].astype(F32), block), axis=0)
        piece = jnp.where(kept, piece, 0.0)
        if chans > lanes:
            gap = jnp.zeros((3 * SUBLANES, chans - lanes), F32)
            piece = jnp.concatenate([piece, gap], axis=1)
        piece = pltpu.roll(piece, target * block, 1) if target else piece
        convolved = piece if convolved is None else convolved + piece
    summed = (points[...] + convolved).astype(BF16).astype(F32)
    centred = summed - jnp.mean(summed, axis=1, keepdims=True)
    variance = jnp.mean(centred * centred, axis=1, keepdims=True)
    normed = (centred * lax.rsqrt(variance + 1e-05)).astype(BF16)
    hidden = jnp.dot(normed, up_ref[...], preferred_element_type=F32)
    hidden = (0.5 * hidden * (1.0 + lax.erf(hidden * 0.5**0.5))).astype(BF16)
    result = summed + jnp.dot(hidden, down_ref[...], preferred_element_type=F32)
    for row in range(rows):
        out_ref[:SUBLANES, row, :] = result[row * SUBLANES : (row + 1) * SUBLANES].astype(BF16)
        at = rows * SUBLANES + row * rest
        out_ref[SUBLANES:, row, :] = result[at : at + rest].astype(BF16)


VMEM = pl.BlockSpec(memory_space=pltpu.VMEM)


def call(kernel, name, out_shape, scratch, work, *operands, space=pltpu.VMEM):
    several = isinstance(out_shape, tuple)
    return pl.pallas_call(
        kernel,
        out_shape=out_shape,
        in_specs=[pl.BlockSpec(memory_space=space)] * len(operands),
        out_specs=(VMEM,) * len(out_shape) if several else VMEM,
        scratch_shapes=scratch,
        compiler_params=pltpu.CompilerParams(vmem_limit_bytes=24 * 2**20),
        cost_estimate=pl.CostEstimate(flops=work, bytes_accessed=10**6, transcendentals=0),
        name=name,
    )(*operands)


def over_columns(messages, count):
    arrived = {0: messages[0]}
    for apart in reversed(range(1, count // 2)):
        pairs = [(i, ((i // 2) ^ apart) * 2 + i % 2) for i in range(count)]
        arrived[apart] = lax.ppermute(messages[apart], "lon", pairs)
    return arrived


def over_sides(block, count):
    return lax.ppermute(block, "lon", [(i, i ^ 1) for i in range(count)])


def around(block, count):
    rows = lax.axis_size("lat")
    lat_even = [i ^ 1 for i in range(rows)]
    lat_odd = [((i - 1) ^ 1) + 1 if i else rows - 1 for i in range(rows)]
    lat_odd[rows - 1] = 0
    lat_self = list(range(rows))

    def swap(lat_of, other_side):
        pairs = [
            (lat * count + lon, lat_of[lat] * count + (lon ^ other_side))
            for lat in range(rows)
            for lon in range(count)
        ]
        return lax.ppermute(block, ("lat", "lon"), pairs)

    even_mate = swap(lat_even, 1)
    mate = swap(lat_self, 1)
    odd_mate = swap(lat_odd, 1)
    odd_own = swap(lat_odd, 0)
    even_own = swap(lat_even, 0)
    return even_mate, mate, odd_mate, odd_own, even_own


def local(latent, lon_filter, mix_weight, band_weight, offsets, w_up, w_down):
    rows, width, chans = latent.shape
    bases, lons = lon_filter.shape
    half, group = mix_weight.shape[1:]
    taps = band_weight.shape[2]
    count = lons // width
    columns = count // 2
    block = 2 * half
    step = up_to(width, 2 * SUBLANES)
    places = count * step
    lanes = lanes_of(block)
    height = message_rows(block)
    assert rows == 2 and taps == 3 and columns & (columns - 1) == 0
    assert SUBLANES < width and rows * (width - SUBLANES) <= SUBLANES
    assert 3 * (block % LANES) <= LANES

    far_first = tuple(reversed(range(columns)))
    near_then_far = (1,) + tuple(reversed(range(2, columns))) + (0,)
    message = jax.ShapeDtypeStruct((height, LANES), BF16)
    messages = (message,) * columns
    stage = pltpu.VMEM((columns, height, LANES), BF16)
    points = pltpu.VMEM((3 * SUBLANES, chans), F32)
    lon_first = jnp.transpose(latent, (1, 0, 2))
    mix_own = jnp.transpose(mix_weight, (0, 2, 1))

    packed = call(
        pack_kernel,
        "pack",
        messages,
        [points, stage, pltpu.VMEM(lon_first.shape, BF16), pltpu.SemaphoreType.DMA],
        10**9,
        lon_first,
        space=pltpu.HBM,
    )
    arrived = over_columns(packed, count)
    mix_mate = over_sides(mix_own, count)
    table = call(
        functools.partial(tables_kernel, width),
        "tables",
        jax.ShapeDtypeStruct((rows, bases * places // 2, taps * places), BF16),
        [pltpu.VMEM((bases, step, places), F32)],
        10**9,
        lon_filter,
        jnp.transpose(band_weight, (2, 1, 0)),
    )
    squares = call(
        squares_kernel,
        "squares",
        jax.ShapeDtypeStruct((bases * lanes, lanes), BF16),
        [pltpu.VMEM((2, bases, up_to(group, 2 * SUBLANES), lanes), F32)],
        10**9,
        mix_own,
        mix_mate,
    )
    gathered = jax.ShapeDtypeStruct((columns, height, LANES), BF16)
    own_side = call(
        functools.partial(column_kernel, far_first),
        "join_columns",
        gathered,
        [],
        10**8,
        *[arrived[apart] for apart in far_first],
    )
    sources = around(own_side, count)
    mixed = call(
        functools.partial(conv_kernel, block, width),
        "conv",
        messages,
        [
            pltpu.VMEM((rows, taps * places, lanes), BF16),
            pltpu.VMEM((rows * places // 2, bases * lanes), BF16),
            stage,
        ],
        10**10,
        *sources,
        own_side,
        table,
        squares,
    )
    back = over_columns(mixed, count)
    result = call(
        functools.partial(tail_kernel, near_then_far),
        "tail",
        jax.ShapeDtypeStruct(lon_first.shape, BF16),
        [points, stage],
        10**9,
        *[back[apart] for apart in near_then_far],
        lon_first,
        w_up,
        w_down,
    )
    return jnp.transpose(result, (1, 0, 2))


def solution(mesh):
    return jax.shard_map(
        local,
        mesh=mesh,
        in_specs=(
            P("lat", "lon", None),
            P(),
            P(None, "lon", None),
            P(None, "lat", None),
            P("lat"),
            P(),
            P(),
        ),
        out_specs=P("lat", "lon", None),
        check_vma=False,
    )
```

```python
import functools

import jax
import jax.numpy as jnp
from jax import lax
from jax.experimental import pallas as pl
from jax.experimental.pallas import tpu as pltpu
from jax.sharding import PartitionSpec as P

F32 = jnp.float32
BF16 = jnp.bfloat16
LANES = 128
SUBLANES = 8


def up_to(size, step):
    return -(-size // step) * step


def column_and_side():
    place = lax.axis_index("lon")
    return place // 2, place % 2


def message_rows(block):
    tiles = block // LANES
    return up_to(3 * SUBLANES * tiles + (SUBLANES if block % LANES else 0), 2 * SUBLANES)


def lanes_of(block):
    return up_to(block, LANES)


def fold(points, block):
    whole, rest = divmod(block, LANES)
    parts = [points[:, tile * LANES : (tile + 1) * LANES] for tile in range(whole)]
    if rest:
        odd = points[:, whole * LANES : (whole + 1) * LANES]
        kept = lax.broadcasted_iota(jnp.int32, (SUBLANES, LANES), 1) < rest
        shared = None
        for third in range(3):
            piece = jnp.where(kept, odd[third * SUBLANES : (third + 1) * SUBLANES], 0.0)
            piece = pltpu.roll(piece, third * rest, 1) if third else piece
            shared = piece if shared is None else shared + piece
        parts.append(shared)
    filled = sum(part.shape[0] for part in parts)
    if message_rows(block) > filled:
        parts.append(jnp.zeros((message_rows(block) - filled, LANES), F32))
    return jnp.concatenate(parts, axis=0).astype(BF16)


def unfold(message, block):
    whole, rest = divmod(block, LANES)
    groups = []
    for third in range(3):
        first = third * SUBLANES
        parts = [
            message[tile * 3 * SUBLANES + first : tile * 3 * SUBLANES + first + SUBLANES]
            for tile in range(whole)
        ]
        if rest:
            odd = message[whole * 3 * SUBLANES : whole * 3 * SUBLANES + SUBLANES]
            parts.append(pltpu.roll(odd, LANES - third * rest, 1) if third else odd)
        groups.append(jnp.concatenate(parts, axis=1) if len(parts) > 1 else parts[0])
    return groups


def group_points(latent_ref, points):
    width, rows, _ = latent_ref.shape
    rest = width - SUBLANES
    for row in range(rows):
        points[row * SUBLANES : (row + 1) * SUBLANES] = latent_ref[:SUBLANES, row, :].astype(F32)
        at = rows * SUBLANES + row * rest
        points[at : at + rest] = latent_ref[SUBLANES:, row, :].astype(F32)


def pack_kernel(latent_ref, *refs):
    *out_refs, points, stage = refs
    columns = len(out_refs)
    chans = latent_ref.shape[2]
    block = chans // columns
    column, _ = column_and_side()
    group_points(latent_ref, points)
    own = points[...]
    for target in range(columns):
        turned = pltpu.roll(own, chans - target * block, 1) if target else own
        stage[target] = fold(turned[:, : lanes_of(block)], block)
    for apart in range(columns):
        out_refs[apart][...] = stage[column ^ apart]


def column_kernel(order, *refs):
    *in_refs, out_ref = refs
    column, _ = column_and_side()
    for apart, ref in zip(order, in_refs):
        out_ref[column ^ apart] = ref[...]


def tables_kernel(width, filter_ref, band_ref, table_ref, first):
    bases, lons = filter_ref.shape
    taps, rows, _ = band_ref.shape
    step, places = first.shape[1:]
    columns = places // (2 * step)
    _, side = column_and_side()
    lat = lax.axis_index("lat")
    below = (lat > 0).astype(F32)
    above = (lat < lax.axis_size("lat") - 1).astype(F32)
    inside = [[below, below, 1.0], [1.0, above, above]]
    slots = [[0, 1, 2], [2, 0, 1]]
    profile = filter_ref[...]
    band = band_ref[...].astype(F32)
    source = lax.broadcasted_iota(jnp.int32, (lons, places), 0)
    place = lax.broadcasted_iota(jnp.int32, (lons, places), 1)
    within = place % step
    apart = source + (place // step) * width + within + (lons - side * width)
    for _ in range(3):
        apart = jnp.where(apart >= lons, apart - lons, apart)
    apart = jnp.where(within < width, apart, -1)
    first[...] = jnp.zeros_like(first)
    for lon in range(width):
        pick = (apart == lon).astype(F32).astype(BF16)
        first[:, lon, :] = jnp.dot(profile, pick, preferred_element_type=F32)
    for basis in range(bases):
        circle = first[basis]
        for column in range(columns):
            turned = pltpu.roll(circle, column * 2 * step, 1) if column else circle
            at = (basis * columns + column) * step
            for row in range(rows):
                for tap in range(taps):
                    weight = band[tap, row : row + 1, basis : basis + 1] * inside[row][tap]
                    to = slots[row][tap] * places
                    table_ref[row, at : at + step, to : to + places] = (weight * turned).astype(
                        BF16
                    )


def squares_kernel(own_ref, mate_ref, squares_ref, padded):
    bases, group, half = own_ref.shape
    lanes = squares_ref.shape[1]
    _, side = column_and_side()
    first = side == 0
    own = own_ref[...].astype(F32)
    mate = mate_ref[...].astype(F32)
    padded[...] = jnp.zeros_like(padded)
    padded[0, :, :group, :half] = jnp.where(first, own, mate)
    padded[1, :, :group, :half] = jnp.where(first, mate, own)
    members = padded.shape[2]
    into = lax.broadcasted_iota(jnp.int32, (lanes, members), 0)
    member = lax.broadcasted_iota(jnp.int32, (lanes, members), 1)
    repeat = (into % group == member).astype(F32).astype(BF16)
    row = lax.broadcasted_iota(jnp.int32, (lanes, lanes), 0)
    column = lax.broadcasted_iota(jnp.int32, (lanes, lanes), 1)
    same = (row // group == column // group) & (row < 2 * half) & (column < 2 * half)
    for basis in range(bases):
        weights = padded[0, basis] + pltpu.roll(padded[1, basis], half, 1)
        repeated = jnp.dot(repeat, weights.astype(BF16), preferred_element_type=F32)
        squares_ref[basis * lanes : (basis + 1) * lanes] = jnp.where(same, repeated, 0.0).astype(
            BF16
        )


def rows_of(message, block, rest):
    groups = unfold(message.astype(F32), block)
    last = (groups[2], pltpu.roll(groups[2], SUBLANES - rest, 0))
    return [jnp.concatenate([groups[row], last[row]], axis=0).astype(BF16) for row in range(2)]


def conv_kernel(block, width, *refs):
    even_mate, mate, even_own, odd_mate, odd_own, home = refs[:6]
    (table_ref, squares_ref), refs = refs[6:8], refs[8:]
    *out_refs, field, spread, stage = refs
    columns = len(out_refs)
    lanes = squares_ref.shape[1]
    bases = squares_ref.shape[0] // lanes
    rows, _, inner = table_ref.shape
    places = inner // 3
    step = places // (2 * columns)
    half = places // 2
    rest = width - SUBLANES
    column, side = column_and_side()
    odd = lax.axis_index("lat") % 2
    for message_side, (own, even, other) in (
        (side, (home, even_own, odd_own)),
        (1 - side, (mate, even_mate, odd_mate)),
    ):
        for at in range(columns):
            first = pl.multiple_of((2 * at + message_side) * step, step)
            for row, read in enumerate(rows_of(own[at], block, rest)):
                field[row, pl.ds(2 * places + first, step)] = read
            for ref, row in ((even, 1 - odd), (other, odd)):
                for slot, read in enumerate(rows_of(ref[at], block, rest)):
                    field[row, pl.ds(slot * places + first, step)] = read
    for row in range(rows):
        over = jnp.dot(table_ref[row], field[row], preferred_element_type=F32).astype(BF16)
        for basis in range(bases):
            spread[row * half : (row + 1) * half, basis * lanes : (basis + 1) * lanes] = over[
                basis * half : (basis + 1) * half
            ]
    mixed = jnp.dot(spread[...], squares_ref[...], preferred_element_type=F32)
    upper = lax.broadcasted_iota(jnp.int32, (SUBLANES, lanes), 0) < rest
    for target in range(columns):
        top = mixed[target * step : (target + 1) * step]
        bottom = mixed[half + target * step : half + (target + 1) * step]
        last = jnp.where(upper, top[SUBLANES:], pltpu.roll(bottom[SUBLANES:], rest, 0))
        points = jnp.concatenate([top[:SUBLANES], bottom[:SUBLANES], last], axis=0)
        stage[target] = fold(points, block)
    for apart in range(columns):
        out_refs[apart][...] = stage[column ^ apart]


def tail_kernel(order, *refs):
    columns = len(order)
    back_refs = refs[:columns]
    latent_ref, up_ref, down_ref, out_ref, points, stage = refs[columns:]
    width, rows, chans = latent_ref.shape
    rest = width - SUBLANES
    block = chans // columns
    lanes = lanes_of(block)
    column, _ = column_and_side()
    for apart, ref in zip(order, back_refs):
        stage[column ^ apart] = ref[...]
    group_points(latent_ref, points)
    kept = lax.broadcasted_iota(jnp.int32, (3 * SUBLANES, lanes), 1) < block
    convolved = None
    for target in range(columns):
        piece = jnp.concatenate(unfold(stage[target].astype(F32), block), axis=0)
        piece = jnp.where(kept, piece, 0.0)
        if chans > lanes:
            gap = jnp.zeros((3 * SUBLANES, chans - lanes), F32)
            piece = jnp.concatenate([piece, gap], axis=1)
        piece = pltpu.roll(piece, target * block, 1) if target else piece
        convolved = piece if convolved is None else convolved + piece
    summed = (points[...] + convolved).astype(BF16).astype(F32)
    centred = summed - jnp.mean(summed, axis=1, keepdims=True)
    variance = jnp.mean(centred * centred, axis=1, keepdims=True)
    normed = (centred * lax.rsqrt(variance + 1e-05)).astype(BF16)
    hidden = jnp.dot(normed, up_ref[...], preferred_element_type=F32)
    hidden = (0.5 * hidden * (1.0 + lax.erf(hidden * 0.5**0.5))).astype(BF16)
    result = summed + jnp.dot(hidden, down_ref[...], preferred_element_type=F32)
    for row in range(rows):
        out_ref[:SUBLANES, row, :] = result[row * SUBLANES : (row + 1) * SUBLANES].astype(BF16)
        at = rows * SUBLANES + row * rest
        out_ref[SUBLANES:, row, :] = result[at : at + rest].astype(BF16)


VMEM = pl.BlockSpec(memory_space=pltpu.VMEM)


def call(kernel, name, out_shape, scratch, work, *operands):
    several = isinstance(out_shape, tuple)
    return pl.pallas_call(
        kernel,
        out_shape=out_shape,
        in_specs=[VMEM] * len(operands),
        out_specs=(VMEM,) * len(out_shape) if several else VMEM,
        scratch_shapes=scratch,
        compiler_params=pltpu.CompilerParams(vmem_limit_bytes=24 * 2**20),
        cost_estimate=pl.CostEstimate(flops=work, bytes_accessed=10**6, transcendentals=0),
        name=name,
    )(*operands)


def over_columns(messages, count):
    arrived = {0: messages[0]}
    for apart in reversed(range(1, count // 2)):
        pairs = [(i, ((i // 2) ^ apart) * 2 + i % 2) for i in range(count)]
        arrived[apart] = lax.ppermute(messages[apart], "lon", pairs)
    return arrived


def over_sides(block, count):
    return lax.ppermute(block, "lon", [(i, i ^ 1) for i in range(count)])


def around(block, count):
    rows = lax.axis_size("lat")

    def swap(partner):
        pairs = []
        for lat in range(rows):
            for lon in range(count):
                to_lat, to_lon = partner(lat, lon)
                pairs.append((lat * count + lon, to_lat * count + to_lon))
        return lax.ppermute(block, ("lat", "lon"), pairs)

    def odd(lat, lon, to_lon):
        to = lat + 1 if lat % 2 else lat - 1
        return (to, to_lon) if 0 <= to < rows else (lat, lon)

    mate = swap(lambda lat, lon: (lat, lon ^ 1))
    even_own = swap(lambda lat, lon: (lat ^ 1, lon))
    even_mate = swap(lambda lat, lon: (lat ^ 1, lon ^ 1))
    odd_own = swap(lambda lat, lon: odd(lat, lon, lon))
    odd_mate = swap(lambda lat, lon: odd(lat, lon, lon ^ 1))
    return even_mate, mate, even_own, odd_mate, odd_own


def local(latent, lon_filter, mix_weight, band_weight, offsets, w_up, w_down):
    rows, width, chans = latent.shape
    bases, lons = lon_filter.shape
    half, group = mix_weight.shape[1:]
    taps = band_weight.shape[2]
    count = lons // width
    columns = count // 2
    block = 2 * half
    step = up_to(width, 2 * SUBLANES)
    places = count * step
    lanes = lanes_of(block)
    height = message_rows(block)
    assert rows == 2 and taps == 3 and columns & (columns - 1) == 0
    assert lax.axis_size("lat") % 2 == 0
    assert SUBLANES < width and rows * (width - SUBLANES) <= SUBLANES
    assert 3 * (block % LANES) <= LANES

    far_first = tuple(reversed(range(columns)))
    near_then_far = (1,) + tuple(reversed(range(2, columns))) + (0,)
    message = jax.ShapeDtypeStruct((height, LANES), BF16)
    messages = (message,) * columns
    stage = pltpu.VMEM((columns, height, LANES), BF16)
    points = pltpu.VMEM((3 * SUBLANES, chans), F32)
    lon_first = jnp.transpose(latent, (1, 0, 2))
    mix_own = jnp.transpose(mix_weight, (0, 2, 1))

    packed = call(pack_kernel, "pack", messages, [points, stage], 10**9, lon_first)
    arrived = over_columns(packed, count)
    mix_mate = over_sides(mix_own, count)
    table = call(
        functools.partial(tables_kernel, width),
        "tables",
        jax.ShapeDtypeStruct((rows, bases * places // 2, taps * places), BF16),
        [pltpu.VMEM((bases, step, places), F32)],
        10**9,
        lon_filter,
        jnp.transpose(band_weight, (2, 1, 0)),
    )
    squares = call(
        squares_kernel,
        "squares",
        jax.ShapeDtypeStruct((bases * lanes, lanes), BF16),
        [pltpu.VMEM((2, bases, up_to(group, 2 * SUBLANES), lanes), F32)],
        10**9,
        mix_own,
        mix_mate,
    )
    gathered = jax.ShapeDtypeStruct((columns, height, LANES), BF16)
    own_side = call(
        functools.partial(column_kernel, far_first),
        "join_columns",
        gathered,
        [],
        10**8,
        *[arrived[apart] for apart in far_first],
    )
    sources = around(own_side, count)
    mixed = call(
        functools.partial(conv_kernel, block, width),
        "conv",
        messages,
        [
            pltpu.VMEM((rows, taps * places, lanes), BF16),
            pltpu.VMEM((rows * places // 2, bases * lanes), BF16),
            stage,
        ],
        10**10,
        *sources,
        own_side,
        table,
        squares,
    )
    back = over_columns(mixed, count)
    result = call(
        functools.partial(tail_kernel, near_then_far),
        "tail",
        jax.ShapeDtypeStruct(lon_first.shape, BF16),
        [points, stage],
        10**9,
        *[back[apart] for apart in near_then_far],
        lon_first,
        w_up,
        w_down,
    )
    return jnp.transpose(result, (1, 0, 2))


def solution(mesh):
    return jax.shard_map(
        local,
        mesh=mesh,
        in_specs=(
            P("lat", "lon", None),
            P(),
            P(None, "lon", None),
            P(None, "lat", None),
            P("lat"),
            P(),
            P(),
        ),
        out_specs=P("lat", "lon", None),
        check_vma=False,
    )
```

```python
import functools

import jax
import jax.numpy as jnp
from jax import lax
from jax.experimental import pallas as pl
from jax.experimental.pallas import tpu as pltpu
from jax.sharding import PartitionSpec as P

F32 = jnp.float32
BF16 = jnp.bfloat16
LANES = 128
SUBLANES = 8


def up_to(size, step):
    return -(-size // step) * step


def column_and_side():
    place = lax.axis_index("lon")
    return place // 2, place % 2


def message_rows(block):
    tiles = block // LANES
    return up_to(3 * SUBLANES * tiles + (SUBLANES if block % LANES else 0), 2 * SUBLANES)


def lanes_of(block):
    return up_to(block, LANES)


def fold(points, block):
    whole, rest = divmod(block, LANES)
    parts = [points[:, tile * LANES : (tile + 1) * LANES] for tile in range(whole)]
    if rest:
        odd = points[:, whole * LANES : (whole + 1) * LANES]
        kept = lax.broadcasted_iota(jnp.int32, (SUBLANES, LANES), 1) < rest
        shared = None
        for third in range(3):
            piece = jnp.where(kept, odd[third * SUBLANES : (third + 1) * SUBLANES], 0.0)
            piece = pltpu.roll(piece, third * rest, 1) if third else piece
            shared = piece if shared is None else shared + piece
        parts.append(shared)
    filled = sum(part.shape[0] for part in parts)
    if message_rows(block) > filled:
        parts.append(jnp.zeros((message_rows(block) - filled, LANES), F32))
    return jnp.concatenate(parts, axis=0).astype(BF16)


def unfold(message, block):
    whole, rest = divmod(block, LANES)
    groups = []
    for third in range(3):
        first = third * SUBLANES
        parts = [
            message[tile * 3 * SUBLANES + first : tile * 3 * SUBLANES + first + SUBLANES]
            for tile in range(whole)
        ]
        if rest:
            odd = message[whole * 3 * SUBLANES : whole * 3 * SUBLANES + SUBLANES]
            parts.append(pltpu.roll(odd, LANES - third * rest, 1) if third else odd)
        groups.append(jnp.concatenate(parts, axis=1) if len(parts) > 1 else parts[0])
    return groups


def group_points(latent_ref, points):
    width, rows, _ = latent_ref.shape
    rest = width - SUBLANES
    for row in range(rows):
        points[row * SUBLANES : (row + 1) * SUBLANES] = latent_ref[:SUBLANES, row, :].astype(F32)
        at = rows * SUBLANES + row * rest
        points[at : at + rest] = latent_ref[SUBLANES:, row, :].astype(F32)


def pack_kernel(latent_ref, *refs):
    *out_refs, points, stage = refs
    columns = len(out_refs)
    chans = latent_ref.shape[2]
    block = chans // columns
    column, _ = column_and_side()
    group_points(latent_ref, points)
    own = points[...]
    for target in range(columns):
        turned = pltpu.roll(own, chans - target * block, 1) if target else own
        stage[target] = fold(turned[:, : lanes_of(block)], block)
    for apart in range(columns):
        out_refs[apart][...] = stage[column ^ apart]


def column_kernel(order, *refs):
    *in_refs, out_ref = refs
    column, _ = column_and_side()
    for apart, ref in zip(order, in_refs):
        out_ref[column ^ apart] = ref[...]


def tables_kernel(width, filter_ref, band_ref, table_ref, first):
    bases, lons = filter_ref.shape
    taps, rows, _ = band_ref.shape
    step, places = first.shape[1:]
    columns = places // (2 * step)
    _, side = column_and_side()
    lat = lax.axis_index("lat")
    below = (lat > 0).astype(F32)
    above = (lat < lax.axis_size("lat") - 1).astype(F32)
    inside = [[below, below, 1.0], [1.0, above, above]]
    slots = [[0, 1, 2], [2, 0, 1]]
    profile = filter_ref[...]
    band = band_ref[...].astype(F32)
    source = lax.broadcasted_iota(jnp.int32, (lons, places), 0)
    place = lax.broadcasted_iota(jnp.int32, (lons, places), 1)
    within = place % step
    apart = source + (place // step) * width + within + (lons - side * width)
    for _ in range(3):
        apart = jnp.where(apart >= lons, apart - lons, apart)
    apart = jnp.where(within < width, apart, -1)
    first[...] = jnp.zeros_like(first)
    for lon in range(width):
        pick = (apart == lon).astype(F32).astype(BF16)
        first[:, lon, :] = jnp.dot(profile, pick, preferred_element_type=F32)
    for basis in range(bases):
        circle = first[basis]
        for column in range(columns):
            turned = pltpu.roll(circle, column * 2 * step, 1) if column else circle
            at = (basis * columns + column) * step
            for row in range(rows):
                for tap in range(taps):
                    weight = band[tap, row : row + 1, basis : basis + 1] * inside[row][tap]
                    to = slots[row][tap] * places
                    table_ref[row, at : at + step, to : to + places] = (weight * turned).astype(
                        BF16
                    )


def squares_kernel(own_ref, mate_ref, squares_ref, padded):
    bases, group, half = own_ref.shape
    lanes = squares_ref.shape[1]
    _, side = column_and_side()
    first = side == 0
    own = own_ref[...].astype(F32)
    mate = mate_ref[...].astype(F32)
    padded[...] = jnp.zeros_like(padded)
    padded[0, :, :group, :half] = jnp.where(first, own, mate)
    padded[1, :, :group, :half] = jnp.where(first, mate, own)
    members = padded.shape[2]
    into = lax.broadcasted_iota(jnp.int32, (lanes, members), 0)
    member = lax.broadcasted_iota(jnp.int32, (lanes, members), 1)
    repeat = (into % group == member).astype(F32).astype(BF16)
    row = lax.broadcasted_iota(jnp.int32, (lanes, lanes), 0)
    column = lax.broadcasted_iota(jnp.int32, (lanes, lanes), 1)
    same = (row // group == column // group) & (row < 2 * half) & (column < 2 * half)
    for basis in range(bases):
        weights = padded[0, basis] + pltpu.roll(padded[1, basis], half, 1)
        repeated = jnp.dot(repeat, weights.astype(BF16), preferred_element_type=F32)
        squares_ref[basis * lanes : (basis + 1) * lanes] = jnp.where(same, repeated, 0.0).astype(
            BF16
        )


def rows_of(message, block, rest):
    groups = unfold(message.astype(F32), block)
    last = (groups[2], pltpu.roll(groups[2], SUBLANES - rest, 0))
    return [jnp.concatenate([groups[row], last[row]], axis=0).astype(BF16) for row in range(2)]


def conv_kernel(block, width, *refs):
    even_mate, mate, even_own, odd_mate, odd_own, home = refs[:6]
    (table_ref, squares_ref), refs = refs[6:8], refs[8:]
    *out_refs, field, spread, stage = refs
    columns = len(out_refs)
    lanes = squares_ref.shape[1]
    bases = squares_ref.shape[0] // lanes
    rows, _, inner = table_ref.shape
    places = inner // 3
    step = places // (2 * columns)
    half = places // 2
    rest = width - SUBLANES
    column, side = column_and_side()
    odd = lax.axis_index("lat") % 2
    for message_side, (own, even, other) in (
        (side, (home, even_own, odd_own)),
        (1 - side, (mate, even_mate, odd_mate)),
    ):
        for at in range(columns):
            first = pl.multiple_of((2 * at + message_side) * step, step)
            for row, read in enumerate(rows_of(own[at], block, rest)):
                field[row, pl.ds(2 * places + first, step)] = read
            for ref, row in ((even, 1 - odd), (other, odd)):
                for slot, read in enumerate(rows_of(ref[at], block, rest)):
                    field[row, pl.ds(slot * places + first, step)] = read
    for row in range(rows):
        over = jnp.dot(table_ref[row], field[row], preferred_element_type=F32).astype(BF16)
        for basis in range(bases):
            spread[row * half : (row + 1) * half, basis * lanes : (basis + 1) * lanes] = over[
                basis * half : (basis + 1) * half
            ]
    mixed = jnp.dot(spread[...], squares_ref[...], preferred_element_type=F32)
    upper = lax.broadcasted_iota(jnp.int32, (SUBLANES, lanes), 0) < rest
    for target in range(columns):
        top = mixed[target * step : (target + 1) * step]
        bottom = mixed[half + target * step : half + (target + 1) * step]
        last = jnp.where(upper, top[SUBLANES:], pltpu.roll(bottom[SUBLANES:], rest, 0))
        points = jnp.concatenate([top[:SUBLANES], bottom[:SUBLANES], last], axis=0)
        stage[target] = fold(points, block)
    for apart in range(columns):
        out_refs[apart][...] = stage[column ^ apart]


def tail_kernel(order, *refs):
    columns = len(order)
    back_refs = refs[:columns]
    latent_ref, up_ref, down_ref, out_ref, points, stage = refs[columns:]
    width, rows, chans = latent_ref.shape
    rest = width - SUBLANES
    block = chans // columns
    lanes = lanes_of(block)
    column, _ = column_and_side()
    for apart, ref in zip(order, back_refs):
        stage[column ^ apart] = ref[...]
    group_points(latent_ref, points)
    kept = lax.broadcasted_iota(jnp.int32, (3 * SUBLANES, lanes), 1) < block
    convolved = None
    for target in range(columns):
        piece = jnp.concatenate(unfold(stage[target].astype(F32), block), axis=0)
        piece = jnp.where(kept, piece, 0.0)
        if chans > lanes:
            gap = jnp.zeros((3 * SUBLANES, chans - lanes), F32)
            piece = jnp.concatenate([piece, gap], axis=1)
        piece = pltpu.roll(piece, target * block, 1) if target else piece
        convolved = piece if convolved is None else convolved + piece
    summed = (points[...] + convolved).astype(BF16).astype(F32)
    centred = summed - jnp.mean(summed, axis=1, keepdims=True)
    variance = jnp.mean(centred * centred, axis=1, keepdims=True)
    normed = (centred * lax.rsqrt(variance + 1e-05)).astype(BF16)
    hidden = jnp.dot(normed, up_ref[...], preferred_element_type=F32)
    hidden = (0.5 * hidden * (1.0 + lax.erf(hidden * 0.5**0.5))).astype(BF16)
    result = summed + jnp.dot(hidden, down_ref[...], preferred_element_type=F32)
    for row in range(rows):
        out_ref[:SUBLANES, row, :] = result[row * SUBLANES : (row + 1) * SUBLANES].astype(BF16)
        at = rows * SUBLANES + row * rest
        out_ref[SUBLANES:, row, :] = result[at : at + rest].astype(BF16)


VMEM = pl.BlockSpec(memory_space=pltpu.VMEM)


def call(kernel, name, out_shape, scratch, work, *operands):
    several = isinstance(out_shape, tuple)
    return pl.pallas_call(
        kernel,
        out_shape=out_shape,
        in_specs=[VMEM] * len(operands),
        out_specs=(VMEM,) * len(out_shape) if several else VMEM,
        scratch_shapes=scratch,
        compiler_params=pltpu.CompilerParams(vmem_limit_bytes=24 * 2**20),
        cost_estimate=pl.CostEstimate(flops=work, bytes_accessed=10**6, transcendentals=0),
        name=name,
    )(*operands)


def over_columns(messages, count):
    arrived = {0: messages[0]}
    for apart in reversed(range(1, count // 2)):
        pairs = [(i, ((i // 2) ^ apart) * 2 + i % 2) for i in range(count)]
        arrived[apart] = lax.ppermute(messages[apart], "lon", pairs)
    return arrived


def over_sides(block, count):
    return lax.ppermute(block, "lon", [(i, i ^ 1) for i in range(count)])


def around(block, count):
    rows = lax.axis_size("lat")

    def swap(partner):
        pairs = []
        for lat in range(rows):
            for lon in range(count):
                to_lat, to_lon = partner(lat, lon)
                pairs.append((lat * count + lon, to_lat * count + to_lon))
        return lax.ppermute(block, ("lat", "lon"), pairs)

    def odd(lat, lon, to_lon):
        to = lat + 1 if lat % 2 else lat - 1
        return (to, to_lon) if 0 <= to < rows else (lat, lon ^ 1)

    mate = swap(lambda lat, lon: (lat, lon ^ 1))
    even_own = swap(lambda lat, lon: (lat ^ 1, lon))
    even_mate = swap(lambda lat, lon: (lat ^ 1, lon ^ 1))
    odd_own = swap(lambda lat, lon: odd(lat, lon, lon))
    odd_mate = swap(lambda lat, lon: odd(lat, lon, lon ^ 1))
    return even_mate, mate, even_own, odd_mate, odd_own


def local(latent, lon_filter, mix_weight, band_weight, offsets, w_up, w_down):
    rows, width, chans = latent.shape
    bases, lons = lon_filter.shape
    half, group = mix_weight.shape[1:]
    taps = band_weight.shape[2]
    count = lons // width
    columns = count // 2
    block = 2 * half
    step = up_to(width, 2 * SUBLANES)
    places = count * step
    lanes = lanes_of(block)
    height = message_rows(block)
    assert rows == 2 and taps == 3 and columns & (columns - 1) == 0
    assert lax.axis_size("lat") % 2 == 0
    assert SUBLANES < width and rows * (width - SUBLANES) <= SUBLANES
    assert 3 * (block % LANES) <= LANES

    far_first = tuple(reversed(range(columns)))
    near_then_far = (1,) + tuple(reversed(range(2, columns))) + (0,)
    message = jax.ShapeDtypeStruct((height, LANES), BF16)
    messages = (message,) * columns
    stage = pltpu.VMEM((columns, height, LANES), BF16)
    points = pltpu.VMEM((3 * SUBLANES, chans), F32)
    lon_first = jnp.transpose(latent, (1, 0, 2))
    mix_own = jnp.transpose(mix_weight, (0, 2, 1))

    packed = call(pack_kernel, "pack", messages, [points, stage], 10**9, lon_first)
    arrived = over_columns(packed, count)
    mix_mate = over_sides(mix_own, count)
    table = call(
        functools.partial(tables_kernel, width),
        "tables",
        jax.ShapeDtypeStruct((rows, bases * places // 2, taps * places), BF16),
        [pltpu.VMEM((bases, step, places), F32)],
        10**9,
        lon_filter,
        jnp.transpose(band_weight, (2, 1, 0)),
    )
    squares = call(
        squares_kernel,
        "squares",
        jax.ShapeDtypeStruct((bases * lanes, lanes), BF16),
        [pltpu.VMEM((2, bases, up_to(group, 2 * SUBLANES), lanes), F32)],
        10**9,
        mix_own,
        mix_mate,
    )
    gathered = jax.ShapeDtypeStruct((columns, height, LANES), BF16)
    own_side = call(
        functools.partial(column_kernel, far_first),
        "join_columns",
        gathered,
        [],
        10**8,
        *[arrived[apart] for apart in far_first],
    )
    sources = around(own_side, count)
    mixed = call(
        functools.partial(conv_kernel, block, width),
        "conv",
        messages,
        [
            pltpu.VMEM((rows, taps * places, lanes), BF16),
            pltpu.VMEM((rows * places // 2, bases * lanes), BF16),
            stage,
        ],
        10**10,
        *sources,
        own_side,
        table,
        squares,
    )
    back = over_columns(mixed, count)
    result = call(
        functools.partial(tail_kernel, near_then_far),
        "tail",
        jax.ShapeDtypeStruct(lon_first.shape, BF16),
        [points, stage],
        10**9,
        *[back[apart] for apart in near_then_far],
        lon_first,
        w_up,
        w_down,
    )
    return jnp.transpose(result, (1, 0, 2))


def solution(mesh):
    return jax.shard_map(
        local,
        mesh=mesh,
        in_specs=(
            P("lat", "lon", None),
            P(),
            P(None, "lon", None),
            P(None, "lat", None),
            P("lat"),
            P(),
            P(),
        ),
        out_specs=P("lat", "lon", None),
        check_vma=False,
    )
```

```python
import functools

import jax
import jax.numpy as jnp
from jax import lax
from jax.experimental import pallas as pl
from jax.experimental.pallas import tpu as pltpu
from jax.sharding import PartitionSpec as P

F32 = jnp.float32
BF16 = jnp.bfloat16
LANES = 128
SUBLANES = 8


def up_to(size, step):
    return -(-size // step) * step


def column_and_side():
    place = lax.axis_index("lon")
    return place // 2, place % 2


def message_rows(block):
    tiles = block // LANES
    return up_to(3 * SUBLANES * tiles + (SUBLANES if block % LANES else 0), 2 * SUBLANES)


def lanes_of(block):
    return up_to(block, LANES)


def fold(points, block):
    whole, rest = divmod(block, LANES)
    parts = [points[:, tile * LANES : (tile + 1) * LANES] for tile in range(whole)]
    if rest:
        odd = points[:, whole * LANES : (whole + 1) * LANES]
        kept = lax.broadcasted_iota(jnp.int32, (SUBLANES, LANES), 1) < rest
        shared = None
        for third in range(3):
            piece = jnp.where(kept, odd[third * SUBLANES : (third + 1) * SUBLANES], 0.0)
            piece = pltpu.roll(piece, third * rest, 1) if third else piece
            shared = piece if shared is None else shared + piece
        parts.append(shared)
    filled = sum(part.shape[0] for part in parts)
    if message_rows(block) > filled:
        parts.append(jnp.zeros((message_rows(block) - filled, LANES), F32))
    return jnp.concatenate(parts, axis=0).astype(BF16)


def unfold(message, block):
    whole, rest = divmod(block, LANES)
    groups = []
    for third in range(3):
        first = third * SUBLANES
        parts = [
            message[tile * 3 * SUBLANES + first : tile * 3 * SUBLANES + first + SUBLANES]
            for tile in range(whole)
        ]
        if rest:
            odd = message[whole * 3 * SUBLANES : whole * 3 * SUBLANES + SUBLANES]
            parts.append(pltpu.roll(odd, LANES - third * rest, 1) if third else odd)
        groups.append(jnp.concatenate(parts, axis=1) if len(parts) > 1 else parts[0])
    return groups


def group_points(latent_ref, points):
    width, rows, _ = latent_ref.shape
    rest = width - SUBLANES
    for row in range(rows):
        points[row * SUBLANES : (row + 1) * SUBLANES] = latent_ref[:SUBLANES, row, :].astype(F32)
        at = rows * SUBLANES + row * rest
        points[at : at + rest] = latent_ref[SUBLANES:, row, :].astype(F32)


def pack_kernel(latent_ref, *refs):
    *out_refs, points, stage = refs
    columns = len(out_refs)
    chans = latent_ref.shape[2]
    block = chans // columns
    column, _ = column_and_side()
    group_points(latent_ref, points)
    own = points[...]
    for target in range(columns):
        turned = pltpu.roll(own, chans - target * block, 1) if target else own
        stage[target] = fold(turned[:, : lanes_of(block)], block)
    for apart in range(columns):
        out_refs[apart][...] = stage[column ^ apart]


def column_kernel(order, *refs):
    *in_refs, out_ref = refs
    column, _ = column_and_side()
    for apart, ref in zip(order, in_refs):
        out_ref[column ^ apart] = ref[...]


def sides_kernel(own_ref, mate_ref, out_ref):
    _, side = column_and_side()
    out_ref[:, side] = own_ref[...]
    out_ref[:, 1 - side] = mate_ref[...]


def tables_kernel(width, filter_ref, band_ref, table_ref, first):
    bases, lons = filter_ref.shape
    taps, rows, _ = band_ref.shape
    step, places = first.shape[1:]
    columns = places // (2 * step)
    _, side = column_and_side()
    lat = lax.axis_index("lat")
    below = (lat > 0).astype(F32)
    above = (lat < lax.axis_size("lat") - 1).astype(F32)
    inside = [[below, below, 1.0], [1.0, above, above]]
    slots = [[0, 1, 2], [2, 0, 1]]
    profile = filter_ref[...]
    band = band_ref[...].astype(F32)
    source = lax.broadcasted_iota(jnp.int32, (lons, places), 0)
    place = lax.broadcasted_iota(jnp.int32, (lons, places), 1)
    within = place % step
    apart = source + (place // step) * width + within + (lons - side * width)
    for _ in range(3):
        apart = jnp.where(apart >= lons, apart - lons, apart)
    apart = jnp.where(within < width, apart, -1)
    first[...] = jnp.zeros_like(first)
    for lon in range(width):
        pick = (apart == lon).astype(F32).astype(BF16)
        first[:, lon, :] = jnp.dot(profile, pick, preferred_element_type=F32)
    for basis in range(bases):
        circle = first[basis]
        for column in range(columns):
            turned = pltpu.roll(circle, column * 2 * step, 1) if column else circle
            at = (basis * columns + column) * step
            for row in range(rows):
                for tap in range(taps):
                    weight = band[tap, row : row + 1, basis : basis + 1] * inside[row][tap]
                    to = slots[row][tap] * places
                    table_ref[row, at : at + step, to : to + places] = (weight * turned).astype(
                        BF16
                    )


def squares_kernel(own_ref, mate_ref, squares_ref, padded):
    bases, group, half = own_ref.shape
    lanes = squares_ref.shape[1]
    _, side = column_and_side()
    first = side == 0
    own = own_ref[...].astype(F32)
    mate = mate_ref[...].astype(F32)
    padded[...] = jnp.zeros_like(padded)
    padded[0, :, :group, :half] = jnp.where(first, own, mate)
    padded[1, :, :group, :half] = jnp.where(first, mate, own)
    members = padded.shape[2]
    into = lax.broadcasted_iota(jnp.int32, (lanes, members), 0)
    member = lax.broadcasted_iota(jnp.int32, (lanes, members), 1)
    repeat = (into % group == member).astype(F32).astype(BF16)
    row = lax.broadcasted_iota(jnp.int32, (lanes, lanes), 0)
    column = lax.broadcasted_iota(jnp.int32, (lanes, lanes), 1)
    same = (row // group == column // group) & (row < 2 * half) & (column < 2 * half)
    for basis in range(bases):
        weights = padded[0, basis] + pltpu.roll(padded[1, basis], half, 1)
        repeated = jnp.dot(repeat, weights.astype(BF16), preferred_element_type=F32)
        squares_ref[basis * lanes : (basis + 1) * lanes] = jnp.where(same, repeated, 0.0).astype(
            BF16
        )


def rows_of(message, block, rest):
    groups = unfold(message.astype(F32), block)
    last = (groups[2], pltpu.roll(groups[2], SUBLANES - rest, 0))
    return [jnp.concatenate([groups[row], last[row]], axis=0).astype(BF16) for row in range(2)]


def conv_kernel(block, width, *refs):
    odd_mate, odd_own, even, home, table_ref, squares_ref, *refs = refs
    *out_refs, field, spread, stage = refs
    columns = len(out_refs)
    lanes = squares_ref.shape[1]
    bases = squares_ref.shape[0] // lanes
    rows, _, inner = table_ref.shape
    places = inner // 3
    step = places // (2 * columns)
    half = places // 2
    rest = width - SUBLANES
    column, side = column_and_side()
    odd = lax.axis_index("lat") % 2

    def place(row, slot, at, read):
        first = pl.multiple_of(slot * places + at * step, step)
        field[row, pl.ds(first, step)] = read

    for at in range(columns):
        for half_at in range(2):
            for row, read in enumerate(rows_of(home[at, half_at], block, rest)):
                place(row, 2, 2 * at + half_at, read)
            for slot, read in enumerate(rows_of(even[at, half_at], block, rest)):
                place(1 - odd, slot, 2 * at + half_at, read)
        for message_side, ref in ((side, odd_own), (1 - side, odd_mate)):
            for slot, read in enumerate(rows_of(ref[at], block, rest)):
                place(odd, slot, 2 * at + message_side, read)
    for row in range(rows):
        over = jnp.dot(table_ref[row], field[row], preferred_element_type=F32).astype(BF16)
        for basis in range(bases):
            spread[row * half : (row + 1) * half, basis * lanes : (basis + 1) * lanes] = over[
                basis * half : (basis + 1) * half
            ]
    mixed = jnp.dot(spread[...], squares_ref[...], preferred_element_type=F32)
    upper = lax.broadcasted_iota(jnp.int32, (SUBLANES, lanes), 0) < rest
    for target in range(columns):
        top = mixed[target * step : (target + 1) * step]
        bottom = mixed[half + target * step : half + (target + 1) * step]
        last = jnp.where(upper, top[SUBLANES:], pltpu.roll(bottom[SUBLANES:], rest, 0))
        points = jnp.concatenate([top[:SUBLANES], bottom[:SUBLANES], last], axis=0)
        stage[target] = fold(points, block)
    for apart in range(columns):
        out_refs[apart][...] = stage[column ^ apart]


def tail_kernel(order, *refs):
    columns = len(order)
    back_refs = refs[:columns]
    latent_ref, up_ref, down_ref, out_ref, points, stage = refs[columns:]
    width, rows, chans = latent_ref.shape
    rest = width - SUBLANES
    block = chans // columns
    lanes = lanes_of(block)
    column, _ = column_and_side()
    for apart, ref in zip(order, back_refs):
        stage[column ^ apart] = ref[...]
    group_points(latent_ref, points)
    kept = lax.broadcasted_iota(jnp.int32, (3 * SUBLANES, lanes), 1) < block
    convolved = None
    for target in range(columns):
        piece = jnp.concatenate(unfold(stage[target].astype(F32), block), axis=0)
        piece = jnp.where(kept, piece, 0.0)
        if chans > lanes:
            gap = jnp.zeros((3 * SUBLANES, chans - lanes), F32)
            piece = jnp.concatenate([piece, gap], axis=1)
        piece = pltpu.roll(piece, target * block, 1) if target else piece
        convolved = piece if convolved is None else convolved + piece
    summed = (points[...] + convolved).astype(BF16).astype(F32)
    centred = summed - jnp.mean(summed, axis=1, keepdims=True)
    variance = jnp.mean(centred * centred, axis=1, keepdims=True)
    normed = (centred * lax.rsqrt(variance + 1e-05)).astype(BF16)
    hidden = jnp.dot(normed, up_ref[...], preferred_element_type=F32)
    hidden = (0.5 * hidden * (1.0 + lax.erf(hidden * 0.5**0.5))).astype(BF16)
    result = summed + jnp.dot(hidden, down_ref[...], preferred_element_type=F32)
    for row in range(rows):
        out_ref[:SUBLANES, row, :] = result[row * SUBLANES : (row + 1) * SUBLANES].astype(BF16)
        at = rows * SUBLANES + row * rest
        out_ref[SUBLANES:, row, :] = result[at : at + rest].astype(BF16)


VMEM = pl.BlockSpec(memory_space=pltpu.VMEM)


def call(kernel, name, out_shape, scratch, work, *operands):
    several = isinstance(out_shape, tuple)
    return pl.pallas_call(
        kernel,
        out_shape=out_shape,
        in_specs=[VMEM] * len(operands),
        out_specs=(VMEM,) * len(out_shape) if several else VMEM,
        scratch_shapes=scratch,
        compiler_params=pltpu.CompilerParams(vmem_limit_bytes=24 * 2**20),
        cost_estimate=pl.CostEstimate(flops=work, bytes_accessed=10**6, transcendentals=0),
        name=name,
    )(*operands)


def over_columns(messages, count):
    arrived = {0: messages[0]}
    for apart in reversed(range(1, count // 2)):
        pairs = [(i, ((i // 2) ^ apart) * 2 + i % 2) for i in range(count)]
        arrived[apart] = lax.ppermute(messages[apart], "lon", pairs)
    return arrived


def over_sides(block, count):
    return lax.ppermute(block, "lon", [(i, i ^ 1) for i in range(count)])


def swap(block, count, partner):
    pairs = []
    for lat in range(lax.axis_size("lat")):
        for lon in range(count):
            to_lat, to_lon = partner(lat, lon)
            pairs.append((lat * count + lon, to_lat * count + to_lon))
    return lax.ppermute(block, ("lat", "lon"), pairs)


def odd_pair(lat, lon, to_lon, rows):
    to = lat + 1 if lat % 2 else lat - 1
    return (to, to_lon) if 0 <= to < rows else (lat, lon ^ 1)


def local(latent, lon_filter, mix_weight, band_weight, offsets, w_up, w_down):
    rows, width, chans = latent.shape
    bases, lons = lon_filter.shape
    half, group = mix_weight.shape[1:]
    taps = band_weight.shape[2]
    count = lons // width
    columns = count // 2
    block = 2 * half
    step = up_to(width, 2 * SUBLANES)
    places = count * step
    lanes = lanes_of(block)
    height = message_rows(block)
    assert rows == 2 and taps == 3 and columns & (columns - 1) == 0
    assert lax.axis_size("lat") % 2 == 0
    assert SUBLANES < width and rows * (width - SUBLANES) <= SUBLANES
    assert 3 * (block % LANES) <= LANES

    far_first = tuple(reversed(range(columns)))
    last_first = (far_first[1:-1] + far_first[:1] + (0,)) if columns > 2 else far_first
    message = jax.ShapeDtypeStruct((height, LANES), BF16)
    messages = (message,) * columns
    stage = pltpu.VMEM((columns, height, LANES), BF16)
    points = pltpu.VMEM((3 * SUBLANES, chans), F32)
    lon_first = jnp.transpose(latent, (1, 0, 2))
    mix_own = jnp.transpose(mix_weight, (0, 2, 1))

    packed = call(pack_kernel, "pack", messages, [points, stage], 10**9, lon_first)
    arrived = over_columns(packed, count)
    mix_mate = over_sides(mix_own, count)
    table = call(
        functools.partial(tables_kernel, width),
        "tables",
        jax.ShapeDtypeStruct((rows, bases * places // 2, taps * places), BF16),
        [pltpu.VMEM((bases, step, places), F32)],
        10**9,
        lon_filter,
        jnp.transpose(band_weight, (2, 1, 0)),
    )
    squares = call(
        squares_kernel,
        "squares",
        jax.ShapeDtypeStruct((bases * lanes, lanes), BF16),
        [pltpu.VMEM((2, bases, up_to(group, 2 * SUBLANES), lanes), F32)],
        10**9,
        mix_own,
        mix_mate,
    )
    gathered = jax.ShapeDtypeStruct((columns, height, LANES), BF16)
    own_side = call(
        functools.partial(column_kernel, far_first),
        "join_columns",
        gathered,
        [],
        10**8,
        *[arrived[apart] for apart in far_first],
    )
    lats = lax.axis_size("lat")
    mate_side = swap(own_side, count, lambda lat, lon: (lat, lon ^ 1))
    odd_mate = swap(own_side, count, lambda lat, lon: odd_pair(lat, lon, lon ^ 1, lats))
    odd_own = swap(own_side, count, lambda lat, lon: odd_pair(lat, lon, lon, lats))
    circle = jax.ShapeDtypeStruct((columns, 2, height, LANES), BF16)
    home = call(sides_kernel, "join_sides", circle, [], 10**8, own_side, mate_side)
    even = swap(home, count, lambda lat, lon: (lat ^ 1, lon))
    mixed = call(
        functools.partial(conv_kernel, block, width),
        "conv",
        messages,
        [
            pltpu.VMEM((rows, taps * places, lanes), BF16),
            pltpu.VMEM((rows * places // 2, bases * lanes), BF16),
            stage,
        ],
        10**10,
        odd_mate,
        odd_own,
        even,
        home,
        table,
        squares,
    )
    back = over_columns(mixed, count)
    result = call(
        functools.partial(tail_kernel, last_first),
        "tail",
        jax.ShapeDtypeStruct(lon_first.shape, BF16),
        [points, stage],
        10**9,
        *[back[apart] for apart in last_first],
        lon_first,
        w_up,
        w_down,
    )
    return jnp.transpose(result, (1, 0, 2))


def solution(mesh):
    return jax.shard_map(
        local,
        mesh=mesh,
        in_specs=(
            P("lat", "lon", None),
            P(),
            P(None, "lon", None),
            P(None, "lat", None),
            P("lat"),
            P(),
            P(),
        ),
        out_specs=P("lat", "lon", None),
        check_vma=False,
    )
```

```python
import functools

import jax
import jax.numpy as jnp
from jax import lax
from jax.experimental import pallas as pl
from jax.experimental.pallas import tpu as pltpu
from jax.sharding import PartitionSpec as P

F32 = jnp.float32
BF16 = jnp.bfloat16
LANES = 128
SUBLANES = 8


def up_to(size, step):
    return -(-size // step) * step


def column_and_side():
    place = lax.axis_index("lon")
    return place // 2, place % 2


def message_rows(block):
    tiles = block // LANES
    return up_to(3 * SUBLANES * tiles + (SUBLANES if block % LANES else 0), 2 * SUBLANES)


def lanes_of(block):
    return up_to(block, LANES)


def fold(points, block):
    whole, rest = divmod(block, LANES)
    parts = [points[:, tile * LANES : (tile + 1) * LANES] for tile in range(whole)]
    if rest:
        odd = points[:, whole * LANES : (whole + 1) * LANES]
        kept = lax.broadcasted_iota(jnp.int32, (SUBLANES, LANES), 1) < rest
        shared = None
        for third in range(3):
            piece = jnp.where(kept, odd[third * SUBLANES : (third + 1) * SUBLANES], 0.0)
            piece = pltpu.roll(piece, third * rest, 1) if third else piece
            shared = piece if shared is None else shared + piece
        parts.append(shared)
    filled = sum(part.shape[0] for part in parts)
    if message_rows(block) > filled:
        parts.append(jnp.zeros((message_rows(block) - filled, LANES), F32))
    return jnp.concatenate(parts, axis=0).astype(BF16)


def unfold(message, block):
    whole, rest = divmod(block, LANES)
    groups = []
    for third in range(3):
        first = third * SUBLANES
        parts = [
            message[tile * 3 * SUBLANES + first : tile * 3 * SUBLANES + first + SUBLANES]
            for tile in range(whole)
        ]
        if rest:
            odd = message[whole * 3 * SUBLANES : whole * 3 * SUBLANES + SUBLANES]
            parts.append(pltpu.roll(odd, LANES - third * rest, 1) if third else odd)
        groups.append(jnp.concatenate(parts, axis=1) if len(parts) > 1 else parts[0])
    return groups


def group_points(latent_ref, points):
    width, rows, _ = latent_ref.shape
    rest = width - SUBLANES
    for row in range(rows):
        points[row * SUBLANES : (row + 1) * SUBLANES] = latent_ref[:SUBLANES, row, :].astype(F32)
        at = rows * SUBLANES + row * rest
        points[at : at + rest] = latent_ref[SUBLANES:, row, :].astype(F32)


def pack_kernel(latent_ref, *refs):
    *out_refs, points, stage = refs
    columns = len(out_refs)
    chans = latent_ref.shape[2]
    block = chans // columns
    column, _ = column_and_side()
    group_points(latent_ref, points)
    own = points[...]
    for target in range(columns):
        turned = pltpu.roll(own, chans - target * block, 1) if target else own
        stage[target] = fold(turned[:, : lanes_of(block)], block)
    for apart in range(columns):
        out_refs[apart][...] = stage[column ^ apart]


def column_kernel(order, *refs):
    *in_refs, out_ref = refs
    column, _ = column_and_side()
    for apart, ref in zip(order, in_refs):
        out_ref[column ^ apart] = ref[...]


def sides_kernel(own_ref, mate_ref, out_ref):
    _, side = column_and_side()
    out_ref[:, side] = own_ref[...]
    out_ref[:, 1 - side] = mate_ref[...]


def tables_kernel(width, filter_ref, band_ref, table_ref, first):
    bases, lons = filter_ref.shape
    taps, rows, _ = band_ref.shape
    step, places = first.shape[1:]
    columns = places // (2 * step)
    _, side = column_and_side()
    lat = lax.axis_index("lat")
    below = (lat > 0).astype(F32)
    above = (lat < lax.axis_size("lat") - 1).astype(F32)
    inside = [[below, below, 1.0], [1.0, above, above]]
    slots = [[0, 1, 2], [2, 0, 1]]
    profile = filter_ref[...]
    band = band_ref[...].astype(F32)
    source = lax.broadcasted_iota(jnp.int32, (lons, places), 0)
    place = lax.broadcasted_iota(jnp.int32, (lons, places), 1)
    within = place % step
    apart = source + (place // step) * width + within + (lons - side * width)
    for _ in range(3):
        apart = jnp.where(apart >= lons, apart - lons, apart)
    apart = jnp.where(within < width, apart, -1)
    first[...] = jnp.zeros_like(first)
    for lon in range(width):
        pick = (apart == lon).astype(F32).astype(BF16)
        first[:, lon, :] = jnp.dot(profile, pick, preferred_element_type=F32)
    for basis in range(bases):
        circle = first[basis]
        for column in range(columns):
            turned = pltpu.roll(circle, column * 2 * step, 1) if column else circle
            at = (basis * columns + column) * step
            for row in range(rows):
                for tap in range(taps):
                    weight = band[tap, row : row + 1, basis : basis + 1] * inside[row][tap]
                    to = slots[row][tap] * places
                    table_ref[row, at : at + step, to : to + places] = (weight * turned).astype(
                        BF16
                    )


def squares_kernel(own_ref, mate_ref, squares_ref, padded):
    bases, group, half = own_ref.shape
    lanes = squares_ref.shape[1]
    _, side = column_and_side()
    first = side == 0
    own = own_ref[...].astype(F32)
    mate = mate_ref[...].astype(F32)
    padded[...] = jnp.zeros_like(padded)
    padded[0, :, :group, :half] = jnp.where(first, own, mate)
    padded[1, :, :group, :half] = jnp.where(first, mate, own)
    members = padded.shape[2]
    into = lax.broadcasted_iota(jnp.int32, (lanes, members), 0)
    member = lax.broadcasted_iota(jnp.int32, (lanes, members), 1)
    repeat = (into % group == member).astype(F32).astype(BF16)
    row = lax.broadcasted_iota(jnp.int32, (lanes, lanes), 0)
    column = lax.broadcasted_iota(jnp.int32, (lanes, lanes), 1)
    same = (row // group == column // group) & (row < 2 * half) & (column < 2 * half)
    for basis in range(bases):
        weights = padded[0, basis] + pltpu.roll(padded[1, basis], half, 1)
        repeated = jnp.dot(repeat, weights.astype(BF16), preferred_element_type=F32)
        squares_ref[basis * lanes : (basis + 1) * lanes] = jnp.where(same, repeated, 0.0).astype(
            BF16
        )


def rows_of(message, block, rest):
    groups = unfold(message.astype(F32), block)
    last = (groups[2], pltpu.roll(groups[2], SUBLANES - rest, 0))
    return [jnp.concatenate([groups[row], last[row]], axis=0).astype(BF16) for row in range(2)]


def unpack_kernel(block, width, own_ref, out_ref):
    for at in range(own_ref.shape[0]):
        for row, read in enumerate(rows_of(own_ref[at], block, width - SUBLANES)):
            out_ref[row, at] = read


def conv_kernel(block, width, *refs):
    odd_mate, odd_own, even, mate, own, table_ref, squares_ref, *refs = refs
    *out_refs, field, spread, stage = refs
    columns = len(out_refs)
    lanes = squares_ref.shape[1]
    bases = squares_ref.shape[0] // lanes
    rows, _, inner = table_ref.shape
    places = inner // 3
    step = places // (2 * columns)
    half = places // 2
    rest = width - SUBLANES
    column, side = column_and_side()
    odd = lax.axis_index("lat") % 2

    def place(row, slot, at, read):
        first = pl.multiple_of(slot * places + at * step, step)
        field[row, pl.ds(first, step)] = read

    for at in range(columns):
        for row in range(rows):
            place(row, 2, 2 * at + side, own[row, at])
        for row, read in enumerate(rows_of(mate[at], block, rest)):
            place(row, 2, 2 * at + 1 - side, read)
        for half_at in range(2):
            for slot, read in enumerate(rows_of(even[at, half_at], block, rest)):
                place(1 - odd, slot, 2 * at + half_at, read)
        for message_side, ref in ((side, odd_own), (1 - side, odd_mate)):
            for slot, read in enumerate(rows_of(ref[at], block, rest)):
                place(odd, slot, 2 * at + message_side, read)
    for row in range(rows):
        over = jnp.dot(table_ref[row], field[row], preferred_element_type=F32).astype(BF16)
        for basis in range(bases):
            spread[row * half : (row + 1) * half, basis * lanes : (basis + 1) * lanes] = over[
                basis * half : (basis + 1) * half
            ]
    mixed = jnp.dot(spread[...], squares_ref[...], preferred_element_type=F32)
    upper = lax.broadcasted_iota(jnp.int32, (SUBLANES, lanes), 0) < rest
    for target in range(columns):
        top = mixed[target * step : (target + 1) * step]
        bottom = mixed[half + target * step : half + (target + 1) * step]
        last = jnp.where(upper, top[SUBLANES:], pltpu.roll(bottom[SUBLANES:], rest, 0))
        points = jnp.concatenate([top[:SUBLANES], bottom[:SUBLANES], last], axis=0)
        stage[target] = fold(points, block)
    for apart in range(columns):
        out_refs[apart][...] = stage[column ^ apart]


def tail_kernel(order, *refs):
    columns = len(order)
    back_refs = refs[:columns]
    latent_ref, up_ref, down_ref, out_ref, points, stage = refs[columns:]
    width, rows, chans = latent_ref.shape
    rest = width - SUBLANES
    block = chans // columns
    lanes = lanes_of(block)
    column, _ = column_and_side()
    for apart, ref in zip(order, back_refs):
        stage[column ^ apart] = ref[...]
    group_points(latent_ref, points)
    kept = lax.broadcasted_iota(jnp.int32, (3 * SUBLANES, lanes), 1) < block
    convolved = None
    for target in range(columns):
        piece = jnp.concatenate(unfold(stage[target].astype(F32), block), axis=0)
        piece = jnp.where(kept, piece, 0.0)
        if chans > lanes:
            gap = jnp.zeros((3 * SUBLANES, chans - lanes), F32)
            piece = jnp.concatenate([piece, gap], axis=1)
        piece = pltpu.roll(piece, target * block, 1) if target else piece
        convolved = piece if convolved is None else convolved + piece
    summed = (points[...] + convolved).astype(BF16).astype(F32)
    centred = summed - jnp.mean(summed, axis=1, keepdims=True)
    variance = jnp.mean(centred * centred, axis=1, keepdims=True)
    normed = (centred * lax.rsqrt(variance + 1e-05)).astype(BF16)
    hidden = jnp.dot(normed, up_ref[...], preferred_element_type=F32)
    hidden = (0.5 * hidden * (1.0 + lax.erf(hidden * 0.5**0.5))).astype(BF16)
    result = summed + jnp.dot(hidden, down_ref[...], preferred_element_type=F32)
    for row in range(rows):
        out_ref[:SUBLANES, row, :] = result[row * SUBLANES : (row + 1) * SUBLANES].astype(BF16)
        at = rows * SUBLANES + row * rest
        out_ref[SUBLANES:, row, :] = result[at : at + rest].astype(BF16)


VMEM = pl.BlockSpec(memory_space=pltpu.VMEM)


def call(kernel, name, out_shape, scratch, work, *operands):
    several = isinstance(out_shape, tuple)
    return pl.pallas_call(
        kernel,
        out_shape=out_shape,
        in_specs=[VMEM] * len(operands),
        out_specs=(VMEM,) * len(out_shape) if several else VMEM,
        scratch_shapes=scratch,
        compiler_params=pltpu.CompilerParams(vmem_limit_bytes=24 * 2**20),
        cost_estimate=pl.CostEstimate(flops=work, bytes_accessed=10**6, transcendentals=0),
        name=name,
    )(*operands)


def over_columns(messages, count):
    arrived = {0: messages[0]}
    for apart in reversed(range(1, count // 2)):
        pairs = [(i, ((i // 2) ^ apart) * 2 + i % 2) for i in range(count)]
        arrived[apart] = lax.ppermute(messages[apart], "lon", pairs)
    return arrived


def over_sides(block, count):
    return lax.ppermute(block, "lon", [(i, i ^ 1) for i in range(count)])


def swap(block, count, partner):
    pairs = []
    for lat in range(lax.axis_size("lat")):
        for lon in range(count):
            to_lat, to_lon = partner(lat, lon)
            pairs.append((lat * count + lon, to_lat * count + to_lon))
    return lax.ppermute(block, ("lat", "lon"), pairs)


def odd_pair(lat, lon, to_lon, rows):
    to = lat + 1 if lat % 2 else lat - 1
    return (to, to_lon) if 0 <= to < rows else (lat, lon ^ 1)


def local(latent, lon_filter, mix_weight, band_weight, offsets, w_up, w_down):
    rows, width, chans = latent.shape
    bases, lons = lon_filter.shape
    half, group = mix_weight.shape[1:]
    taps = band_weight.shape[2]
    count = lons // width
    columns = count // 2
    block = 2 * half
    step = up_to(width, 2 * SUBLANES)
    places = count * step
    lanes = lanes_of(block)
    height = message_rows(block)
    assert rows == 2 and taps == 3 and columns & (columns - 1) == 0
    assert lax.axis_size("lat") % 2 == 0
    assert SUBLANES < width and rows * (width - SUBLANES) <= SUBLANES
    assert 3 * (block % LANES) <= LANES

    far_first = tuple(reversed(range(columns)))
    last_first = (far_first[1:-1] + far_first[:1] + (0,)) if columns > 2 else far_first
    message = jax.ShapeDtypeStruct((height, LANES), BF16)
    messages = (message,) * columns
    stage = pltpu.VMEM((columns, height, LANES), BF16)
    points = pltpu.VMEM((3 * SUBLANES, chans), F32)
    lon_first = jnp.transpose(latent, (1, 0, 2))
    mix_own = jnp.transpose(mix_weight, (0, 2, 1))

    packed = call(pack_kernel, "pack", messages, [points, stage], 10**9, lon_first)
    arrived = over_columns(packed, count)
    mix_mate = over_sides(mix_own, count)
    table = call(
        functools.partial(tables_kernel, width),
        "tables",
        jax.ShapeDtypeStruct((rows, bases * places // 2, taps * places), BF16),
        [pltpu.VMEM((bases, step, places), F32)],
        10**9,
        lon_filter,
        jnp.transpose(band_weight, (2, 1, 0)),
    )
    squares = call(
        squares_kernel,
        "squares",
        jax.ShapeDtypeStruct((bases * lanes, lanes), BF16),
        [pltpu.VMEM((2, bases, up_to(group, 2 * SUBLANES), lanes), F32)],
        10**9,
        mix_own,
        mix_mate,
    )
    gathered = jax.ShapeDtypeStruct((columns, height, LANES), BF16)
    own_side = call(
        functools.partial(column_kernel, far_first),
        "join_columns",
        gathered,
        [],
        10**8,
        *[arrived[apart] for apart in far_first],
    )
    lats = lax.axis_size("lat")
    mate_side = swap(own_side, count, lambda lat, lon: (lat, lon ^ 1))
    odd_mate = swap(own_side, count, lambda lat, lon: odd_pair(lat, lon, lon ^ 1, lats))
    odd_own = swap(own_side, count, lambda lat, lon: odd_pair(lat, lon, lon, lats))
    own_rows = call(
        functools.partial(unpack_kernel, block, width),
        "unpack",
        jax.ShapeDtypeStruct((rows, columns, step, lanes), BF16),
        [],
        10**9,
        own_side,
    )
    circle = jax.ShapeDtypeStruct((columns, 2, height, LANES), BF16)
    home = call(sides_kernel, "join_sides", circle, [], 10**8, own_side, mate_side)
    even = swap(home, count, lambda lat, lon: (lat ^ 1, lon))
    mixed = call(
        functools.partial(conv_kernel, block, width),
        "conv",
        messages,
        [
            pltpu.VMEM((rows, taps * places, lanes), BF16),
            pltpu.VMEM((rows * places // 2, bases * lanes), BF16),
            stage,
        ],
        10**10,
        odd_mate,
        odd_own,
        even,
        mate_side,
        own_rows,
        table,
        squares,
    )
    back = over_columns(mixed, count)
    result = call(
        functools.partial(tail_kernel, last_first),
        "tail",
        jax.ShapeDtypeStruct(lon_first.shape, BF16),
        [points, stage],
        10**9,
        *[back[apart] for apart in last_first],
        lon_first,
        w_up,
        w_down,
    )
    return jnp.transpose(result, (1, 0, 2))


def solution(mesh):
    return jax.shard_map(
        local,
        mesh=mesh,
        in_specs=(
            P("lat", "lon", None),
            P(),
            P(None, "lon", None),
            P(None, "lat", None),
            P("lat"),
            P(),
            P(),
        ),
        out_specs=P("lat", "lon", None),
        check_vma=False,
    )
```

```python
import functools

import jax
import jax.numpy as jnp
from jax import lax
from jax.experimental import pallas as pl
from jax.experimental.pallas import tpu as pltpu
from jax.sharding import PartitionSpec as P

F32 = jnp.float32
BF16 = jnp.bfloat16
LANES = 128
SUBLANES = 8


def up_to(size, step):
    return -(-size // step) * step


def column_and_side():
    place = lax.axis_index("lon")
    return place // 2, place % 2


def message_rows(block):
    tiles = block // LANES
    return up_to(3 * SUBLANES * tiles + (SUBLANES if block % LANES else 0), 2 * SUBLANES)


def lanes_of(block):
    return up_to(block, LANES)


def fold(points, block):
    whole, rest = divmod(block, LANES)
    parts = [points[:, tile * LANES : (tile + 1) * LANES] for tile in range(whole)]
    if rest:
        odd = points[:, whole * LANES : (whole + 1) * LANES]
        kept = lax.broadcasted_iota(jnp.int32, (SUBLANES, LANES), 1) < rest
        shared = None
        for third in range(3):
            piece = jnp.where(kept, odd[third * SUBLANES : (third + 1) * SUBLANES], 0.0)
            piece = pltpu.roll(piece, third * rest, 1) if third else piece
            shared = piece if shared is None else shared + piece
        parts.append(shared)
    filled = sum(part.shape[0] for part in parts)
    if message_rows(block) > filled:
        parts.append(jnp.zeros((message_rows(block) - filled, LANES), F32))
    return jnp.concatenate(parts, axis=0).astype(BF16)


def unfold(message, block):
    whole, rest = divmod(block, LANES)
    groups = []
    for third in range(3):
        first = third * SUBLANES
        parts = [
            message[tile * 3 * SUBLANES + first : tile * 3 * SUBLANES + first + SUBLANES]
            for tile in range(whole)
        ]
        if rest:
            odd = message[whole * 3 * SUBLANES : whole * 3 * SUBLANES + SUBLANES]
            parts.append(pltpu.roll(odd, LANES - third * rest, 1) if third else odd)
        groups.append(jnp.concatenate(parts, axis=1) if len(parts) > 1 else parts[0])
    return groups


def group_points(latent_ref, points):
    width, rows, _ = latent_ref.shape
    rest = width - SUBLANES
    for row in range(rows):
        points[row * SUBLANES : (row + 1) * SUBLANES] = latent_ref[:SUBLANES, row, :].astype(F32)
        at = rows * SUBLANES + row * rest
        points[at : at + rest] = latent_ref[SUBLANES:, row, :].astype(F32)


def pack_kernel(latent_ref, *refs):
    *out_refs, points, stage = refs
    columns = len(out_refs)
    chans = latent_ref.shape[2]
    block = chans // columns
    column, _ = column_and_side()
    group_points(latent_ref, points)
    own = points[...]
    for target in range(columns):
        turned = pltpu.roll(own, chans - target * block, 1) if target else own
        stage[target] = fold(turned[:, : lanes_of(block)], block)
    for apart in range(columns):
        out_refs[apart][...] = stage[column ^ apart]


def column_kernel(order, *refs):
    *in_refs, out_ref = refs
    column, _ = column_and_side()
    for apart, ref in zip(order, in_refs):
        out_ref[column ^ apart] = ref[...]


def sides_kernel(own_ref, mate_ref, out_ref):
    _, side = column_and_side()
    out_ref[:, side] = own_ref[...]
    out_ref[:, 1 - side] = mate_ref[...]


def tables_kernel(width, filter_ref, band_ref, table_ref, first):
    bases, lons = filter_ref.shape
    taps, rows, _ = band_ref.shape
    step, places = first.shape[1:]
    columns = places // (2 * step)
    _, side = column_and_side()
    lat = lax.axis_index("lat")
    below = (lat > 0).astype(F32)
    above = (lat < lax.axis_size("lat") - 1).astype(F32)
    inside = [[below, below, 1.0], [1.0, above, above]]
    slots = [[0, 1, 2], [2, 0, 1]]
    profile = filter_ref[...]
    band = band_ref[...].astype(F32)
    source = lax.broadcasted_iota(jnp.int32, (lons, places), 0)
    place = lax.broadcasted_iota(jnp.int32, (lons, places), 1)
    within = place % step
    apart = source + (place // step) * width + within + (lons - side * width)
    for _ in range(3):
        apart = jnp.where(apart >= lons, apart - lons, apart)
    apart = jnp.where(within < width, apart, -1)
    first[...] = jnp.zeros_like(first)
    for lon in range(width):
        pick = (apart == lon).astype(F32).astype(BF16)
        first[:, lon, :] = jnp.dot(profile, pick, preferred_element_type=F32)
    for basis in range(bases):
        circle = first[basis]
        for column in range(columns):
            turned = pltpu.roll(circle, column * 2 * step, 1) if column else circle
            at = (basis * columns + column) * step
            for row in range(rows):
                for tap in range(taps):
                    weight = band[tap, row : row + 1, basis : basis + 1] * inside[row][tap]
                    to = slots[row][tap] * places
                    table_ref[row, at : at + step, to : to + places] = (weight * turned).astype(
                        BF16
                    )


def squares_kernel(own_ref, mate_ref, squares_ref, padded):
    bases, group, half = own_ref.shape
    lanes = squares_ref.shape[1]
    _, side = column_and_side()
    first = side == 0
    own = own_ref[...].astype(F32)
    mate = mate_ref[...].astype(F32)
    padded[...] = jnp.zeros_like(padded)
    padded[0, :, :group, :half] = jnp.where(first, own, mate)
    padded[1, :, :group, :half] = jnp.where(first, mate, own)
    members = padded.shape[2]
    into = lax.broadcasted_iota(jnp.int32, (lanes, members), 0)
    member = lax.broadcasted_iota(jnp.int32, (lanes, members), 1)
    repeat = (into % group == member).astype(F32).astype(BF16)
    row = lax.broadcasted_iota(jnp.int32, (lanes, lanes), 0)
    column = lax.broadcasted_iota(jnp.int32, (lanes, lanes), 1)
    same = (row // group == column // group) & (row < 2 * half) & (column < 2 * half)
    for basis in range(bases):
        weights = padded[0, basis] + pltpu.roll(padded[1, basis], half, 1)
        repeated = jnp.dot(repeat, weights.astype(BF16), preferred_element_type=F32)
        squares_ref[basis * lanes : (basis + 1) * lanes] = jnp.where(same, repeated, 0.0).astype(
            BF16
        )


def rows_of(message, block, rest):
    groups = unfold(message.astype(F32), block)
    last = (groups[2], pltpu.roll(groups[2], SUBLANES - rest, 0))
    return [jnp.concatenate([groups[row], last[row]], axis=0).astype(BF16) for row in range(2)]


def unpack_kernel(block, width, own_ref, out_ref):
    for at in range(own_ref.shape[0]):
        for row, read in enumerate(rows_of(own_ref[at], block, width - SUBLANES)):
            out_ref[row, at] = read


def own_kernel(block, width, mate, own, table_ref, part_ref, field):
    rows, columns, step, _ = own.shape
    places = field.shape[1]
    side = lax.axis_index("lon") % 2
    for at in range(columns):
        first = pl.multiple_of((2 * at + side) * step, step)
        other = pl.multiple_of((2 * at + 1 - side) * step, step)
        for row, read in enumerate(rows_of(mate[at], block, width - SUBLANES)):
            field[row, pl.ds(first, step)] = own[row, at]
            field[row, pl.ds(other, step)] = read
    for row in range(rows):
        part_ref[row] = jnp.dot(
            table_ref[row, :, 2 * places :], field[row], preferred_element_type=F32
        )


def conv_kernel(
    block, width, odd_own, odd_mate, even, part_ref, table_ref, squares_ref, *refs
):
    *out_refs, field, spread, stage = refs
    columns = len(out_refs)
    lanes = squares_ref.shape[1]
    bases = squares_ref.shape[0] // lanes
    rows, _, inner = table_ref.shape
    places = inner // 3
    step = places // (2 * columns)
    half = places // 2
    rest = width - SUBLANES
    column, side = column_and_side()
    odd = lax.axis_index("lat") % 2

    def place(row, at, message):
        for slot, read in enumerate(rows_of(message, block, rest)):
            first = pl.multiple_of(slot * places + at * step, step)
            field[row, pl.ds(first, step)] = read

    for at in range(columns):
        place(1 - odd, 2 * at, even[at, 0])
        place(1 - odd, 2 * at + 1, even[at, 1])
        place(odd, 2 * at + side, odd_own[at])
        place(odd, 2 * at + 1 - side, odd_mate[at])
    for row in range(rows):
        over = jnp.dot(
            table_ref[row, :, : 2 * places], field[row], preferred_element_type=F32
        )
        over = (over + part_ref[row]).astype(BF16)
        for basis in range(bases):
            spread[row * half : (row + 1) * half, basis * lanes : (basis + 1) * lanes] = over[
                basis * half : (basis + 1) * half
            ]
    mixed = jnp.dot(spread[...], squares_ref[...], preferred_element_type=F32)
    upper = lax.broadcasted_iota(jnp.int32, (SUBLANES, lanes), 0) < rest
    for target in range(columns):
        top = mixed[target * step : (target + 1) * step]
        bottom = mixed[half + target * step : half + (target + 1) * step]
        last = jnp.where(upper, top[SUBLANES:], pltpu.roll(bottom[SUBLANES:], rest, 0))
        points = jnp.concatenate([top[:SUBLANES], bottom[:SUBLANES], last], axis=0)
        stage[target] = fold(points, block)
    for apart in range(columns):
        out_refs[apart][...] = stage[column ^ apart]


def tail_kernel(order, *refs):
    columns = len(order)
    back_refs = refs[:columns]
    latent_ref, up_ref, down_ref, out_ref, points, stage = refs[columns:]
    width, rows, chans = latent_ref.shape
    rest = width - SUBLANES
    block = chans // columns
    lanes = lanes_of(block)
    column, _ = column_and_side()
    for apart, ref in zip(order, back_refs):
        stage[column ^ apart] = ref[...]
    group_points(latent_ref, points)
    kept = lax.broadcasted_iota(jnp.int32, (3 * SUBLANES, lanes), 1) < block
    convolved = None
    for target in range(columns):
        piece = jnp.concatenate(unfold(stage[target].astype(F32), block), axis=0)
        piece = jnp.where(kept, piece, 0.0)
        if chans > lanes:
            gap = jnp.zeros((3 * SUBLANES, chans - lanes), F32)
            piece = jnp.concatenate([piece, gap], axis=1)
        piece = pltpu.roll(piece, target * block, 1) if target else piece
        convolved = piece if convolved is None else convolved + piece
    summed = (points[...] + convolved).astype(BF16).astype(F32)
    centred = summed - jnp.mean(summed, axis=1, keepdims=True)
    variance = jnp.mean(centred * centred, axis=1, keepdims=True)
    normed = (centred * lax.rsqrt(variance + 1e-05)).astype(BF16)
    hidden = jnp.dot(normed, up_ref[...], preferred_element_type=F32)
    hidden = (0.5 * hidden * (1.0 + lax.erf(hidden * 0.5**0.5))).astype(BF16)
    result = summed + jnp.dot(hidden, down_ref[...], preferred_element_type=F32)
    for row in range(rows):
        out_ref[:SUBLANES, row, :] = result[row * SUBLANES : (row + 1) * SUBLANES].astype(BF16)
        at = rows * SUBLANES + row * rest
        out_ref[SUBLANES:, row, :] = result[at : at + rest].astype(BF16)


VMEM = pl.BlockSpec(memory_space=pltpu.VMEM)


def call(kernel, name, out_shape, scratch, work, *operands):
    several = isinstance(out_shape, tuple)
    return pl.pallas_call(
        kernel,
        out_shape=out_shape,
        in_specs=[VMEM] * len(operands),
        out_specs=(VMEM,) * len(out_shape) if several else VMEM,
        scratch_shapes=scratch,
        compiler_params=pltpu.CompilerParams(vmem_limit_bytes=24 * 2**20),
        cost_estimate=pl.CostEstimate(flops=work, bytes_accessed=10**6, transcendentals=0),
        name=name,
    )(*operands)


def over_columns(messages, count):
    arrived = {0: messages[0]}
    for apart in reversed(range(1, count // 2)):
        pairs = [(i, ((i // 2) ^ apart) * 2 + i % 2) for i in range(count)]
        arrived[apart] = lax.ppermute(messages[apart], "lon", pairs)
    return arrived


def over_sides(block, count):
    return lax.ppermute(block, "lon", [(i, i ^ 1) for i in range(count)])


def swap(block, count, partner):
    pairs = []
    for lat in range(lax.axis_size("lat")):
        for lon in range(count):
            to_lat, to_lon = partner(lat, lon)
            pairs.append((lat * count + lon, to_lat * count + to_lon))
    return lax.ppermute(block, ("lat", "lon"), pairs)


def odd_pair(lat, lon, to_lon, rows):
    to = lat + 1 if lat % 2 else lat - 1
    return (to, to_lon) if 0 <= to < rows else (lat, lon ^ 1)


def local(latent, lon_filter, mix_weight, band_weight, offsets, w_up, w_down):
    rows, width, chans = latent.shape
    bases, lons = lon_filter.shape
    half, group = mix_weight.shape[1:]
    taps = band_weight.shape[2]
    count = lons // width
    columns = count // 2
    block = 2 * half
    step = up_to(width, 2 * SUBLANES)
    places = count * step
    lanes = lanes_of(block)
    height = message_rows(block)
    assert rows == 2 and taps == 3 and columns & (columns - 1) == 0
    assert lax.axis_size("lat") % 2 == 0
    assert SUBLANES < width and rows * (width - SUBLANES) <= SUBLANES
    assert 3 * (block % LANES) <= LANES

    far_first = tuple(reversed(range(columns)))
    if columns > 3:
        far_first = (far_first[1], far_first[0]) + far_first[2:]
    message = jax.ShapeDtypeStruct((height, LANES), BF16)
    messages = (message,) * columns
    stage = pltpu.VMEM((columns, height, LANES), BF16)
    points = pltpu.VMEM((3 * SUBLANES, chans), F32)
    lon_first = jnp.transpose(latent, (1, 0, 2))
    mix_own = jnp.transpose(mix_weight, (0, 2, 1))

    packed = call(pack_kernel, "pack", messages, [points, stage], 10**9, lon_first)
    arrived = over_columns(packed, count)
    mix_mate = over_sides(mix_own, count)
    table = call(
        functools.partial(tables_kernel, width),
        "tables",
        jax.ShapeDtypeStruct((rows, bases * places // 2, taps * places), BF16),
        [pltpu.VMEM((bases, step, places), F32)],
        10**9,
        lon_filter,
        jnp.transpose(band_weight, (2, 1, 0)),
    )
    gathered = jax.ShapeDtypeStruct((columns, height, LANES), BF16)
    own_side = call(
        functools.partial(column_kernel, far_first),
        "join_columns",
        gathered,
        [],
        10**8,
        *[arrived[apart] for apart in far_first],
    )
    lats = lax.axis_size("lat")
    mate_side = swap(own_side, count, lambda lat, lon: (lat, lon ^ 1))
    odd_mate = swap(own_side, count, lambda lat, lon: odd_pair(lat, lon, lon ^ 1, lats))
    odd_own = swap(own_side, count, lambda lat, lon: odd_pair(lat, lon, lon, lats))
    own_rows = call(
        functools.partial(unpack_kernel, block, width),
        "unpack",
        jax.ShapeDtypeStruct((rows, columns, step, lanes), BF16),
        [],
        10**9,
        own_side,
    )
    circle = jax.ShapeDtypeStruct((columns, 2, height, LANES), BF16)
    home = call(sides_kernel, "join_sides", circle, [], 10**8, own_side, mate_side)
    even = swap(home, count, lambda lat, lon: (lat ^ 1, lon))
    mix_mate, _ = lax.optimization_barrier((mix_mate, home))
    squares = call(
        squares_kernel,
        "squares",
        jax.ShapeDtypeStruct((bases * lanes, lanes), BF16),
        [pltpu.VMEM((2, bases, up_to(group, 2 * SUBLANES), lanes), F32)],
        10**9,
        mix_own,
        mix_mate,
    )
    part = call(
        functools.partial(own_kernel, block, width),
        "conv_own",
        jax.ShapeDtypeStruct((rows, bases * places // 2, lanes), F32),
        [pltpu.VMEM((rows, places, lanes), BF16)],
        10**9,
        mate_side,
        own_rows,
        table,
    )
    mixed = call(
        functools.partial(conv_kernel, block, width),
        "conv",
        messages,
        [
            pltpu.VMEM((rows, 2 * places, lanes), BF16),
            pltpu.VMEM((rows * places // 2, bases * lanes), BF16),
            pltpu.VMEM((columns, height, LANES), BF16),
        ],
        10**10,
        odd_own,
        odd_mate,
        even,
        part,
        table,
        squares,
    )
    back = over_columns(mixed, count)
    result = call(
        functools.partial(tail_kernel, far_first),
        "tail",
        jax.ShapeDtypeStruct(lon_first.shape, BF16),
        [points, stage],
        10**9,
        *[back[apart] for apart in far_first],
        lon_first,
        w_up,
        w_down,
    )
    return jnp.transpose(result, (1, 0, 2))


def solution(mesh):
    return jax.shard_map(
        local,
        mesh=mesh,
        in_specs=(
            P("lat", "lon", None),
            P(),
            P(None, "lon", None),
            P(None, "lat", None),
            P("lat"),
            P(),
            P(),
        ),
        out_specs=P("lat", "lon", None),
        check_vma=False,
    )
```

```python
import functools

import jax
import jax.numpy as jnp
from jax import lax
from jax.experimental import pallas as pl
from jax.experimental.pallas import tpu as pltpu
from jax.sharding import PartitionSpec as P

F32 = jnp.float32
BF16 = jnp.bfloat16
LANES = 128
SUBLANES = 8


def up_to(size, step):
    return -(-size // step) * step


def column_and_side():
    place = lax.axis_index("lon")
    return place // 2, place % 2


def message_rows(block):
    tiles = block // LANES
    return up_to(3 * SUBLANES * tiles + (SUBLANES if block % LANES else 0), 2 * SUBLANES)


def lanes_of(block):
    return up_to(block, LANES)


def fold(points, block):
    whole, rest = divmod(block, LANES)
    parts = [points[:, tile * LANES : (tile + 1) * LANES] for tile in range(whole)]
    if rest:
        odd = points[:, whole * LANES : (whole + 1) * LANES]
        kept = lax.broadcasted_iota(jnp.int32, (SUBLANES, LANES), 1) < rest
        shared = None
        for third in range(3):
            piece = jnp.where(kept, odd[third * SUBLANES : (third + 1) * SUBLANES], 0.0)
            piece = pltpu.roll(piece, third * rest, 1) if third else piece
            shared = piece if shared is None else shared + piece
        parts.append(shared)
    filled = sum(part.shape[0] for part in parts)
    if message_rows(block) > filled:
        parts.append(jnp.zeros((message_rows(block) - filled, LANES), F32))
    return jnp.concatenate(parts, axis=0).astype(BF16)


def unfold(message, block):
    whole, rest = divmod(block, LANES)
    groups = []
    for third in range(3):
        first = third * SUBLANES
        parts = [
            message[tile * 3 * SUBLANES + first : tile * 3 * SUBLANES + first + SUBLANES]
            for tile in range(whole)
        ]
        if rest:
            odd = message[whole * 3 * SUBLANES : whole * 3 * SUBLANES + SUBLANES]
            parts.append(pltpu.roll(odd, LANES - third * rest, 1) if third else odd)
        groups.append(jnp.concatenate(parts, axis=1) if len(parts) > 1 else parts[0])
    return groups


def group_points(latent_ref, points):
    width, rows, _ = latent_ref.shape
    rest = width - SUBLANES
    for row in range(rows):
        points[row * SUBLANES : (row + 1) * SUBLANES] = latent_ref[:SUBLANES, row, :].astype(F32)
        at = rows * SUBLANES + row * rest
        points[at : at + rest] = latent_ref[SUBLANES:, row, :].astype(F32)


def pack_kernel(latent_ref, *refs):
    *out_refs, points, stage = refs
    columns = len(out_refs)
    chans = latent_ref.shape[2]
    block = chans // columns
    column, _ = column_and_side()
    group_points(latent_ref, points)
    own = points[...]
    for target in range(columns):
        turned = pltpu.roll(own, chans - target * block, 1) if target else own
        stage[target] = fold(turned[:, : lanes_of(block)], block)
    for apart in range(columns):
        out_refs[apart][...] = stage[column ^ apart]


def column_kernel(order, *refs):
    *in_refs, out_ref = refs
    column, _ = column_and_side()
    for apart, ref in zip(order, in_refs):
        out_ref[column ^ apart] = ref[...]


def sides_kernel(own_ref, mate_ref, out_ref):
    _, side = column_and_side()
    out_ref[:, side] = own_ref[...]
    out_ref[:, 1 - side] = mate_ref[...]


def tables_kernel(width, filter_ref, band_ref, table_ref, first):
    bases, lons = filter_ref.shape
    taps, rows, _ = band_ref.shape
    step, places = first.shape[1:]
    columns = places // (2 * step)
    _, side = column_and_side()
    lat = lax.axis_index("lat")
    below = (lat > 0).astype(F32)
    above = (lat < lax.axis_size("lat") - 1).astype(F32)
    inside = [[below, below, 1.0], [1.0, above, above]]
    slots = [[0, 1, 2], [2, 0, 1]]
    profile = filter_ref[...]
    band = band_ref[...].astype(F32)
    source = lax.broadcasted_iota(jnp.int32, (lons, places), 0)
    place = lax.broadcasted_iota(jnp.int32, (lons, places), 1)
    within = place % step
    apart = source + (place // step) * width + within + (lons - side * width)
    for _ in range(3):
        apart = jnp.where(apart >= lons, apart - lons, apart)
    apart = jnp.where(within < width, apart, -1)
    first[...] = jnp.zeros_like(first)
    for lon in range(width):
        pick = (apart == lon).astype(F32).astype(BF16)
        first[:, lon, :] = jnp.dot(profile, pick, preferred_element_type=F32)
    for basis in range(bases):
        circle = first[basis]
        for column in range(columns):
            turned = pltpu.roll(circle, column * 2 * step, 1) if column else circle
            at = (basis * columns + column) * step
            for row in range(rows):
                for tap in range(taps):
                    weight = band[tap, row : row + 1, basis : basis + 1] * inside[row][tap]
                    to = slots[row][tap] * places
                    table_ref[row, at : at + step, to : to + places] = (weight * turned).astype(
                        BF16
                    )


def squares_kernel(own_ref, mate_ref, squares_ref, padded):
    bases, group, half = own_ref.shape
    lanes = squares_ref.shape[1]
    _, side = column_and_side()
    first = side == 0
    own = own_ref[...].astype(F32)
    mate = mate_ref[...].astype(F32)
    padded[...] = jnp.zeros_like(padded)
    padded[0, :, :group, :half] = jnp.where(first, own, mate)
    padded[1, :, :group, :half] = jnp.where(first, mate, own)
    members = padded.shape[2]
    into = lax.broadcasted_iota(jnp.int32, (lanes, members), 0)
    member = lax.broadcasted_iota(jnp.int32, (lanes, members), 1)
    repeat = (into % group == member).astype(F32).astype(BF16)
    row = lax.broadcasted_iota(jnp.int32, (lanes, lanes), 0)
    column = lax.broadcasted_iota(jnp.int32, (lanes, lanes), 1)
    same = (row // group == column // group) & (row < 2 * half) & (column < 2 * half)
    for basis in range(bases):
        weights = padded[0, basis] + pltpu.roll(padded[1, basis], half, 1)
        repeated = jnp.dot(repeat, weights.astype(BF16), preferred_element_type=F32)
        squares_ref[basis * lanes : (basis + 1) * lanes] = jnp.where(same, repeated, 0.0).astype(
            BF16
        )


def rows_of(message, block, rest):
    groups = unfold(message.astype(F32), block)
    last = (groups[2], pltpu.roll(groups[2], SUBLANES - rest, 0))
    return [jnp.concatenate([groups[row], last[row]], axis=0).astype(BF16) for row in range(2)]


def unpack_kernel(block, width, own_ref, out_ref):
    for at in range(own_ref.shape[0]):
        for row, read in enumerate(rows_of(own_ref[at], block, width - SUBLANES)):
            out_ref[row, at] = read


def own_kernel(block, width, mate, own, table_ref, part_ref, field):
    rows, columns, step, _ = own.shape
    places = field.shape[1]
    side = lax.axis_index("lon") % 2
    for at in range(columns):
        first = pl.multiple_of((2 * at + side) * step, step)
        other = pl.multiple_of((2 * at + 1 - side) * step, step)
        for row, read in enumerate(rows_of(mate[at], block, width - SUBLANES)):
            field[row, pl.ds(first, step)] = own[row, at]
            field[row, pl.ds(other, step)] = read
    for row in range(rows):
        part_ref[row] = jnp.dot(
            table_ref[row, :, 2 * places :], field[row], preferred_element_type=F32
        )


def conv_kernel(
    block, width, odd_own, odd_mate, even, part_ref, table_ref, squares_ref, *refs
):
    *out_refs, field, spread, stage = refs
    columns = len(out_refs)
    lanes = squares_ref.shape[1]
    bases = squares_ref.shape[0] // lanes
    rows, _, inner = table_ref.shape
    places = inner // 3
    step = places // (2 * columns)
    half = places // 2
    rest = width - SUBLANES
    column, side = column_and_side()
    odd = lax.axis_index("lat") % 2

    def place(row, at, message):
        for slot, read in enumerate(rows_of(message, block, rest)):
            first = pl.multiple_of(slot * places + at * step, step)
            field[row, pl.ds(first, step)] = read

    for at in range(columns):
        place(1 - odd, 2 * at, even[at, 0])
        place(1 - odd, 2 * at + 1, even[at, 1])
        place(odd, 2 * at + side, odd_own[at])
        place(odd, 2 * at + 1 - side, odd_mate[at])
    for row in range(rows):
        over = jnp.dot(
            table_ref[row, :, : 2 * places], field[row], preferred_element_type=F32
        )
        over = (over + part_ref[row]).astype(BF16)
        for basis in range(bases):
            spread[row * half : (row + 1) * half, basis * lanes : (basis + 1) * lanes] = over[
                basis * half : (basis + 1) * half
            ]
    mixed = jnp.dot(spread[...], squares_ref[...], preferred_element_type=F32)
    upper = lax.broadcasted_iota(jnp.int32, (SUBLANES, lanes), 0) < rest
    for target in range(columns):
        top = mixed[target * step : (target + 1) * step]
        bottom = mixed[half + target * step : half + (target + 1) * step]
        last = jnp.where(upper, top[SUBLANES:], pltpu.roll(bottom[SUBLANES:], rest, 0))
        points = jnp.concatenate([top[:SUBLANES], bottom[:SUBLANES], last], axis=0)
        stage[target] = fold(points, block)
    for apart in range(columns):
        out_refs[apart][...] = stage[column ^ apart]


def tail_kernel(order, *refs):
    columns = len(order)
    back_refs = refs[:columns]
    latent_ref, up_ref, down_ref, out_ref, points, stage = refs[columns:]
    width, rows, chans = latent_ref.shape
    rest = width - SUBLANES
    block = chans // columns
    lanes = lanes_of(block)
    column, _ = column_and_side()
    for apart, ref in zip(order, back_refs):
        stage[column ^ apart] = ref[...]
    group_points(latent_ref, points)
    kept = lax.broadcasted_iota(jnp.int32, (3 * SUBLANES, lanes), 1) < block
    convolved = None
    for target in range(columns):
        piece = jnp.concatenate(unfold(stage[target].astype(F32), block), axis=0)
        piece = jnp.where(kept, piece, 0.0)
        if chans > lanes:
            gap = jnp.zeros((3 * SUBLANES, chans - lanes), F32)
            piece = jnp.concatenate([piece, gap], axis=1)
        piece = pltpu.roll(piece, target * block, 1) if target else piece
        convolved = piece if convolved is None else convolved + piece
    summed = (points[...] + convolved).astype(BF16)
    ones = jnp.ones((2 * SUBLANES, chans), BF16)
    count = summed.shape[0]
    raised = jnp.dot(
        jnp.concatenate([summed, ones[: up_to(count, 2 * SUBLANES) - count]], axis=0),
        up_ref[...],
        preferred_element_type=F32,
    )
    summed = summed.astype(F32)
    mean = jnp.mean(summed, axis=1, keepdims=True)
    centred = summed - mean
    scale = lax.rsqrt(jnp.mean(centred * centred, axis=1, keepdims=True) + 1e-05)
    hidden = scale * (raised[:count] - mean * raised[count : count + 1])
    hidden = (0.5 * hidden * (1.0 + lax.erf(hidden * 0.5**0.5))).astype(BF16)
    result = summed + jnp.dot(hidden, down_ref[...], preferred_element_type=F32)
    for row in range(rows):
        out_ref[:SUBLANES, row, :] = result[row * SUBLANES : (row + 1) * SUBLANES].astype(BF16)
        at = rows * SUBLANES + row * rest
        out_ref[SUBLANES:, row, :] = result[at : at + rest].astype(BF16)


VMEM = pl.BlockSpec(memory_space=pltpu.VMEM)


def call(kernel, name, out_shape, scratch, work, *operands):
    several = isinstance(out_shape, tuple)
    return pl.pallas_call(
        kernel,
        out_shape=out_shape,
        in_specs=[VMEM] * len(operands),
        out_specs=(VMEM,) * len(out_shape) if several else VMEM,
        scratch_shapes=scratch,
        compiler_params=pltpu.CompilerParams(vmem_limit_bytes=24 * 2**20),
        cost_estimate=pl.CostEstimate(flops=work, bytes_accessed=10**6, transcendentals=0),
        name=name,
    )(*operands)


def over_columns(messages, count):
    arrived = {0: messages[0]}
    for apart in reversed(range(1, count // 2)):
        pairs = [(i, ((i // 2) ^ apart) * 2 + i % 2) for i in range(count)]
        arrived[apart] = lax.ppermute(messages[apart], "lon", pairs)
    return arrived


def over_sides(block, count):
    return lax.ppermute(block, "lon", [(i, i ^ 1) for i in range(count)])


def swap(block, count, partner):
    pairs = []
    for lat in range(lax.axis_size("lat")):
        for lon in range(count):
            to_lat, to_lon = partner(lat, lon)
            pairs.append((lat * count + lon, to_lat * count + to_lon))
    return lax.ppermute(block, ("lat", "lon"), pairs)


def odd_pair(lat, lon, to_lon, rows):
    to = lat + 1 if lat % 2 else lat - 1
    return (to, to_lon) if 0 <= to < rows else (lat, lon ^ 1)


def local(latent, lon_filter, mix_weight, band_weight, offsets, w_up, w_down):
    rows, width, chans = latent.shape
    bases, lons = lon_filter.shape
    half, group = mix_weight.shape[1:]
    taps = band_weight.shape[2]
    count = lons // width
    columns = count // 2
    block = 2 * half
    step = up_to(width, 2 * SUBLANES)
    places = count * step
    lanes = lanes_of(block)
    height = message_rows(block)
    assert rows == 2 and taps == 3 and columns & (columns - 1) == 0
    assert lax.axis_size("lat") % 2 == 0
    assert SUBLANES < width and rows * (width - SUBLANES) <= SUBLANES
    assert 3 * (block % LANES) <= LANES

    far_first = tuple(reversed(range(columns)))
    inward = far_first
    if columns > 3:
        inward = (far_first[1], far_first[0]) + far_first[2:]
    message = jax.ShapeDtypeStruct((height, LANES), BF16)
    messages = (message,) * columns
    stage = pltpu.VMEM((columns, height, LANES), BF16)
    points = pltpu.VMEM((3 * SUBLANES, chans), F32)
    lon_first = jnp.transpose(latent, (1, 0, 2))
    mix_own = jnp.transpose(mix_weight, (0, 2, 1))

    packed = call(pack_kernel, "pack", messages, [points, stage], 10**9, lon_first)
    arrived = over_columns(packed, count)
    mix_mate = over_sides(mix_own, count)
    table = call(
        functools.partial(tables_kernel, width),
        "tables",
        jax.ShapeDtypeStruct((rows, bases * places // 2, taps * places), BF16),
        [pltpu.VMEM((bases, step, places), F32)],
        10**9,
        lon_filter,
        jnp.transpose(band_weight, (2, 1, 0)),
    )
    gathered = jax.ShapeDtypeStruct((columns, height, LANES), BF16)
    own_side = call(
        functools.partial(column_kernel, inward),
        "join_columns",
        gathered,
        [],
        10**8,
        *[arrived[apart] for apart in inward],
    )
    lats = lax.axis_size("lat")
    mate_side = swap(own_side, count, lambda lat, lon: (lat, lon ^ 1))
    odd_mate = swap(own_side, count, lambda lat, lon: odd_pair(lat, lon, lon ^ 1, lats))
    odd_own = swap(own_side, count, lambda lat, lon: odd_pair(lat, lon, lon, lats))
    own_rows = call(
        functools.partial(unpack_kernel, block, width),
        "unpack",
        jax.ShapeDtypeStruct((rows, columns, step, lanes), BF16),
        [],
        10**9,
        own_side,
    )
    circle = jax.ShapeDtypeStruct((columns, 2, height, LANES), BF16)
    home = call(sides_kernel, "join_sides", circle, [], 10**8, own_side, mate_side)
    even = swap(home, count, lambda lat, lon: (lat ^ 1, lon))
    mix_mate, _ = lax.optimization_barrier((mix_mate, home))
    squares = call(
        squares_kernel,
        "squares",
        jax.ShapeDtypeStruct((bases * lanes, lanes), BF16),
        [pltpu.VMEM((2, bases, up_to(group, 2 * SUBLANES), lanes), F32)],
        10**9,
        mix_own,
        mix_mate,
    )
    part = call(
        functools.partial(own_kernel, block, width),
        "conv_own",
        jax.ShapeDtypeStruct((rows, bases * places // 2, lanes), F32),
        [pltpu.VMEM((rows, places, lanes), BF16)],
        10**9,
        mate_side,
        own_rows,
        table,
    )
    mixed = call(
        functools.partial(conv_kernel, block, width),
        "conv",
        messages,
        [
            pltpu.VMEM((rows, 2 * places, lanes), BF16),
            pltpu.VMEM((rows * places // 2, bases * lanes), BF16),
            pltpu.VMEM((columns, height, LANES), BF16),
        ],
        10**10,
        odd_own,
        odd_mate,
        even,
        part,
        table,
        squares,
    )
    back = over_columns(mixed, count)
    result = call(
        functools.partial(tail_kernel, far_first),
        "tail",
        jax.ShapeDtypeStruct(lon_first.shape, BF16),
        [points, stage],
        10**9,
        *[back[apart] for apart in far_first],
        lon_first,
        w_up,
        w_down,
    )
    return jnp.transpose(result, (1, 0, 2))


def solution(mesh):
    return jax.shard_map(
        local,
        mesh=mesh,
        in_specs=(
            P("lat", "lon", None),
            P(),
            P(None, "lon", None),
            P(None, "lat", None),
            P("lat"),
            P(),
            P(),
        ),
        out_specs=P("lat", "lon", None),
        check_vma=False,
    )
```

```python
import functools

import jax
import jax.numpy as jnp
from jax import lax
from jax.experimental import pallas as pl
from jax.experimental.pallas import tpu as pltpu
from jax.sharding import PartitionSpec as P

F32 = jnp.float32
BF16 = jnp.bfloat16
LANES = 128
SUBLANES = 8


def up_to(size, step):
    return -(-size // step) * step


def column_and_side():
    place = lax.axis_index("lon")
    return place // 2, place % 2


def message_rows(block):
    tiles = block // LANES
    return up_to(3 * SUBLANES * tiles + (SUBLANES if block % LANES else 0), 2 * SUBLANES)


def lanes_of(block):
    return up_to(block, LANES)


def fold(points, block):
    whole, rest = divmod(block, LANES)
    parts = [points[:, tile * LANES : (tile + 1) * LANES] for tile in range(whole)]
    if rest:
        odd = points[:, whole * LANES : (whole + 1) * LANES]
        kept = lax.broadcasted_iota(jnp.int32, (SUBLANES, LANES), 1) < rest
        shared = None
        for third in range(3):
            piece = jnp.where(kept, odd[third * SUBLANES : (third + 1) * SUBLANES], 0.0)
            piece = pltpu.roll(piece, third * rest, 1) if third else piece
            shared = piece if shared is None else shared + piece
        parts.append(shared)
    filled = sum(part.shape[0] for part in parts)
    if message_rows(block) > filled:
        parts.append(jnp.zeros((message_rows(block) - filled, LANES), F32))
    return jnp.concatenate(parts, axis=0).astype(BF16)


def unfold(message, block):
    whole, rest = divmod(block, LANES)
    groups = []
    for third in range(3):
        first = third * SUBLANES
        parts = [
            message[tile * 3 * SUBLANES + first : tile * 3 * SUBLANES + first + SUBLANES]
            for tile in range(whole)
        ]
        if rest:
            odd = message[whole * 3 * SUBLANES : whole * 3 * SUBLANES + SUBLANES]
            parts.append(pltpu.roll(odd, LANES - third * rest, 1) if third else odd)
        groups.append(jnp.concatenate(parts, axis=1) if len(parts) > 1 else parts[0])
    return groups


def group_points(latent_ref, points):
    width, rows, _ = latent_ref.shape
    rest = width - SUBLANES
    for row in range(rows):
        points[row * SUBLANES : (row + 1) * SUBLANES] = latent_ref[:SUBLANES, row, :].astype(F32)
        at = rows * SUBLANES + row * rest
        points[at : at + rest] = latent_ref[SUBLANES:, row, :].astype(F32)


def pack_kernel(latent_ref, *refs):
    *out_refs, points, stage = refs
    columns = len(out_refs)
    chans = latent_ref.shape[2]
    block = chans // columns
    column, _ = column_and_side()
    group_points(latent_ref, points)
    own = points[...]
    for target in range(columns):
        turned = pltpu.roll(own, chans - target * block, 1) if target else own
        stage[target] = fold(turned[:, : lanes_of(block)], block)
    for apart in range(columns):
        out_refs[apart][...] = stage[column ^ apart]


def column_kernel(order, *refs):
    *in_refs, out_ref = refs
    column, _ = column_and_side()
    for apart, ref in zip(order, in_refs):
        out_ref[column ^ apart] = ref[...]


def sides_kernel(own_ref, mate_ref, out_ref):
    _, side = column_and_side()
    out_ref[:, side] = own_ref[...]
    out_ref[:, 1 - side] = mate_ref[...]


def tables_kernel(width, filter_ref, band_ref, table_ref, first):
    bases, lons = filter_ref.shape
    taps, rows, _ = band_ref.shape
    step, places = first.shape[1:]
    columns = places // (2 * step)
    _, side = column_and_side()
    lat = lax.axis_index("lat")
    below = (lat > 0).astype(F32)
    above = (lat < lax.axis_size("lat") - 1).astype(F32)
    inside = [[below, below, 1.0], [1.0, above, above]]
    slots = [[0, 1, 2], [2, 0, 1]]
    profile = filter_ref[...]
    band = band_ref[...].astype(F32)
    source = lax.broadcasted_iota(jnp.int32, (lons, places), 0)
    place = lax.broadcasted_iota(jnp.int32, (lons, places), 1)
    within = place % step
    apart = source + (place // step) * width + within + (lons - side * width)
    for _ in range(3):
        apart = jnp.where(apart >= lons, apart - lons, apart)
    apart = jnp.where(within < width, apart, -1)
    first[...] = jnp.zeros_like(first)
    for lon in range(width):
        pick = (apart == lon).astype(F32).astype(BF16)
        first[:, lon, :] = jnp.dot(profile, pick, preferred_element_type=F32)
    for basis in range(bases):
        circle = first[basis]
        for column in range(columns):
            turned = pltpu.roll(circle, column * 2 * step, 1) if column else circle
            at = (basis * columns + column) * step
            for row in range(rows):
                for tap in range(taps):
                    weight = band[tap, row : row + 1, basis : basis + 1] * inside[row][tap]
                    to = slots[row][tap] * places
                    table_ref[row, at : at + step, to : to + places] = (weight * turned).astype(
                        BF16
                    )


def squares_kernel(own_ref, mate_ref, squares_ref, padded):
    bases, group, half = own_ref.shape
    lanes = squares_ref.shape[1]
    _, side = column_and_side()
    first = side == 0
    own = own_ref[...].astype(F32)
    mate = mate_ref[...].astype(F32)
    padded[...] = jnp.zeros_like(padded)
    padded[0, :, :group, :half] = jnp.where(first, own, mate)
    padded[1, :, :group, :half] = jnp.where(first, mate, own)
    members = padded.shape[2]
    into = lax.broadcasted_iota(jnp.int32, (lanes, members), 0)
    member = lax.broadcasted_iota(jnp.int32, (lanes, members), 1)
    repeat = (into % group == member).astype(F32).astype(BF16)
    row = lax.broadcasted_iota(jnp.int32, (lanes, lanes), 0)
    column = lax.broadcasted_iota(jnp.int32, (lanes, lanes), 1)
    same = (row // group == column // group) & (row < 2 * half) & (column < 2 * half)
    for basis in range(bases):
        weights = padded[0, basis] + pltpu.roll(padded[1, basis], half, 1)
        repeated = jnp.dot(repeat, weights.astype(BF16), preferred_element_type=F32)
        squares_ref[basis * lanes : (basis + 1) * lanes] = jnp.where(same, repeated, 0.0).astype(
            BF16
        )


def rows_of(message, block, rest):
    groups = unfold(message.astype(F32), block)
    last = (groups[2], pltpu.roll(groups[2], SUBLANES - rest, 0))
    return [jnp.concatenate([groups[row], last[row]], axis=0).astype(BF16) for row in range(2)]


def unpack_kernel(block, width, own_ref, out_ref):
    for at in range(own_ref.shape[0]):
        for row, read in enumerate(rows_of(own_ref[at], block, width - SUBLANES)):
            out_ref[row, at] = read


def own_kernel(block, width, mate, own, table_ref, part_ref, field):
    rows, columns, step, _ = own.shape
    places = field.shape[1]
    side = lax.axis_index("lon") % 2
    for at in range(columns):
        first = pl.multiple_of((2 * at + side) * step, step)
        other = pl.multiple_of((2 * at + 1 - side) * step, step)
        for row, read in enumerate(rows_of(mate[at], block, width - SUBLANES)):
            field[row, pl.ds(first, step)] = own[row, at]
            field[row, pl.ds(other, step)] = read
    for row in range(rows):
        part_ref[row] = jnp.dot(
            table_ref[row, :, 2 * places :], field[row], preferred_element_type=F32
        )


def conv_kernel(
    block, width, odd_own, odd_mate, even, part_ref, table_ref, squares_ref, *refs
):
    *out_refs, field, stage = refs
    columns = len(out_refs)
    lanes = squares_ref.shape[1]
    bases = squares_ref.shape[0] // lanes
    rows, _, inner = table_ref.shape
    places = inner // 3
    step = places // (2 * columns)
    half = places // 2
    rest = width - SUBLANES
    column, side = column_and_side()
    odd = lax.axis_index("lat") % 2

    def place(row, at, message):
        for slot, read in enumerate(rows_of(message, block, rest)):
            first = pl.multiple_of(slot * places + at * step, step)
            field[row, pl.ds(first, step)] = read

    for at in range(columns):
        place(1 - odd, 2 * at, even[at, 0])
        place(1 - odd, 2 * at + 1, even[at, 1])
        place(odd, 2 * at + side, odd_own[at])
        place(odd, 2 * at + 1 - side, odd_mate[at])
    over = [
        jnp.dot(table_ref[row, :, : 2 * places], field[row], preferred_element_type=F32)
        for row in range(rows)
    ]
    mixed = None
    for basis in range(bases):
        taken = slice(basis * half, (basis + 1) * half)
        both = [(over[row][taken] + part_ref[row, taken]).astype(BF16) for row in range(rows)]
        square = squares_ref[basis * lanes : (basis + 1) * lanes]
        product = jnp.dot(
            jnp.concatenate(both, axis=0), square, preferred_element_type=F32
        )
        mixed = product if mixed is None else mixed + product
    upper = lax.broadcasted_iota(jnp.int32, (SUBLANES, lanes), 0) < rest
    for target in range(columns):
        top = mixed[target * step : (target + 1) * step]
        bottom = mixed[half + target * step : half + (target + 1) * step]
        last = jnp.where(upper, top[SUBLANES:], pltpu.roll(bottom[SUBLANES:], rest, 0))
        points = jnp.concatenate([top[:SUBLANES], bottom[:SUBLANES], last], axis=0)
        stage[target] = fold(points, block)
    for apart in range(columns):
        out_refs[apart][...] = stage[column ^ apart]


def tail_kernel(order, *refs):
    columns = len(order)
    back_refs = refs[:columns]
    latent_ref, up_ref, down_ref, out_ref, points, stage = refs[columns:]
    width, rows, chans = latent_ref.shape
    rest = width - SUBLANES
    block = chans // columns
    lanes = lanes_of(block)
    column, _ = column_and_side()
    for apart, ref in zip(order, back_refs):
        stage[column ^ apart] = ref[...]
    group_points(latent_ref, points)
    kept = lax.broadcasted_iota(jnp.int32, (3 * SUBLANES, lanes), 1) < block
    convolved = None
    for target in range(columns):
        piece = jnp.concatenate(unfold(stage[target].astype(F32), block), axis=0)
        piece = jnp.where(kept, piece, 0.0)
        if chans > lanes:
            gap = jnp.zeros((3 * SUBLANES, chans - lanes), F32)
            piece = jnp.concatenate([piece, gap], axis=1)
        piece = pltpu.roll(piece, target * block, 1) if target else piece
        convolved = piece if convolved is None else convolved + piece
    summed = (points[...] + convolved).astype(BF16)
    count = summed.shape[0]
    ones = jnp.ones((up_to(count, 2 * SUBLANES) - count, chans), BF16)
    rows_and_ones = jnp.concatenate([summed, ones], axis=0)
    summed = summed.astype(F32)
    mean = jnp.mean(summed, axis=1, keepdims=True)
    centred = summed - mean
    scale = lax.rsqrt(jnp.mean(centred * centred, axis=1, keepdims=True) + 1e-05)
    result = summed
    units = up_ref.shape[1]
    for first in range(0, units, 2 * LANES):
        taken = slice(first, min(first + 2 * LANES, units))
        raised = jnp.dot(rows_and_ones, up_ref[:, taken], preferred_element_type=F32)
        hidden = scale * (raised[:count] - mean * raised[count : count + 1])
        hidden = (0.5 * hidden * (1.0 + lax.erf(hidden * 0.5**0.5))).astype(BF16)
        result = result + jnp.dot(hidden, down_ref[taken], preferred_element_type=F32)
    for row in range(rows):
        out_ref[:SUBLANES, row, :] = result[row * SUBLANES : (row + 1) * SUBLANES].astype(BF16)
        at = rows * SUBLANES + row * rest
        out_ref[SUBLANES:, row, :] = result[at : at + rest].astype(BF16)


VMEM = pl.BlockSpec(memory_space=pltpu.VMEM)


def call(kernel, name, out_shape, scratch, work, *operands):
    several = isinstance(out_shape, tuple)
    return pl.pallas_call(
        kernel,
        out_shape=out_shape,
        in_specs=[VMEM] * len(operands),
        out_specs=(VMEM,) * len(out_shape) if several else VMEM,
        scratch_shapes=scratch,
        compiler_params=pltpu.CompilerParams(vmem_limit_bytes=24 * 2**20),
        cost_estimate=pl.CostEstimate(flops=work, bytes_accessed=10**6, transcendentals=0),
        name=name,
    )(*operands)


def over_columns(messages, count):
    arrived = {0: messages[0]}
    for apart in reversed(range(1, count // 2)):
        pairs = [(i, ((i // 2) ^ apart) * 2 + i % 2) for i in range(count)]
        arrived[apart] = lax.ppermute(messages[apart], "lon", pairs)
    return arrived


def over_sides(block, count):
    return lax.ppermute(block, "lon", [(i, i ^ 1) for i in range(count)])


def swap(block, count, partner):
    pairs = []
    for lat in range(lax.axis_size("lat")):
        for lon in range(count):
            to_lat, to_lon = partner(lat, lon)
            pairs.append((lat * count + lon, to_lat * count + to_lon))
    return lax.ppermute(block, ("lat", "lon"), pairs)


def odd_pair(lat, lon, to_lon, rows):
    to = lat + 1 if lat % 2 else lat - 1
    return (to, to_lon) if 0 <= to < rows else (lat, lon ^ 1)


def local(latent, lon_filter, mix_weight, band_weight, offsets, w_up, w_down):
    rows, width, chans = latent.shape
    bases, lons = lon_filter.shape
    half, group = mix_weight.shape[1:]
    taps = band_weight.shape[2]
    count = lons // width
    columns = count // 2
    block = 2 * half
    step = up_to(width, 2 * SUBLANES)
    places = count * step
    lanes = lanes_of(block)
    height = message_rows(block)
    assert rows == 2 and taps == 3 and columns & (columns - 1) == 0
    assert lax.axis_size("lat") % 2 == 0
    assert SUBLANES < width and rows * (width - SUBLANES) <= SUBLANES
    assert 3 * (block % LANES) <= LANES

    far_first = tuple(reversed(range(columns)))
    inward = far_first
    if columns > 3:
        inward = (far_first[1], far_first[0]) + far_first[2:]
    message = jax.ShapeDtypeStruct((height, LANES), BF16)
    messages = (message,) * columns
    stage = pltpu.VMEM((columns, height, LANES), BF16)
    points = pltpu.VMEM((3 * SUBLANES, chans), F32)
    lon_first = jnp.transpose(latent, (1, 0, 2))
    mix_own = jnp.transpose(mix_weight, (0, 2, 1))

    packed = call(pack_kernel, "pack", messages, [points, stage], 10**9, lon_first)
    arrived = over_columns(packed, count)
    mix_mate = over_sides(mix_own, count)
    table = call(
        functools.partial(tables_kernel, width),
        "tables",
        jax.ShapeDtypeStruct((rows, bases * places // 2, taps * places), BF16),
        [pltpu.VMEM((bases, step, places), F32)],
        10**9,
        lon_filter,
        jnp.transpose(band_weight, (2, 1, 0)),
    )
    gathered = jax.ShapeDtypeStruct((columns, height, LANES), BF16)
    own_side = call(
        functools.partial(column_kernel, inward),
        "join_columns",
        gathered,
        [],
        10**8,
        *[arrived[apart] for apart in inward],
    )
    lats = lax.axis_size("lat")
    mate_side = swap(own_side, count, lambda lat, lon: (lat, lon ^ 1))
    odd_mate = swap(own_side, count, lambda lat, lon: odd_pair(lat, lon, lon ^ 1, lats))
    odd_own = swap(own_side, count, lambda lat, lon: odd_pair(lat, lon, lon, lats))
    own_rows = call(
        functools.partial(unpack_kernel, block, width),
        "unpack",
        jax.ShapeDtypeStruct((rows, columns, step, lanes), BF16),
        [],
        10**9,
        own_side,
    )
    circle = jax.ShapeDtypeStruct((columns, 2, height, LANES), BF16)
    home = call(sides_kernel, "join_sides", circle, [], 10**8, own_side, mate_side)
    even = swap(home, count, lambda lat, lon: (lat ^ 1, lon))
    mix_mate, _ = lax.optimization_barrier((mix_mate, home))
    squares = call(
        squares_kernel,
        "squares",
        jax.ShapeDtypeStruct((bases * lanes, lanes), BF16),
        [pltpu.VMEM((2, bases, up_to(group, 2 * SUBLANES), lanes), F32)],
        10**9,
        mix_own,
        mix_mate,
    )
    part = call(
        functools.partial(own_kernel, block, width),
        "conv_own",
        jax.ShapeDtypeStruct((rows, bases * places // 2, lanes), F32),
        [pltpu.VMEM((rows, places, lanes), BF16)],
        10**9,
        mate_side,
        own_rows,
        table,
    )
    mixed = call(
        functools.partial(conv_kernel, block, width),
        "conv",
        messages,
        [
            pltpu.VMEM((rows, 2 * places, lanes), BF16),
            pltpu.VMEM((columns, height, LANES), BF16),
        ],
        10**10,
        odd_own,
        odd_mate,
        even,
        part,
        table,
        squares,
    )
    back = over_columns(mixed, count)
    result = call(
        functools.partial(tail_kernel, far_first),
        "tail",
        jax.ShapeDtypeStruct(lon_first.shape, BF16),
        [points, stage],
        10**9,
        *[back[apart] for apart in far_first],
        lon_first,
        w_up,
        w_down,
    )
    return jnp.transpose(result, (1, 0, 2))


def solution(mesh):
    return jax.shard_map(
        local,
        mesh=mesh,
        in_specs=(
            P("lat", "lon", None),
            P(),
            P(None, "lon", None),
            P(None, "lat", None),
            P("lat"),
            P(),
            P(),
        ),
        out_specs=P("lat", "lon", None),
        check_vma=False,
    )
```

```python
import functools

import jax
import jax.numpy as jnp
from jax import lax
from jax.experimental import pallas as pl
from jax.experimental.pallas import tpu as pltpu
from jax.sharding import PartitionSpec as P

F32 = jnp.float32
BF16 = jnp.bfloat16
LANES = 128
SUBLANES = 8


def up_to(size, step):
    return -(-size // step) * step


def column_and_side():
    place = lax.axis_index("lon")
    return place // 2, place % 2


def message_rows(block):
    tiles = block // LANES
    return up_to(3 * SUBLANES * tiles + (SUBLANES if block % LANES else 0), 2 * SUBLANES)


def lanes_of(block):
    return up_to(block, LANES)


def fold(points, block):
    whole, rest = divmod(block, LANES)
    parts = [points[:, tile * LANES : (tile + 1) * LANES] for tile in range(whole)]
    if rest:
        odd = points[:, whole * LANES : (whole + 1) * LANES]
        kept = lax.broadcasted_iota(jnp.int32, (SUBLANES, LANES), 1) < rest
        shared = None
        for third in range(3):
            piece = jnp.where(kept, odd[third * SUBLANES : (third + 1) * SUBLANES], 0.0)
            piece = pltpu.roll(piece, third * rest, 1) if third else piece
            shared = piece if shared is None else shared + piece
        parts.append(shared)
    filled = sum(part.shape[0] for part in parts)
    if message_rows(block) > filled:
        parts.append(jnp.zeros((message_rows(block) - filled, LANES), F32))
    return jnp.concatenate(parts, axis=0).astype(BF16)


def unfold(message, block):
    whole, rest = divmod(block, LANES)
    groups = []
    for third in range(3):
        first = third * SUBLANES
        parts = [
            message[tile * 3 * SUBLANES + first : tile * 3 * SUBLANES + first + SUBLANES]
            for tile in range(whole)
        ]
        if rest:
            odd = message[whole * 3 * SUBLANES : whole * 3 * SUBLANES + SUBLANES]
            parts.append(pltpu.roll(odd, LANES - third * rest, 1) if third else odd)
        groups.append(jnp.concatenate(parts, axis=1) if len(parts) > 1 else parts[0])
    return groups


def group_points(latent_ref, points):
    width, rows, _ = latent_ref.shape
    rest = width - SUBLANES
    for row in range(rows):
        points[row * SUBLANES : (row + 1) * SUBLANES] = latent_ref[:SUBLANES, row, :].astype(F32)
        at = rows * SUBLANES + row * rest
        points[at : at + rest] = latent_ref[SUBLANES:, row, :].astype(F32)


def pack_kernel(order, latent_ref, *refs):
    *out_refs, points, stage = refs
    columns = stage.shape[0]
    chans = latent_ref.shape[2]
    block = chans // columns
    column, _ = column_and_side()
    group_points(latent_ref, points)
    own = points[...]
    for target in range(columns):
        turned = pltpu.roll(own, chans - target * block, 1) if target else own
        stage[target] = fold(turned[:, : lanes_of(block)], block)
    for apart, ref in zip(order, out_refs):
        ref[...] = stage[column ^ apart]


def cut_kernel(raw_ref, out_ref, points):
    chans = raw_ref.shape[2]
    block = chans // (lax.axis_size("lon") // 2)
    column, _ = column_and_side()
    group_points(raw_ref, points)
    turned = pltpu.roll(points[...], (chans - column * block) % chans, 1)
    out_ref[...] = fold(turned[:, : lanes_of(block)], block)


def column_kernel(order, *refs):
    *in_refs, out_ref = refs
    column, _ = column_and_side()
    for apart, ref in zip(order, in_refs):
        out_ref[column ^ apart] = ref[...]


def sides_kernel(own_ref, mate_ref, out_ref):
    _, side = column_and_side()
    out_ref[:, side] = own_ref[...]
    out_ref[:, 1 - side] = mate_ref[...]


def apart_kernel(width, step, out_ref):
    lons = out_ref.shape[0]
    side = lax.axis_index("lon") % 2
    source = lax.broadcasted_iota(jnp.int32, out_ref.shape, 0)
    place = lax.broadcasted_iota(jnp.int32, out_ref.shape, 1)
    within = place % step
    apart = source + (place // step) * width + within + (lons - side * width)
    for _ in range(3):
        apart = jnp.where(apart >= lons, apart - lons, apart)
    out_ref[...] = jnp.where(within < width, apart, -1)


def tables_kernel(width, filter_ref, band_ref, apart_ref, table_ref, first):
    bases, lons = filter_ref.shape
    taps, rows, _ = band_ref.shape
    step, places = first.shape[1:]
    columns = places // (2 * step)
    lat = lax.axis_index("lat")
    below = (lat > 0).astype(F32)
    above = (lat < lax.axis_size("lat") - 1).astype(F32)
    inside = [[below, below, 1.0], [1.0, above, above]]
    slots = [[0, 1, 2], [2, 0, 1]]
    profile = filter_ref[...]
    band = band_ref[...].astype(F32)
    apart = apart_ref[...]
    first[...] = jnp.zeros_like(first)
    for lon in range(width):
        pick = (apart == lon).astype(F32).astype(BF16)
        first[:, lon, :] = jnp.dot(profile, pick, preferred_element_type=F32)
    for basis in range(bases):
        circle = first[basis]
        for column in range(columns):
            turned = pltpu.roll(circle, column * 2 * step, 1) if column else circle
            at = (basis * columns + column) * step
            for row in range(rows):
                for tap in range(taps):
                    weight = band[tap, row : row + 1, basis : basis + 1] * inside[row][tap]
                    to = slots[row][tap] * places
                    table_ref[row, at : at + step, to : to + places] = (weight * turned).astype(
                        BF16
                    )


def squares_kernel(own_ref, mate_ref, squares_ref, padded):
    bases, group, half = own_ref.shape
    lanes = squares_ref.shape[1]
    _, side = column_and_side()
    first = side == 0
    own = own_ref[...].astype(F32)
    mate = mate_ref[...].astype(F32)
    padded[...] = jnp.zeros_like(padded)
    padded[0, :, :group, :half] = jnp.where(first, own, mate)
    padded[1, :, :group, :half] = jnp.where(first, mate, own)
    members = padded.shape[2]
    into = lax.broadcasted_iota(jnp.int32, (lanes, members), 0)
    member = lax.broadcasted_iota(jnp.int32, (lanes, members), 1)
    repeat = (into % group == member).astype(F32).astype(BF16)
    row = lax.broadcasted_iota(jnp.int32, (lanes, lanes), 0)
    column = lax.broadcasted_iota(jnp.int32, (lanes, lanes), 1)
    same = (row // group == column // group) & (row < 2 * half) & (column < 2 * half)
    for basis in range(bases):
        weights = padded[0, basis] + pltpu.roll(padded[1, basis], half, 1)
        repeated = jnp.dot(repeat, weights.astype(BF16), preferred_element_type=F32)
        squares_ref[basis * lanes : (basis + 1) * lanes] = jnp.where(same, repeated, 0.0).astype(
            BF16
        )


def rows_of(message, block, rest):
    groups = unfold(message.astype(F32), block)
    last = (groups[2], pltpu.roll(groups[2], SUBLANES - rest, 0))
    return [jnp.concatenate([groups[row], last[row]], axis=0).astype(BF16) for row in range(2)]


def unpack_kernel(block, width, own_ref, out_ref):
    for at in range(own_ref.shape[0]):
        for row, read in enumerate(rows_of(own_ref[at], block, width - SUBLANES)):
            out_ref[row, at] = read


def own_kernel(block, width, mate, own, table_ref, part_ref, field):
    rows, columns, step, _ = own.shape
    places = field.shape[1]
    side = lax.axis_index("lon") % 2
    for at in range(columns):
        first = pl.multiple_of((2 * at + side) * step, step)
        other = pl.multiple_of((2 * at + 1 - side) * step, step)
        for row, read in enumerate(rows_of(mate[at], block, width - SUBLANES)):
            field[row, pl.ds(first, step)] = own[row, at]
            field[row, pl.ds(other, step)] = read
    for row in range(rows):
        part_ref[row] = jnp.dot(
            table_ref[row, :, 2 * places :], field[row], preferred_element_type=F32
        )


def conv_kernel(
    block, width, odd_mate, odd_own, even, part_ref, table_ref, squares_ref, *refs
):
    *out_refs, field, spread, stage = refs
    columns = len(out_refs)
    lanes = squares_ref.shape[1]
    bases = squares_ref.shape[0] // lanes
    rows, _, inner = table_ref.shape
    places = inner // 3
    step = places // (2 * columns)
    half = places // 2
    rest = width - SUBLANES
    column, side = column_and_side()
    odd = lax.axis_index("lat") % 2

    def place(row, at, message):
        for slot, read in enumerate(rows_of(message, block, rest)):
            first = pl.multiple_of(slot * places + at * step, step)
            field[row, pl.ds(first, step)] = read

    for at in range(columns):
        place(1 - odd, 2 * at, even[at, 0])
        place(1 - odd, 2 * at + 1, even[at, 1])
        place(odd, 2 * at + side, odd_own[at])
        place(odd, 2 * at + 1 - side, odd_mate[at])
    for row in range(rows):
        over = jnp.dot(
            table_ref[row, :, : 2 * places], field[row], preferred_element_type=F32
        )
        over = (over + part_ref[row]).astype(BF16)
        for basis in range(bases):
            spread[row * half : (row + 1) * half, basis * lanes : (basis + 1) * lanes] = over[
                basis * half : (basis + 1) * half
            ]
    mixed = jnp.dot(spread[...], squares_ref[...], preferred_element_type=F32)
    upper = lax.broadcasted_iota(jnp.int32, (SUBLANES, lanes), 0) < rest
    for target in range(columns):
        top = mixed[target * step : (target + 1) * step]
        bottom = mixed[half + target * step : half + (target + 1) * step]
        last = jnp.where(upper, top[SUBLANES:], pltpu.roll(bottom[SUBLANES:], rest, 0))
        points = jnp.concatenate([top[:SUBLANES], bottom[:SUBLANES], last], axis=0)
        stage[target] = fold(points, block)
    for apart in range(columns):
        out_refs[apart][...] = stage[column ^ apart]


def tail_kernel(order, *refs):
    columns = len(order)
    back_refs = refs[:columns]
    latent_ref, up_ref, down_ref, out_ref, points, stage = refs[columns:]
    width, rows, chans = latent_ref.shape
    rest = width - SUBLANES
    block = chans // columns
    lanes = lanes_of(block)
    column, _ = column_and_side()
    for apart, ref in zip(order, back_refs):
        stage[column ^ apart] = ref[...]
    group_points(latent_ref, points)
    kept = lax.broadcasted_iota(jnp.int32, (3 * SUBLANES, lanes), 1) < block
    convolved = None
    for target in range(columns):
        piece = jnp.concatenate(unfold(stage[target].astype(F32), block), axis=0)
        piece = jnp.where(kept, piece, 0.0)
        if chans > lanes:
            gap = jnp.zeros((3 * SUBLANES, chans - lanes), F32)
            piece = jnp.concatenate([piece, gap], axis=1)
        piece = pltpu.roll(piece, target * block, 1) if target else piece
        convolved = piece if convolved is None else convolved + piece
    summed = (points[...] + convolved).astype(BF16)
    ones = jnp.ones((2 * SUBLANES, chans), BF16)
    count = summed.shape[0]
    raised = jnp.dot(
        jnp.concatenate([summed, ones[: up_to(count, 2 * SUBLANES) - count]], axis=0),
        up_ref[...],
        preferred_element_type=F32,
    )
    summed = summed.astype(F32)
    mean = jnp.mean(summed, axis=1, keepdims=True)
    centred = summed - mean
    scale = lax.rsqrt(jnp.mean(centred * centred, axis=1, keepdims=True) + 1e-05)
    hidden = scale * (raised[:count] - mean * raised[count : count + 1])
    hidden = (0.5 * hidden * (1.0 + lax.erf(hidden * 0.5**0.5))).astype(BF16)
    result = summed + jnp.dot(hidden, down_ref[...], preferred_element_type=F32)
    for row in range(rows):
        out_ref[:SUBLANES, row, :] = result[row * SUBLANES : (row + 1) * SUBLANES].astype(BF16)
        at = rows * SUBLANES + row * rest
        out_ref[SUBLANES:, row, :] = result[at : at + rest].astype(BF16)


VMEM = pl.BlockSpec(memory_space=pltpu.VMEM)


def call(kernel, name, out_shape, scratch, work, *operands):
    several = isinstance(out_shape, tuple)
    return pl.pallas_call(
        kernel,
        out_shape=out_shape,
        in_specs=[VMEM] * len(operands),
        out_specs=(VMEM,) * len(out_shape) if several else VMEM,
        scratch_shapes=scratch,
        compiler_params=pltpu.CompilerParams(vmem_limit_bytes=24 * 2**20),
        cost_estimate=pl.CostEstimate(flops=work, bytes_accessed=10**6, transcendentals=0),
        name=name,
    )(*operands)


def over_columns(message, count, apart):
    pairs = [(i, ((i // 2) ^ apart) * 2 + i % 2) for i in range(count)]
    return lax.ppermute(message, "lon", pairs) if apart else message


def over_sides(block, count):
    return lax.ppermute(block, "lon", [(i, i ^ 1) for i in range(count)])


def swap(block, count, partner):
    pairs = []
    for lat in range(lax.axis_size("lat")):
        for lon in range(count):
            to_lat, to_lon = partner(lat, lon)
            pairs.append((lat * count + lon, to_lat * count + to_lon))
    return lax.ppermute(block, ("lat", "lon"), pairs)


def odd_pair(lat, lon, to_lon, rows):
    to = lat + 1 if lat % 2 else lat - 1
    return (to, to_lon) if 0 <= to < rows else (lat, lon ^ 1)


def local(latent, lon_filter, mix_weight, band_weight, offsets, w_up, w_down):
    rows, width, chans = latent.shape
    bases, lons = lon_filter.shape
    half, group = mix_weight.shape[1:]
    taps = band_weight.shape[2]
    count = lons // width
    columns = count // 2
    block = 2 * half
    step = up_to(width, 2 * SUBLANES)
    places = count * step
    lanes = lanes_of(block)
    height = message_rows(block)
    assert rows == 2 and taps == 3 and columns & (columns - 1) == 0
    assert lax.axis_size("lat") % 2 == 0
    assert SUBLANES < width and rows * (width - SUBLANES) <= SUBLANES
    assert 3 * (block % LANES) <= LANES

    far_first = tuple(reversed(range(columns)))
    inward = far_first
    if columns > 3:
        inward = (far_first[1], far_first[0]) + far_first[2:]
    message = jax.ShapeDtypeStruct((height, LANES), BF16)
    messages = (message,) * columns
    stage = pltpu.VMEM((columns, height, LANES), BF16)
    points = pltpu.VMEM((3 * SUBLANES, chans), F32)
    lon_first = jnp.transpose(latent, (1, 0, 2))
    mix_own = jnp.transpose(mix_weight, (0, 2, 1))

    raw = over_columns(lon_first, count, inward[0])
    apart = call(
        functools.partial(apart_kernel, width, step),
        "apart",
        jax.ShapeDtypeStruct((lons, places), jnp.int32),
        [],
        10**9,
    )
    loaded, apart = lax.optimization_barrier((lon_first, apart))
    packed = call(
        functools.partial(pack_kernel, inward[1:]),
        "pack",
        (message,) * (columns - 1),
        [points, stage],
        10**9,
        loaded,
    )
    arrived = [call(cut_kernel, "cut", message, [points], 5 * 10**9, raw)]
    arrived += [over_columns(*pair) for pair in zip(packed, [count] * columns, inward[1:])]
    mix_mate = over_sides(mix_own, count)
    table = call(
        functools.partial(tables_kernel, width),
        "tables",
        jax.ShapeDtypeStruct((rows, bases * places // 2, taps * places), BF16),
        [pltpu.VMEM((bases, step, places), F32)],
        10**6,
        lon_filter,
        jnp.transpose(band_weight, (2, 1, 0)),
        apart,
    )
    gathered = jax.ShapeDtypeStruct((columns, height, LANES), BF16)
    own_side = call(
        functools.partial(column_kernel, inward),
        "join_columns",
        gathered,
        [],
        10**8,
        *arrived,
    )
    lats = lax.axis_size("lat")
    mate_side = swap(own_side, count, lambda lat, lon: (lat, lon ^ 1))
    odd_mate = swap(own_side, count, lambda lat, lon: odd_pair(lat, lon, lon ^ 1, lats))
    odd_own = swap(own_side, count, lambda lat, lon: odd_pair(lat, lon, lon, lats))
    own_rows = call(
        functools.partial(unpack_kernel, block, width),
        "unpack",
        jax.ShapeDtypeStruct((rows, columns, step, lanes), BF16),
        [],
        10**9,
        own_side,
    )
    circle = jax.ShapeDtypeStruct((columns, 2, height, LANES), BF16)
    home = call(sides_kernel, "join_sides", circle, [], 10**8, own_side, mate_side)
    even = swap(home, count, lambda lat, lon: (lat ^ 1, lon))
    mix_mate, _ = lax.optimization_barrier((mix_mate, home))
    squares = call(
        squares_kernel,
        "squares",
        jax.ShapeDtypeStruct((bases * lanes, lanes), BF16),
        [pltpu.VMEM((2, bases, up_to(group, 2 * SUBLANES), lanes), F32)],
        10**9,
        mix_own,
        mix_mate,
    )
    part = call(
        functools.partial(own_kernel, block, width),
        "conv_own",
        jax.ShapeDtypeStruct((rows, bases * places // 2, lanes), F32),
        [pltpu.VMEM((rows, places, lanes), BF16)],
        10**9,
        mate_side,
        own_rows,
        table,
    )
    mixed = call(
        functools.partial(conv_kernel, block, width),
        "conv",
        messages,
        [
            pltpu.VMEM((rows, 2 * places, lanes), BF16),
            pltpu.VMEM((rows * places // 2, bases * lanes), BF16),
            pltpu.VMEM((columns, height, LANES), BF16),
        ],
        10**10,
        odd_mate,
        odd_own,
        even,
        part,
        table,
        squares,
    )
    outward = far_first[1:-1] + far_first[:1] + far_first[-1:]
    back = [over_columns(mixed[apart], count, apart) for apart in outward]
    result = call(
        functools.partial(tail_kernel, outward),
        "tail",
        jax.ShapeDtypeStruct(lon_first.shape, BF16),
        [points, stage],
        10**9,
        *back,
        lon_first,
        w_up,
        w_down,
    )
    return jnp.transpose(result, (1, 0, 2))


def solution(mesh):
    return jax.shard_map(
        local,
        mesh=mesh,
        in_specs=(
            P("lat", "lon", None),
            P(),
            P(None, "lon", None),
            P(None, "lat", None),
            P("lat"),
            P(),
            P(),
        ),
        out_specs=P("lat", "lon", None),
        check_vma=False,
    )
```

```python
import functools

import jax
import jax.numpy as jnp
from jax import lax
from jax.experimental import pallas as pl
from jax.experimental.pallas import tpu as pltpu
from jax.sharding import PartitionSpec as P

F32 = jnp.float32
BF16 = jnp.bfloat16
LANES = 128
SUBLANES = 8


def up_to(size, step):
    return -(-size // step) * step


def column_and_side():
    place = lax.axis_index("lon")
    return place // 2, place % 2


def message_rows(block):
    tiles = block // LANES
    return up_to(3 * SUBLANES * tiles + (SUBLANES if block % LANES else 0), 2 * SUBLANES)


def lanes_of(block):
    return up_to(block, LANES)


def fold(points, block):
    whole, rest = divmod(block, LANES)
    parts = [points[:, tile * LANES : (tile + 1) * LANES] for tile in range(whole)]
    if rest:
        odd = points[:, whole * LANES : (whole + 1) * LANES]
        kept = lax.broadcasted_iota(jnp.int32, (SUBLANES, LANES), 1) < rest
        shared = None
        for third in range(3):
            piece = jnp.where(kept, odd[third * SUBLANES : (third + 1) * SUBLANES], 0.0)
            piece = pltpu.roll(piece, third * rest, 1) if third else piece
            shared = piece if shared is None else shared + piece
        parts.append(shared)
    filled = sum(part.shape[0] for part in parts)
    if message_rows(block) > filled:
        parts.append(jnp.zeros((message_rows(block) - filled, LANES), F32))
    return jnp.concatenate(parts, axis=0).astype(BF16)


def unfold(message, block):
    whole, rest = divmod(block, LANES)
    groups = []
    for third in range(3):
        first = third * SUBLANES
        parts = [
            message[tile * 3 * SUBLANES + first : tile * 3 * SUBLANES + first + SUBLANES]
            for tile in range(whole)
        ]
        if rest:
            odd = message[whole * 3 * SUBLANES : whole * 3 * SUBLANES + SUBLANES]
            parts.append(pltpu.roll(odd, LANES - third * rest, 1) if third else odd)
        groups.append(jnp.concatenate(parts, axis=1) if len(parts) > 1 else parts[0])
    return groups


def group_points(latent_ref, points):
    width, rows, _ = latent_ref.shape
    rest = width - SUBLANES
    for row in range(rows):
        points[row * SUBLANES : (row + 1) * SUBLANES] = latent_ref[:SUBLANES, row, :].astype(F32)
        at = rows * SUBLANES + row * rest
        points[at : at + rest] = latent_ref[SUBLANES:, row, :].astype(F32)


def pack_kernel(order, latent_ref, *refs):
    *out_refs, points, stage = refs
    columns = stage.shape[0]
    chans = latent_ref.shape[2]
    block = chans // columns
    column, _ = column_and_side()
    group_points(latent_ref, points)
    own = points[...]
    for target in range(columns):
        turned = pltpu.roll(own, chans - target * block, 1) if target else own
        stage[target] = fold(turned[:, : lanes_of(block)], block)
    for apart, ref in zip(order, out_refs):
        ref[...] = stage[column ^ apart]


def cut_kernel(raw_ref, out_ref, points):
    chans = raw_ref.shape[2]
    block = chans // (lax.axis_size("lon") // 2)
    column, _ = column_and_side()
    group_points(raw_ref, points)
    turned = pltpu.roll(points[...], (chans - column * block) % chans, 1)
    out_ref[...] = fold(turned[:, : lanes_of(block)], block)


def column_kernel(order, *refs):
    *in_refs, out_ref = refs
    column, _ = column_and_side()
    for apart, ref in zip(order, in_refs):
        out_ref[column ^ apart] = ref[...]


def sides_kernel(own_ref, mate_ref, out_ref):
    _, side = column_and_side()
    out_ref[:, side] = own_ref[...]
    out_ref[:, 1 - side] = mate_ref[...]


def apart_kernel(width, step, out_ref):
    lons = out_ref.shape[0]
    side = lax.axis_index("lon") % 2
    source = lax.broadcasted_iota(jnp.int32, out_ref.shape, 0)
    place = lax.broadcasted_iota(jnp.int32, out_ref.shape, 1)
    within = place % step
    apart = source + (place // step) * width + within + (lons - side * width)
    for _ in range(3):
        apart = jnp.where(apart >= lons, apart - lons, apart)
    out_ref[...] = jnp.where(within < width, apart, -1)


def tables_kernel(width, filter_ref, band_ref, apart_ref, table_ref, first):
    bases, lons = filter_ref.shape
    taps, rows, _ = band_ref.shape
    step, places = first.shape[1:]
    columns = places // (2 * step)
    lat = lax.axis_index("lat")
    below = (lat > 0).astype(F32)
    above = (lat < lax.axis_size("lat") - 1).astype(F32)
    inside = [[below, below, 1.0], [1.0, above, above]]
    slots = [[0, 1, 2], [2, 0, 1]]
    profile = filter_ref[...]
    band = band_ref[...].astype(F32)
    apart = apart_ref[...]
    first[...] = jnp.zeros_like(first)
    for lon in range(width):
        pick = (apart == lon).astype(F32).astype(BF16)
        first[:, lon, :] = jnp.dot(profile, pick, preferred_element_type=F32)
    upper = lax.broadcasted_iota(jnp.int32, (SUBLANES, places), 0) < SUBLANES // 2
    count = columns * width
    for basis in range(bases):
        circle = first[basis]
        turned = [
            pltpu.roll(circle, column * 2 * step, 1) if column else circle
            for column in range(columns)
        ]
        last = [block[SUBLANES:] for block in turned]
        pairs = [
            jnp.where(upper, one, pltpu.roll(other, SUBLANES // 2, 0))
            for one, other in zip(last[::2], last[1::2])
        ]
        turned = jnp.concatenate([block[:SUBLANES] for block in turned] + pairs, axis=0)
        at = basis * count
        for row in range(rows):
            for tap in range(taps):
                weight = band[tap, row : row + 1, basis : basis + 1] * inside[row][tap]
                to = slots[row][tap] * places
                table_ref[row, at : at + count, to : to + places] = (weight * turned).astype(BF16)


def squares_kernel(own_ref, mate_ref, squares_ref, padded):
    bases, group, half = own_ref.shape
    lanes = squares_ref.shape[1]
    _, side = column_and_side()
    first = side == 0
    own = own_ref[...].astype(F32)
    mate = mate_ref[...].astype(F32)
    padded[...] = jnp.zeros_like(padded)
    padded[0, :, :group, :half] = jnp.where(first, own, mate)
    padded[1, :, :group, :half] = jnp.where(first, mate, own)
    members = padded.shape[2]
    into = lax.broadcasted_iota(jnp.int32, (lanes, members), 0)
    member = lax.broadcasted_iota(jnp.int32, (lanes, members), 1)
    repeat = (into % group == member).astype(F32).astype(BF16)
    row = lax.broadcasted_iota(jnp.int32, (lanes, lanes), 0)
    column = lax.broadcasted_iota(jnp.int32, (lanes, lanes), 1)
    same = (row // group == column // group) & (row < 2 * half) & (column < 2 * half)
    for basis in range(bases):
        weights = padded[0, basis] + pltpu.roll(padded[1, basis], half, 1)
        repeated = jnp.dot(repeat, weights.astype(BF16), preferred_element_type=F32)
        squares_ref[basis * lanes : (basis + 1) * lanes] = jnp.where(same, repeated, 0.0).astype(
            BF16
        )


def rows_of(message, block, rest):
    groups = unfold(message.astype(F32), block)
    last = (groups[2], pltpu.roll(groups[2], SUBLANES - rest, 0))
    return [jnp.concatenate([groups[row], last[row]], axis=0).astype(BF16) for row in range(2)]


def unpack_kernel(block, width, own_ref, out_ref):
    for at in range(own_ref.shape[0]):
        for row, read in enumerate(rows_of(own_ref[at], block, width - SUBLANES)):
            out_ref[row, at] = read


def own_kernel(block, width, mate, own, table_ref, part_ref, field):
    rows, columns, step, _ = own.shape
    places = field.shape[1]
    side = lax.axis_index("lon") % 2
    for at in range(columns):
        first = pl.multiple_of((2 * at + side) * step, step)
        other = pl.multiple_of((2 * at + 1 - side) * step, step)
        for row, read in enumerate(rows_of(mate[at], block, width - SUBLANES)):
            field[row, pl.ds(first, step)] = own[row, at]
            field[row, pl.ds(other, step)] = read
    for row in range(rows):
        part_ref[row] = jnp.dot(
            table_ref[row, :, 2 * places :], field[row], preferred_element_type=F32
        )


def conv_kernel(
    block, width, odd_mate, odd_own, even, part_ref, table_ref, squares_ref, *refs
):
    *out_refs, field, spread, stage = refs
    columns = len(out_refs)
    lanes = squares_ref.shape[1]
    bases = squares_ref.shape[0] // lanes
    rows, _, inner = table_ref.shape
    places = inner // 3
    step = places // (2 * columns)
    half = columns * width
    rest = width - SUBLANES
    column, side = column_and_side()
    odd = lax.axis_index("lat") % 2

    def place(row, at, message):
        for slot, read in enumerate(rows_of(message, block, rest)):
            first = pl.multiple_of(slot * places + at * step, step)
            field[row, pl.ds(first, step)] = read

    for at in range(columns):
        place(1 - odd, 2 * at, even[at, 0])
        place(1 - odd, 2 * at + 1, even[at, 1])
        place(odd, 2 * at + side, odd_own[at])
        place(odd, 2 * at + 1 - side, odd_mate[at])
    for row in range(rows):
        over = jnp.dot(
            table_ref[row, :, : 2 * places], field[row], preferred_element_type=F32
        )
        over = (over + part_ref[row]).astype(BF16)
        for basis in range(bases):
            spread[row * half : (row + 1) * half, basis * lanes : (basis + 1) * lanes] = over[
                basis * half : (basis + 1) * half
            ]
    mixed = jnp.dot(spread[...], squares_ref[...], preferred_element_type=F32)
    upper = lax.broadcasted_iota(jnp.int32, (SUBLANES, lanes), 0) < rest
    top, bottom = mixed[:half], mixed[half:]
    for target in range(columns):
        at = target * SUBLANES
        pair = (columns + target // 2) * SUBLANES
        first, second = top[pair : pair + SUBLANES], bottom[pair : pair + SUBLANES]
        if target % 2:
            first = pltpu.roll(first, rest, 0)
        else:
            second = pltpu.roll(second, rest, 0)
        last = jnp.where(upper, first, second)
        points = jnp.concatenate(
            [top[at : at + SUBLANES], bottom[at : at + SUBLANES], last], axis=0
        )
        stage[target] = fold(points, block)
    for apart in range(columns):
        out_refs[apart][...] = stage[column ^ apart]


def tail_kernel(order, *refs):
    columns = len(order)
    back_refs = refs[:columns]
    latent_ref, up_ref, down_ref, out_ref, points, stage = refs[columns:]
    width, rows, chans = latent_ref.shape
    rest = width - SUBLANES
    block = chans // columns
    lanes = lanes_of(block)
    column, _ = column_and_side()
    for apart, ref in zip(order, back_refs):
        stage[column ^ apart] = ref[...]
    group_points(latent_ref, points)
    kept = lax.broadcasted_iota(jnp.int32, (3 * SUBLANES, lanes), 1) < block
    convolved = None
    for target in range(columns):
        piece = jnp.concatenate(unfold(stage[target].astype(F32), block), axis=0)
        piece = jnp.where(kept, piece, 0.0)
        if chans > lanes:
            gap = jnp.zeros((3 * SUBLANES, chans - lanes), F32)
            piece = jnp.concatenate([piece, gap], axis=1)
        piece = pltpu.roll(piece, target * block, 1) if target else piece
        convolved = piece if convolved is None else convolved + piece
    summed = (points[...] + convolved).astype(BF16)
    ones = jnp.ones((2 * SUBLANES, chans), BF16)
    count = summed.shape[0]
    raised = jnp.dot(
        jnp.concatenate([summed, ones[: up_to(count, 2 * SUBLANES) - count]], axis=0),
        up_ref[...],
        preferred_element_type=F32,
    )
    summed = summed.astype(F32)
    mean = jnp.mean(summed, axis=1, keepdims=True)
    centred = summed - mean
    scale = lax.rsqrt(jnp.mean(centred * centred, axis=1, keepdims=True) + 1e-05)
    hidden = scale * (raised[:count] - mean * raised[count : count + 1])
    hidden = (0.5 * hidden * (1.0 + lax.erf(hidden * 0.5**0.5))).astype(BF16)
    result = summed + jnp.dot(hidden, down_ref[...], preferred_element_type=F32)
    for row in range(rows):
        out_ref[:SUBLANES, row, :] = result[row * SUBLANES : (row + 1) * SUBLANES].astype(BF16)
        at = rows * SUBLANES + row * rest
        out_ref[SUBLANES:, row, :] = result[at : at + rest].astype(BF16)


VMEM = pl.BlockSpec(memory_space=pltpu.VMEM)


def call(kernel, name, out_shape, scratch, work, *operands):
    several = isinstance(out_shape, tuple)
    return pl.pallas_call(
        kernel,
        out_shape=out_shape,
        in_specs=[VMEM] * len(operands),
        out_specs=(VMEM,) * len(out_shape) if several else VMEM,
        scratch_shapes=scratch,
        compiler_params=pltpu.CompilerParams(vmem_limit_bytes=24 * 2**20),
        cost_estimate=pl.CostEstimate(flops=work, bytes_accessed=10**6, transcendentals=0),
        name=name,
    )(*operands)


def over_columns(message, count, apart):
    pairs = [(i, ((i // 2) ^ apart) * 2 + i % 2) for i in range(count)]
    return lax.ppermute(message, "lon", pairs) if apart else message


def over_sides(block, count):
    return lax.ppermute(block, "lon", [(i, i ^ 1) for i in range(count)])


def swap(block, count, partner):
    pairs = []
    for lat in range(lax.axis_size("lat")):
        for lon in range(count):
            to_lat, to_lon = partner(lat, lon)
            pairs.append((lat * count + lon, to_lat * count + to_lon))
    return lax.ppermute(block, ("lat", "lon"), pairs)


def odd_pair(lat, lon, to_lon, rows):
    to = lat + 1 if lat % 2 else lat - 1
    return (to, to_lon) if 0 <= to < rows else (lat, lon ^ 1)


def local(latent, lon_filter, mix_weight, band_weight, offsets, w_up, w_down):
    rows, width, chans = latent.shape
    bases, lons = lon_filter.shape
    half, group = mix_weight.shape[1:]
    taps = band_weight.shape[2]
    count = lons // width
    columns = count // 2
    block = 2 * half
    step = up_to(width, 2 * SUBLANES)
    places = count * step
    lanes = lanes_of(block)
    height = message_rows(block)
    assert rows == 2 and taps == 3 and columns & (columns - 1) == 0
    assert lax.axis_size("lat") % 2 == 0
    assert 2 * width == 3 * SUBLANES and columns * width % (2 * SUBLANES) == 0
    assert 3 * (block % LANES) <= LANES

    far_first = tuple(reversed(range(columns)))
    inward = far_first
    if columns > 3:
        inward = (far_first[1], far_first[0]) + far_first[2:]
    message = jax.ShapeDtypeStruct((height, LANES), BF16)
    messages = (message,) * columns
    stage = pltpu.VMEM((columns, height, LANES), BF16)
    points = pltpu.VMEM((3 * SUBLANES, chans), F32)
    lon_first = jnp.transpose(latent, (1, 0, 2))
    mix_own = jnp.transpose(mix_weight, (0, 2, 1))

    raw = over_columns(lon_first, count, inward[0])
    apart = call(
        functools.partial(apart_kernel, width, step),
        "apart",
        jax.ShapeDtypeStruct((lons, places), jnp.int32),
        [],
        10**9,
    )
    loaded, apart = lax.optimization_barrier((lon_first, apart))
    packed = call(
        functools.partial(pack_kernel, inward[1:]),
        "pack",
        (message,) * (columns - 1),
        [points, stage],
        10**9,
        loaded,
    )
    arrived = [call(cut_kernel, "cut", message, [points], 5 * 10**9, raw)]
    arrived += [over_columns(*pair) for pair in zip(packed, [count] * columns, inward[1:])]
    mix_mate = over_sides(mix_own, count)
    table = call(
        functools.partial(tables_kernel, width),
        "tables",
        jax.ShapeDtypeStruct((rows, bases * columns * width, taps * places), BF16),
        [pltpu.VMEM((bases, step, places), F32)],
        10**6,
        lon_filter,
        jnp.transpose(band_weight, (2, 1, 0)),
        apart,
    )
    gathered = jax.ShapeDtypeStruct((columns, height, LANES), BF16)
    own_side = call(
        functools.partial(column_kernel, inward),
        "join_columns",
        gathered,
        [],
        10**8,
        *arrived,
    )
    lats = lax.axis_size("lat")
    mate_side = swap(own_side, count, lambda lat, lon: (lat, lon ^ 1))
    odd_mate = swap(own_side, count, lambda lat, lon: odd_pair(lat, lon, lon ^ 1, lats))
    odd_own = swap(own_side, count, lambda lat, lon: odd_pair(lat, lon, lon, lats))
    own_rows = call(
        functools.partial(unpack_kernel, block, width),
        "unpack",
        jax.ShapeDtypeStruct((rows, columns, step, lanes), BF16),
        [],
        10**9,
        own_side,
    )
    circle = jax.ShapeDtypeStruct((columns, 2, height, LANES), BF16)
    home = call(sides_kernel, "join_sides", circle, [], 10**8, own_side, mate_side)
    even = swap(home, count, lambda lat, lon: (lat ^ 1, lon))
    mix_mate, _ = lax.optimization_barrier((mix_mate, home))
    squares = call(
        squares_kernel,
        "squares",
        jax.ShapeDtypeStruct((bases * lanes, lanes), BF16),
        [pltpu.VMEM((2, bases, up_to(group, 2 * SUBLANES), lanes), F32)],
        10**9,
        mix_own,
        mix_mate,
    )
    part = call(
        functools.partial(own_kernel, block, width),
        "conv_own",
        jax.ShapeDtypeStruct((rows, bases * columns * width, lanes), F32),
        [pltpu.VMEM((rows, places, lanes), BF16)],
        10**9,
        mate_side,
        own_rows,
        table,
    )
    mixed = call(
        functools.partial(conv_kernel, block, width),
        "conv",
        messages,
        [
            pltpu.VMEM((rows, 2 * places, lanes), BF16),
            pltpu.VMEM((rows * columns * width, bases * lanes), BF16),
            pltpu.VMEM((columns, height, LANES), BF16),
        ],
        10**10,
        odd_mate,
        odd_own,
        even,
        part,
        table,
        squares,
    )
    outward = far_first[1:-1] + far_first[:1] + far_first[-1:]
    back = [over_columns(mixed[apart], count, apart) for apart in outward]
    result = call(
        functools.partial(tail_kernel, outward),
        "tail",
        jax.ShapeDtypeStruct(lon_first.shape, BF16),
        [points, stage],
        10**9,
        *back,
        lon_first,
        w_up,
        w_down,
    )
    return jnp.transpose(result, (1, 0, 2))


def solution(mesh):
    return jax.shard_map(
        local,
        mesh=mesh,
        in_specs=(
            P("lat", "lon", None),
            P(),
            P(None, "lon", None),
            P(None, "lat", None),
            P("lat"),
            P(),
            P(),
        ),
        out_specs=P("lat", "lon", None),
        check_vma=False,
    )
```

```python
import functools

import jax
import jax.numpy as jnp
from jax import lax
from jax.experimental import pallas as pl
from jax.experimental.pallas import tpu as pltpu
from jax.sharding import PartitionSpec as P

F32 = jnp.float32
BF16 = jnp.bfloat16
LANES = 128
SUBLANES = 8


def up_to(size, step):
    return -(-size // step) * step


def column_and_side():
    place = lax.axis_index("lon")
    return place // 2, place % 2


def message_rows(block):
    tiles = block // LANES
    return up_to(3 * SUBLANES * tiles + (SUBLANES if block % LANES else 0), 2 * SUBLANES)


def lanes_of(block):
    return up_to(block, LANES)


def fold(points, block):
    whole, rest = divmod(block, LANES)
    parts = [points[:, tile * LANES : (tile + 1) * LANES] for tile in range(whole)]
    if rest:
        odd = points[:, whole * LANES : (whole + 1) * LANES]
        kept = lax.broadcasted_iota(jnp.int32, (SUBLANES, LANES), 1) < rest
        shared = None
        for third in range(3):
            piece = jnp.where(kept, odd[third * SUBLANES : (third + 1) * SUBLANES], 0.0)
            piece = pltpu.roll(piece, third * rest, 1) if third else piece
            shared = piece if shared is None else shared + piece
        parts.append(shared)
    filled = sum(part.shape[0] for part in parts)
    if message_rows(block) > filled:
        parts.append(jnp.zeros((message_rows(block) - filled, LANES), F32))
    return jnp.concatenate(parts, axis=0).astype(BF16)


def unfold(message, block):
    whole, rest = divmod(block, LANES)
    groups = []
    for third in range(3):
        first = third * SUBLANES
        parts = [
            message[tile * 3 * SUBLANES + first : tile * 3 * SUBLANES + first + SUBLANES]
            for tile in range(whole)
        ]
        if rest:
            odd = message[whole * 3 * SUBLANES : whole * 3 * SUBLANES + SUBLANES]
            parts.append(pltpu.roll(odd, LANES - third * rest, 1) if third else odd)
        groups.append(jnp.concatenate(parts, axis=1) if len(parts) > 1 else parts[0])
    return groups


def group_points(latent_ref, points):
    width, rows, _ = latent_ref.shape
    rest = width - SUBLANES
    for row in range(rows):
        points[row * SUBLANES : (row + 1) * SUBLANES] = latent_ref[:SUBLANES, row, :].astype(F32)
        at = rows * SUBLANES + row * rest
        points[at : at + rest] = latent_ref[SUBLANES:, row, :].astype(F32)


def pack_kernel(order, latent_ref, *refs):
    *out_refs, points, stage = refs
    columns = stage.shape[0]
    chans = latent_ref.shape[2]
    block = chans // columns
    column, _ = column_and_side()
    group_points(latent_ref, points)
    own = points[...]
    for target in range(columns):
        turned = pltpu.roll(own, chans - target * block, 1) if target else own
        stage[target] = fold(turned[:, : lanes_of(block)], block)
    for apart, ref in zip(order, out_refs):
        ref[...] = stage[column ^ apart]


def cut_kernel(raw_ref, out_ref, points):
    chans = raw_ref.shape[2]
    block = chans // (lax.axis_size("lon") // 2)
    column, _ = column_and_side()
    group_points(raw_ref, points)
    turned = pltpu.roll(points[...], (chans - column * block) % chans, 1)
    out_ref[...] = fold(turned[:, : lanes_of(block)], block)


def column_kernel(order, *refs):
    *in_refs, out_ref = refs
    column, _ = column_and_side()
    for apart, ref in zip(order, in_refs):
        out_ref[column ^ apart] = ref[...]


def sides_kernel(own_ref, mate_ref, out_ref):
    _, side = column_and_side()
    out_ref[:, side] = own_ref[...]
    out_ref[:, 1 - side] = mate_ref[...]


def apart_kernel(width, step, out_ref):
    lons = out_ref.shape[0]
    side = lax.axis_index("lon") % 2
    source = lax.broadcasted_iota(jnp.int32, out_ref.shape, 0)
    place = lax.broadcasted_iota(jnp.int32, out_ref.shape, 1)
    within = place % step
    apart = source + (place // step) * width + within + (lons - side * width)
    for _ in range(3):
        apart = jnp.where(apart >= lons, apart - lons, apart)
    out_ref[...] = jnp.where(within < width, apart, -1)


def tables_kernel(width, filter_ref, band_ref, apart_ref, table_ref, first):
    bases, lons = filter_ref.shape
    taps, rows, _ = band_ref.shape
    step, places = first.shape[1:]
    columns = places // (2 * step)
    lat = lax.axis_index("lat")
    below = (lat > 0).astype(F32)
    above = (lat < lax.axis_size("lat") - 1).astype(F32)
    inside = [[below, below, 1.0], [1.0, above, above]]
    slots = [[0, 1, 2], [2, 0, 1]]
    profile = filter_ref[...]
    band = band_ref[...].astype(F32)
    apart = apart_ref[...]
    first[...] = jnp.zeros_like(first)
    for lon in range(width):
        pick = (apart == lon).astype(F32).astype(BF16)
        first[:, lon, :] = jnp.dot(profile, pick, preferred_element_type=F32)
    upper = lax.broadcasted_iota(jnp.int32, (SUBLANES, places), 0) < SUBLANES // 2
    count = columns * width
    for basis in range(bases):
        circle = first[basis]
        turned = [
            pltpu.roll(circle, column * 2 * step, 1) if column else circle
            for column in range(columns)
        ]
        last = [block[SUBLANES:] for block in turned]
        pairs = [
            jnp.where(upper, one, pltpu.roll(other, SUBLANES // 2, 0))
            for one, other in zip(last[::2], last[1::2])
        ]
        turned = jnp.concatenate([block[:SUBLANES] for block in turned] + pairs, axis=0)
        at = basis * count
        for row in range(rows):
            for tap in range(taps):
                weight = band[tap, row : row + 1, basis : basis + 1] * inside[row][tap]
                to = slots[row][tap] * places
                table_ref[row, at : at + count, to : to + places] = (weight * turned).astype(BF16)


def squares_kernel(own_ref, mate_ref, squares_ref, padded):
    bases, group, half = own_ref.shape
    lanes = squares_ref.shape[1]
    _, side = column_and_side()
    first = side == 0
    own = own_ref[...].astype(F32)
    mate = mate_ref[...].astype(F32)
    padded[...] = jnp.zeros_like(padded)
    padded[0, :, :group, :half] = jnp.where(first, own, mate)
    padded[1, :, :group, :half] = jnp.where(first, mate, own)
    members = padded.shape[2]
    into = lax.broadcasted_iota(jnp.int32, (lanes, members), 0)
    member = lax.broadcasted_iota(jnp.int32, (lanes, members), 1)
    repeat = (into % group == member).astype(F32).astype(BF16)
    row = lax.broadcasted_iota(jnp.int32, (lanes, lanes), 0)
    column = lax.broadcasted_iota(jnp.int32, (lanes, lanes), 1)
    same = (row // group == column // group) & (row < 2 * half) & (column < 2 * half)
    for basis in range(bases):
        weights = padded[0, basis] + pltpu.roll(padded[1, basis], half, 1)
        repeated = jnp.dot(repeat, weights.astype(BF16), preferred_element_type=F32)
        squares_ref[basis * lanes : (basis + 1) * lanes] = jnp.where(same, repeated, 0.0).astype(
            BF16
        )


def rows_of(message, block, rest):
    groups = unfold(message.astype(F32), block)
    last = (groups[2], pltpu.roll(groups[2], SUBLANES - rest, 0))
    return [jnp.concatenate([groups[row], last[row]], axis=0).astype(BF16) for row in range(2)]


def unpack_kernel(block, width, own_ref, out_ref):
    for at in range(own_ref.shape[0]):
        for row, read in enumerate(rows_of(own_ref[at], block, width - SUBLANES)):
            out_ref[row, at] = read


def own_kernel(block, width, mate, own, table_ref, part_ref, field):
    rows, columns, step, _ = own.shape
    places = field.shape[1]
    side = lax.axis_index("lon") % 2
    for at in range(columns):
        first = pl.multiple_of((2 * at + side) * step, step)
        other = pl.multiple_of((2 * at + 1 - side) * step, step)
        for row, read in enumerate(rows_of(mate[at], block, width - SUBLANES)):
            field[row, pl.ds(first, step)] = own[row, at]
            field[row, pl.ds(other, step)] = read
    for row in range(rows):
        part_ref[row] = jnp.dot(
            table_ref[row, :, 2 * places :], field[row], preferred_element_type=F32
        )


def conv_kernel(
    block, width, odd_mate, odd_own, even, part_ref, table_ref, squares_ref, *refs
):
    *out_refs, field, spread, stage = refs
    columns = len(out_refs)
    lanes = squares_ref.shape[1]
    bases = squares_ref.shape[0] // lanes
    rows, _, inner = table_ref.shape
    places = inner // 3
    step = places // (2 * columns)
    half = columns * width
    rest = width - SUBLANES
    column, side = column_and_side()
    odd = lax.axis_index("lat") % 2

    def place(row, at, message):
        for slot, read in enumerate(rows_of(message, block, rest)):
            first = pl.multiple_of(slot * places + at * step, step)
            field[row, pl.ds(first, step)] = read

    for at in range(columns):
        place(1 - odd, 2 * at, even[at, 0])
        place(1 - odd, 2 * at + 1, even[at, 1])
        place(odd, 2 * at + side, odd_own[at])
        place(odd, 2 * at + 1 - side, odd_mate[at])
    for row in range(rows):
        over = jnp.dot(
            table_ref[row, :, : 2 * places], field[row], preferred_element_type=F32
        )
        over = (over + part_ref[row]).astype(BF16)
        for basis in range(bases):
            spread[row * half : (row + 1) * half, basis * lanes : (basis + 1) * lanes] = over[
                basis * half : (basis + 1) * half
            ]
    mixed = jnp.dot(spread[...], squares_ref[...], preferred_element_type=F32)
    upper = lax.broadcasted_iota(jnp.int32, (SUBLANES, lanes), 0) < rest
    top, bottom = mixed[:half], mixed[half:]
    for target in range(columns):
        at = target * SUBLANES
        pair = (columns + target // 2) * SUBLANES
        first, second = top[pair : pair + SUBLANES], bottom[pair : pair + SUBLANES]
        if target % 2:
            first = pltpu.roll(first, rest, 0)
        else:
            second = pltpu.roll(second, rest, 0)
        last = jnp.where(upper, first, second)
        points = jnp.concatenate(
            [top[at : at + SUBLANES], bottom[at : at + SUBLANES], last], axis=0
        )
        stage[target] = fold(points, block)
    for apart in range(columns):
        out_refs[apart][...] = stage[column ^ apart]


def placed(message, column, chans, block):
    lanes = lanes_of(block)
    kept = lax.broadcasted_iota(jnp.int32, (3 * SUBLANES, lanes), 1) < block
    piece = jnp.concatenate(unfold(message.astype(F32), block), axis=0)
    piece = jnp.where(kept, piece, 0.0)
    if chans > lanes:
        gap = jnp.zeros((3 * SUBLANES, chans - lanes), F32)
        piece = jnp.concatenate([piece, gap], axis=1)
    return pltpu.roll(piece, column * block, 1)


def residual_kernel(columns, own_ref, latent_ref, out_ref, points):
    chans = latent_ref.shape[2]
    column, _ = column_and_side()
    group_points(latent_ref, points)
    out_ref[...] = points[...] + placed(own_ref[...], column, chans, chans // columns)


def tail_kernel(order, *refs):
    columns = len(order) + 1
    back_refs = refs[: columns - 1]
    residual_ref, up_ref, down_ref, out_ref = refs[columns - 1 :]
    width, rows, chans = out_ref.shape
    rest = width - SUBLANES
    column, _ = column_and_side()
    convolved = residual_ref[...]
    for apart, ref in zip(order, back_refs):
        convolved = convolved + placed(ref[...], column ^ apart, chans, chans // columns)
    summed = convolved.astype(BF16)
    ones = jnp.ones((2 * SUBLANES, chans), BF16)
    count = summed.shape[0]
    raised = jnp.dot(
        jnp.concatenate([summed, ones[: up_to(count, 2 * SUBLANES) - count]], axis=0),
        up_ref[...],
        preferred_element_type=F32,
    )
    summed = summed.astype(F32)
    mean = jnp.mean(summed, axis=1, keepdims=True)
    centred = summed - mean
    scale = lax.rsqrt(jnp.mean(centred * centred, axis=1, keepdims=True) + 1e-05)
    hidden = scale * (raised[:count] - mean * raised[count : count + 1])
    hidden = (0.5 * hidden * (1.0 + lax.erf(hidden * 0.5**0.5))).astype(BF16)
    result = summed + jnp.dot(hidden, down_ref[...], preferred_element_type=F32)
    for row in range(rows):
        out_ref[:SUBLANES, row, :] = result[row * SUBLANES : (row + 1) * SUBLANES].astype(BF16)
        at = rows * SUBLANES + row * rest
        out_ref[SUBLANES:, row, :] = result[at : at + rest].astype(BF16)


VMEM = pl.BlockSpec(memory_space=pltpu.VMEM)


def call(kernel, name, out_shape, scratch, work, *operands):
    several = isinstance(out_shape, tuple)
    return pl.pallas_call(
        kernel,
        out_shape=out_shape,
        in_specs=[VMEM] * len(operands),
        out_specs=(VMEM,) * len(out_shape) if several else VMEM,
        scratch_shapes=scratch,
        compiler_params=pltpu.CompilerParams(vmem_limit_bytes=24 * 2**20),
        cost_estimate=pl.CostEstimate(flops=work, bytes_accessed=10**6, transcendentals=0),
        name=name,
    )(*operands)


def over_columns(message, count, apart):
    pairs = [(i, ((i // 2) ^ apart) * 2 + i % 2) for i in range(count)]
    return lax.ppermute(message, "lon", pairs) if apart else message


def over_sides(block, count):
    return lax.ppermute(block, "lon", [(i, i ^ 1) for i in range(count)])


def swap(block, count, partner):
    pairs = []
    for lat in range(lax.axis_size("lat")):
        for lon in range(count):
            to_lat, to_lon = partner(lat, lon)
            pairs.append((lat * count + lon, to_lat * count + to_lon))
    return lax.ppermute(block, ("lat", "lon"), pairs)


def odd_pair(lat, lon, to_lon, rows):
    to = lat + 1 if lat % 2 else lat - 1
    return (to, to_lon) if 0 <= to < rows else (lat, lon ^ 1)


def local(latent, lon_filter, mix_weight, band_weight, offsets, w_up, w_down):
    rows, width, chans = latent.shape
    bases, lons = lon_filter.shape
    half, group = mix_weight.shape[1:]
    taps = band_weight.shape[2]
    count = lons // width
    columns = count // 2
    block = 2 * half
    step = up_to(width, 2 * SUBLANES)
    places = count * step
    lanes = lanes_of(block)
    height = message_rows(block)
    assert rows == 2 and taps == 3 and columns & (columns - 1) == 0
    assert lax.axis_size("lat") % 2 == 0
    assert 2 * width == 3 * SUBLANES and columns * width % (2 * SUBLANES) == 0
    assert 3 * (block % LANES) <= LANES

    far_first = tuple(reversed(range(columns)))
    inward = far_first
    if columns > 3:
        inward = (far_first[1], far_first[0]) + far_first[2:]
    message = jax.ShapeDtypeStruct((height, LANES), BF16)
    messages = (message,) * columns
    stage = pltpu.VMEM((columns, height, LANES), BF16)
    points = pltpu.VMEM((3 * SUBLANES, chans), F32)
    lon_first = jnp.transpose(latent, (1, 0, 2))
    mix_own = jnp.transpose(mix_weight, (0, 2, 1))

    raw = over_columns(lon_first, count, inward[0])
    apart = call(
        functools.partial(apart_kernel, width, step),
        "apart",
        jax.ShapeDtypeStruct((lons, places), jnp.int32),
        [],
        10**9,
    )
    loaded, apart = lax.optimization_barrier((lon_first, apart))
    packed = call(
        functools.partial(pack_kernel, inward[1:]),
        "pack",
        (message,) * (columns - 1),
        [points, stage],
        10**9,
        loaded,
    )
    arrived = [call(cut_kernel, "cut", message, [points], 5 * 10**9, raw)]
    arrived += [over_columns(*pair) for pair in zip(packed, [count] * columns, inward[1:])]
    mix_mate = over_sides(mix_own, count)
    table = call(
        functools.partial(tables_kernel, width),
        "tables",
        jax.ShapeDtypeStruct((rows, bases * columns * width, taps * places), BF16),
        [pltpu.VMEM((bases, step, places), F32)],
        10**6,
        lon_filter,
        jnp.transpose(band_weight, (2, 1, 0)),
        apart,
    )
    gathered = jax.ShapeDtypeStruct((columns, height, LANES), BF16)
    own_side = call(
        functools.partial(column_kernel, inward),
        "join_columns",
        gathered,
        [],
        10**8,
        *arrived,
    )
    lats = lax.axis_size("lat")
    mate_side = swap(own_side, count, lambda lat, lon: (lat, lon ^ 1))
    odd_mate = swap(own_side, count, lambda lat, lon: odd_pair(lat, lon, lon ^ 1, lats))
    odd_own = swap(own_side, count, lambda lat, lon: odd_pair(lat, lon, lon, lats))
    own_rows = call(
        functools.partial(unpack_kernel, block, width),
        "unpack",
        jax.ShapeDtypeStruct((rows, columns, step, lanes), BF16),
        [],
        10**9,
        own_side,
    )
    circle = jax.ShapeDtypeStruct((columns, 2, height, LANES), BF16)
    home = call(sides_kernel, "join_sides", circle, [], 10**8, own_side, mate_side)
    even = swap(home, count, lambda lat, lon: (lat ^ 1, lon))
    mix_mate, _ = lax.optimization_barrier((mix_mate, home))
    squares = call(
        squares_kernel,
        "squares",
        jax.ShapeDtypeStruct((bases * lanes, lanes), BF16),
        [pltpu.VMEM((2, bases, up_to(group, 2 * SUBLANES), lanes), F32)],
        10**9,
        mix_own,
        mix_mate,
    )
    part = call(
        functools.partial(own_kernel, block, width),
        "conv_own",
        jax.ShapeDtypeStruct((rows, bases * columns * width, lanes), F32),
        [pltpu.VMEM((rows, places, lanes), BF16)],
        10**9,
        mate_side,
        own_rows,
        table,
    )
    mixed = call(
        functools.partial(conv_kernel, block, width),
        "conv",
        messages,
        [
            pltpu.VMEM((rows, 2 * places, lanes), BF16),
            pltpu.VMEM((rows * columns * width, bases * lanes), BF16),
            pltpu.VMEM((columns, height, LANES), BF16),
        ],
        10**10,
        odd_mate,
        odd_own,
        even,
        part,
        table,
        squares,
    )
    outward = far_first[1:-1] + far_first[:1]
    back = [over_columns(mixed[apart], count, apart) for apart in outward]
    residual = call(
        functools.partial(residual_kernel, columns),
        "residual",
        jax.ShapeDtypeStruct((3 * SUBLANES, chans), F32),
        [points],
        10**9,
        mixed[0],
        lon_first,
    )
    result = call(
        functools.partial(tail_kernel, outward),
        "tail",
        jax.ShapeDtypeStruct(lon_first.shape, BF16),
        [],
        10**9,
        *back,
        residual,
        w_up,
        w_down,
    )
    return jnp.transpose(result, (1, 0, 2))


def solution(mesh):
    return jax.shard_map(
        local,
        mesh=mesh,
        in_specs=(
            P("lat", "lon", None),
            P(),
            P(None, "lon", None),
            P(None, "lat", None),
            P("lat"),
            P(),
            P(),
        ),
        out_specs=P("lat", "lon", None),
        check_vma=False,
    )
```

```python
import functools

import jax
import jax.numpy as jnp
from jax import lax
from jax.experimental import pallas as pl
from jax.experimental.pallas import tpu as pltpu
from jax.sharding import PartitionSpec as P

F32 = jnp.float32
BF16 = jnp.bfloat16
LANES = 128
SUBLANES = 8


def up_to(size, step):
    return -(-size // step) * step


def column_and_side():
    place = lax.axis_index("lon")
    return place // 2, place % 2


def message_rows(block):
    tiles = block // LANES
    return up_to(3 * SUBLANES * tiles + (SUBLANES if block % LANES else 0), 2 * SUBLANES)


def lanes_of(block):
    return up_to(block, LANES)


def fold(points, block):
    whole, rest = divmod(block, LANES)
    parts = [points[:, tile * LANES : (tile + 1) * LANES] for tile in range(whole)]
    if rest:
        odd = points[:, whole * LANES : (whole + 1) * LANES]
        kept = lax.broadcasted_iota(jnp.int32, (SUBLANES, LANES), 1) < rest
        shared = None
        for third in range(3):
            piece = jnp.where(kept, odd[third * SUBLANES : (third + 1) * SUBLANES], 0.0)
            piece = pltpu.roll(piece, third * rest, 1) if third else piece
            shared = piece if shared is None else shared + piece
        parts.append(shared)
    filled = sum(part.shape[0] for part in parts)
    if message_rows(block) > filled:
        parts.append(jnp.zeros((message_rows(block) - filled, LANES), F32))
    return jnp.concatenate(parts, axis=0).astype(BF16)


def unfold(message, block):
    whole, rest = divmod(block, LANES)
    groups = []
    for third in range(3):
        first = third * SUBLANES
        parts = [
            message[tile * 3 * SUBLANES + first : tile * 3 * SUBLANES + first + SUBLANES]
            for tile in range(whole)
        ]
        if rest:
            odd = message[whole * 3 * SUBLANES : whole * 3 * SUBLANES + SUBLANES]
            parts.append(pltpu.roll(odd, LANES - third * rest, 1) if third else odd)
        groups.append(jnp.concatenate(parts, axis=1) if len(parts) > 1 else parts[0])
    return groups


def group_points(latent_ref, points):
    width, rows, _ = latent_ref.shape
    rest = width - SUBLANES
    for row in range(rows):
        points[row * SUBLANES : (row + 1) * SUBLANES] = latent_ref[:SUBLANES, row, :].astype(F32)
        at = rows * SUBLANES + row * rest
        points[at : at + rest] = latent_ref[SUBLANES:, row, :].astype(F32)


def pack_kernel(order, latent_ref, *refs):
    *out_refs, points, stage = refs
    columns = stage.shape[0]
    chans = latent_ref.shape[2]
    block = chans // columns
    column, _ = column_and_side()
    group_points(latent_ref, points)
    own = points[...]
    for target in range(columns):
        turned = pltpu.roll(own, chans - target * block, 1) if target else own
        stage[target] = fold(turned[:, : lanes_of(block)], block)
    for apart, ref in zip(order, out_refs):
        ref[...] = stage[column ^ apart]


def cut_kernel(raw_ref, out_ref, points):
    chans = raw_ref.shape[2]
    block = chans // (lax.axis_size("lon") // 2)
    column, _ = column_and_side()
    group_points(raw_ref, points)
    turned = pltpu.roll(points[...], (chans - column * block) % chans, 1)
    out_ref[...] = fold(turned[:, : lanes_of(block)], block)


def column_kernel(order, *refs):
    *in_refs, out_ref = refs
    column, _ = column_and_side()
    for apart, ref in zip(order, in_refs):
        out_ref[column ^ apart] = ref[...]


def sides_kernel(own_ref, mate_ref, out_ref):
    _, side = column_and_side()
    out_ref[:, side] = own_ref[...]
    out_ref[:, 1 - side] = mate_ref[...]


def apart_kernel(width, step, out_ref):
    lons = out_ref.shape[0]
    side = lax.axis_index("lon") % 2
    source = lax.broadcasted_iota(jnp.int32, out_ref.shape, 0)
    place = lax.broadcasted_iota(jnp.int32, out_ref.shape, 1)
    within = place % step
    apart = source + (place // step) * width + within + (lons - side * width)
    for _ in range(3):
        apart = jnp.where(apart >= lons, apart - lons, apart)
    out_ref[...] = jnp.where(within < width, apart, -1)


def tables_kernel(width, filter_ref, band_ref, apart_ref, table_ref, first):
    bases, lons = filter_ref.shape
    taps, rows, _ = band_ref.shape
    step, places = first.shape[1:]
    columns = places // (2 * step)
    lat = lax.axis_index("lat")
    below = (lat > 0).astype(F32)
    above = (lat < lax.axis_size("lat") - 1).astype(F32)
    inside = [[below, below, 1.0], [1.0, above, above]]
    slots = [[0, 1, 2], [2, 0, 1]]
    profile = filter_ref[...]
    band = band_ref[...].astype(F32)
    apart = apart_ref[...]
    first[...] = jnp.zeros_like(first)
    for lon in range(width):
        pick = (apart == lon).astype(F32).astype(BF16)
        first[:, lon, :] = jnp.dot(profile, pick, preferred_element_type=F32)
    upper = lax.broadcasted_iota(jnp.int32, (SUBLANES, places), 0) < SUBLANES // 2
    count = columns * width
    for basis in range(bases):
        circle = first[basis]
        turned = [
            pltpu.roll(circle, column * 2 * step, 1) if column else circle
            for column in range(columns)
        ]
        last = [block[SUBLANES:] for block in turned]
        pairs = [
            jnp.where(upper, one, pltpu.roll(other, SUBLANES // 2, 0))
            for one, other in zip(last[::2], last[1::2])
        ]
        turned = jnp.concatenate([block[:SUBLANES] for block in turned] + pairs, axis=0)
        at = basis * count
        for row in range(rows):
            for tap in range(taps):
                weight = band[tap, row : row + 1, basis : basis + 1] * inside[row][tap]
                to = slots[row][tap] * places
                table_ref[row, at : at + count, to : to + places] = (weight * turned).astype(BF16)


def squares_kernel(own_ref, mate_ref, squares_ref, padded):
    bases, group, half = own_ref.shape
    lanes = squares_ref.shape[1]
    _, side = column_and_side()
    first = side == 0
    own = own_ref[...].astype(F32)
    mate = mate_ref[...].astype(F32)
    padded[...] = jnp.zeros_like(padded)
    padded[0, :, :group, :half] = jnp.where(first, own, mate)
    padded[1, :, :group, :half] = jnp.where(first, mate, own)
    members = padded.shape[2]
    into = lax.broadcasted_iota(jnp.int32, (lanes, members), 0)
    member = lax.broadcasted_iota(jnp.int32, (lanes, members), 1)
    repeat = (into % group == member).astype(F32).astype(BF16)
    row = lax.broadcasted_iota(jnp.int32, (lanes, lanes), 0)
    column = lax.broadcasted_iota(jnp.int32, (lanes, lanes), 1)
    same = (row // group == column // group) & (row < 2 * half) & (column < 2 * half)
    for basis in range(bases):
        weights = padded[0, basis] + pltpu.roll(padded[1, basis], half, 1)
        repeated = jnp.dot(repeat, weights.astype(BF16), preferred_element_type=F32)
        squares_ref[basis * lanes : (basis + 1) * lanes] = jnp.where(same, repeated, 0.0).astype(
            BF16
        )


def rows_of(message, block, rest):
    groups = unfold(message.astype(F32), block)
    last = (groups[2], pltpu.roll(groups[2], SUBLANES - rest, 0))
    return [jnp.concatenate([groups[row], last[row]], axis=0).astype(BF16) for row in range(2)]


def unpack_kernel(block, width, own_ref, out_ref):
    for at in range(own_ref.shape[0]):
        for row, read in enumerate(rows_of(own_ref[at], block, width - SUBLANES)):
            out_ref[row, at] = read


def own_kernel(block, width, mate, own, table_ref, part_ref, field):
    rows, columns, step, _ = own.shape
    places = field.shape[1]
    side = lax.axis_index("lon") % 2
    for at in range(columns):
        first = pl.multiple_of((2 * at + side) * step, step)
        other = pl.multiple_of((2 * at + 1 - side) * step, step)
        for row, read in enumerate(rows_of(mate[at], block, width - SUBLANES)):
            field[row, pl.ds(first, step)] = own[row, at]
            field[row, pl.ds(other, step)] = read
    for row in range(rows):
        part_ref[row] = jnp.dot(
            table_ref[row, :, 2 * places :], field[row], preferred_element_type=F32
        )


def conv_kernel(
    block, width, odd_mate, odd_own, even, part_ref, table_ref, squares_ref, *refs
):
    *out_refs, field, spread, stage = refs
    columns = len(out_refs)
    lanes = squares_ref.shape[1]
    bases = squares_ref.shape[0] // lanes
    rows, _, inner = table_ref.shape
    places = inner // 3
    step = places // (2 * columns)
    half = columns * width
    rest = width - SUBLANES
    column, side = column_and_side()
    odd = lax.axis_index("lat") % 2

    def place(row, at, message):
        for slot, read in enumerate(rows_of(message, block, rest)):
            first = pl.multiple_of(slot * places + at * step, step)
            field[row, pl.ds(first, step)] = read

    for at in range(columns):
        place(1 - odd, 2 * at, even[at, 0])
        place(1 - odd, 2 * at + 1, even[at, 1])
        place(odd, 2 * at + side, odd_own[at])
        place(odd, 2 * at + 1 - side, odd_mate[at])
    for row in range(rows):
        over = jnp.dot(
            table_ref[row, :, : 2 * places], field[row], preferred_element_type=F32
        )
        over = (over + part_ref[row]).astype(BF16)
        for basis in range(bases):
            spread[row * half : (row + 1) * half, basis * lanes : (basis + 1) * lanes] = over[
                basis * half : (basis + 1) * half
            ]
    mixed = jnp.dot(spread[...], squares_ref[...], preferred_element_type=F32)
    upper = lax.broadcasted_iota(jnp.int32, (SUBLANES, lanes), 0) < rest
    top, bottom = mixed[:half], mixed[half:]
    for target in range(columns):
        at = target * SUBLANES
        pair = (columns + target // 2) * SUBLANES
        first, second = top[pair : pair + SUBLANES], bottom[pair : pair + SUBLANES]
        if target % 2:
            first = pltpu.roll(first, rest, 0)
        else:
            second = pltpu.roll(second, rest, 0)
        last = jnp.where(upper, first, second)
        points = jnp.concatenate(
            [top[at : at + SUBLANES], bottom[at : at + SUBLANES], last], axis=0
        )
        stage[target] = fold(points, block)
    for apart in range(columns):
        out_refs[apart][...] = stage[column ^ apart]


def summed_block(latent_block, message, block):
    convolved = jnp.concatenate(unfold(message.astype(F32), block), axis=0)
    kept = lax.broadcasted_iota(jnp.int32, convolved.shape, 1) < block
    return jnp.where(kept, latent_block + convolved, 0.0).astype(BF16)


def raised_block(summed, column, block, up_ref):
    count = summed.shape[0]
    ones = jnp.ones((up_to(count, 2 * SUBLANES) - count, block), BF16)
    rows = pl.multiple_of(column * block, block)
    return jnp.dot(
        jnp.concatenate([summed[:, :block], ones], axis=0),
        up_ref[pl.ds(rows, block), :],
        preferred_element_type=F32,
    )


def placed(summed, column, chans, block):
    piece = summed.astype(F32)
    if chans > piece.shape[1]:
        gap = jnp.zeros((piece.shape[0], chans - piece.shape[1]), F32)
        piece = jnp.concatenate([piece, gap], axis=1)
    return pltpu.roll(piece, column * block, 1)


def lift_kernel(
    apart, own_ref, first_ref, latent_ref, up_ref, blocks_ref, summed_ref, raised_ref, points
):
    columns = blocks_ref.shape[0]
    chans = latent_ref.shape[2]
    block = chans // columns
    column, _ = column_and_side()
    group_points(latent_ref, points)
    own = points[...]
    for target in range(columns):
        turned = pltpu.roll(own, chans - target * block, 1) if target else own
        blocks_ref[target] = turned[:, : lanes_of(block)]
    other = column ^ apart
    here = summed_block(blocks_ref[column], own_ref[...], block)
    there = summed_block(blocks_ref[other], first_ref[...], block)
    summed_ref[...] = placed(here, column, chans, block) + placed(there, other, chans, block)
    raised_ref[...] = raised_block(here, column, block, up_ref) + raised_block(
        there, other, block, up_ref
    )


def tail_kernel(order, *refs):
    back_refs = refs[: len(order)]
    blocks_ref, summed_ref, raised_ref, up_ref, down_ref, out_ref = refs[len(order) :]
    width, rows, chans = out_ref.shape
    rest = width - SUBLANES
    block = chans // blocks_ref.shape[0]
    column, _ = column_and_side()
    summed = summed_ref[...]
    raised = raised_ref[...]
    for apart, ref in zip(order, back_refs):
        other = column ^ apart
        there = summed_block(blocks_ref[other], ref[...], block)
        raised = raised + raised_block(there, other, block, up_ref)
        summed = summed + placed(there, other, chans, block)
    count = summed.shape[0]
    mean = jnp.mean(summed, axis=1, keepdims=True)
    centred = summed - mean
    scale = lax.rsqrt(jnp.mean(centred * centred, axis=1, keepdims=True) + 1e-05)
    hidden = scale * (raised[:count] - mean * raised[count : count + 1])
    hidden = (0.5 * hidden * (1.0 + lax.erf(hidden * 0.5**0.5))).astype(BF16)
    result = summed + jnp.dot(hidden, down_ref[...], preferred_element_type=F32)
    for row in range(rows):
        out_ref[:SUBLANES, row, :] = result[row * SUBLANES : (row + 1) * SUBLANES].astype(BF16)
        at = rows * SUBLANES + row * rest
        out_ref[SUBLANES:, row, :] = result[at : at + rest].astype(BF16)


VMEM = pl.BlockSpec(memory_space=pltpu.VMEM)


def call(kernel, name, out_shape, scratch, work, *operands):
    several = isinstance(out_shape, tuple)
    return pl.pallas_call(
        kernel,
        out_shape=out_shape,
        in_specs=[VMEM] * len(operands),
        out_specs=(VMEM,) * len(out_shape) if several else VMEM,
        scratch_shapes=scratch,
        compiler_params=pltpu.CompilerParams(vmem_limit_bytes=24 * 2**20),
        cost_estimate=pl.CostEstimate(flops=work, bytes_accessed=10**6, transcendentals=0),
        name=name,
    )(*operands)


def over_columns(message, count, apart):
    pairs = [(i, ((i // 2) ^ apart) * 2 + i % 2) for i in range(count)]
    return lax.ppermute(message, "lon", pairs) if apart else message


def over_sides(block, count):
    return lax.ppermute(block, "lon", [(i, i ^ 1) for i in range(count)])


def swap(block, count, partner):
    pairs = []
    for lat in range(lax.axis_size("lat")):
        for lon in range(count):
            to_lat, to_lon = partner(lat, lon)
            pairs.append((lat * count + lon, to_lat * count + to_lon))
    return lax.ppermute(block, ("lat", "lon"), pairs)


def odd_pair(lat, lon, to_lon, rows):
    to = lat + 1 if lat % 2 else lat - 1
    return (to, to_lon) if 0 <= to < rows else (lat, lon ^ 1)


def local(latent, lon_filter, mix_weight, band_weight, offsets, w_up, w_down):
    rows, width, chans = latent.shape
    bases, lons = lon_filter.shape
    half, group = mix_weight.shape[1:]
    taps = band_weight.shape[2]
    count = lons // width
    columns = count // 2
    block = 2 * half
    step = up_to(width, 2 * SUBLANES)
    places = count * step
    lanes = lanes_of(block)
    height = message_rows(block)
    assert rows == 2 and taps == 3 and columns & (columns - 1) == 0
    assert lax.axis_size("lat") % 2 == 0
    assert 2 * width == 3 * SUBLANES and columns * width % (2 * SUBLANES) == 0
    assert 3 * (block % LANES) <= LANES

    far_first = tuple(reversed(range(columns)))
    inward = far_first
    if columns > 3:
        inward = (far_first[1], far_first[0]) + far_first[2:]
    message = jax.ShapeDtypeStruct((height, LANES), BF16)
    messages = (message,) * columns
    stage = pltpu.VMEM((columns, height, LANES), BF16)
    points = pltpu.VMEM((3 * SUBLANES, chans), F32)
    lon_first = jnp.transpose(latent, (1, 0, 2))
    mix_own = jnp.transpose(mix_weight, (0, 2, 1))

    raw = over_columns(lon_first, count, inward[0])
    apart = call(
        functools.partial(apart_kernel, width, step),
        "apart",
        jax.ShapeDtypeStruct((lons, places), jnp.int32),
        [],
        10**9,
    )
    loaded, apart = lax.optimization_barrier((lon_first, apart))
    packed = call(
        functools.partial(pack_kernel, inward[1:]),
        "pack",
        (message,) * (columns - 1),
        [points, stage],
        10**9,
        loaded,
    )
    arrived = [call(cut_kernel, "cut", message, [points], 5 * 10**9, raw)]
    arrived += [over_columns(*pair) for pair in zip(packed, [count] * columns, inward[1:])]
    mix_mate = over_sides(mix_own, count)
    table = call(
        functools.partial(tables_kernel, width),
        "tables",
        jax.ShapeDtypeStruct((rows, bases * columns * width, taps * places), BF16),
        [pltpu.VMEM((bases, step, places), F32)],
        10**6,
        lon_filter,
        jnp.transpose(band_weight, (2, 1, 0)),
        apart,
    )
    gathered = jax.ShapeDtypeStruct((columns, height, LANES), BF16)
    own_side = call(
        functools.partial(column_kernel, inward),
        "join_columns",
        gathered,
        [],
        10**8,
        *arrived,
    )
    lats = lax.axis_size("lat")
    mate_side = swap(own_side, count, lambda lat, lon: (lat, lon ^ 1))
    odd_mate = swap(own_side, count, lambda lat, lon: odd_pair(lat, lon, lon ^ 1, lats))
    odd_own = swap(own_side, count, lambda lat, lon: odd_pair(lat, lon, lon, lats))
    own_rows = call(
        functools.partial(unpack_kernel, block, width),
        "unpack",
        jax.ShapeDtypeStruct((rows, columns, step, lanes), BF16),
        [],
        10**9,
        own_side,
    )
    circle = jax.ShapeDtypeStruct((columns, 2, height, LANES), BF16)
    home = call(sides_kernel, "join_sides", circle, [], 10**8, own_side, mate_side)
    even = swap(home, count, lambda lat, lon: (lat ^ 1, lon))
    mix_mate, _ = lax.optimization_barrier((mix_mate, home))
    squares = call(
        squares_kernel,
        "squares",
        jax.ShapeDtypeStruct((bases * lanes, lanes), BF16),
        [pltpu.VMEM((2, bases, up_to(group, 2 * SUBLANES), lanes), F32)],
        10**9,
        mix_own,
        mix_mate,
    )
    part = call(
        functools.partial(own_kernel, block, width),
        "conv_own",
        jax.ShapeDtypeStruct((rows, bases * columns * width, lanes), F32),
        [pltpu.VMEM((rows, places, lanes), BF16)],
        10**9,
        mate_side,
        own_rows,
        table,
    )
    mixed = call(
        functools.partial(conv_kernel, block, width),
        "conv",
        messages,
        [
            pltpu.VMEM((rows, 2 * places, lanes), BF16),
            pltpu.VMEM((rows * columns * width, bases * lanes), BF16),
            pltpu.VMEM((columns, height, LANES), BF16),
        ],
        10**10,
        odd_mate,
        odd_own,
        even,
        part,
        table,
        squares,
    )
    outward = far_first[1:-1] + far_first[:1]
    back = [over_columns(mixed[apart], count, apart) for apart in outward]
    first = outward.index(far_first[0])
    lifted = call(
        functools.partial(lift_kernel, far_first[0]),
        "lift",
        (
            jax.ShapeDtypeStruct((columns, 3 * SUBLANES, lanes), F32),
            jax.ShapeDtypeStruct((3 * SUBLANES, chans), F32),
            jax.ShapeDtypeStruct((up_to(3 * SUBLANES, 2 * SUBLANES), w_up.shape[1]), F32),
        ),
        [points],
        10**8,
        mixed[0],
        back[first],
        lon_first,
        w_up,
    )
    result = call(
        functools.partial(tail_kernel, outward[:first] + outward[first + 1 :]),
        "tail",
        jax.ShapeDtypeStruct(lon_first.shape, BF16),
        [],
        10**9,
        *back[:first],
        *back[first + 1 :],
        *lifted,
        w_up,
        w_down,
    )
    return jnp.transpose(result, (1, 0, 2))


def solution(mesh):
    return jax.shard_map(
        local,
        mesh=mesh,
        in_specs=(
            P("lat", "lon", None),
            P(),
            P(None, "lon", None),
            P(None, "lat", None),
            P("lat"),
            P(),
            P(),
        ),
        out_specs=P("lat", "lon", None),
        check_vma=False,
    )
```

```python
import functools

import jax
import jax.numpy as jnp
from jax import lax
from jax.experimental import pallas as pl
from jax.experimental.pallas import tpu as pltpu
from jax.sharding import PartitionSpec as P

F32 = jnp.float32
BF16 = jnp.bfloat16
LANES = 128
SUBLANES = 8


def up_to(size, step):
    return -(-size // step) * step


def column_and_side():
    place = lax.axis_index("lon")
    return place // 2, place % 2


def message_rows(block):
    tiles = block // LANES
    return up_to(3 * SUBLANES * tiles + (SUBLANES if block % LANES else 0), 2 * SUBLANES)


def lanes_of(block):
    return up_to(block, LANES)


def fold(points, block):
    whole, rest = divmod(block, LANES)
    parts = [points[:, tile * LANES : (tile + 1) * LANES] for tile in range(whole)]
    if rest:
        odd = points[:, whole * LANES : (whole + 1) * LANES]
        kept = lax.broadcasted_iota(jnp.int32, (SUBLANES, LANES), 1) < rest
        shared = None
        for third in range(3):
            piece = jnp.where(kept, odd[third * SUBLANES : (third + 1) * SUBLANES], 0.0)
            piece = pltpu.roll(piece, third * rest, 1) if third else piece
            shared = piece if shared is None else shared + piece
        parts.append(shared)
    filled = sum(part.shape[0] for part in parts)
    if message_rows(block) > filled:
        parts.append(jnp.zeros((message_rows(block) - filled, LANES), F32))
    return jnp.concatenate(parts, axis=0).astype(BF16)


def unfold(message, block):
    whole, rest = divmod(block, LANES)
    groups = []
    for third in range(3):
        first = third * SUBLANES
        parts = [
            message[tile * 3 * SUBLANES + first : tile * 3 * SUBLANES + first + SUBLANES]
            for tile in range(whole)
        ]
        if rest:
            odd = message[whole * 3 * SUBLANES : whole * 3 * SUBLANES + SUBLANES]
            parts.append(pltpu.roll(odd, LANES - third * rest, 1) if third else odd)
        groups.append(jnp.concatenate(parts, axis=1) if len(parts) > 1 else parts[0])
    return groups


def group_points(latent_ref, points):
    width, rows, _ = latent_ref.shape
    rest = width - SUBLANES
    for row in range(rows):
        points[row * SUBLANES : (row + 1) * SUBLANES] = latent_ref[:SUBLANES, row, :].astype(F32)
        at = rows * SUBLANES + row * rest
        points[at : at + rest] = latent_ref[SUBLANES:, row, :].astype(F32)


def pack_kernel(order, latent_ref, *refs):
    *out_refs, points, stage = refs
    columns = stage.shape[0]
    chans = latent_ref.shape[2]
    block = chans // columns
    column, _ = column_and_side()
    group_points(latent_ref, points)
    own = points[...]
    for target in range(columns):
        turned = pltpu.roll(own, chans - target * block, 1) if target else own
        stage[target] = fold(turned[:, : lanes_of(block)], block)
    for apart, ref in zip(order, out_refs):
        ref[...] = stage[column ^ apart]


def cut_kernel(raw_ref, out_ref, points):
    chans = raw_ref.shape[2]
    block = chans // (lax.axis_size("lon") // 2)
    column, _ = column_and_side()
    group_points(raw_ref, points)
    turned = pltpu.roll(points[...], (chans - column * block) % chans, 1)
    out_ref[...] = fold(turned[:, : lanes_of(block)], block)


def column_kernel(order, *refs):
    *in_refs, out_ref = refs
    column, _ = column_and_side()
    for apart, ref in zip(order, in_refs):
        out_ref[column ^ apart] = ref[...]


def sides_kernel(own_ref, mate_ref, out_ref):
    _, side = column_and_side()
    out_ref[:, side] = own_ref[...]
    out_ref[:, 1 - side] = mate_ref[...]


def apart_kernel(width, step, out_ref):
    lons = out_ref.shape[0]
    side = lax.axis_index("lon") % 2
    source = lax.broadcasted_iota(jnp.int32, out_ref.shape, 0)
    place = lax.broadcasted_iota(jnp.int32, out_ref.shape, 1)
    within = place % step
    apart = source + (place // step) * width + within + (lons - side * width)
    for _ in range(3):
        apart = jnp.where(apart >= lons, apart - lons, apart)
    out_ref[...] = jnp.where(within < width, apart, -1)


def tables_kernel(width, filter_ref, band_ref, apart_ref, table_ref, first):
    bases, lons = filter_ref.shape
    taps, rows, _ = band_ref.shape
    step, places = first.shape[1:]
    columns = places // (2 * step)
    lat = lax.axis_index("lat")
    below = (lat > 0).astype(F32)
    above = (lat < lax.axis_size("lat") - 1).astype(F32)
    inside = [[below, below, 1.0], [1.0, above, above]]
    slots = [[0, 1, 2], [2, 0, 1]]
    profile = filter_ref[...]
    band = band_ref[...].astype(F32)
    apart = apart_ref[...]
    first[...] = jnp.zeros_like(first)
    for lon in range(width):
        pick = (apart == lon).astype(F32).astype(BF16)
        first[:, lon, :] = jnp.dot(profile, pick, preferred_element_type=F32)
    upper = lax.broadcasted_iota(jnp.int32, (SUBLANES, places), 0) < SUBLANES // 2
    count = columns * width
    for basis in range(bases):
        circle = first[basis]
        turned = [
            pltpu.roll(circle, column * 2 * step, 1) if column else circle
            for column in range(columns)
        ]
        last = [block[SUBLANES:] for block in turned]
        pairs = [
            jnp.where(upper, one, pltpu.roll(other, SUBLANES // 2, 0))
            for one, other in zip(last[::2], last[1::2])
        ]
        turned = jnp.concatenate([block[:SUBLANES] for block in turned] + pairs, axis=0)
        at = basis * count
        for row in range(rows):
            for tap in range(taps):
                weight = band[tap, row : row + 1, basis : basis + 1] * inside[row][tap]
                to = slots[row][tap] * places
                table_ref[row, at : at + count, to : to + places] = (weight * turned).astype(BF16)


def squares_kernel(own_ref, mate_ref, squares_ref, padded):
    bases, group, half = own_ref.shape
    lanes = squares_ref.shape[1]
    _, side = column_and_side()
    first = side == 0
    own = own_ref[...].astype(F32)
    mate = mate_ref[...].astype(F32)
    padded[...] = jnp.zeros_like(padded)
    padded[0, :, :group, :half] = jnp.where(first, own, mate)
    padded[1, :, :group, :half] = jnp.where(first, mate, own)
    members = padded.shape[2]
    into = lax.broadcasted_iota(jnp.int32, (lanes, members), 0)
    member = lax.broadcasted_iota(jnp.int32, (lanes, members), 1)
    repeat = (into % group == member).astype(F32).astype(BF16)
    row = lax.broadcasted_iota(jnp.int32, (lanes, lanes), 0)
    column = lax.broadcasted_iota(jnp.int32, (lanes, lanes), 1)
    same = (row // group == column // group) & (row < 2 * half) & (column < 2 * half)
    for basis in range(bases):
        weights = padded[0, basis] + pltpu.roll(padded[1, basis], half, 1)
        repeated = jnp.dot(repeat, weights.astype(BF16), preferred_element_type=F32)
        squares_ref[basis * lanes : (basis + 1) * lanes] = jnp.where(same, repeated, 0.0).astype(
            BF16
        )


def rows_of(message, block, rest):
    groups = unfold(message.astype(F32), block)
    last = (groups[2], pltpu.roll(groups[2], SUBLANES - rest, 0))
    return [jnp.concatenate([groups[row], last[row]], axis=0).astype(BF16) for row in range(2)]


def unpack_kernel(block, width, own_ref, out_ref):
    for at in range(own_ref.shape[0]):
        for row, read in enumerate(rows_of(own_ref[at], block, width - SUBLANES)):
            out_ref[row, at] = read


def own_kernel(block, width, mate, own, table_ref, part_ref, field):
    rows, columns, step, _ = own.shape
    places = field.shape[1]
    side = lax.axis_index("lon") % 2
    for at in range(columns):
        first = pl.multiple_of((2 * at + side) * step, step)
        other = pl.multiple_of((2 * at + 1 - side) * step, step)
        for row, read in enumerate(rows_of(mate[at], block, width - SUBLANES)):
            field[row, pl.ds(first, step)] = own[row, at]
            field[row, pl.ds(other, step)] = read
    for row in range(rows):
        part_ref[row] = jnp.dot(
            table_ref[row, :, 2 * places :], field[row], preferred_element_type=F32
        )


def conv_kernel(
    block, width, odd_mate, odd_own, even, part_ref, table_ref, squares_ref, *refs
):
    *out_refs, field, spread, stage = refs
    columns = len(out_refs)
    lanes = squares_ref.shape[1]
    bases = squares_ref.shape[0] // lanes
    rows, _, inner = table_ref.shape
    places = inner // 3
    step = places // (2 * columns)
    half = columns * width
    rest = width - SUBLANES
    column, side = column_and_side()
    odd = lax.axis_index("lat") % 2

    def place(row, at, message):
        for slot, read in enumerate(rows_of(message, block, rest)):
            first = pl.multiple_of(slot * places + at * step, step)
            field[row, pl.ds(first, step)] = read

    for at in range(columns):
        place(1 - odd, 2 * at, even[at, 0])
        place(1 - odd, 2 * at + 1, even[at, 1])
        place(odd, 2 * at + side, odd_own[at])
        place(odd, 2 * at + 1 - side, odd_mate[at])
    for row in range(rows):
        over = jnp.dot(
            table_ref[row, :, : 2 * places], field[row], preferred_element_type=F32
        )
        over = (over + part_ref[row]).astype(BF16)
        for basis in range(bases):
            spread[row * half : (row + 1) * half, basis * lanes : (basis + 1) * lanes] = over[
                basis * half : (basis + 1) * half
            ]
    mixed = jnp.dot(spread[...], squares_ref[...], preferred_element_type=F32)
    upper = lax.broadcasted_iota(jnp.int32, (SUBLANES, lanes), 0) < rest
    top, bottom = mixed[:half], mixed[half:]
    for target in range(columns):
        at = target * SUBLANES
        pair = (columns + target // 2) * SUBLANES
        first, second = top[pair : pair + SUBLANES], bottom[pair : pair + SUBLANES]
        if target % 2:
            first = pltpu.roll(first, rest, 0)
        else:
            second = pltpu.roll(second, rest, 0)
        last = jnp.where(upper, first, second)
        points = jnp.concatenate(
            [top[at : at + SUBLANES], bottom[at : at + SUBLANES], last], axis=0
        )
        stage[target] = fold(points, block)
    for apart in range(columns):
        out_refs[apart][...] = stage[column ^ apart]


def summed_block(latent_block, message, block):
    convolved = jnp.concatenate(unfold(message.astype(F32), block), axis=0)
    kept = lax.broadcasted_iota(jnp.int32, convolved.shape, 1) < block
    return jnp.where(kept, latent_block + convolved, 0.0).astype(BF16)


def raised_block(summed, column, block, up_ref):
    count = summed.shape[0]
    ones = jnp.ones((up_to(count, 2 * SUBLANES) - count, block), BF16)
    rows = pl.multiple_of(column * block, block)
    return jnp.dot(
        jnp.concatenate([summed[:, :block], ones], axis=0),
        up_ref[pl.ds(rows, block), :],
        preferred_element_type=F32,
    )


def placed(summed, column, chans, block):
    piece = summed.astype(F32)
    if chans > piece.shape[1]:
        gap = jnp.zeros((piece.shape[0], chans - piece.shape[1]), F32)
        piece = jnp.concatenate([piece, gap], axis=1)
    return pltpu.roll(piece, column * block, 1)


def deviations(summed, mean, block):
    kept = lax.broadcasted_iota(jnp.int32, summed.shape, 1) < block
    return jnp.where(kept, summed.astype(F32) - mean, 0.0)


def over_lanes(values):
    return jnp.sum(values, axis=1, keepdims=True)


def lift_kernel(
    apart,
    own_ref,
    first_ref,
    latent_ref,
    up_ref,
    blocks_ref,
    summed_ref,
    raised_ref,
    stats_ref,
    points,
):
    columns = blocks_ref.shape[0]
    chans = latent_ref.shape[2]
    block = chans // columns
    column, _ = column_and_side()
    group_points(latent_ref, points)
    own = points[...]
    for target in range(columns):
        turned = pltpu.roll(own, chans - target * block, 1) if target else own
        blocks_ref[target] = turned[:, : lanes_of(block)]
    other = column ^ apart
    here = summed_block(blocks_ref[column], own_ref[...], block)
    there = summed_block(blocks_ref[other], first_ref[...], block)
    summed_ref[...] = placed(here, column, chans, block) + placed(there, other, chans, block)
    raised_ref[...] = raised_block(here, column, block, up_ref) + raised_block(
        there, other, block, up_ref
    )
    mean = over_lanes(here.astype(F32) + there.astype(F32)) / (2 * block)
    squares = sum(deviations(summed, mean, block) ** 2 for summed in (here, there))
    stats_ref[0] = jnp.broadcast_to(mean, stats_ref.shape[1:])
    stats_ref[1] = jnp.broadcast_to(over_lanes(squares), stats_ref.shape[1:])


def tail_kernel(order, *refs):
    back_refs = refs[: len(order)]
    blocks_ref, summed_ref, raised_ref, stats_ref, up_ref, down_ref, out_ref = refs[len(order) :]
    width, rows, chans = out_ref.shape
    rest = width - SUBLANES
    block = chans // blocks_ref.shape[0]
    column, _ = column_and_side()
    raised = raised_ref[...]
    early_mean, early_squares = stats_ref[0, :, :1], stats_ref[1, :, :1]
    theirs = []
    away = squares = None
    for apart, ref in zip(order, back_refs):
        other = column ^ apart
        there = summed_block(blocks_ref[other], ref[...], block)
        theirs.append((there, other))
        raised = raised + raised_block(there, other, block, up_ref)
        apart_from = deviations(there, early_mean, block)
        away = apart_from if away is None else away + apart_from
        squares = apart_from**2 if squares is None else squares + apart_from**2
    away, squares = over_lanes(away), over_lanes(squares)
    mean = early_mean + away / chans
    variance = (early_squares + squares - away * away / chans) / chans
    scale = lax.rsqrt(variance + 1e-05)
    count = summed_ref.shape[0]
    hidden = scale * (raised[:count] - mean * raised[count : count + 1])
    hidden = (0.5 * hidden * (1.0 + lax.erf(hidden * 0.5**0.5))).astype(BF16)
    summed = summed_ref[...]
    for there, other in theirs:
        summed = summed + placed(there, other, chans, block)
    result = summed + jnp.dot(hidden, down_ref[...], preferred_element_type=F32)
    for row in range(rows):
        out_ref[:SUBLANES, row, :] = result[row * SUBLANES : (row + 1) * SUBLANES].astype(BF16)
        at = rows * SUBLANES + row * rest
        out_ref[SUBLANES:, row, :] = result[at : at + rest].astype(BF16)


VMEM = pl.BlockSpec(memory_space=pltpu.VMEM)


def call(kernel, name, out_shape, scratch, work, *operands):
    several = isinstance(out_shape, tuple)
    return pl.pallas_call(
        kernel,
        out_shape=out_shape,
        in_specs=[VMEM] * len(operands),
        out_specs=(VMEM,) * len(out_shape) if several else VMEM,
        scratch_shapes=scratch,
        compiler_params=pltpu.CompilerParams(vmem_limit_bytes=24 * 2**20),
        cost_estimate=pl.CostEstimate(flops=work, bytes_accessed=10**6, transcendentals=0),
        name=name,
    )(*operands)


def over_columns(message, count, apart):
    pairs = [(i, ((i // 2) ^ apart) * 2 + i % 2) for i in range(count)]
    return lax.ppermute(message, "lon", pairs) if apart else message


def over_sides(block, count):
    return lax.ppermute(block, "lon", [(i, i ^ 1) for i in range(count)])


def swap(block, count, partner):
    pairs = []
    for lat in range(lax.axis_size("lat")):
        for lon in range(count):
            to_lat, to_lon = partner(lat, lon)
            pairs.append((lat * count + lon, to_lat * count + to_lon))
    return lax.ppermute(block, ("lat", "lon"), pairs)


def odd_pair(lat, lon, to_lon, rows):
    to = lat + 1 if lat % 2 else lat - 1
    return (to, to_lon) if 0 <= to < rows else (lat, lon ^ 1)


def local(latent, lon_filter, mix_weight, band_weight, offsets, w_up, w_down):
    rows, width, chans = latent.shape
    bases, lons = lon_filter.shape
    half, group = mix_weight.shape[1:]
    taps = band_weight.shape[2]
    count = lons // width
    columns = count // 2
    block = 2 * half
    step = up_to(width, 2 * SUBLANES)
    places = count * step
    lanes = lanes_of(block)
    height = message_rows(block)
    assert rows == 2 and taps == 3 and columns & (columns - 1) == 0
    assert lax.axis_size("lat") % 2 == 0
    assert 2 * width == 3 * SUBLANES and columns * width % (2 * SUBLANES) == 0
    assert 3 * (block % LANES) <= LANES

    far_first = tuple(reversed(range(columns)))
    inward = far_first
    if columns > 3:
        inward = (far_first[1], far_first[0]) + far_first[2:]
    message = jax.ShapeDtypeStruct((height, LANES), BF16)
    messages = (message,) * columns
    stage = pltpu.VMEM((columns, height, LANES), BF16)
    points = pltpu.VMEM((3 * SUBLANES, chans), F32)
    lon_first = jnp.transpose(latent, (1, 0, 2))
    mix_own = jnp.transpose(mix_weight, (0, 2, 1))

    raw = over_columns(lon_first, count, inward[0])
    apart = call(
        functools.partial(apart_kernel, width, step),
        "apart",
        jax.ShapeDtypeStruct((lons, places), jnp.int32),
        [],
        10**9,
    )
    loaded, apart = lax.optimization_barrier((lon_first, apart))
    packed = call(
        functools.partial(pack_kernel, inward[1:]),
        "pack",
        (message,) * (columns - 1),
        [points, stage],
        10**9,
        loaded,
    )
    arrived = [call(cut_kernel, "cut", message, [points], 5 * 10**9, raw)]
    arrived += [over_columns(*pair) for pair in zip(packed, [count] * columns, inward[1:])]
    mix_mate = over_sides(mix_own, count)
    table = call(
        functools.partial(tables_kernel, width),
        "tables",
        jax.ShapeDtypeStruct((rows, bases * columns * width, taps * places), BF16),
        [pltpu.VMEM((bases, step, places), F32)],
        10**6,
        lon_filter,
        jnp.transpose(band_weight, (2, 1, 0)),
        apart,
    )
    gathered = jax.ShapeDtypeStruct((columns, height, LANES), BF16)
    own_side = call(
        functools.partial(column_kernel, inward),
        "join_columns",
        gathered,
        [],
        10**8,
        *arrived,
    )
    lats = lax.axis_size("lat")
    mate_side = swap(own_side, count, lambda lat, lon: (lat, lon ^ 1))
    odd_mate = swap(own_side, count, lambda lat, lon: odd_pair(lat, lon, lon ^ 1, lats))
    odd_own = swap(own_side, count, lambda lat, lon: odd_pair(lat, lon, lon, lats))
    own_rows = call(
        functools.partial(unpack_kernel, block, width),
        "unpack",
        jax.ShapeDtypeStruct((rows, columns, step, lanes), BF16),
        [],
        10**9,
        own_side,
    )
    circle = jax.ShapeDtypeStruct((columns, 2, height, LANES), BF16)
    home = call(sides_kernel, "join_sides", circle, [], 10**8, own_side, mate_side)
    even = swap(home, count, lambda lat, lon: (lat ^ 1, lon))
    mix_mate, _ = lax.optimization_barrier((mix_mate, home))
    squares = call(
        squares_kernel,
        "squares",
        jax.ShapeDtypeStruct((bases * lanes, lanes), BF16),
        [pltpu.VMEM((2, bases, up_to(group, 2 * SUBLANES), lanes), F32)],
        10**9,
        mix_own,
        mix_mate,
    )
    part = call(
        functools.partial(own_kernel, block, width),
        "conv_own",
        jax.ShapeDtypeStruct((rows, bases * columns * width, lanes), F32),
        [pltpu.VMEM((rows, places, lanes), BF16)],
        10**9,
        mate_side,
        own_rows,
        table,
    )
    mixed = call(
        functools.partial(conv_kernel, block, width),
        "conv",
        messages,
        [
            pltpu.VMEM((rows, 2 * places, lanes), BF16),
            pltpu.VMEM((rows * columns * width, bases * lanes), BF16),
            pltpu.VMEM((columns, height, LANES), BF16),
        ],
        10**10,
        odd_mate,
        odd_own,
        even,
        part,
        table,
        squares,
    )
    outward = far_first[1:-1] + far_first[:1]
    back = [over_columns(mixed[apart], count, apart) for apart in outward]
    first = outward.index(far_first[0])
    lifted = call(
        functools.partial(lift_kernel, far_first[0]),
        "lift",
        (
            jax.ShapeDtypeStruct((columns, 3 * SUBLANES, lanes), F32),
            jax.ShapeDtypeStruct((3 * SUBLANES, chans), F32),
            jax.ShapeDtypeStruct((up_to(3 * SUBLANES, 2 * SUBLANES), w_up.shape[1]), F32),
            jax.ShapeDtypeStruct((2, 3 * SUBLANES, LANES), F32),
        ),
        [points],
        10**8,
        mixed[0],
        back[first],
        lon_first,
        w_up,
    )
    result = call(
        functools.partial(tail_kernel, outward[:first] + outward[first + 1 :]),
        "tail",
        jax.ShapeDtypeStruct(lon_first.shape, BF16),
        [],
        10**9,
        *back[:first],
        *back[first + 1 :],
        *lifted,
        w_up,
        w_down,
    )
    return jnp.transpose(result, (1, 0, 2))


def solution(mesh):
    return jax.shard_map(
        local,
        mesh=mesh,
        in_specs=(
            P("lat", "lon", None),
            P(),
            P(None, "lon", None),
            P(None, "lat", None),
            P("lat"),
            P(),
            P(),
        ),
        out_specs=P("lat", "lon", None),
        check_vma=False,
    )
```

```python
import functools

import jax
import jax.numpy as jnp
from jax import lax
from jax.experimental import pallas as pl
from jax.experimental.pallas import tpu as pltpu
from jax.sharding import PartitionSpec as P

F32 = jnp.float32
BF16 = jnp.bfloat16
LANES = 128
SUBLANES = 8


def up_to(size, step):
    return -(-size // step) * step


def column_and_side():
    place = lax.axis_index("lon")
    return place // 2, place % 2


def message_rows(block):
    tiles = block // LANES
    return up_to(3 * SUBLANES * tiles + (SUBLANES if block % LANES else 0), 2 * SUBLANES)


def lanes_of(block):
    return up_to(block, LANES)


def fold(points, block):
    whole, rest = divmod(block, LANES)
    parts = [points[:, tile * LANES : (tile + 1) * LANES] for tile in range(whole)]
    if rest:
        odd = points[:, whole * LANES : (whole + 1) * LANES]
        kept = lax.broadcasted_iota(jnp.int32, (SUBLANES, LANES), 1) < rest
        shared = None
        for third in range(3):
            piece = jnp.where(kept, odd[third * SUBLANES : (third + 1) * SUBLANES], 0.0)
            piece = pltpu.roll(piece, third * rest, 1) if third else piece
            shared = piece if shared is None else shared + piece
        parts.append(shared)
    filled = sum(part.shape[0] for part in parts)
    if message_rows(block) > filled:
        parts.append(jnp.zeros((message_rows(block) - filled, LANES), F32))
    return jnp.concatenate(parts, axis=0).astype(BF16)


def unfold(message, block):
    whole, rest = divmod(block, LANES)
    groups = []
    for third in range(3):
        first = third * SUBLANES
        parts = [
            message[tile * 3 * SUBLANES + first : tile * 3 * SUBLANES + first + SUBLANES]
            for tile in range(whole)
        ]
        if rest:
            odd = message[whole * 3 * SUBLANES : whole * 3 * SUBLANES + SUBLANES]
            parts.append(pltpu.roll(odd, LANES - third * rest, 1) if third else odd)
        groups.append(jnp.concatenate(parts, axis=1) if len(parts) > 1 else parts[0])
    return groups


def group_points(latent_ref, points):
    width, rows, _ = latent_ref.shape
    rest = width - SUBLANES
    for row in range(rows):
        points[row * SUBLANES : (row + 1) * SUBLANES] = latent_ref[:SUBLANES, row, :].astype(F32)
        at = rows * SUBLANES + row * rest
        points[at : at + rest] = latent_ref[SUBLANES:, row, :].astype(F32)


def pack_kernel(order, latent_ref, *refs):
    *out_refs, points, stage = refs
    columns = stage.shape[0]
    chans = latent_ref.shape[2]
    block = chans // columns
    column, _ = column_and_side()
    group_points(latent_ref, points)
    own = points[...]
    for target in range(columns):
        turned = pltpu.roll(own, chans - target * block, 1) if target else own
        stage[target] = fold(turned[:, : lanes_of(block)], block)
    for apart, ref in zip(order, out_refs):
        ref[...] = stage[column ^ apart]


def cut_kernel(raw_ref, out_ref, points):
    chans = raw_ref.shape[2]
    block = chans // (lax.axis_size("lon") // 2)
    column, _ = column_and_side()
    group_points(raw_ref, points)
    turned = pltpu.roll(points[...], (chans - column * block) % chans, 1)
    out_ref[...] = fold(turned[:, : lanes_of(block)], block)


def column_kernel(order, *refs):
    *in_refs, out_ref = refs
    column, _ = column_and_side()
    for apart, ref in zip(order, in_refs):
        out_ref[column ^ apart] = ref[...]


def apart_kernel(width, step, out_ref):
    lons = out_ref.shape[0]
    side = lax.axis_index("lon") % 2
    source = lax.broadcasted_iota(jnp.int32, out_ref.shape, 0)
    place = lax.broadcasted_iota(jnp.int32, out_ref.shape, 1)
    within = place % step
    apart = source + (place // step) * width + within + (lons - side * width)
    for _ in range(3):
        apart = jnp.where(apart >= lons, apart - lons, apart)
    out_ref[...] = jnp.where(within < width, apart, -1)


def tables_kernel(width, filter_ref, band_ref, apart_ref, table_ref, first):
    bases, lons = filter_ref.shape
    taps, rows, _ = band_ref.shape
    step, places = first.shape[1:]
    columns = places // (2 * step)
    lat = lax.axis_index("lat")
    below = (lat > 0).astype(F32)
    above = (lat < lax.axis_size("lat") - 1).astype(F32)
    inside = [[below, below, 1.0], [1.0, above, above]]
    slots = [[0, 1, 2], [2, 0, 1]]
    profile = filter_ref[...]
    band = band_ref[...].astype(F32)
    apart = apart_ref[...]
    first[...] = jnp.zeros_like(first)
    for lon in range(width):
        pick = (apart == lon).astype(F32).astype(BF16)
        first[:, lon, :] = jnp.dot(profile, pick, preferred_element_type=F32)
    upper = lax.broadcasted_iota(jnp.int32, (SUBLANES, places), 0) < SUBLANES // 2
    count = columns * width
    for basis in range(bases):
        circle = first[basis]
        turned = [
            pltpu.roll(circle, column * 2 * step, 1) if column else circle
            for column in range(columns)
        ]
        last = [block[SUBLANES:] for block in turned]
        pairs = [
            jnp.where(upper, one, pltpu.roll(other, SUBLANES // 2, 0))
            for one, other in zip(last[::2], last[1::2])
        ]
        turned = jnp.concatenate([block[:SUBLANES] for block in turned] + pairs, axis=0)
        at = basis * count
        for row in range(rows):
            for tap in range(taps):
                weight = band[tap, row : row + 1, basis : basis + 1] * inside[row][tap]
                to = slots[row][tap] * places
                table_ref[row, at : at + count, to : to + places] = (weight * turned).astype(BF16)


def squares_kernel(own_ref, mate_ref, squares_ref, padded):
    bases, group, half = own_ref.shape
    lanes = squares_ref.shape[1]
    _, side = column_and_side()
    first = side == 0
    own = own_ref[...].astype(F32)
    mate = mate_ref[...].astype(F32)
    padded[...] = jnp.zeros_like(padded)
    padded[0, :, :group, :half] = jnp.where(first, own, mate)
    padded[1, :, :group, :half] = jnp.where(first, mate, own)
    members = padded.shape[2]
    into = lax.broadcasted_iota(jnp.int32, (lanes, members), 0)
    member = lax.broadcasted_iota(jnp.int32, (lanes, members), 1)
    repeat = (into % group == member).astype(F32).astype(BF16)
    row = lax.broadcasted_iota(jnp.int32, (lanes, lanes), 0)
    column = lax.broadcasted_iota(jnp.int32, (lanes, lanes), 1)
    same = (row // group == column // group) & (row < 2 * half) & (column < 2 * half)
    for basis in range(bases):
        weights = padded[0, basis] + pltpu.roll(padded[1, basis], half, 1)
        repeated = jnp.dot(repeat, weights.astype(BF16), preferred_element_type=F32)
        squares_ref[basis * lanes : (basis + 1) * lanes] = jnp.where(same, repeated, 0.0).astype(
            BF16
        )


def rows_of(message, block, rest):
    groups = unfold(message.astype(F32), block)
    last = (groups[2], pltpu.roll(groups[2], SUBLANES - rest, 0))
    return [jnp.concatenate([groups[row], last[row]], axis=0).astype(BF16) for row in range(2)]


def unpack_kernel(block, width, own_ref, out_ref):
    for at in range(own_ref.shape[0]):
        for row, read in enumerate(rows_of(own_ref[at], block, width - SUBLANES)):
            out_ref[row, at] = read


def own_kernel(block, width, mate, own, table_ref, part_ref, field):
    rows, columns, step, _ = own.shape
    places = field.shape[1]
    side = lax.axis_index("lon") % 2
    for at in range(columns):
        first = pl.multiple_of((2 * at + side) * step, step)
        other = pl.multiple_of((2 * at + 1 - side) * step, step)
        for row, read in enumerate(rows_of(mate[at], block, width - SUBLANES)):
            field[row, pl.ds(first, step)] = own[row, at]
            field[row, pl.ds(other, step)] = read
    for row in range(rows):
        part_ref[row] = jnp.dot(
            table_ref[row, :, 2 * places :], field[row], preferred_element_type=F32
        )


def conv_kernel(
    block,
    width,
    odd_mate,
    odd_own,
    even_own,
    even_mate,
    part_ref,
    table_ref,
    squares_ref,
    *refs,
):
    *out_refs, field, spread, stage = refs
    columns = len(out_refs)
    lanes = squares_ref.shape[1]
    bases = squares_ref.shape[0] // lanes
    rows, _, inner = table_ref.shape
    places = inner // 3
    step = places // (2 * columns)
    half = columns * width
    rest = width - SUBLANES
    column, side = column_and_side()
    odd = lax.axis_index("lat") % 2

    def place(row, at, message):
        for slot, read in enumerate(rows_of(message, block, rest)):
            first = pl.multiple_of(slot * places + at * step, step)
            field[row, pl.ds(first, step)] = read

    for at in range(columns):
        place(1 - odd, 2 * at + side, even_own[at])
        place(1 - odd, 2 * at + 1 - side, even_mate[at])
        place(odd, 2 * at + side, odd_own[at])
        place(odd, 2 * at + 1 - side, odd_mate[at])
    for row in range(rows):
        over = jnp.dot(
            table_ref[row, :, : 2 * places], field[row], preferred_element_type=F32
        )
        over = (over + part_ref[row]).astype(BF16)
        for basis in range(bases):
            spread[row * half : (row + 1) * half, basis * lanes : (basis + 1) * lanes] = over[
                basis * half : (basis + 1) * half
            ]
    mixed = jnp.dot(spread[...], squares_ref[...], preferred_element_type=F32)
    upper = lax.broadcasted_iota(jnp.int32, (SUBLANES, lanes), 0) < rest
    top, bottom = mixed[:half], mixed[half:]
    for target in range(columns):
        at = target * SUBLANES
        pair = (columns + target // 2) * SUBLANES
        first, second = top[pair : pair + SUBLANES], bottom[pair : pair + SUBLANES]
        if target % 2:
            first = pltpu.roll(first, rest, 0)
        else:
            second = pltpu.roll(second, rest, 0)
        last = jnp.where(upper, first, second)
        points = jnp.concatenate(
            [top[at : at + SUBLANES], bottom[at : at + SUBLANES], last], axis=0
        )
        stage[target] = fold(points, block)
    for apart in range(columns):
        out_refs[apart][...] = stage[column ^ apart]


def summed_block(latent_block, message, block):
    convolved = jnp.concatenate(unfold(message.astype(F32), block), axis=0)
    kept = lax.broadcasted_iota(jnp.int32, convolved.shape, 1) < block
    return jnp.where(kept, latent_block + convolved, 0.0).astype(BF16)


def raised_block(summed, column, block, up_ref):
    count = summed.shape[0]
    ones = jnp.ones((up_to(count, 2 * SUBLANES) - count, block), BF16)
    rows = pl.multiple_of(column * block, block)
    return jnp.dot(
        jnp.concatenate([summed[:, :block], ones], axis=0),
        up_ref[pl.ds(rows, block), :],
        preferred_element_type=F32,
    )


def placed(summed, column, chans, block):
    piece = summed.astype(F32)
    if chans > piece.shape[1]:
        gap = jnp.zeros((piece.shape[0], chans - piece.shape[1]), F32)
        piece = jnp.concatenate([piece, gap], axis=1)
    return pltpu.roll(piece, column * block, 1)


def deviations(summed, mean, block):
    kept = lax.broadcasted_iota(jnp.int32, summed.shape, 1) < block
    return jnp.where(kept, summed.astype(F32) - mean, 0.0)


def over_lanes(values):
    return jnp.sum(values, axis=1, keepdims=True)


def lift_kernel(
    apart,
    own_ref,
    first_ref,
    latent_ref,
    up_ref,
    blocks_ref,
    summed_ref,
    raised_ref,
    stats_ref,
    points,
):
    columns = blocks_ref.shape[0]
    chans = latent_ref.shape[2]
    block = chans // columns
    column, _ = column_and_side()
    group_points(latent_ref, points)
    own = points[...]
    for target in range(columns):
        turned = pltpu.roll(own, chans - target * block, 1) if target else own
        blocks_ref[target] = turned[:, : lanes_of(block)]
    other = column ^ apart
    here = summed_block(blocks_ref[column], own_ref[...], block)
    there = summed_block(blocks_ref[other], first_ref[...], block)
    summed_ref[...] = placed(here, column, chans, block) + placed(there, other, chans, block)
    raised_ref[...] = raised_block(here, column, block, up_ref) + raised_block(
        there, other, block, up_ref
    )
    mean = over_lanes(here.astype(F32) + there.astype(F32)) / (2 * block)
    squares = sum(deviations(summed, mean, block) ** 2 for summed in (here, there))
    stats_ref[0] = jnp.broadcast_to(mean, stats_ref.shape[1:])
    stats_ref[1] = jnp.broadcast_to(over_lanes(squares), stats_ref.shape[1:])


def tail_kernel(order, *refs):
    back_refs = refs[: len(order)]
    blocks_ref, summed_ref, raised_ref, stats_ref, up_ref, down_ref, out_ref = refs[len(order) :]
    width, rows, chans = out_ref.shape
    rest = width - SUBLANES
    block = chans // blocks_ref.shape[0]
    column, _ = column_and_side()
    raised = raised_ref[...]
    early_mean, early_squares = stats_ref[0, :, :1], stats_ref[1, :, :1]
    theirs = []
    away = squares = None
    for apart, ref in zip(order, back_refs):
        other = column ^ apart
        there = summed_block(blocks_ref[other], ref[...], block)
        theirs.append((there, other))
        raised = raised + raised_block(there, other, block, up_ref)
        apart_from = deviations(there, early_mean, block)
        away = apart_from if away is None else away + apart_from
        squares = apart_from**2 if squares is None else squares + apart_from**2
    away, squares = over_lanes(away), over_lanes(squares)
    mean = early_mean + away / chans
    variance = (early_squares + squares - away * away / chans) / chans
    scale = lax.rsqrt(variance + 1e-05)
    count = summed_ref.shape[0]
    hidden = scale * (raised[:count] - mean * raised[count : count + 1])
    hidden = (0.5 * hidden * (1.0 + lax.erf(hidden * 0.5**0.5))).astype(BF16)
    summed = summed_ref[...]
    for there, other in theirs:
        summed = summed + placed(there, other, chans, block)
    result = summed + jnp.dot(hidden, down_ref[...], preferred_element_type=F32)
    for row in range(rows):
        out_ref[:SUBLANES, row, :] = result[row * SUBLANES : (row + 1) * SUBLANES].astype(BF16)
        at = rows * SUBLANES + row * rest
        out_ref[SUBLANES:, row, :] = result[at : at + rest].astype(BF16)


VMEM = pl.BlockSpec(memory_space=pltpu.VMEM)


def call(kernel, name, out_shape, scratch, work, *operands):
    several = isinstance(out_shape, tuple)
    return pl.pallas_call(
        kernel,
        out_shape=out_shape,
        in_specs=[VMEM] * len(operands),
        out_specs=(VMEM,) * len(out_shape) if several else VMEM,
        scratch_shapes=scratch,
        compiler_params=pltpu.CompilerParams(vmem_limit_bytes=24 * 2**20),
        cost_estimate=pl.CostEstimate(flops=work, bytes_accessed=10**6, transcendentals=0),
        name=name,
    )(*operands)


def over_columns(message, count, apart):
    pairs = [(i, ((i // 2) ^ apart) * 2 + i % 2) for i in range(count)]
    return lax.ppermute(message, "lon", pairs) if apart else message


def over_sides(block, count):
    return lax.ppermute(block, "lon", [(i, i ^ 1) for i in range(count)])


def swap(block, count, partner):
    pairs = []
    for lat in range(lax.axis_size("lat")):
        for lon in range(count):
            to_lat, to_lon = partner(lat, lon)
            pairs.append((lat * count + lon, to_lat * count + to_lon))
    return lax.ppermute(block, ("lat", "lon"), pairs)


def odd_pair(lat, lon, to_lon, rows):
    to = lat + 1 if lat % 2 else lat - 1
    return (to, to_lon) if 0 <= to < rows else (lat, lon ^ 1)


def local(latent, lon_filter, mix_weight, band_weight, offsets, w_up, w_down):
    rows, width, chans = latent.shape
    bases, lons = lon_filter.shape
    half, group = mix_weight.shape[1:]
    taps = band_weight.shape[2]
    count = lons // width
    columns = count // 2
    block = 2 * half
    step = up_to(width, 2 * SUBLANES)
    places = count * step
    lanes = lanes_of(block)
    height = message_rows(block)
    assert rows == 2 and taps == 3 and columns & (columns - 1) == 0
    assert lax.axis_size("lat") % 2 == 0
    assert 2 * width == 3 * SUBLANES and columns * width % (2 * SUBLANES) == 0
    assert 3 * (block % LANES) <= LANES

    far_first = tuple(reversed(range(columns)))
    inward = far_first
    if columns > 3:
        inward = (far_first[1], far_first[0]) + far_first[2:]
    message = jax.ShapeDtypeStruct((height, LANES), BF16)
    messages = (message,) * columns
    stage = pltpu.VMEM((columns, height, LANES), BF16)
    points = pltpu.VMEM((3 * SUBLANES, chans), F32)
    lon_first = jnp.transpose(latent, (1, 0, 2))
    mix_own = jnp.transpose(mix_weight, (0, 2, 1))

    raw = over_columns(lon_first, count, inward[0])
    apart = call(
        functools.partial(apart_kernel, width, step),
        "apart",
        jax.ShapeDtypeStruct((lons, places), jnp.int32),
        [],
        10**9,
    )
    loaded, apart = lax.optimization_barrier((lon_first, apart))
    packed = call(
        functools.partial(pack_kernel, inward[1:]),
        "pack",
        (message,) * (columns - 1),
        [points, stage],
        10**9,
        loaded,
    )
    arrived = [call(cut_kernel, "cut", message, [points], 5 * 10**9, raw)]
    arrived += [over_columns(*pair) for pair in zip(packed, [count] * columns, inward[1:])]
    mix_mate = over_sides(mix_own, count)
    table = call(
        functools.partial(tables_kernel, width),
        "tables",
        jax.ShapeDtypeStruct((rows, bases * columns * width, taps * places), BF16),
        [pltpu.VMEM((bases, step, places), F32)],
        10**6,
        lon_filter,
        jnp.transpose(band_weight, (2, 1, 0)),
        apart,
    )
    gathered = jax.ShapeDtypeStruct((columns, height, LANES), BF16)
    own_side = call(
        functools.partial(column_kernel, inward),
        "join_columns",
        gathered,
        [],
        10**8,
        *arrived,
    )
    lats = lax.axis_size("lat")
    mate_side = swap(own_side, count, lambda lat, lon: (lat, lon ^ 1))
    odd_mate = swap(own_side, count, lambda lat, lon: odd_pair(lat, lon, lon ^ 1, lats))
    odd_own = swap(own_side, count, lambda lat, lon: odd_pair(lat, lon, lon, lats))
    own_rows = call(
        functools.partial(unpack_kernel, block, width),
        "unpack",
        jax.ShapeDtypeStruct((rows, columns, step, lanes), BF16),
        [],
        10**9,
        own_side,
    )
    even_own = swap(own_side, count, lambda lat, lon: (lat ^ 1, lon))
    even_mate = swap(mate_side, count, lambda lat, lon: (lat ^ 1, lon))
    mix_mate, _ = lax.optimization_barrier((mix_mate, mate_side))
    squares = call(
        squares_kernel,
        "squares",
        jax.ShapeDtypeStruct((bases * lanes, lanes), BF16),
        [pltpu.VMEM((2, bases, up_to(group, 2 * SUBLANES), lanes), F32)],
        3 * 10**8,
        mix_own,
        mix_mate,
    )
    part = call(
        functools.partial(own_kernel, block, width),
        "conv_own",
        jax.ShapeDtypeStruct((rows, bases * columns * width, lanes), F32),
        [pltpu.VMEM((rows, places, lanes), BF16)],
        3 * 10**8,
        mate_side,
        own_rows,
        table,
    )
    mixed = call(
        functools.partial(conv_kernel, block, width),
        "conv",
        messages,
        [
            pltpu.VMEM((rows, 2 * places, lanes), BF16),
            pltpu.VMEM((rows * columns * width, bases * lanes), BF16),
            pltpu.VMEM((columns, height, LANES), BF16),
        ],
        10**10,
        odd_mate,
        odd_own,
        even_own,
        even_mate,
        part,
        table,
        squares,
    )
    outward = tuple(reversed(far_first[:-1]))
    back = [over_columns(mixed[apart], count, apart) for apart in outward]
    first = outward.index(far_first[0])
    lifted = call(
        functools.partial(lift_kernel, far_first[0]),
        "lift",
        (
            jax.ShapeDtypeStruct((columns, 3 * SUBLANES, lanes), F32),
            jax.ShapeDtypeStruct((3 * SUBLANES, chans), F32),
            jax.ShapeDtypeStruct((up_to(3 * SUBLANES, 2 * SUBLANES), w_up.shape[1]), F32),
            jax.ShapeDtypeStruct((2, 3 * SUBLANES, LANES), F32),
        ),
        [points],
        10**8,
        mixed[0],
        back[first],
        lon_first,
        w_up,
    )
    result = call(
        functools.partial(tail_kernel, outward[:first] + outward[first + 1 :]),
        "tail",
        jax.ShapeDtypeStruct(lon_first.shape, BF16),
        [],
        10**9,
        *back[:first],
        *back[first + 1 :],
        *lifted,
        w_up,
        w_down,
    )
    return jnp.transpose(result, (1, 0, 2))


def solution(mesh):
    return jax.shard_map(
        local,
        mesh=mesh,
        in_specs=(
            P("lat", "lon", None),
            P(),
            P(None, "lon", None),
            P(None, "lat", None),
            P("lat"),
            P(),
            P(),
        ),
        out_specs=P("lat", "lon", None),
        check_vma=False,
    )
```

```python
import functools

import jax
import jax.numpy as jnp
from jax import lax
from jax.experimental import pallas as pl
from jax.experimental.pallas import tpu as pltpu
from jax.sharding import PartitionSpec as P

F32 = jnp.float32
BF16 = jnp.bfloat16
LANES = 128
SUBLANES = 8


def up_to(size, step):
    return -(-size // step) * step


def column_and_side():
    place = lax.axis_index("lon")
    return place // 2, place % 2


def message_rows(block):
    tiles = block // LANES
    return up_to(3 * SUBLANES * tiles + (SUBLANES if block % LANES else 0), 2 * SUBLANES)


def lanes_of(block):
    return up_to(block, LANES)


def fold(points, block):
    whole, rest = divmod(block, LANES)
    parts = [points[:, tile * LANES : (tile + 1) * LANES] for tile in range(whole)]
    if rest:
        odd = points[:, whole * LANES : (whole + 1) * LANES]
        kept = lax.broadcasted_iota(jnp.int32, (SUBLANES, LANES), 1) < rest
        shared = None
        for third in range(3):
            piece = jnp.where(kept, odd[third * SUBLANES : (third + 1) * SUBLANES], 0.0)
            piece = pltpu.roll(piece, third * rest, 1) if third else piece
            shared = piece if shared is None else shared + piece
        parts.append(shared)
    filled = sum(part.shape[0] for part in parts)
    if message_rows(block) > filled:
        parts.append(jnp.zeros((message_rows(block) - filled, LANES), F32))
    return jnp.concatenate(parts, axis=0).astype(BF16)


def unfold(message, block):
    whole, rest = divmod(block, LANES)
    groups = []
    for third in range(3):
        first = third * SUBLANES
        parts = [
            message[tile * 3 * SUBLANES + first : tile * 3 * SUBLANES + first + SUBLANES]
            for tile in range(whole)
        ]
        if rest:
            odd = message[whole * 3 * SUBLANES : whole * 3 * SUBLANES + SUBLANES]
            parts.append(pltpu.roll(odd, LANES - third * rest, 1) if third else odd)
        groups.append(jnp.concatenate(parts, axis=1) if len(parts) > 1 else parts[0])
    return groups


def group_points(latent_ref, points):
    width, rows, _ = latent_ref.shape
    rest = width - SUBLANES
    for row in range(rows):
        points[row * SUBLANES : (row + 1) * SUBLANES] = latent_ref[:SUBLANES, row, :].astype(F32)
        at = rows * SUBLANES + row * rest
        points[at : at + rest] = latent_ref[SUBLANES:, row, :].astype(F32)


def pack_kernel(order, latent_ref, *refs):
    *out_refs, points, stage = refs
    columns = stage.shape[0]
    chans = latent_ref.shape[2]
    block = chans // columns
    column, _ = column_and_side()
    group_points(latent_ref, points)
    own = points[...]
    for target in range(columns):
        turned = pltpu.roll(own, chans - target * block, 1) if target else own
        stage[target] = fold(turned[:, : lanes_of(block)], block)
    for apart, ref in zip(order, out_refs):
        ref[...] = stage[column ^ apart]


def cut_kernel(raw_ref, out_ref, points):
    chans = raw_ref.shape[2]
    block = chans // (lax.axis_size("lon") // 2)
    column, _ = column_and_side()
    group_points(raw_ref, points)
    turned = pltpu.roll(points[...], (chans - column * block) % chans, 1)
    out_ref[...] = fold(turned[:, : lanes_of(block)], block)


def column_kernel(order, *refs):
    *in_refs, out_ref = refs
    column, _ = column_and_side()
    for apart, ref in zip(order, in_refs):
        out_ref[column ^ apart] = ref[...]


def apart_kernel(width, step, out_ref):
    lons = out_ref.shape[0]
    side = lax.axis_index("lon") % 2
    source = lax.broadcasted_iota(jnp.int32, out_ref.shape, 0)
    place = lax.broadcasted_iota(jnp.int32, out_ref.shape, 1)
    within = place % step
    apart = source + (place // step) * width + within + (lons - side * width)
    for _ in range(3):
        apart = jnp.where(apart >= lons, apart - lons, apart)
    out_ref[...] = jnp.where(within < width, apart, -1)


def tables_kernel(width, filter_ref, band_ref, apart_ref, table_ref, first):
    bases, lons = filter_ref.shape
    taps, rows, _ = band_ref.shape
    step, places = first.shape[1:]
    columns = places // (2 * step)
    lat = lax.axis_index("lat")
    below = (lat > 0).astype(F32)
    above = (lat < lax.axis_size("lat") - 1).astype(F32)
    inside = [[below, below, 1.0], [1.0, above, above]]
    slots = [[0, 1, 2], [2, 0, 1]]
    profile = filter_ref[...]
    band = band_ref[...].astype(F32)
    apart = apart_ref[...]
    first[...] = jnp.zeros_like(first)
    for lon in range(width):
        pick = (apart == lon).astype(F32).astype(BF16)
        first[:, lon, :] = jnp.dot(profile, pick, preferred_element_type=F32)
    upper = lax.broadcasted_iota(jnp.int32, (SUBLANES, places), 0) < SUBLANES // 2
    count = columns * width
    for basis in range(bases):
        circle = first[basis]
        turned = [
            pltpu.roll(circle, column * 2 * step, 1) if column else circle
            for column in range(columns)
        ]
        last = [block[SUBLANES:] for block in turned]
        pairs = [
            jnp.where(upper, one, pltpu.roll(other, SUBLANES // 2, 0))
            for one, other in zip(last[::2], last[1::2])
        ]
        turned = jnp.concatenate([block[:SUBLANES] for block in turned] + pairs, axis=0)
        at = basis * count
        for row in range(rows):
            for tap in range(taps):
                weight = band[tap, row : row + 1, basis : basis + 1] * inside[row][tap]
                to = slots[row][tap] * places
                table_ref[row, at : at + count, to : to + places] = (weight * turned).astype(BF16)


def squares_kernel(own_ref, mate_ref, squares_ref, padded):
    bases, group, half = own_ref.shape
    lanes = squares_ref.shape[1]
    _, side = column_and_side()
    first = side == 0
    own = own_ref[...].astype(F32)
    mate = mate_ref[...].astype(F32)
    padded[...] = jnp.zeros_like(padded)
    padded[0, :, :group, :half] = jnp.where(first, own, mate)
    padded[1, :, :group, :half] = jnp.where(first, mate, own)
    members = padded.shape[2]
    into = lax.broadcasted_iota(jnp.int32, (lanes, members), 0)
    member = lax.broadcasted_iota(jnp.int32, (lanes, members), 1)
    repeat = (into % group == member).astype(F32).astype(BF16)
    row = lax.broadcasted_iota(jnp.int32, (lanes, lanes), 0)
    column = lax.broadcasted_iota(jnp.int32, (lanes, lanes), 1)
    same = (row // group == column // group) & (row < 2 * half) & (column < 2 * half)
    for basis in range(bases):
        weights = padded[0, basis] + pltpu.roll(padded[1, basis], half, 1)
        repeated = jnp.dot(repeat, weights.astype(BF16), preferred_element_type=F32)
        squares_ref[basis * lanes : (basis + 1) * lanes] = jnp.where(same, repeated, 0.0).astype(
            BF16
        )


def rows_of(message, block, rest):
    groups = unfold(message.astype(F32), block)
    last = (groups[2], pltpu.roll(groups[2], SUBLANES - rest, 0))
    return [jnp.concatenate([groups[row], last[row]], axis=0).astype(BF16) for row in range(2)]


def unpack_kernel(block, width, own_ref, out_ref):
    for at in range(own_ref.shape[0]):
        for row, read in enumerate(rows_of(own_ref[at], block, width - SUBLANES)):
            out_ref[row, at] = read


def own_kernel(block, width, mate, own, table_ref, part_ref, field):
    rows, columns, step, _ = own.shape
    places = field.shape[1]
    side = lax.axis_index("lon") % 2
    for at in range(columns):
        first = pl.multiple_of((2 * at + side) * step, step)
        other = pl.multiple_of((2 * at + 1 - side) * step, step)
        for row, read in enumerate(rows_of(mate[at], block, width - SUBLANES)):
            field[row, pl.ds(first, step)] = own[row, at]
            field[row, pl.ds(other, step)] = read
    for row in range(rows):
        part_ref[row] = jnp.dot(
            table_ref[row, :, 2 * places :], field[row], preferred_element_type=F32
        )


def conv_kernel(
    block,
    width,
    odd_mate,
    odd_own,
    even_own,
    even_mate,
    part_ref,
    table_ref,
    squares_ref,
    *refs,
):
    *out_refs, field, stage = refs
    columns = len(out_refs)
    lanes = squares_ref.shape[1]
    bases = squares_ref.shape[0] // lanes
    rows, _, inner = table_ref.shape
    places = inner // 3
    step = places // (2 * columns)
    half = columns * width
    rest = width - SUBLANES
    column, side = column_and_side()
    odd = lax.axis_index("lat") % 2

    def place(row, at, message):
        for slot, read in enumerate(rows_of(message, block, rest)):
            first = pl.multiple_of(slot * places + at * step, step)
            field[row, pl.ds(first, step)] = read

    for at in range(columns):
        place(1 - odd, 2 * at + side, even_own[at])
        place(1 - odd, 2 * at + 1 - side, even_mate[at])
        place(odd, 2 * at + side, odd_own[at])
        place(odd, 2 * at + 1 - side, odd_mate[at])
    over = [
        jnp.dot(table_ref[row, :, : 2 * places], field[row], preferred_element_type=F32)
        for row in range(rows)
    ]
    mixed = None
    for basis in range(bases):
        taken = slice(basis * half, (basis + 1) * half)
        both = [(over[row][taken] + part_ref[row, taken]).astype(BF16) for row in range(rows)]
        product = jnp.dot(
            jnp.concatenate(both, axis=0)[:, :block],
            squares_ref[basis * lanes : basis * lanes + block],
            preferred_element_type=F32,
        )
        mixed = product if mixed is None else mixed + product
    upper = lax.broadcasted_iota(jnp.int32, (SUBLANES, lanes), 0) < rest
    top, bottom = mixed[:half], mixed[half:]
    for target in range(columns):
        at = target * SUBLANES
        pair = (columns + target // 2) * SUBLANES
        first, second = top[pair : pair + SUBLANES], bottom[pair : pair + SUBLANES]
        if target % 2:
            first = pltpu.roll(first, rest, 0)
        else:
            second = pltpu.roll(second, rest, 0)
        last = jnp.where(upper, first, second)
        points = jnp.concatenate(
            [top[at : at + SUBLANES], bottom[at : at + SUBLANES], last], axis=0
        )
        stage[target] = fold(points, block)
    for apart in range(columns):
        out_refs[apart][...] = stage[column ^ apart]


def summed_block(latent_block, message, block):
    convolved = jnp.concatenate(unfold(message.astype(F32), block), axis=0)
    kept = lax.broadcasted_iota(jnp.int32, convolved.shape, 1) < block
    return jnp.where(kept, latent_block + convolved, 0.0).astype(BF16)


def raised_block(summed, column, block, up_ref):
    count = summed.shape[0]
    ones = jnp.ones((up_to(count, 2 * SUBLANES) - count, block), BF16)
    rows = pl.multiple_of(column * block, block)
    return jnp.dot(
        jnp.concatenate([summed[:, :block], ones], axis=0),
        up_ref[pl.ds(rows, block), :],
        preferred_element_type=F32,
    )


def placed(summed, column, chans, block):
    piece = summed.astype(F32)
    if chans > piece.shape[1]:
        gap = jnp.zeros((piece.shape[0], chans - piece.shape[1]), F32)
        piece = jnp.concatenate([piece, gap], axis=1)
    return pltpu.roll(piece, column * block, 1)


def deviations(summed, mean, block):
    kept = lax.broadcasted_iota(jnp.int32, summed.shape, 1) < block
    return jnp.where(kept, summed.astype(F32) - mean, 0.0)


def over_lanes(values):
    return jnp.sum(values, axis=1, keepdims=True)


def lift_kernel(
    apart,
    own_ref,
    first_ref,
    latent_ref,
    up_ref,
    blocks_ref,
    summed_ref,
    raised_ref,
    stats_ref,
    points,
):
    columns = blocks_ref.shape[0]
    chans = latent_ref.shape[2]
    block = chans // columns
    column, _ = column_and_side()
    group_points(latent_ref, points)
    own = points[...]
    for target in range(columns):
        turned = pltpu.roll(own, chans - target * block, 1) if target else own
        blocks_ref[target] = turned[:, : lanes_of(block)]
    other = column ^ apart
    here = summed_block(blocks_ref[column], own_ref[...], block)
    there = summed_block(blocks_ref[other], first_ref[...], block)
    summed_ref[...] = placed(here, column, chans, block) + placed(there, other, chans, block)
    raised_ref[...] = raised_block(here, column, block, up_ref) + raised_block(
        there, other, block, up_ref
    )
    mean = over_lanes(here.astype(F32) + there.astype(F32)) / (2 * block)
    squares = sum(deviations(summed, mean, block) ** 2 for summed in (here, there))
    stats_ref[0] = jnp.broadcast_to(mean, stats_ref.shape[1:])
    stats_ref[1] = jnp.broadcast_to(over_lanes(squares), stats_ref.shape[1:])


def tail_kernel(order, *refs):
    back_refs = refs[: len(order)]
    blocks_ref, summed_ref, raised_ref, stats_ref, up_ref, down_ref, out_ref = refs[len(order) :]
    width, rows, chans = out_ref.shape
    rest = width - SUBLANES
    block = chans // blocks_ref.shape[0]
    column, _ = column_and_side()
    raised = raised_ref[...]
    early_mean, early_squares = stats_ref[0, :, :1], stats_ref[1, :, :1]
    theirs = []
    away = squares = None
    for apart, ref in zip(order, back_refs):
        other = column ^ apart
        there = summed_block(blocks_ref[other], ref[...], block)
        theirs.append((there, other))
        raised = raised + raised_block(there, other, block, up_ref)
        apart_from = deviations(there, early_mean, block)
        away = apart_from if away is None else away + apart_from
        squares = apart_from**2 if squares is None else squares + apart_from**2
    away, squares = over_lanes(away), over_lanes(squares)
    mean = early_mean + away / chans
    variance = (early_squares + squares - away * away / chans) / chans
    scale = lax.rsqrt(variance + 1e-05)
    count = summed_ref.shape[0]
    hidden = scale * (raised[:count] - mean * raised[count : count + 1])
    hidden = (0.5 * hidden * (1.0 + lax.erf(hidden * 0.5**0.5))).astype(BF16)
    summed = summed_ref[...]
    for there, other in theirs:
        summed = summed + placed(there, other, chans, block)
    result = summed + jnp.dot(hidden, down_ref[...], preferred_element_type=F32)
    for row in range(rows):
        out_ref[:SUBLANES, row, :] = result[row * SUBLANES : (row + 1) * SUBLANES].astype(BF16)
        at = rows * SUBLANES + row * rest
        out_ref[SUBLANES:, row, :] = result[at : at + rest].astype(BF16)


VMEM = pl.BlockSpec(memory_space=pltpu.VMEM)


def call(kernel, name, out_shape, scratch, work, *operands):
    several = isinstance(out_shape, tuple)
    return pl.pallas_call(
        kernel,
        out_shape=out_shape,
        in_specs=[VMEM] * len(operands),
        out_specs=(VMEM,) * len(out_shape) if several else VMEM,
        scratch_shapes=scratch,
        compiler_params=pltpu.CompilerParams(vmem_limit_bytes=24 * 2**20),
        cost_estimate=pl.CostEstimate(flops=work, bytes_accessed=10**6, transcendentals=0),
        name=name,
    )(*operands)


def over_columns(message, count, apart):
    pairs = [(i, ((i // 2) ^ apart) * 2 + i % 2) for i in range(count)]
    return lax.ppermute(message, "lon", pairs) if apart else message


def over_sides(block, count):
    return lax.ppermute(block, "lon", [(i, i ^ 1) for i in range(count)])


def swap(block, count, partner):
    pairs = []
    for lat in range(lax.axis_size("lat")):
        for lon in range(count):
            to_lat, to_lon = partner(lat, lon)
            pairs.append((lat * count + lon, to_lat * count + to_lon))
    return lax.ppermute(block, ("lat", "lon"), pairs)


def odd_pair(lat, lon, to_lon, rows):
    to = lat + 1 if lat % 2 else lat - 1
    return (to, to_lon) if 0 <= to < rows else (lat, lon ^ 1)


def local(latent, lon_filter, mix_weight, band_weight, offsets, w_up, w_down):
    rows, width, chans = latent.shape
    bases, lons = lon_filter.shape
    half, group = mix_weight.shape[1:]
    taps = band_weight.shape[2]
    count = lons // width
    columns = count // 2
    block = 2 * half
    step = up_to(width, 2 * SUBLANES)
    places = count * step
    lanes = lanes_of(block)
    height = message_rows(block)
    assert rows == 2 and taps == 3 and columns & (columns - 1) == 0
    assert lax.axis_size("lat") % 2 == 0
    assert 2 * width == 3 * SUBLANES and columns * width % (2 * SUBLANES) == 0
    assert 3 * (block % LANES) <= LANES

    far_first = tuple(reversed(range(columns)))
    inward = far_first
    if columns > 3:
        inward = (far_first[1], far_first[0]) + far_first[2:]
    message = jax.ShapeDtypeStruct((height, LANES), BF16)
    messages = (message,) * columns
    stage = pltpu.VMEM((columns, height, LANES), BF16)
    points = pltpu.VMEM((3 * SUBLANES, chans), F32)
    lon_first = jnp.transpose(latent, (1, 0, 2))
    mix_own = jnp.transpose(mix_weight, (0, 2, 1))

    raw = over_columns(lon_first, count, inward[0])
    apart = call(
        functools.partial(apart_kernel, width, step),
        "apart",
        jax.ShapeDtypeStruct((lons, places), jnp.int32),
        [],
        10**9,
    )
    loaded, apart = lax.optimization_barrier((lon_first, apart))
    packed = call(
        functools.partial(pack_kernel, inward[1:]),
        "pack",
        (message,) * (columns - 1),
        [points, stage],
        10**9,
        loaded,
    )
    arrived = [call(cut_kernel, "cut", message, [points], 5 * 10**9, raw)]
    arrived += [over_columns(*pair) for pair in zip(packed, [count] * columns, inward[1:])]
    mix_mate = over_sides(mix_own, count)
    table = call(
        functools.partial(tables_kernel, width),
        "tables",
        jax.ShapeDtypeStruct((rows, bases * columns * width, taps * places), BF16),
        [pltpu.VMEM((bases, step, places), F32)],
        10**6,
        lon_filter,
        jnp.transpose(band_weight, (2, 1, 0)),
        apart,
    )
    gathered = jax.ShapeDtypeStruct((columns, height, LANES), BF16)
    own_side = call(
        functools.partial(column_kernel, inward),
        "join_columns",
        gathered,
        [],
        10**8,
        *arrived,
    )
    lats = lax.axis_size("lat")
    mate_side = swap(own_side, count, lambda lat, lon: (lat, lon ^ 1))
    odd_mate = swap(own_side, count, lambda lat, lon: odd_pair(lat, lon, lon ^ 1, lats))
    odd_own = swap(own_side, count, lambda lat, lon: odd_pair(lat, lon, lon, lats))
    own_rows = call(
        functools.partial(unpack_kernel, block, width),
        "unpack",
        jax.ShapeDtypeStruct((rows, columns, step, lanes), BF16),
        [],
        10**9,
        own_side,
    )
    even_own = swap(own_side, count, lambda lat, lon: (lat ^ 1, lon))
    even_mate = swap(mate_side, count, lambda lat, lon: (lat ^ 1, lon))
    mix_mate, _ = lax.optimization_barrier((mix_mate, mate_side))
    squares = call(
        squares_kernel,
        "squares",
        jax.ShapeDtypeStruct((bases * lanes, lanes), BF16),
        [pltpu.VMEM((2, bases, up_to(group, 2 * SUBLANES), lanes), F32)],
        3 * 10**8,
        mix_own,
        mix_mate,
    )
    part = call(
        functools.partial(own_kernel, block, width),
        "conv_own",
        jax.ShapeDtypeStruct((rows, bases * columns * width, lanes), F32),
        [pltpu.VMEM((rows, places, lanes), BF16)],
        3 * 10**8,
        mate_side,
        own_rows,
        table,
    )
    mixed = call(
        functools.partial(conv_kernel, block, width),
        "conv",
        messages,
        [
            pltpu.VMEM((rows, 2 * places, lanes), BF16),
            pltpu.VMEM((columns, height, LANES), BF16),
        ],
        10**10,
        odd_mate,
        odd_own,
        even_own,
        even_mate,
        part,
        table,
        squares,
    )
    outward = tuple(reversed(far_first[:-1]))
    back = [over_columns(mixed[apart], count, apart) for apart in outward]
    first = outward.index(far_first[0])
    lifted = call(
        functools.partial(lift_kernel, far_first[0]),
        "lift",
        (
            jax.ShapeDtypeStruct((columns, 3 * SUBLANES, lanes), F32),
            jax.ShapeDtypeStruct((3 * SUBLANES, chans), F32),
            jax.ShapeDtypeStruct((up_to(3 * SUBLANES, 2 * SUBLANES), w_up.shape[1]), F32),
            jax.ShapeDtypeStruct((2, 3 * SUBLANES, LANES), F32),
        ),
        [points],
        10**8,
        mixed[0],
        back[first],
        lon_first,
        w_up,
    )
    result = call(
        functools.partial(tail_kernel, outward[:first] + outward[first + 1 :]),
        "tail",
        jax.ShapeDtypeStruct(lon_first.shape, BF16),
        [],
        10**9,
        *back[:first],
        *back[first + 1 :],
        *lifted,
        w_up,
        w_down,
    )
    return jnp.transpose(result, (1, 0, 2))


def solution(mesh):
    return jax.shard_map(
        local,
        mesh=mesh,
        in_specs=(
            P("lat", "lon", None),
            P(),
            P(None, "lon", None),
            P(None, "lat", None),
            P("lat"),
            P(),
            P(),
        ),
        out_specs=P("lat", "lon", None),
        check_vma=False,
    )
```

```python
import functools

import jax
import jax.numpy as jnp
from jax import lax
from jax.experimental import pallas as pl
from jax.experimental.pallas import tpu as pltpu
from jax.sharding import PartitionSpec as P

F32 = jnp.float32
BF16 = jnp.bfloat16
LANES = 128
SUBLANES = 8


def up_to(size, step):
    return -(-size // step) * step


def column_and_side():
    place = lax.axis_index("lon")
    return place // 2, place % 2


def message_rows(block):
    tiles = block // LANES
    return up_to(3 * SUBLANES * tiles + (SUBLANES if block % LANES else 0), 2 * SUBLANES)


def lanes_of(block):
    return up_to(block, LANES)


def fold(points, block):
    whole, rest = divmod(block, LANES)
    parts = [points[:, tile * LANES : (tile + 1) * LANES] for tile in range(whole)]
    if rest:
        odd = points[:, whole * LANES : (whole + 1) * LANES]
        kept = lax.broadcasted_iota(jnp.int32, (SUBLANES, LANES), 1) < rest
        shared = None
        for third in range(3):
            piece = jnp.where(kept, odd[third * SUBLANES : (third + 1) * SUBLANES], 0.0)
            piece = pltpu.roll(piece, third * rest, 1) if third else piece
            shared = piece if shared is None else shared + piece
        parts.append(shared)
    filled = sum(part.shape[0] for part in parts)
    if message_rows(block) > filled:
        parts.append(jnp.zeros((message_rows(block) - filled, LANES), F32))
    return jnp.concatenate(parts, axis=0).astype(BF16)


def unfold(message, block):
    whole, rest = divmod(block, LANES)
    groups = []
    for third in range(3):
        first = third * SUBLANES
        parts = [
            message[tile * 3 * SUBLANES + first : tile * 3 * SUBLANES + first + SUBLANES]
            for tile in range(whole)
        ]
        if rest:
            odd = message[whole * 3 * SUBLANES : whole * 3 * SUBLANES + SUBLANES]
            parts.append(pltpu.roll(odd, LANES - third * rest, 1) if third else odd)
        groups.append(jnp.concatenate(parts, axis=1) if len(parts) > 1 else parts[0])
    return groups


def group_points(latent_ref, points):
    width, rows, _ = latent_ref.shape
    rest = width - SUBLANES
    for row in range(rows):
        points[row * SUBLANES : (row + 1) * SUBLANES] = latent_ref[:SUBLANES, row, :].astype(F32)
        at = rows * SUBLANES + row * rest
        points[at : at + rest] = latent_ref[SUBLANES:, row, :].astype(F32)


def pack_kernel(order, latent_ref, *refs):
    *out_refs, points, stage = refs
    columns = stage.shape[0]
    chans = latent_ref.shape[2]
    block = chans // columns
    column, _ = column_and_side()
    group_points(latent_ref, points)
    own = points[...]
    for target in range(columns):
        turned = pltpu.roll(own, chans - target * block, 1) if target else own
        stage[target] = fold(turned[:, : lanes_of(block)], block)
    for apart, ref in zip(order, out_refs):
        ref[...] = stage[column ^ apart]


def cut_kernel(raw_ref, out_ref, points):
    chans = raw_ref.shape[2]
    block = chans // (lax.axis_size("lon") // 2)
    column, _ = column_and_side()
    group_points(raw_ref, points)
    turned = pltpu.roll(points[...], (chans - column * block) % chans, 1)
    out_ref[...] = fold(turned[:, : lanes_of(block)], block)


def column_kernel(order, *refs):
    *in_refs, out_ref = refs
    column, _ = column_and_side()
    for apart, ref in zip(order, in_refs):
        out_ref[column ^ apart] = ref[...]


def apart_kernel(width, step, out_ref):
    lons = out_ref.shape[0]
    side = lax.axis_index("lon") % 2
    source = lax.broadcasted_iota(jnp.int32, out_ref.shape, 0)
    place = lax.broadcasted_iota(jnp.int32, out_ref.shape, 1)
    within = place % step
    apart = source + (place // step) * width + within + (lons - side * width)
    for _ in range(3):
        apart = jnp.where(apart >= lons, apart - lons, apart)
    out_ref[...] = jnp.where(within < width, apart, -1)


def tables_kernel(width, filter_ref, band_ref, apart_ref, table_ref, first):
    bases, lons = filter_ref.shape
    taps, rows, _ = band_ref.shape
    step, places = first.shape[1:]
    columns = places // (2 * step)
    lat = lax.axis_index("lat")
    below = (lat > 0).astype(F32)
    above = (lat < lax.axis_size("lat") - 1).astype(F32)
    inside = [[below, below, 1.0], [1.0, above, above]]
    slots = [[0, 1, 2], [2, 0, 1]]
    profile = filter_ref[...]
    band = band_ref[...].astype(F32)
    apart = apart_ref[...]
    first[...] = jnp.zeros_like(first)
    for lon in range(width):
        pick = (apart == lon).astype(F32).astype(BF16)
        first[:, lon, :] = jnp.dot(profile, pick, preferred_element_type=F32)
    upper = lax.broadcasted_iota(jnp.int32, (SUBLANES, places), 0) < SUBLANES // 2
    count = columns * width
    for basis in range(bases):
        circle = first[basis]
        turned = [
            pltpu.roll(circle, column * 2 * step, 1) if column else circle
            for column in range(columns)
        ]
        last = [block[SUBLANES:] for block in turned]
        pairs = [
            jnp.where(upper, one, pltpu.roll(other, SUBLANES // 2, 0))
            for one, other in zip(last[::2], last[1::2])
        ]
        turned = jnp.concatenate([block[:SUBLANES] for block in turned] + pairs, axis=0)
        at = basis * count
        for row in range(rows):
            for tap in range(taps):
                weight = band[tap, row : row + 1, basis : basis + 1] * inside[row][tap]
                to = slots[row][tap] * places
                table_ref[row, at : at + count, to : to + places] = (weight * turned).astype(BF16)


def squares_kernel(own_ref, mate_ref, squares_ref, padded):
    bases, group, half = own_ref.shape
    lanes = squares_ref.shape[1]
    _, side = column_and_side()
    first = side == 0
    own = own_ref[...].astype(F32)
    mate = mate_ref[...].astype(F32)
    padded[...] = jnp.zeros_like(padded)
    padded[0, :, :group, :half] = jnp.where(first, own, mate)
    padded[1, :, :group, :half] = jnp.where(first, mate, own)
    members = padded.shape[2]
    into = lax.broadcasted_iota(jnp.int32, (lanes, members), 0)
    member = lax.broadcasted_iota(jnp.int32, (lanes, members), 1)
    repeat = (into % group == member).astype(F32).astype(BF16)
    row = lax.broadcasted_iota(jnp.int32, (lanes, lanes), 0)
    column = lax.broadcasted_iota(jnp.int32, (lanes, lanes), 1)
    same = (row // group == column // group) & (row < 2 * half) & (column < 2 * half)
    for basis in range(bases):
        weights = padded[0, basis] + pltpu.roll(padded[1, basis], half, 1)
        repeated = jnp.dot(repeat, weights.astype(BF16), preferred_element_type=F32)
        squares_ref[basis * lanes : (basis + 1) * lanes] = jnp.where(same, repeated, 0.0).astype(
            BF16
        )


def rows_of(message, block, rest):
    groups = unfold(message.astype(F32), block)
    last = (groups[2], pltpu.roll(groups[2], SUBLANES - rest, 0))
    return [jnp.concatenate([groups[row], last[row]], axis=0).astype(BF16) for row in range(2)]


def unpack_kernel(block, width, own_ref, out_ref):
    for at in range(own_ref.shape[0]):
        for row, read in enumerate(rows_of(own_ref[at], block, width - SUBLANES)):
            out_ref[row, at] = read


def own_kernel(block, width, mate, own, table_ref, part_ref, field):
    rows, columns, step, _ = own.shape
    places = field.shape[1]
    side = lax.axis_index("lon") % 2
    for at in range(columns):
        first = pl.multiple_of((2 * at + side) * step, step)
        other = pl.multiple_of((2 * at + 1 - side) * step, step)
        for row, read in enumerate(rows_of(mate[at], block, width - SUBLANES)):
            field[row, pl.ds(first, step)] = own[row, at]
            field[row, pl.ds(other, step)] = read
    for row in range(rows):
        part_ref[row] = jnp.dot(
            table_ref[row, :, 2 * places :], field[row], preferred_element_type=F32
        )


def conv_kernel(
    block,
    width,
    odd_mate,
    odd_own,
    even_own,
    even_mate,
    part_ref,
    table_ref,
    squares_ref,
    *refs,
):
    *out_refs, field, stage = refs
    columns = len(out_refs)
    lanes = squares_ref.shape[1]
    bases = squares_ref.shape[0] // lanes
    rows, _, inner = table_ref.shape
    places = inner // 3
    step = places // (2 * columns)
    half = columns * width
    rest = width - SUBLANES
    column, side = column_and_side()
    odd = lax.axis_index("lat") % 2

    def place(row, at, message):
        for slot, read in enumerate(rows_of(message, block, rest)):
            first = pl.multiple_of(slot * places + at * step, step)
            field[row, pl.ds(first, step)] = read

    for at in range(columns):
        place(1 - odd, 2 * at + side, even_own[at])
        place(1 - odd, 2 * at + 1 - side, even_mate[at])
        place(odd, 2 * at + side, odd_own[at])
        place(odd, 2 * at + 1 - side, odd_mate[at])
    over = [
        jnp.dot(table_ref[row, :, : 2 * places], field[row], preferred_element_type=F32)
        for row in range(rows)
    ]
    mixed = None
    for basis in range(bases):
        taken = slice(basis * half, (basis + 1) * half)
        both = [(over[row][taken] + part_ref[row, taken]).astype(BF16) for row in range(rows)]
        product = jnp.dot(
            jnp.concatenate(both, axis=0)[:, :block],
            squares_ref[basis * lanes : basis * lanes + block],
            preferred_element_type=F32,
        )
        mixed = product if mixed is None else mixed + product
    upper = lax.broadcasted_iota(jnp.int32, (SUBLANES, lanes), 0) < rest
    top, bottom = mixed[:half], mixed[half:]
    for target in range(columns):
        at = target * SUBLANES
        pair = (columns + target // 2) * SUBLANES
        first, second = top[pair : pair + SUBLANES], bottom[pair : pair + SUBLANES]
        if target % 2:
            first = pltpu.roll(first, rest, 0)
        else:
            second = pltpu.roll(second, rest, 0)
        last = jnp.where(upper, first, second)
        points = jnp.concatenate(
            [top[at : at + SUBLANES], bottom[at : at + SUBLANES], last], axis=0
        )
        stage[target] = fold(points, block)
    for apart in range(columns):
        out_refs[apart][...] = stage[column ^ apart]


def summed_block(latent_block, message, block):
    convolved = jnp.concatenate(unfold(message.astype(F32), block), axis=0)
    kept = lax.broadcasted_iota(jnp.int32, convolved.shape, 1) < block
    return jnp.where(kept, latent_block + convolved, 0.0).astype(BF16)


def raised_block(summed, column, block, up_ref):
    count = summed.shape[0]
    ones = jnp.ones((up_to(count, 2 * SUBLANES) - count, block), BF16)
    rows = pl.multiple_of(column * block, block)
    return jnp.dot(
        jnp.concatenate([summed[:, :block], ones], axis=0),
        up_ref[pl.ds(rows, block), :],
        preferred_element_type=F32,
    )


def placed(summed, column, chans, block):
    piece = summed.astype(F32)
    if chans > piece.shape[1]:
        gap = jnp.zeros((piece.shape[0], chans - piece.shape[1]), F32)
        piece = jnp.concatenate([piece, gap], axis=1)
    return pltpu.roll(piece, column * block, 1)


def deviations(summed, mean, block):
    kept = lax.broadcasted_iota(jnp.int32, summed.shape, 1) < block
    return jnp.where(kept, summed.astype(F32) - mean, 0.0)


def over_lanes(values):
    return jnp.sum(values, axis=1, keepdims=True)


def lift_kernel(
    apart,
    own_ref,
    first_ref,
    latent_ref,
    up_ref,
    blocks_ref,
    summed_ref,
    raised_ref,
    stats_ref,
    points,
):
    columns = blocks_ref.shape[0]
    chans = latent_ref.shape[2]
    block = chans // columns
    column, _ = column_and_side()
    group_points(latent_ref, points)
    own = points[...]
    for target in range(columns):
        turned = pltpu.roll(own, chans - target * block, 1) if target else own
        blocks_ref[target] = turned[:, : lanes_of(block)]
    other = column ^ apart
    here = summed_block(blocks_ref[column], own_ref[...], block)
    there = summed_block(blocks_ref[other], first_ref[...], block)
    summed_ref[...] = placed(here, column, chans, block) + placed(there, other, chans, block)
    raised_ref[...] = raised_block(here, column, block, up_ref) + raised_block(
        there, other, block, up_ref
    )
    mean = over_lanes(here.astype(F32) + there.astype(F32)) / (2 * block)
    squares = sum(deviations(summed, mean, block) ** 2 for summed in (here, there))
    stats_ref[0] = jnp.broadcast_to(mean, stats_ref.shape[1:])
    stats_ref[1] = jnp.broadcast_to(over_lanes(squares), stats_ref.shape[1:])


def tail_kernel(order, *refs):
    back_refs = refs[: len(order)]
    blocks_ref, summed_ref, raised_ref, stats_ref, up_ref, down_ref, out_ref = refs[len(order) :]
    width, rows, chans = out_ref.shape
    rest = width - SUBLANES
    block = chans // blocks_ref.shape[0]
    column, _ = column_and_side()
    raised = raised_ref[...]
    early_mean, early_squares = stats_ref[0, :, :1], stats_ref[1, :, :1]
    theirs = []
    away = squares = None
    for apart, ref in zip(order, back_refs):
        other = column ^ apart
        there = summed_block(blocks_ref[other], ref[...], block)
        theirs.append((there, other))
        raised = raised + raised_block(there, other, block, up_ref)
        apart_from = deviations(there, early_mean, block)
        away = apart_from if away is None else away + apart_from
        squares = apart_from**2 if squares is None else squares + apart_from**2
    away, squares = over_lanes(away), over_lanes(squares)
    mean = early_mean + away / chans
    variance = (early_squares + squares - away * away / chans) / chans
    scale = lax.rsqrt(variance + 1e-05)
    count = summed_ref.shape[0]
    hidden = scale * (raised[:count] - mean * raised[count : count + 1])
    hidden = (0.5 * hidden * (1.0 + lax.erf(hidden * 0.5**0.5))).astype(BF16)
    summed = summed_ref[...]
    for there, other in theirs:
        summed = summed + placed(there, other, chans, block)
    result = summed + jnp.dot(hidden, down_ref[...], preferred_element_type=F32)
    for row in range(rows):
        out_ref[:SUBLANES, row, :] = result[row * SUBLANES : (row + 1) * SUBLANES].astype(BF16)
        at = rows * SUBLANES + row * rest
        out_ref[SUBLANES:, row, :] = result[at : at + rest].astype(BF16)


VMEM = pl.BlockSpec(memory_space=pltpu.VMEM)


def call(kernel, name, out_shape, scratch, work, *operands):
    several = isinstance(out_shape, tuple)
    return pl.pallas_call(
        kernel,
        out_shape=out_shape,
        in_specs=[VMEM] * len(operands),
        out_specs=(VMEM,) * len(out_shape) if several else VMEM,
        scratch_shapes=scratch,
        compiler_params=pltpu.CompilerParams(vmem_limit_bytes=24 * 2**20),
        cost_estimate=pl.CostEstimate(flops=work, bytes_accessed=10**6, transcendentals=0),
        name=name,
    )(*operands)


def over_columns(message, count, apart):
    pairs = [(i, ((i // 2) ^ apart) * 2 + i % 2) for i in range(count)]
    return lax.ppermute(message, "lon", pairs) if apart else message


def over_sides(block, count):
    return lax.ppermute(block, "lon", [(i, i ^ 1) for i in range(count)])


def swap(block, count, partner):
    pairs = []
    for lat in range(lax.axis_size("lat")):
        for lon in range(count):
            to_lat, to_lon = partner(lat, lon)
            pairs.append((lat * count + lon, to_lat * count + to_lon))
    return lax.ppermute(block, ("lat", "lon"), pairs)


def odd_pair(lat, lon, other_side, rows):
    to = lat + 1 if lat % 2 else lat - 1
    if 0 <= to < rows:
        return to, lon ^ other_side
    return (lat, lon ^ 1) if other_side else (rows - 1 - lat, lon)


def local(latent, lon_filter, mix_weight, band_weight, offsets, w_up, w_down):
    rows, width, chans = latent.shape
    bases, lons = lon_filter.shape
    half, group = mix_weight.shape[1:]
    taps = band_weight.shape[2]
    count = lons // width
    columns = count // 2
    block = 2 * half
    step = up_to(width, 2 * SUBLANES)
    places = count * step
    lanes = lanes_of(block)
    height = message_rows(block)
    assert rows == 2 and taps == 3 and columns & (columns - 1) == 0
    assert lax.axis_size("lat") % 2 == 0
    assert 2 * width == 3 * SUBLANES and columns * width % (2 * SUBLANES) == 0
    assert 3 * (block % LANES) <= LANES

    far_first = tuple(reversed(range(columns)))
    inward = far_first
    if columns > 3:
        inward = (far_first[1], far_first[0]) + far_first[2:]
    message = jax.ShapeDtypeStruct((height, LANES), BF16)
    messages = (message,) * columns
    stage = pltpu.VMEM((columns, height, LANES), BF16)
    points = pltpu.VMEM((3 * SUBLANES, chans), F32)
    lon_first = jnp.transpose(latent, (1, 0, 2))
    mix_own = jnp.transpose(mix_weight, (0, 2, 1))

    raw = over_columns(lon_first, count, inward[0])
    apart = call(
        functools.partial(apart_kernel, width, step),
        "apart",
        jax.ShapeDtypeStruct((lons, places), jnp.int32),
        [],
        10**9,
    )
    loaded, apart = lax.optimization_barrier((lon_first, apart))
    packed = call(
        functools.partial(pack_kernel, inward[1:]),
        "pack",
        (message,) * (columns - 1),
        [points, stage],
        10**9,
        loaded,
    )
    arrived = [call(cut_kernel, "cut", message, [points], 5 * 10**9, raw)]
    arrived += [over_columns(*pair) for pair in zip(packed, [count] * columns, inward[1:])]
    mix_mate = over_sides(mix_own, count)
    table = call(
        functools.partial(tables_kernel, width),
        "tables",
        jax.ShapeDtypeStruct((rows, bases * columns * width, taps * places), BF16),
        [pltpu.VMEM((bases, step, places), F32)],
        10**6,
        lon_filter,
        jnp.transpose(band_weight, (2, 1, 0)),
        apart,
    )
    gathered = jax.ShapeDtypeStruct((columns, height, LANES), BF16)
    own_side = call(
        functools.partial(column_kernel, inward),
        "join_columns",
        gathered,
        [],
        10**8,
        *arrived,
    )
    lats = lax.axis_size("lat")
    mate_side = swap(own_side, count, lambda lat, lon: (lat, lon ^ 1))
    odd_mate = swap(own_side, count, lambda lat, lon: odd_pair(lat, lon, 1, lats))
    odd_own = swap(own_side, count, lambda lat, lon: odd_pair(lat, lon, 0, lats))
    own_rows = call(
        functools.partial(unpack_kernel, block, width),
        "unpack",
        jax.ShapeDtypeStruct((rows, columns, step, lanes), BF16),
        [],
        10**9,
        own_side,
    )
    even_own = swap(own_side, count, lambda lat, lon: (lat ^ 1, lon))
    even_mate = swap(mate_side, count, lambda lat, lon: (lat ^ 1, lon))
    mix_mate, _ = lax.optimization_barrier((mix_mate, mate_side))
    squares = call(
        squares_kernel,
        "squares",
        jax.ShapeDtypeStruct((bases * lanes, lanes), BF16),
        [pltpu.VMEM((2, bases, up_to(group, 2 * SUBLANES), lanes), F32)],
        3 * 10**8,
        mix_own,
        mix_mate,
    )
    part = call(
        functools.partial(own_kernel, block, width),
        "conv_own",
        jax.ShapeDtypeStruct((rows, bases * columns * width, lanes), F32),
        [pltpu.VMEM((rows, places, lanes), BF16)],
        3 * 10**8,
        mate_side,
        own_rows,
        table,
    )
    mixed = call(
        functools.partial(conv_kernel, block, width),
        "conv",
        messages,
        [
            pltpu.VMEM((rows, 2 * places, lanes), BF16),
            pltpu.VMEM((columns, height, LANES), BF16),
        ],
        10**10,
        odd_mate,
        odd_own,
        even_own,
        even_mate,
        part,
        table,
        squares,
    )
    outward = tuple(reversed(far_first[:-1]))
    back = [over_columns(mixed[apart], count, apart) for apart in outward]
    first = outward.index(far_first[0])
    lifted = call(
        functools.partial(lift_kernel, far_first[0]),
        "lift",
        (
            jax.ShapeDtypeStruct((columns, 3 * SUBLANES, lanes), F32),
            jax.ShapeDtypeStruct((3 * SUBLANES, chans), F32),
            jax.ShapeDtypeStruct((up_to(3 * SUBLANES, 2 * SUBLANES), w_up.shape[1]), F32),
            jax.ShapeDtypeStruct((2, 3 * SUBLANES, LANES), F32),
        ),
        [points],
        10**8,
        mixed[0],
        back[first],
        lon_first,
        w_up,
    )
    result = call(
        functools.partial(tail_kernel, outward[:first] + outward[first + 1 :]),
        "tail",
        jax.ShapeDtypeStruct(lon_first.shape, BF16),
        [],
        10**9,
        *back[:first],
        *back[first + 1 :],
        *lifted,
        w_up,
        w_down,
    )
    return jnp.transpose(result, (1, 0, 2))


def solution(mesh):
    return jax.shard_map(
        local,
        mesh=mesh,
        in_specs=(
            P("lat", "lon", None),
            P(),
            P(None, "lon", None),
            P(None, "lat", None),
            P("lat"),
            P(),
            P(),
        ),
        out_specs=P("lat", "lon", None),
        check_vma=False,
    )
```

```python
import functools

import jax
import jax.numpy as jnp
from jax import lax
from jax.experimental import pallas as pl
from jax.experimental.pallas import tpu as pltpu
from jax.sharding import PartitionSpec as P

F32 = jnp.float32
BF16 = jnp.bfloat16
LANES = 128
SUBLANES = 8


def up_to(size, step):
    return -(-size // step) * step


def column_and_side():
    place = lax.axis_index("lon")
    return place // 2, place % 2


def message_rows(block):
    tiles = block // LANES
    return up_to(3 * SUBLANES * tiles + (SUBLANES if block % LANES else 0), 2 * SUBLANES)


def lanes_of(block):
    return up_to(block, LANES)


def fold(points, block):
    whole, rest = divmod(block, LANES)
    parts = [points[:, tile * LANES : (tile + 1) * LANES] for tile in range(whole)]
    if rest:
        odd = points[:, whole * LANES : (whole + 1) * LANES]
        kept = lax.broadcasted_iota(jnp.int32, (SUBLANES, LANES), 1) < rest
        shared = None
        for third in range(3):
            piece = jnp.where(kept, odd[third * SUBLANES : (third + 1) * SUBLANES], 0.0)
            piece = pltpu.roll(piece, third * rest, 1) if third else piece
            shared = piece if shared is None else shared + piece
        parts.append(shared)
    filled = sum(part.shape[0] for part in parts)
    if message_rows(block) > filled:
        parts.append(jnp.zeros((message_rows(block) - filled, LANES), F32))
    return jnp.concatenate(parts, axis=0).astype(BF16)


def unfold(message, block):
    whole, rest = divmod(block, LANES)
    groups = []
    for third in range(3):
        first = third * SUBLANES
        parts = [
            message[tile * 3 * SUBLANES + first : tile * 3 * SUBLANES + first + SUBLANES]
            for tile in range(whole)
        ]
        if rest:
            odd = message[whole * 3 * SUBLANES : whole * 3 * SUBLANES + SUBLANES]
            parts.append(pltpu.roll(odd, LANES - third * rest, 1) if third else odd)
        groups.append(jnp.concatenate(parts, axis=1) if len(parts) > 1 else parts[0])
    return groups


def group_points(latent_ref, points):
    width, rows, _ = latent_ref.shape
    rest = width - SUBLANES
    for row in range(rows):
        points[row * SUBLANES : (row + 1) * SUBLANES] = latent_ref[:SUBLANES, row, :].astype(F32)
        at = rows * SUBLANES + row * rest
        points[at : at + rest] = latent_ref[SUBLANES:, row, :].astype(F32)


def pack_kernel(order, latent_ref, *refs):
    *out_refs, points, stage = refs
    columns = stage.shape[0]
    chans = latent_ref.shape[2]
    block = chans // columns
    column, _ = column_and_side()
    group_points(latent_ref, points)
    own = points[...]
    for target in range(columns):
        turned = pltpu.roll(own, chans - target * block, 1) if target else own
        stage[target] = fold(turned[:, : lanes_of(block)], block)
    for apart, ref in zip(order, out_refs):
        ref[...] = stage[column ^ apart]


def cut_kernel(raw_ref, out_ref, points):
    chans = raw_ref.shape[2]
    block = chans // (lax.axis_size("lon") // 2)
    column, _ = column_and_side()
    group_points(raw_ref, points)
    turned = pltpu.roll(points[...], (chans - column * block) % chans, 1)
    out_ref[...] = fold(turned[:, : lanes_of(block)], block)


def column_kernel(order, *refs):
    *in_refs, out_ref = refs
    column, _ = column_and_side()
    for apart, ref in zip(order, in_refs):
        out_ref[column ^ apart] = ref[...]


def apart_kernel(width, step, out_ref):
    lons = out_ref.shape[0]
    side = lax.axis_index("lon") % 2
    source = lax.broadcasted_iota(jnp.int32, out_ref.shape, 0)
    place = lax.broadcasted_iota(jnp.int32, out_ref.shape, 1)
    within = place % step
    apart = source + (place // step) * width + within + (lons - side * width)
    for _ in range(3):
        apart = jnp.where(apart >= lons, apart - lons, apart)
    out_ref[...] = jnp.where(within < width, apart, -1)


def tables_kernel(width, filter_ref, band_ref, apart_ref, table_ref, first):
    bases, lons = filter_ref.shape
    taps, rows, _ = band_ref.shape
    step, places = first.shape[1:]
    columns = places // (2 * step)
    lat = lax.axis_index("lat")
    below = (lat > 0).astype(F32)
    above = (lat < lax.axis_size("lat") - 1).astype(F32)
    inside = [[below, below, 1.0], [1.0, above, above]]
    slots = [[0, 1, 2], [2, 0, 1]]
    profile = filter_ref[...]
    band = band_ref[...].astype(F32)
    apart = apart_ref[...]
    first[...] = jnp.zeros_like(first)
    for lon in range(width):
        pick = (apart == lon).astype(F32).astype(BF16)
        first[:, lon, :] = jnp.dot(profile, pick, preferred_element_type=F32)
    upper = lax.broadcasted_iota(jnp.int32, (SUBLANES, places), 0) < SUBLANES // 2
    count = columns * width
    for basis in range(bases):
        circle = first[basis]
        turned = [
            pltpu.roll(circle, column * 2 * step, 1) if column else circle
            for column in range(columns)
        ]
        last = [block[SUBLANES:] for block in turned]
        pairs = [
            jnp.where(upper, one, pltpu.roll(other, SUBLANES // 2, 0))
            for one, other in zip(last[::2], last[1::2])
        ]
        turned = jnp.concatenate([block[:SUBLANES] for block in turned] + pairs, axis=0)
        at = basis * count
        for row in range(rows):
            for tap in range(taps):
                weight = band[tap, row : row + 1, basis : basis + 1] * inside[row][tap]
                to = slots[row][tap] * places
                table_ref[row, at : at + count, to : to + places] = (weight * turned).astype(BF16)


def squares_kernel(own_ref, mate_ref, squares_ref, padded):
    bases, group, half = own_ref.shape
    lanes = squares_ref.shape[1]
    _, side = column_and_side()
    first = side == 0
    own = own_ref[...].astype(F32)
    mate = mate_ref[...].astype(F32)
    padded[...] = jnp.zeros_like(padded)
    padded[0, :, :group, :half] = jnp.where(first, own, mate)
    padded[1, :, :group, :half] = jnp.where(first, mate, own)
    members = padded.shape[2]
    into = lax.broadcasted_iota(jnp.int32, (lanes, members), 0)
    member = lax.broadcasted_iota(jnp.int32, (lanes, members), 1)
    repeat = (into % group == member).astype(F32).astype(BF16)
    row = lax.broadcasted_iota(jnp.int32, (lanes, lanes), 0)
    column = lax.broadcasted_iota(jnp.int32, (lanes, lanes), 1)
    same = (row // group == column // group) & (row < 2 * half) & (column < 2 * half)
    for basis in range(bases):
        weights = padded[0, basis] + pltpu.roll(padded[1, basis], half, 1)
        repeated = jnp.dot(repeat, weights.astype(BF16), preferred_element_type=F32)
        squares_ref[basis * lanes : (basis + 1) * lanes] = jnp.where(same, repeated, 0.0).astype(
            BF16
        )


def rows_of(message, block, rest):
    groups = unfold(message.astype(F32), block)
    last = (groups[2], pltpu.roll(groups[2], SUBLANES - rest, 0))
    return [jnp.concatenate([groups[row], last[row]], axis=0).astype(BF16) for row in range(2)]


def unpack_kernel(block, width, own_ref, out_ref):
    for at in range(own_ref.shape[0]):
        for row, read in enumerate(rows_of(own_ref[at], block, width - SUBLANES)):
            out_ref[row, at] = read


def own_kernel(block, width, mate, own, table_ref, part_ref, field):
    rows, columns, step, _ = own.shape
    places = field.shape[1]
    side = lax.axis_index("lon") % 2
    for at in range(columns):
        first = pl.multiple_of((2 * at + side) * step, step)
        other = pl.multiple_of((2 * at + 1 - side) * step, step)
        for row, read in enumerate(rows_of(mate[at], block, width - SUBLANES)):
            field[row, pl.ds(first, step)] = own[row, at]
            field[row, pl.ds(other, step)] = read
    for row in range(rows):
        part_ref[row] = jnp.dot(
            table_ref[row, :, 2 * places :], field[row], preferred_element_type=F32
        )


def conv_kernel(
    block,
    width,
    odd_mate,
    odd_own,
    even_own,
    even_mate,
    part_ref,
    table_ref,
    squares_ref,
    *refs,
):
    *out_refs, field, stage = refs
    columns = len(out_refs)
    lanes = squares_ref.shape[1]
    bases = squares_ref.shape[0] // lanes
    rows, _, inner = table_ref.shape
    places = inner // 3
    step = places // (2 * columns)
    half = columns * width
    rest = width - SUBLANES
    column, side = column_and_side()
    odd = lax.axis_index("lat") % 2

    def place(row, at, message):
        for slot, read in enumerate(rows_of(message, block, rest)):
            first = pl.multiple_of(slot * places + at * step, step)
            field[row, pl.ds(first, step)] = read

    for at in range(columns):
        place(1 - odd, 2 * at + side, even_own[at])
        place(1 - odd, 2 * at + 1 - side, even_mate[at])
        place(odd, 2 * at + side, odd_own[at])
        place(odd, 2 * at + 1 - side, odd_mate[at])
    over = [
        jnp.dot(table_ref[row, :, : 2 * places], field[row], preferred_element_type=F32)
        for row in range(rows)
    ]
    mixed = None
    for basis in range(bases):
        taken = slice(basis * half, (basis + 1) * half)
        both = [(over[row][taken] + part_ref[row, taken]).astype(BF16) for row in range(rows)]
        product = jnp.dot(
            jnp.concatenate(both, axis=0)[:, :block],
            squares_ref[basis * lanes : basis * lanes + block],
            preferred_element_type=F32,
        )
        mixed = product if mixed is None else mixed + product
    upper = lax.broadcasted_iota(jnp.int32, (SUBLANES, lanes), 0) < rest
    top, bottom = mixed[:half], mixed[half:]
    for target in range(columns):
        at = target * SUBLANES
        pair = (columns + target // 2) * SUBLANES
        first, second = top[pair : pair + SUBLANES], bottom[pair : pair + SUBLANES]
        if target % 2:
            first = pltpu.roll(first, rest, 0)
        else:
            second = pltpu.roll(second, rest, 0)
        last = jnp.where(upper, first, second)
        points = jnp.concatenate(
            [top[at : at + SUBLANES], bottom[at : at + SUBLANES], last], axis=0
        )
        stage[target] = fold(points, block)
    for apart in range(columns):
        out_refs[apart][...] = stage[column ^ apart]


def summed_block(latent_block, message, block):
    convolved = jnp.concatenate(unfold(message.astype(F32), block), axis=0)
    kept = lax.broadcasted_iota(jnp.int32, convolved.shape, 1) < block
    return jnp.where(kept, latent_block + convolved, 0.0).astype(BF16)


def raised_block(summed, column, block, up_ref):
    count = summed.shape[0]
    ones = jnp.ones((up_to(count, 2 * SUBLANES) - count, block), BF16)
    rows = pl.multiple_of(column * block, block)
    return jnp.dot(
        jnp.concatenate([summed[:, :block], ones], axis=0),
        up_ref[pl.ds(rows, block), :],
        preferred_element_type=F32,
    )


def placed(summed, column, chans, block):
    piece = summed.astype(F32)
    if chans > piece.shape[1]:
        gap = jnp.zeros((piece.shape[0], chans - piece.shape[1]), F32)
        piece = jnp.concatenate([piece, gap], axis=1)
    return pltpu.roll(piece, column * block, 1)


def deviations(summed, mean, block):
    kept = lax.broadcasted_iota(jnp.int32, summed.shape, 1) < block
    return jnp.where(kept, summed.astype(F32) - mean, 0.0)


def over_lanes(values):
    return jnp.sum(values, axis=1, keepdims=True)


def lift_kernel(
    apart,
    own_ref,
    first_ref,
    latent_ref,
    up_ref,
    blocks_ref,
    summed_ref,
    raised_ref,
    stats_ref,
    points,
):
    columns = blocks_ref.shape[0]
    chans = latent_ref.shape[2]
    block = chans // columns
    column, _ = column_and_side()
    group_points(latent_ref, points)
    own = points[...]
    for target in range(columns):
        turned = pltpu.roll(own, chans - target * block, 1) if target else own
        blocks_ref[target] = turned[:, : lanes_of(block)]
    other = column ^ apart
    here = summed_block(blocks_ref[column], own_ref[...], block)
    there = summed_block(blocks_ref[other], first_ref[...], block)
    summed_ref[...] = placed(here, column, chans, block) + placed(there, other, chans, block)
    raised_ref[...] = raised_block(here, column, block, up_ref) + raised_block(
        there, other, block, up_ref
    )
    mean = over_lanes(here.astype(F32) + there.astype(F32)) / (2 * block)
    squares = sum(deviations(summed, mean, block) ** 2 for summed in (here, there))
    stats_ref[0] = jnp.broadcast_to(mean, stats_ref.shape[1:])
    stats_ref[1] = jnp.broadcast_to(over_lanes(squares), stats_ref.shape[1:])


def tail_kernel(order, *refs):
    back_refs = refs[: len(order)]
    blocks_ref, summed_ref, raised_ref, stats_ref, up_ref, down_ref, out_ref = refs[len(order) :]
    width, rows, chans = out_ref.shape
    rest = width - SUBLANES
    block = chans // blocks_ref.shape[0]
    column, _ = column_and_side()
    raised = raised_ref[...]
    early_mean, early_squares = stats_ref[0, :, :1], stats_ref[1, :, :1]
    theirs = []
    away = squares = None
    for apart, ref in zip(order, back_refs):
        other = column ^ apart
        there = summed_block(blocks_ref[other], ref[...], block)
        theirs.append((there, other))
        raised = raised + raised_block(there, other, block, up_ref)
        apart_from = deviations(there, early_mean, block)
        away = apart_from if away is None else away + apart_from
        squares = apart_from**2 if squares is None else squares + apart_from**2
    away, squares = over_lanes(away), over_lanes(squares)
    mean = early_mean + away / chans
    variance = (early_squares + squares - away * away / chans) / chans
    scale = lax.rsqrt(variance + 1e-05)
    count = summed_ref.shape[0]
    hidden = scale * (raised[:count] - mean * raised[count : count + 1])
    hidden = (0.5 * hidden * (1.0 + lax.erf(hidden * 0.5**0.5))).astype(BF16)
    summed = summed_ref[...]
    for there, other in theirs:
        summed = summed + placed(there, other, chans, block)
    result = summed + jnp.dot(hidden, down_ref[...], preferred_element_type=F32)
    for row in range(rows):
        out_ref[:SUBLANES, row, :] = result[row * SUBLANES : (row + 1) * SUBLANES].astype(BF16)
        at = rows * SUBLANES + row * rest
        out_ref[SUBLANES:, row, :] = result[at : at + rest].astype(BF16)


VMEM = pl.BlockSpec(memory_space=pltpu.VMEM)


def call(kernel, name, out_shape, scratch, work, *operands):
    several = isinstance(out_shape, tuple)
    return pl.pallas_call(
        kernel,
        out_shape=out_shape,
        in_specs=[VMEM] * len(operands),
        out_specs=(VMEM,) * len(out_shape) if several else VMEM,
        scratch_shapes=scratch,
        compiler_params=pltpu.CompilerParams(vmem_limit_bytes=24 * 2**20),
        cost_estimate=pl.CostEstimate(flops=work, bytes_accessed=10**6, transcendentals=0),
        name=name,
    )(*operands)


def over_columns(message, count, apart):
    pairs = [(i, ((i // 2) ^ apart) * 2 + i % 2) for i in range(count)]
    return lax.ppermute(message, "lon", pairs) if apart else message


def over_sides(block, count):
    return lax.ppermute(block, "lon", [(i, i ^ 1) for i in range(count)])


def swap(block, count, partner):
    pairs = []
    for lat in range(lax.axis_size("lat")):
        for lon in range(count):
            to_lat, to_lon = partner(lat, lon)
            pairs.append((lat * count + lon, to_lat * count + to_lon))
    return lax.ppermute(block, ("lat", "lon"), pairs)


def odd_pair(lat, lon, other_side, rows):
    to = lat + 1 if lat % 2 else lat - 1
    if 0 <= to < rows:
        return to, lon ^ other_side
    return rows - 1 - lat, lon


def local(latent, lon_filter, mix_weight, band_weight, offsets, w_up, w_down):
    rows, width, chans = latent.shape
    bases, lons = lon_filter.shape
    half, group = mix_weight.shape[1:]
    taps = band_weight.shape[2]
    count = lons // width
    columns = count // 2
    block = 2 * half
    step = up_to(width, 2 * SUBLANES)
    places = count * step
    lanes = lanes_of(block)
    height = message_rows(block)
    assert rows == 2 and taps == 3 and columns & (columns - 1) == 0
    assert lax.axis_size("lat") % 2 == 0
    assert 2 * width == 3 * SUBLANES and columns * width % (2 * SUBLANES) == 0
    assert 3 * (block % LANES) <= LANES

    far_first = tuple(reversed(range(columns)))
    inward = far_first
    if columns > 3:
        inward = (far_first[1], far_first[0]) + far_first[2:]
    message = jax.ShapeDtypeStruct((height, LANES), BF16)
    messages = (message,) * columns
    stage = pltpu.VMEM((columns, height, LANES), BF16)
    points = pltpu.VMEM((3 * SUBLANES, chans), F32)
    lon_first = jnp.transpose(latent, (1, 0, 2))
    mix_own = jnp.transpose(mix_weight, (0, 2, 1))

    raw = over_columns(lon_first, count, inward[0])
    apart = call(
        functools.partial(apart_kernel, width, step),
        "apart",
        jax.ShapeDtypeStruct((lons, places), jnp.int32),
        [],
        10**9,
    )
    loaded, apart = lax.optimization_barrier((lon_first, apart))
    packed = call(
        functools.partial(pack_kernel, inward[1:]),
        "pack",
        (message,) * (columns - 1),
        [points, stage],
        10**9,
        loaded,
    )
    arrived = [call(cut_kernel, "cut", message, [points], 5 * 10**9, raw)]
    arrived += [over_columns(*pair) for pair in zip(packed, [count] * columns, inward[1:])]
    mix_mate = over_sides(mix_own, count)
    table = call(
        functools.partial(tables_kernel, width),
        "tables",
        jax.ShapeDtypeStruct((rows, bases * columns * width, taps * places), BF16),
        [pltpu.VMEM((bases, step, places), F32)],
        10**6,
        lon_filter,
        jnp.transpose(band_weight, (2, 1, 0)),
        apart,
    )
    gathered = jax.ShapeDtypeStruct((columns, height, LANES), BF16)
    own_side = call(
        functools.partial(column_kernel, inward),
        "join_columns",
        gathered,
        [],
        10**8,
        *arrived,
    )
    lats = lax.axis_size("lat")
    mate_side = swap(own_side, count, lambda lat, lon: (lat, lon ^ 1))
    odd_mate = swap(own_side, count, lambda lat, lon: odd_pair(lat, lon, 1, lats))
    odd_own = swap(own_side, count, lambda lat, lon: odd_pair(lat, lon, 0, lats))
    own_rows = call(
        functools.partial(unpack_kernel, block, width),
        "unpack",
        jax.ShapeDtypeStruct((rows, columns, step, lanes), BF16),
        [],
        10**9,
        own_side,
    )
    even_own = swap(own_side, count, lambda lat, lon: (lat ^ 1, lon))
    even_mate = swap(mate_side, count, lambda lat, lon: (lat ^ 1, lon))
    mix_mate, _ = lax.optimization_barrier((mix_mate, mate_side))
    squares = call(
        squares_kernel,
        "squares",
        jax.ShapeDtypeStruct((bases * lanes, lanes), BF16),
        [pltpu.VMEM((2, bases, up_to(group, 2 * SUBLANES), lanes), F32)],
        3 * 10**8,
        mix_own,
        mix_mate,
    )
    part = call(
        functools.partial(own_kernel, block, width),
        "conv_own",
        jax.ShapeDtypeStruct((rows, bases * columns * width, lanes), F32),
        [pltpu.VMEM((rows, places, lanes), BF16)],
        3 * 10**8,
        mate_side,
        own_rows,
        table,
    )
    mixed = call(
        functools.partial(conv_kernel, block, width),
        "conv",
        messages,
        [
            pltpu.VMEM((rows, 2 * places, lanes), BF16),
            pltpu.VMEM((columns, height, LANES), BF16),
        ],
        10**10,
        odd_mate,
        odd_own,
        even_own,
        even_mate,
        part,
        table,
        squares,
    )
    outward = tuple(reversed(far_first[:-1]))
    back = [over_columns(mixed[apart], count, apart) for apart in outward]
    first = outward.index(far_first[0])
    lifted = call(
        functools.partial(lift_kernel, far_first[0]),
        "lift",
        (
            jax.ShapeDtypeStruct((columns, 3 * SUBLANES, lanes), F32),
            jax.ShapeDtypeStruct((3 * SUBLANES, chans), F32),
            jax.ShapeDtypeStruct((up_to(3 * SUBLANES, 2 * SUBLANES), w_up.shape[1]), F32),
            jax.ShapeDtypeStruct((2, 3 * SUBLANES, LANES), F32),
        ),
        [points],
        10**8,
        mixed[0],
        back[first],
        lon_first,
        w_up,
    )
    result = call(
        functools.partial(tail_kernel, outward[:first] + outward[first + 1 :]),
        "tail",
        jax.ShapeDtypeStruct(lon_first.shape, BF16),
        [],
        10**9,
        *back[:first],
        *back[first + 1 :],
        *lifted,
        w_up,
        w_down,
    )
    return jnp.transpose(result, (1, 0, 2))


def solution(mesh):
    return jax.shard_map(
        local,
        mesh=mesh,
        in_specs=(
            P("lat", "lon", None),
            P(),
            P(None, "lon", None),
            P(None, "lat", None),
            P("lat"),
            P(),
            P(),
        ),
        out_specs=P("lat", "lon", None),
        check_vma=False,
    )
```

```python
import functools

import jax
import jax.numpy as jnp
from jax import lax
from jax.experimental import pallas as pl
from jax.experimental.pallas import tpu as pltpu
from jax.sharding import PartitionSpec as P

F32 = jnp.float32
BF16 = jnp.bfloat16
LANES = 128
SUBLANES = 8


def up_to(size, step):
    return -(-size // step) * step


def column_and_side():
    place = lax.axis_index("lon")
    return place // 2, place % 2


def message_rows(block):
    tiles = block // LANES
    return up_to(3 * SUBLANES * tiles + (SUBLANES if block % LANES else 0), 2 * SUBLANES)


def lanes_of(block):
    return up_to(block, LANES)


def fold(points, block):
    whole, rest = divmod(block, LANES)
    parts = [points[:, tile * LANES : (tile + 1) * LANES] for tile in range(whole)]
    if rest:
        odd = points[:, whole * LANES : (whole + 1) * LANES]
        kept = lax.broadcasted_iota(jnp.int32, (SUBLANES, LANES), 1) < rest
        shared = None
        for third in range(3):
            piece = jnp.where(kept, odd[third * SUBLANES : (third + 1) * SUBLANES], 0.0)
            piece = pltpu.roll(piece, third * rest, 1) if third else piece
            shared = piece if shared is None else shared + piece
        parts.append(shared)
    filled = sum(part.shape[0] for part in parts)
    if message_rows(block) > filled:
        parts.append(jnp.zeros((message_rows(block) - filled, LANES), F32))
    return jnp.concatenate(parts, axis=0).astype(BF16)


def unfold(message, block):
    whole, rest = divmod(block, LANES)
    groups = []
    for third in range(3):
        first = third * SUBLANES
        parts = [
            message[tile * 3 * SUBLANES + first : tile * 3 * SUBLANES + first + SUBLANES]
            for tile in range(whole)
        ]
        if rest:
            odd = message[whole * 3 * SUBLANES : whole * 3 * SUBLANES + SUBLANES]
            parts.append(pltpu.roll(odd, LANES - third * rest, 1) if third else odd)
        groups.append(jnp.concatenate(parts, axis=1) if len(parts) > 1 else parts[0])
    return groups


def group_points(latent_ref, points):
    width, rows, _ = latent_ref.shape
    rest = width - SUBLANES
    for row in range(rows):
        points[row * SUBLANES : (row + 1) * SUBLANES] = latent_ref[:SUBLANES, row, :].astype(F32)
        at = rows * SUBLANES + row * rest
        points[at : at + rest] = latent_ref[SUBLANES:, row, :].astype(F32)


def pack_kernel(order, latent_ref, *refs):
    *out_refs, points, stage = refs
    columns = stage.shape[0]
    chans = latent_ref.shape[2]
    block = chans // columns
    column, _ = column_and_side()
    group_points(latent_ref, points)
    own = points[...]
    for target in range(columns):
        turned = pltpu.roll(own, chans - target * block, 1) if target else own
        stage[target] = fold(turned[:, : lanes_of(block)], block)
    for apart, ref in zip(order, out_refs):
        ref[...] = stage[column ^ apart]


def cut_kernel(raw_ref, out_ref, points):
    chans = raw_ref.shape[2]
    block = chans // (lax.axis_size("lon") // 2)
    column, _ = column_and_side()
    group_points(raw_ref, points)
    turned = pltpu.roll(points[...], (chans - column * block) % chans, 1)
    out_ref[...] = fold(turned[:, : lanes_of(block)], block)


def column_kernel(order, *refs):
    *in_refs, out_ref = refs
    column, _ = column_and_side()
    for apart, ref in zip(order, in_refs):
        out_ref[column ^ apart] = ref[...]


def apart_kernel(width, step, out_ref):
    lons = out_ref.shape[0]
    side = lax.axis_index("lon") % 2
    source = lax.broadcasted_iota(jnp.int32, out_ref.shape, 0)
    place = lax.broadcasted_iota(jnp.int32, out_ref.shape, 1)
    within = place % step
    apart = source + (place // step) * width + within + (lons - side * width)
    for _ in range(3):
        apart = jnp.where(apart >= lons, apart - lons, apart)
    out_ref[...] = jnp.where(within < width, apart, -1)


def tables_kernel(width, filter_ref, band_ref, apart_ref, table_ref, first):
    bases, lons = filter_ref.shape
    taps, rows, _ = band_ref.shape
    step, places = first.shape[1:]
    columns = places // (2 * step)
    lat = lax.axis_index("lat")
    below = (lat > 0).astype(F32)
    above = (lat < lax.axis_size("lat") - 1).astype(F32)
    inside = [[below, below, 1.0], [1.0, above, above]]
    slots = [[0, 1, 2], [2, 0, 1]]
    profile = filter_ref[...]
    band = band_ref[...].astype(F32)
    apart = apart_ref[...]
    first[...] = jnp.zeros_like(first)
    for lon in range(width):
        pick = (apart == lon).astype(F32).astype(BF16)
        first[:, lon, :] = jnp.dot(profile, pick, preferred_element_type=F32)
    upper = lax.broadcasted_iota(jnp.int32, (SUBLANES, places), 0) < SUBLANES // 2
    count = columns * width
    for basis in range(bases):
        circle = first[basis]
        turned = [
            pltpu.roll(circle, column * 2 * step, 1) if column else circle
            for column in range(columns)
        ]
        last = [block[SUBLANES:] for block in turned]
        pairs = [
            jnp.where(upper, one, pltpu.roll(other, SUBLANES // 2, 0))
            for one, other in zip(last[::2], last[1::2])
        ]
        turned = jnp.concatenate([block[:SUBLANES] for block in turned] + pairs, axis=0)
        at = basis * count
        for row in range(rows):
            for tap in range(taps):
                weight = band[tap, row : row + 1, basis : basis + 1] * inside[row][tap]
                to = slots[row][tap] * places
                table_ref[row, at : at + count, to : to + places] = (weight * turned).astype(BF16)


def squares_kernel(own_ref, mate_ref, squares_ref, padded):
    bases, group, half = own_ref.shape
    lanes = squares_ref.shape[1]
    _, side = column_and_side()
    first = side == 0
    own = own_ref[...].astype(F32)
    mate = mate_ref[...].astype(F32)
    padded[...] = jnp.zeros_like(padded)
    padded[0, :, :group, :half] = jnp.where(first, own, mate)
    padded[1, :, :group, :half] = jnp.where(first, mate, own)
    members = padded.shape[2]
    into = lax.broadcasted_iota(jnp.int32, (lanes, members), 0)
    member = lax.broadcasted_iota(jnp.int32, (lanes, members), 1)
    repeat = (into % group == member).astype(F32).astype(BF16)
    row = lax.broadcasted_iota(jnp.int32, (lanes, lanes), 0)
    column = lax.broadcasted_iota(jnp.int32, (lanes, lanes), 1)
    same = (row // group == column // group) & (row < 2 * half) & (column < 2 * half)
    for basis in range(bases):
        weights = padded[0, basis] + pltpu.roll(padded[1, basis], half, 1)
        repeated = jnp.dot(repeat, weights.astype(BF16), preferred_element_type=F32)
        squares_ref[basis * lanes : (basis + 1) * lanes] = jnp.where(same, repeated, 0.0).astype(
            BF16
        )


def rows_of(message, block, rest):
    groups = unfold(message.astype(F32), block)
    last = (groups[2], pltpu.roll(groups[2], SUBLANES - rest, 0))
    return [jnp.concatenate([groups[row], last[row]], axis=0).astype(BF16) for row in range(2)]


def unpack_kernel(block, width, own_ref, out_ref):
    for at in range(own_ref.shape[0]):
        for row, read in enumerate(rows_of(own_ref[at], block, width - SUBLANES)):
            out_ref[row, at] = read


def own_kernel(block, width, mate, own, table_ref, part_ref, field):
    rows, columns, step, _ = own.shape
    places = field.shape[1]
    side = lax.axis_index("lon") % 2
    for at in range(columns):
        first = pl.multiple_of((2 * at + side) * step, step)
        other = pl.multiple_of((2 * at + 1 - side) * step, step)
        for row, read in enumerate(rows_of(mate[at], block, width - SUBLANES)):
            field[row, pl.ds(first, step)] = own[row, at]
            field[row, pl.ds(other, step)] = read
    for row in range(rows):
        part_ref[row] = jnp.dot(
            table_ref[row, :, 2 * places :], field[row], preferred_element_type=F32
        )


def conv_kernel(
    block,
    width,
    odd_mate,
    odd_own,
    even_own,
    even_mate,
    part_ref,
    table_ref,
    squares_ref,
    *refs,
):
    *out_refs, field, stage = refs
    columns = len(out_refs)
    lanes = squares_ref.shape[1]
    bases = squares_ref.shape[0] // lanes
    rows, _, inner = table_ref.shape
    places = inner // 3
    step = places // (2 * columns)
    half = columns * width
    rest = width - SUBLANES
    column, side = column_and_side()
    odd = lax.axis_index("lat") % 2

    def place(row, at, message):
        for slot, read in enumerate(rows_of(message, block, rest)):
            first = pl.multiple_of(slot * places + at * step, step)
            field[row, pl.ds(first, step)] = read

    for at in range(columns):
        place(1 - odd, 2 * at + side, even_own[at])
        place(1 - odd, 2 * at + 1 - side, even_mate[at])
        place(odd, 2 * at + side, odd_own[at])
        place(odd, 2 * at + 1 - side, odd_mate[at])
    over = [
        jnp.dot(table_ref[row, :, : 2 * places], field[row], preferred_element_type=F32)
        for row in range(rows)
    ]
    mixed = None
    for basis in range(bases):
        taken = slice(basis * half, (basis + 1) * half)
        both = [(over[row][taken] + part_ref[row, taken]).astype(BF16) for row in range(rows)]
        product = jnp.dot(
            jnp.concatenate(both, axis=0)[:, :block],
            squares_ref[basis * lanes : basis * lanes + block],
            preferred_element_type=F32,
        )
        mixed = product if mixed is None else mixed + product
    upper = lax.broadcasted_iota(jnp.int32, (SUBLANES, lanes), 0) < rest
    top, bottom = mixed[:half], mixed[half:]
    for target in range(columns):
        at = target * SUBLANES
        pair = (columns + target // 2) * SUBLANES
        first, second = top[pair : pair + SUBLANES], bottom[pair : pair + SUBLANES]
        if target % 2:
            first = pltpu.roll(first, rest, 0)
        else:
            second = pltpu.roll(second, rest, 0)
        last = jnp.where(upper, first, second)
        points = jnp.concatenate(
            [top[at : at + SUBLANES], bottom[at : at + SUBLANES], last], axis=0
        )
        stage[target] = fold(points, block)
    for apart in range(columns):
        out_refs[apart][...] = stage[column ^ apart]


def summed_block(latent_block, message, block):
    convolved = jnp.concatenate(unfold(message.astype(F32), block), axis=0)
    kept = lax.broadcasted_iota(jnp.int32, convolved.shape, 1) < block
    return jnp.where(kept, latent_block + convolved, 0.0).astype(BF16)


def raised_block(summed, column, block, up_ref):
    count = summed.shape[0]
    ones = jnp.ones((up_to(count, 2 * SUBLANES) - count, block), BF16)
    rows = pl.multiple_of(column * block, block)
    return jnp.dot(
        jnp.concatenate([summed[:, :block], ones], axis=0),
        up_ref[pl.ds(rows, block), :],
        preferred_element_type=F32,
    )


def placed(summed, column, chans, block):
    piece = summed.astype(F32)
    if chans > piece.shape[1]:
        gap = jnp.zeros((piece.shape[0], chans - piece.shape[1]), F32)
        piece = jnp.concatenate([piece, gap], axis=1)
    return pltpu.roll(piece, column * block, 1)


def deviations(summed, mean, block):
    kept = lax.broadcasted_iota(jnp.int32, summed.shape, 1) < block
    return jnp.where(kept, summed.astype(F32) - mean, 0.0)


def over_lanes(values):
    return jnp.sum(values, axis=1, keepdims=True)


def lift_kernel(
    apart,
    own_ref,
    first_ref,
    latent_ref,
    up_ref,
    blocks_ref,
    summed_ref,
    raised_ref,
    stats_ref,
    points,
):
    columns = blocks_ref.shape[0]
    chans = latent_ref.shape[2]
    block = chans // columns
    column, _ = column_and_side()
    group_points(latent_ref, points)
    own = points[...]
    for target in range(columns):
        turned = pltpu.roll(own, chans - target * block, 1) if target else own
        blocks_ref[target] = turned[:, : lanes_of(block)]
    other = column ^ apart
    here = summed_block(blocks_ref[column], own_ref[...], block)
    there = summed_block(blocks_ref[other], first_ref[...], block)
    summed_ref[...] = placed(here, column, chans, block) + placed(there, other, chans, block)
    raised_ref[...] = raised_block(here, column, block, up_ref) + raised_block(
        there, other, block, up_ref
    )
    mean = over_lanes(here.astype(F32) + there.astype(F32)) / (2 * block)
    squares = sum(deviations(summed, mean, block) ** 2 for summed in (here, there))
    stats_ref[0] = jnp.broadcast_to(mean, stats_ref.shape[1:])
    stats_ref[1] = jnp.broadcast_to(over_lanes(squares), stats_ref.shape[1:])


def tail_kernel(order, *refs):
    back_refs = refs[: len(order)]
    blocks_ref, summed_ref, raised_ref, stats_ref, up_ref, down_ref, out_ref, ordered = refs[
        len(order) :
    ]
    width, rows, chans = out_ref.shape
    rest = width - SUBLANES
    block = chans // blocks_ref.shape[0]
    column, _ = column_and_side()
    raised = raised_ref[...]
    early_mean, early_squares = stats_ref[0, :, :1], stats_ref[1, :, :1]
    theirs = []
    away = squares = None
    for apart, ref in zip(order, back_refs):
        other = column ^ apart
        there = summed_block(blocks_ref[other], ref[...], block)
        theirs.append((there, other))
        raised = raised + raised_block(there, other, block, up_ref)
        apart_from = deviations(there, early_mean, block)
        away = apart_from if away is None else away + apart_from
        squares = apart_from**2 if squares is None else squares + apart_from**2
    away, squares = over_lanes(away), over_lanes(squares)
    mean = early_mean + away / chans
    variance = (early_squares + squares - away * away / chans) / chans
    scale = lax.rsqrt(variance + 1e-05)
    count = summed_ref.shape[0]
    hidden = scale * (raised[:count] - mean * raised[count : count + 1])
    hidden = (0.5 * hidden * (1.0 + lax.erf(hidden * 0.5**0.5))).astype(BF16)
    summed = summed_ref[...]
    for there, other in theirs:
        summed = summed + placed(there, other, chans, block)
    result = summed + jnp.dot(hidden, down_ref[...], preferred_element_type=F32)
    for tile in range(chans // LANES):
        part = result[:, tile * LANES : (tile + 1) * LANES]
        for row in range(rows):
            first = part[row * SUBLANES : (row + 1) * SUBLANES]
            ordered[tile, pl.ds(row, SUBLANES, rows), :] = first
            at = rows * SUBLANES + row * rest
            ordered[tile, pl.ds(rows * SUBLANES + row, rest, rows), :] = part[at : at + rest]
        for lon in range(width):
            taken = ordered[tile, lon * rows : (lon + 1) * rows].astype(BF16)
            out_ref[lon, :, tile * LANES : (tile + 1) * LANES] = taken


VMEM = pl.BlockSpec(memory_space=pltpu.VMEM)


def call(kernel, name, out_shape, scratch, work, *operands):
    several = isinstance(out_shape, tuple)
    return pl.pallas_call(
        kernel,
        out_shape=out_shape,
        in_specs=[VMEM] * len(operands),
        out_specs=(VMEM,) * len(out_shape) if several else VMEM,
        scratch_shapes=scratch,
        compiler_params=pltpu.CompilerParams(vmem_limit_bytes=24 * 2**20),
        cost_estimate=pl.CostEstimate(flops=work, bytes_accessed=10**6, transcendentals=0),
        name=name,
    )(*operands)


def over_columns(message, count, apart):
    pairs = [(i, ((i // 2) ^ apart) * 2 + i % 2) for i in range(count)]
    return lax.ppermute(message, "lon", pairs) if apart else message


def over_sides(block, count):
    return lax.ppermute(block, "lon", [(i, i ^ 1) for i in range(count)])


def swap(block, count, partner):
    pairs = []
    for lat in range(lax.axis_size("lat")):
        for lon in range(count):
            to_lat, to_lon = partner(lat, lon)
            pairs.append((lat * count + lon, to_lat * count + to_lon))
    return lax.ppermute(block, ("lat", "lon"), pairs)


def odd_pair(lat, lon, other_side, rows):
    to = lat + 1 if lat % 2 else lat - 1
    if 0 <= to < rows:
        return to, lon ^ other_side
    return (lat, lon ^ 1) if other_side else (rows - 1 - lat, lon)


def local(latent, lon_filter, mix_weight, band_weight, offsets, w_up, w_down):
    rows, width, chans = latent.shape
    bases, lons = lon_filter.shape
    half, group = mix_weight.shape[1:]
    taps = band_weight.shape[2]
    count = lons // width
    columns = count // 2
    block = 2 * half
    step = up_to(width, 2 * SUBLANES)
    places = count * step
    lanes = lanes_of(block)
    height = message_rows(block)
    assert rows == 2 and taps == 3 and columns & (columns - 1) == 0
    assert lax.axis_size("lat") % 2 == 0
    assert 2 * width == 3 * SUBLANES and columns * width % (2 * SUBLANES) == 0
    assert 3 * (block % LANES) <= LANES

    far_first = tuple(reversed(range(columns)))
    inward = far_first
    if columns > 3:
        inward = (far_first[1], far_first[0]) + far_first[2:]
    message = jax.ShapeDtypeStruct((height, LANES), BF16)
    messages = (message,) * columns
    stage = pltpu.VMEM((columns, height, LANES), BF16)
    points = pltpu.VMEM((3 * SUBLANES, chans), F32)
    lon_first = jnp.transpose(latent, (1, 0, 2))
    mix_own = jnp.transpose(mix_weight, (0, 2, 1))

    raw = over_columns(lon_first, count, inward[0])
    apart = call(
        functools.partial(apart_kernel, width, step),
        "apart",
        jax.ShapeDtypeStruct((lons, places), jnp.int32),
        [],
        10**9,
    )
    loaded, apart = lax.optimization_barrier((lon_first, apart))
    packed = call(
        functools.partial(pack_kernel, inward[1:]),
        "pack",
        (message,) * (columns - 1),
        [points, stage],
        10**9,
        loaded,
    )
    arrived = [call(cut_kernel, "cut", message, [points], 5 * 10**9, raw)]
    arrived += [over_columns(*pair) for pair in zip(packed, [count] * columns, inward[1:])]
    mix_mate = over_sides(mix_own, count)
    table = call(
        functools.partial(tables_kernel, width),
        "tables",
        jax.ShapeDtypeStruct((rows, bases * columns * width, taps * places), BF16),
        [pltpu.VMEM((bases, step, places), F32)],
        10**6,
        lon_filter,
        jnp.transpose(band_weight, (2, 1, 0)),
        apart,
    )
    gathered = jax.ShapeDtypeStruct((columns, height, LANES), BF16)
    own_side = call(
        functools.partial(column_kernel, inward),
        "join_columns",
        gathered,
        [],
        10**8,
        *arrived,
    )
    lats = lax.axis_size("lat")
    mate_side = swap(own_side, count, lambda lat, lon: (lat, lon ^ 1))
    odd_mate = swap(own_side, count, lambda lat, lon: odd_pair(lat, lon, 1, lats))
    odd_own = swap(own_side, count, lambda lat, lon: odd_pair(lat, lon, 0, lats))
    own_rows = call(
        functools.partial(unpack_kernel, block, width),
        "unpack",
        jax.ShapeDtypeStruct((rows, columns, step, lanes), BF16),
        [],
        10**9,
        own_side,
    )
    even_own = swap(own_side, count, lambda lat, lon: (lat ^ 1, lon))
    even_mate = swap(mate_side, count, lambda lat, lon: (lat ^ 1, lon))
    mix_mate, _ = lax.optimization_barrier((mix_mate, mate_side))
    squares = call(
        squares_kernel,
        "squares",
        jax.ShapeDtypeStruct((bases * lanes, lanes), BF16),
        [pltpu.VMEM((2, bases, up_to(group, 2 * SUBLANES), lanes), F32)],
        3 * 10**8,
        mix_own,
        mix_mate,
    )
    part = call(
        functools.partial(own_kernel, block, width),
        "conv_own",
        jax.ShapeDtypeStruct((rows, bases * columns * width, lanes), F32),
        [pltpu.VMEM((rows, places, lanes), BF16)],
        3 * 10**8,
        mate_side,
        own_rows,
        table,
    )
    mixed = call(
        functools.partial(conv_kernel, block, width),
        "conv",
        messages,
        [
            pltpu.VMEM((rows, 2 * places, lanes), BF16),
            pltpu.VMEM((columns, height, LANES), BF16),
        ],
        10**10,
        odd_mate,
        odd_own,
        even_own,
        even_mate,
        part,
        table,
        squares,
    )
    outward = tuple(reversed(far_first[:-1]))
    back = [over_columns(mixed[apart], count, apart) for apart in outward]
    first = outward.index(far_first[0])
    lifted = call(
        functools.partial(lift_kernel, far_first[0]),
        "lift",
        (
            jax.ShapeDtypeStruct((columns, 3 * SUBLANES, lanes), F32),
            jax.ShapeDtypeStruct((3 * SUBLANES, chans), F32),
            jax.ShapeDtypeStruct((up_to(3 * SUBLANES, 2 * SUBLANES), w_up.shape[1]), F32),
            jax.ShapeDtypeStruct((2, 3 * SUBLANES, LANES), F32),
        ),
        [points],
        10**8,
        mixed[0],
        back[first],
        lon_first,
        w_up,
    )
    result = call(
        functools.partial(tail_kernel, outward[:first] + outward[first + 1 :]),
        "tail",
        jax.ShapeDtypeStruct(lon_first.shape, BF16),
        [pltpu.VMEM((chans // LANES, 3 * SUBLANES, LANES), F32)],
        10**9,
        *back[:first],
        *back[first + 1 :],
        *lifted,
        w_up,
        w_down,
    )
    return jnp.transpose(result, (1, 0, 2))


def solution(mesh):
    return jax.shard_map(
        local,
        mesh=mesh,
        in_specs=(
            P("lat", "lon", None),
            P(),
            P(None, "lon", None),
            P(None, "lat", None),
            P("lat"),
            P(),
            P(),
        ),
        out_specs=P("lat", "lon", None),
        check_vma=False,
    )
```

```python
import functools

import jax
import jax.numpy as jnp
from jax import lax
from jax.experimental import pallas as pl
from jax.experimental.pallas import tpu as pltpu
from jax.sharding import PartitionSpec as P

F32 = jnp.float32
BF16 = jnp.bfloat16
LANES = 128
SUBLANES = 8


def up_to(size, step):
    return -(-size // step) * step


def column_and_side():
    place = lax.axis_index("lon")
    return place // 2, place % 2


def message_rows(block):
    tiles = block // LANES
    return up_to(3 * SUBLANES * tiles + (SUBLANES if block % LANES else 0), 2 * SUBLANES)


def lanes_of(block):
    return up_to(block, LANES)


def fold(points, block):
    whole, rest = divmod(block, LANES)
    parts = [points[:, tile * LANES : (tile + 1) * LANES] for tile in range(whole)]
    if rest:
        odd = points[:, whole * LANES : (whole + 1) * LANES]
        kept = lax.broadcasted_iota(jnp.int32, (SUBLANES, LANES), 1) < rest
        shared = None
        for third in range(3):
            piece = jnp.where(kept, odd[third * SUBLANES : (third + 1) * SUBLANES], 0.0)
            piece = pltpu.roll(piece, third * rest, 1) if third else piece
            shared = piece if shared is None else shared + piece
        parts.append(shared)
    filled = sum(part.shape[0] for part in parts)
    if message_rows(block) > filled:
        parts.append(jnp.zeros((message_rows(block) - filled, LANES), F32))
    return jnp.concatenate(parts, axis=0).astype(BF16)


def unfold(message, block):
    whole, rest = divmod(block, LANES)
    groups = []
    for third in range(3):
        first = third * SUBLANES
        parts = [
            message[tile * 3 * SUBLANES + first : tile * 3 * SUBLANES + first + SUBLANES]
            for tile in range(whole)
        ]
        if rest:
            odd = message[whole * 3 * SUBLANES : whole * 3 * SUBLANES + SUBLANES]
            parts.append(pltpu.roll(odd, LANES - third * rest, 1) if third else odd)
        groups.append(jnp.concatenate(parts, axis=1) if len(parts) > 1 else parts[0])
    return groups


def group_points(latent_ref, points):
    rows = latent_ref.shape[1]
    latent = latent_ref[...].astype(F32)
    split = [latent[:, row, :] for row in range(rows)]
    parts = [block[:SUBLANES] for block in split] + [block[SUBLANES:] for block in split]
    points[...] = jnp.concatenate(parts, axis=0)


def pack_kernel(order, latent_ref, *refs):
    *out_refs, points, stage = refs
    columns = stage.shape[0]
    chans = latent_ref.shape[2]
    block = chans // columns
    column, _ = column_and_side()
    group_points(latent_ref, points)
    own = points[...]
    for target in range(columns):
        turned = pltpu.roll(own, chans - target * block, 1) if target else own
        stage[target] = fold(turned[:, : lanes_of(block)], block)
    for apart, ref in zip(order, out_refs):
        ref[...] = stage[column ^ apart]


def cut_kernel(raw_ref, out_ref, points):
    chans = raw_ref.shape[2]
    block = chans // (lax.axis_size("lon") // 2)
    column, _ = column_and_side()
    group_points(raw_ref, points)
    turned = pltpu.roll(points[...], (chans - column * block) % chans, 1)
    out_ref[...] = fold(turned[:, : lanes_of(block)], block)


def column_kernel(order, *refs):
    *in_refs, out_ref = refs
    column, _ = column_and_side()
    for apart, ref in zip(order, in_refs):
        out_ref[column ^ apart] = ref[...]


def apart_kernel(width, step, out_ref):
    lons = out_ref.shape[0]
    side = lax.axis_index("lon") % 2
    source = lax.broadcasted_iota(jnp.int32, out_ref.shape, 0)
    place = lax.broadcasted_iota(jnp.int32, out_ref.shape, 1)
    within = place % step
    apart = source + (place // step) * width + within + (lons - side * width)
    for _ in range(3):
        apart = jnp.where(apart >= lons, apart - lons, apart)
    out_ref[...] = jnp.where(within < width, apart, -1)


def tables_kernel(width, filter_ref, band_ref, apart_ref, table_ref, first):
    bases, lons = filter_ref.shape
    taps, rows, _ = band_ref.shape
    step, places = first.shape[1:]
    columns = places // (2 * step)
    lat = lax.axis_index("lat")
    below = (lat > 0).astype(F32)
    above = (lat < lax.axis_size("lat") - 1).astype(F32)
    inside = [[below, below, 1.0], [1.0, above, above]]
    slots = [[0, 1, 2], [2, 0, 1]]
    profile = filter_ref[...]
    band = band_ref[...].astype(F32)
    apart = apart_ref[...]
    first[...] = jnp.zeros_like(first)
    for lon in range(width):
        pick = (apart == lon).astype(F32).astype(BF16)
        first[:, lon, :] = jnp.dot(profile, pick, preferred_element_type=F32)
    upper = lax.broadcasted_iota(jnp.int32, (SUBLANES, places), 0) < SUBLANES // 2
    count = columns * width
    for basis in range(bases):
        circle = first[basis]
        turned = [
            pltpu.roll(circle, column * 2 * step, 1) if column else circle
            for column in range(columns)
        ]
        last = [block[SUBLANES:] for block in turned]
        pairs = [
            jnp.where(upper, one, pltpu.roll(other, SUBLANES // 2, 0))
            for one, other in zip(last[::2], last[1::2])
        ]
        turned = jnp.concatenate([block[:SUBLANES] for block in turned] + pairs, axis=0)
        at = basis * count
        for row in range(rows):
            for tap in range(taps):
                weight = band[tap, row : row + 1, basis : basis + 1] * inside[row][tap]
                to = slots[row][tap] * places
                table_ref[row, at : at + count, to : to + places] = (weight * turned).astype(BF16)


def squares_kernel(own_ref, mate_ref, squares_ref, padded):
    bases, group, half = own_ref.shape
    lanes = squares_ref.shape[1]
    _, side = column_and_side()
    first = side == 0
    own = own_ref[...].astype(F32)
    mate = mate_ref[...].astype(F32)
    padded[...] = jnp.zeros_like(padded)
    padded[0, :, :group, :half] = jnp.where(first, own, mate)
    padded[1, :, :group, :half] = jnp.where(first, mate, own)
    members = padded.shape[2]
    into = lax.broadcasted_iota(jnp.int32, (lanes, members), 0)
    member = lax.broadcasted_iota(jnp.int32, (lanes, members), 1)
    repeat = (into % group == member).astype(F32).astype(BF16)
    row = lax.broadcasted_iota(jnp.int32, (lanes, lanes), 0)
    column = lax.broadcasted_iota(jnp.int32, (lanes, lanes), 1)
    same = (row // group == column // group) & (row < 2 * half) & (column < 2 * half)
    for basis in range(bases):
        weights = padded[0, basis] + pltpu.roll(padded[1, basis], half, 1)
        repeated = jnp.dot(repeat, weights.astype(BF16), preferred_element_type=F32)
        squares_ref[basis * lanes : (basis + 1) * lanes] = jnp.where(same, repeated, 0.0).astype(
            BF16
        )


def rows_of(message, block, rest):
    groups = unfold(message.astype(F32), block)
    last = (groups[2], pltpu.roll(groups[2], SUBLANES - rest, 0))
    return [jnp.concatenate([groups[row], last[row]], axis=0).astype(BF16) for row in range(2)]


def unpack_kernel(block, width, own_ref, out_ref):
    for at in range(own_ref.shape[0]):
        for row, read in enumerate(rows_of(own_ref[at], block, width - SUBLANES)):
            out_ref[row, at] = read


def own_kernel(block, width, mate, own, table_ref, part_ref, field):
    rows, columns, step, _ = own.shape
    places = field.shape[1]
    side = lax.axis_index("lon") % 2
    for at in range(columns):
        first = pl.multiple_of((2 * at + side) * step, step)
        other = pl.multiple_of((2 * at + 1 - side) * step, step)
        for row, read in enumerate(rows_of(mate[at], block, width - SUBLANES)):
            field[row, pl.ds(first, step)] = own[row, at]
            field[row, pl.ds(other, step)] = read
    for row in range(rows):
        part_ref[row] = jnp.dot(
            table_ref[row, :, 2 * places :], field[row], preferred_element_type=F32
        )


def conv_kernel(
    block,
    width,
    odd_mate,
    odd_own,
    even_own,
    even_mate,
    part_ref,
    table_ref,
    squares_ref,
    *refs,
):
    *out_refs, field, stage = refs
    columns = len(out_refs)
    lanes = squares_ref.shape[1]
    bases = squares_ref.shape[0] // lanes
    rows, _, inner = table_ref.shape
    places = inner // 3
    step = places // (2 * columns)
    half = columns * width
    rest = width - SUBLANES
    column, side = column_and_side()
    odd = lax.axis_index("lat") % 2

    def place(row, at, message):
        for slot, read in enumerate(rows_of(message, block, rest)):
            first = pl.multiple_of(slot * places + at * step, step)
            field[row, pl.ds(first, step)] = read

    for at in range(columns):
        place(1 - odd, 2 * at + side, even_own[at])
        place(1 - odd, 2 * at + 1 - side, even_mate[at])
        place(odd, 2 * at + side, odd_own[at])
        place(odd, 2 * at + 1 - side, odd_mate[at])
    over = [
        jnp.dot(table_ref[row, :, : 2 * places], field[row], preferred_element_type=F32)
        for row in range(rows)
    ]
    mixed = None
    for basis in range(bases):
        taken = slice(basis * half, (basis + 1) * half)
        both = [(over[row][taken] + part_ref[row, taken]).astype(BF16) for row in range(rows)]
        product = jnp.dot(
            jnp.concatenate(both, axis=0)[:, :block],
            squares_ref[basis * lanes : basis * lanes + block],
            preferred_element_type=F32,
        )
        mixed = product if mixed is None else mixed + product
    upper = lax.broadcasted_iota(jnp.int32, (SUBLANES, lanes), 0) < rest
    top, bottom = mixed[:half], mixed[half:]
    for target in range(columns):
        at = target * SUBLANES
        pair = (columns + target // 2) * SUBLANES
        first, second = top[pair : pair + SUBLANES], bottom[pair : pair + SUBLANES]
        if target % 2:
            first = pltpu.roll(first, rest, 0)
        else:
            second = pltpu.roll(second, rest, 0)
        last = jnp.where(upper, first, second)
        points = jnp.concatenate(
            [top[at : at + SUBLANES], bottom[at : at + SUBLANES], last], axis=0
        )
        stage[target] = fold(points, block)
    for apart in range(columns):
        out_refs[apart][...] = stage[column ^ apart]


def summed_block(latent_block, message, block):
    convolved = jnp.concatenate(unfold(message.astype(F32), block), axis=0)
    kept = lax.broadcasted_iota(jnp.int32, convolved.shape, 1) < block
    return jnp.where(kept, latent_block + convolved, 0.0).astype(BF16)


def raised_block(summed, column, block, up_ref):
    count = summed.shape[0]
    ones = jnp.ones((up_to(count, 2 * SUBLANES) - count, block), BF16)
    rows = pl.multiple_of(column * block, block)
    return jnp.dot(
        jnp.concatenate([summed[:, :block], ones], axis=0),
        up_ref[pl.ds(rows, block), :],
        preferred_element_type=F32,
    )


def placed(summed, column, chans, block):
    piece = summed.astype(F32)
    if chans > piece.shape[1]:
        gap = jnp.zeros((piece.shape[0], chans - piece.shape[1]), F32)
        piece = jnp.concatenate([piece, gap], axis=1)
    return pltpu.roll(piece, column * block, 1)


def deviations(summed, mean, block):
    kept = lax.broadcasted_iota(jnp.int32, summed.shape, 1) < block
    return jnp.where(kept, summed.astype(F32) - mean, 0.0)


def over_lanes(values):
    return jnp.sum(values, axis=1, keepdims=True)


def lift_kernel(
    apart,
    own_ref,
    first_ref,
    latent_ref,
    up_ref,
    blocks_ref,
    summed_ref,
    raised_ref,
    stats_ref,
    points,
):
    columns = blocks_ref.shape[0]
    chans = latent_ref.shape[2]
    block = chans // columns
    column, _ = column_and_side()
    group_points(latent_ref, points)
    own = points[...]
    for target in range(columns):
        turned = pltpu.roll(own, chans - target * block, 1) if target else own
        blocks_ref[target] = turned[:, : lanes_of(block)]
    other = column ^ apart
    here = summed_block(blocks_ref[column], own_ref[...], block)
    there = summed_block(blocks_ref[other], first_ref[...], block)
    summed_ref[...] = placed(here, column, chans, block) + placed(there, other, chans, block)
    raised_ref[...] = raised_block(here, column, block, up_ref) + raised_block(
        there, other, block, up_ref
    )
    mean = over_lanes(here.astype(F32) + there.astype(F32)) / (2 * block)
    squares = sum(deviations(summed, mean, block) ** 2 for summed in (here, there))
    stats_ref[0] = jnp.broadcast_to(mean, stats_ref.shape[1:])
    stats_ref[1] = jnp.broadcast_to(over_lanes(squares), stats_ref.shape[1:])


def tail_kernel(order, *refs):
    back_refs = refs[: len(order)]
    blocks_ref, summed_ref, raised_ref, stats_ref, up_ref, down_ref, out_ref = refs[len(order) :]
    width, rows, chans = out_ref.shape
    rest = width - SUBLANES
    block = chans // blocks_ref.shape[0]
    column, _ = column_and_side()
    raised = raised_ref[...]
    early_mean, early_squares = stats_ref[0, :, :1], stats_ref[1, :, :1]
    theirs = []
    away = squares = None
    for apart, ref in zip(order, back_refs):
        other = column ^ apart
        there = summed_block(blocks_ref[other], ref[...], block)
        theirs.append((there, other))
        raised = raised + raised_block(there, other, block, up_ref)
        apart_from = deviations(there, early_mean, block)
        away = apart_from if away is None else away + apart_from
        squares = apart_from**2 if squares is None else squares + apart_from**2
    away, squares = over_lanes(away), over_lanes(squares)
    mean = early_mean + away / chans
    variance = (early_squares + squares - away * away / chans) / chans
    scale = lax.rsqrt(variance + 1e-05)
    count = summed_ref.shape[0]
    hidden = scale * (raised[:count] - mean * raised[count : count + 1])
    hidden = (0.5 * hidden * (1.0 + lax.erf(hidden * 0.5**0.5))).astype(BF16)
    summed = summed_ref[...]
    for there, other in theirs:
        summed = summed + placed(there, other, chans, block)
    result = summed + jnp.dot(hidden, down_ref[...], preferred_element_type=F32)
    for row in range(rows):
        out_ref[:SUBLANES, row, :] = result[row * SUBLANES : (row + 1) * SUBLANES].astype(BF16)
        at = rows * SUBLANES + row * rest
        out_ref[SUBLANES:, row, :] = result[at : at + rest].astype(BF16)


VMEM = pl.BlockSpec(memory_space=pltpu.VMEM)


def call(kernel, name, out_shape, scratch, work, *operands):
    several = isinstance(out_shape, tuple)
    return pl.pallas_call(
        kernel,
        out_shape=out_shape,
        in_specs=[VMEM] * len(operands),
        out_specs=(VMEM,) * len(out_shape) if several else VMEM,
        scratch_shapes=scratch,
        compiler_params=pltpu.CompilerParams(vmem_limit_bytes=24 * 2**20),
        cost_estimate=pl.CostEstimate(flops=work, bytes_accessed=10**6, transcendentals=0),
        name=name,
    )(*operands)


def over_columns(message, count, apart):
    pairs = [(i, ((i // 2) ^ apart) * 2 + i % 2) for i in range(count)]
    return lax.ppermute(message, "lon", pairs) if apart else message


def over_sides(block, count):
    return lax.ppermute(block, "lon", [(i, i ^ 1) for i in range(count)])


def swap(block, count, partner):
    pairs = []
    for lat in range(lax.axis_size("lat")):
        for lon in range(count):
            to_lat, to_lon = partner(lat, lon)
            pairs.append((lat * count + lon, to_lat * count + to_lon))
    return lax.ppermute(block, ("lat", "lon"), pairs)


def odd_pair(lat, lon, other_side, rows):
    to = lat + 1 if lat % 2 else lat - 1
    if 0 <= to < rows:
        return to, lon ^ other_side
    return (lat, lon ^ 1) if other_side else (rows - 1 - lat, lon)


def local(latent, lon_filter, mix_weight, band_weight, offsets, w_up, w_down):
    rows, width, chans = latent.shape
    bases, lons = lon_filter.shape
    half, group = mix_weight.shape[1:]
    taps = band_weight.shape[2]
    count = lons // width
    columns = count // 2
    block = 2 * half
    step = up_to(width, 2 * SUBLANES)
    places = count * step
    lanes = lanes_of(block)
    height = message_rows(block)
    assert rows == 2 and taps == 3 and columns & (columns - 1) == 0
    assert lax.axis_size("lat") % 2 == 0
    assert 2 * width == 3 * SUBLANES and columns * width % (2 * SUBLANES) == 0
    assert 3 * (block % LANES) <= LANES

    far_first = tuple(reversed(range(columns)))
    inward = far_first
    if columns > 3:
        inward = (far_first[1], far_first[0]) + far_first[2:]
    message = jax.ShapeDtypeStruct((height, LANES), BF16)
    messages = (message,) * columns
    stage = pltpu.VMEM((columns, height, LANES), BF16)
    points = pltpu.VMEM((3 * SUBLANES, chans), F32)
    lon_first = jnp.transpose(latent, (1, 0, 2))
    mix_own = jnp.transpose(mix_weight, (0, 2, 1))

    raw = over_columns(lon_first, count, inward[0])
    apart = call(
        functools.partial(apart_kernel, width, step),
        "apart",
        jax.ShapeDtypeStruct((lons, places), jnp.int32),
        [],
        10**9,
    )
    loaded, apart = lax.optimization_barrier((lon_first, apart))
    packed = call(
        functools.partial(pack_kernel, inward[1:]),
        "pack",
        (message,) * (columns - 1),
        [points, stage],
        10**9,
        loaded,
    )
    arrived = [call(cut_kernel, "cut", message, [points], 5 * 10**9, raw)]
    arrived += [over_columns(*pair) for pair in zip(packed, [count] * columns, inward[1:])]
    mix_mate = over_sides(mix_own, count)
    table = call(
        functools.partial(tables_kernel, width),
        "tables",
        jax.ShapeDtypeStruct((rows, bases * columns * width, taps * places), BF16),
        [pltpu.VMEM((bases, step, places), F32)],
        10**6,
        lon_filter,
        jnp.transpose(band_weight, (2, 1, 0)),
        apart,
    )
    gathered = jax.ShapeDtypeStruct((columns, height, LANES), BF16)
    own_side = call(
        functools.partial(column_kernel, inward),
        "join_columns",
        gathered,
        [],
        10**8,
        *arrived,
    )
    lats = lax.axis_size("lat")
    mate_side = swap(own_side, count, lambda lat, lon: (lat, lon ^ 1))
    odd_mate = swap(own_side, count, lambda lat, lon: odd_pair(lat, lon, 1, lats))
    odd_own = swap(own_side, count, lambda lat, lon: odd_pair(lat, lon, 0, lats))
    own_rows = call(
        functools.partial(unpack_kernel, block, width),
        "unpack",
        jax.ShapeDtypeStruct((rows, columns, step, lanes), BF16),
        [],
        10**9,
        own_side,
    )
    even_own = swap(own_side, count, lambda lat, lon: (lat ^ 1, lon))
    even_mate = swap(mate_side, count, lambda lat, lon: (lat ^ 1, lon))
    mix_mate, _ = lax.optimization_barrier((mix_mate, mate_side))
    squares = call(
        squares_kernel,
        "squares",
        jax.ShapeDtypeStruct((bases * lanes, lanes), BF16),
        [pltpu.VMEM((2, bases, up_to(group, 2 * SUBLANES), lanes), F32)],
        3 * 10**8,
        mix_own,
        mix_mate,
    )
    part = call(
        functools.partial(own_kernel, block, width),
        "conv_own",
        jax.ShapeDtypeStruct((rows, bases * columns * width, lanes), F32),
        [pltpu.VMEM((rows, places, lanes), BF16)],
        3 * 10**8,
        mate_side,
        own_rows,
        table,
    )
    mixed = call(
        functools.partial(conv_kernel, block, width),
        "conv",
        messages,
        [
            pltpu.VMEM((rows, 2 * places, lanes), BF16),
            pltpu.VMEM((columns, height, LANES), BF16),
        ],
        10**10,
        odd_mate,
        odd_own,
        even_own,
        even_mate,
        part,
        table,
        squares,
    )
    outward = tuple(reversed(far_first[:-1]))
    back = [over_columns(mixed[apart], count, apart) for apart in outward]
    first = outward.index(far_first[0])
    lifted = call(
        functools.partial(lift_kernel, far_first[0]),
        "lift",
        (
            jax.ShapeDtypeStruct((columns, 3 * SUBLANES, lanes), F32),
            jax.ShapeDtypeStruct((3 * SUBLANES, chans), F32),
            jax.ShapeDtypeStruct((up_to(3 * SUBLANES, 2 * SUBLANES), w_up.shape[1]), F32),
            jax.ShapeDtypeStruct((2, 3 * SUBLANES, LANES), F32),
        ),
        [points],
        10**8,
        mixed[0],
        back[first],
        lon_first,
        w_up,
    )
    result = call(
        functools.partial(tail_kernel, outward[:first] + outward[first + 1 :]),
        "tail",
        jax.ShapeDtypeStruct(lon_first.shape, BF16),
        [],
        10**9,
        *back[:first],
        *back[first + 1 :],
        *lifted,
        w_up,
        w_down,
    )
    return jnp.transpose(result, (1, 0, 2))


def solution(mesh):
    return jax.shard_map(
        local,
        mesh=mesh,
        in_specs=(
            P("lat", "lon", None),
            P(),
            P(None, "lon", None),
            P(None, "lat", None),
            P("lat"),
            P(),
            P(),
        ),
        out_specs=P("lat", "lon", None),
        check_vma=False,
    )
```

```python
import functools

import jax
import jax.numpy as jnp
from jax import lax
from jax.experimental import pallas as pl
from jax.experimental.pallas import tpu as pltpu
from jax.sharding import PartitionSpec as P

F32 = jnp.float32
BF16 = jnp.bfloat16
LANES = 128
SUBLANES = 8


def up_to(size, step):
    return -(-size // step) * step


def column_and_side():
    place = lax.axis_index("lon")
    return place // 2, place % 2


def message_rows(block):
    tiles = block // LANES
    return up_to(3 * SUBLANES * tiles + (SUBLANES if block % LANES else 0), 2 * SUBLANES)


def lanes_of(block):
    return up_to(block, LANES)


def fold(points, block):
    whole, rest = divmod(block, LANES)
    parts = [points[:, tile * LANES : (tile + 1) * LANES] for tile in range(whole)]
    if rest:
        odd = points[:, whole * LANES : (whole + 1) * LANES]
        kept = lax.broadcasted_iota(jnp.int32, (SUBLANES, LANES), 1) < rest
        shared = None
        for third in range(3):
            piece = jnp.where(kept, odd[third * SUBLANES : (third + 1) * SUBLANES], 0.0)
            piece = pltpu.roll(piece, third * rest, 1) if third else piece
            shared = piece if shared is None else shared + piece
        parts.append(shared)
    filled = sum(part.shape[0] for part in parts)
    if message_rows(block) > filled:
        parts.append(jnp.zeros((message_rows(block) - filled, LANES), F32))
    return jnp.concatenate(parts, axis=0).astype(BF16)


def unfold(message, block):
    whole, rest = divmod(block, LANES)
    groups = []
    for third in range(3):
        first = third * SUBLANES
        parts = [
            message[tile * 3 * SUBLANES + first : tile * 3 * SUBLANES + first + SUBLANES]
            for tile in range(whole)
        ]
        if rest:
            odd = message[whole * 3 * SUBLANES : whole * 3 * SUBLANES + SUBLANES]
            parts.append(pltpu.roll(odd, LANES - third * rest, 1) if third else odd)
        groups.append(jnp.concatenate(parts, axis=1) if len(parts) > 1 else parts[0])
    return groups


def group_points(latent_ref, points):
    width, rows, _ = latent_ref.shape
    rest = width - SUBLANES
    for row in range(rows):
        points[row * SUBLANES : (row + 1) * SUBLANES] = latent_ref[:SUBLANES, row, :].astype(F32)
        at = rows * SUBLANES + row * rest
        points[at : at + rest] = latent_ref[SUBLANES:, row, :].astype(F32)


def pack_kernel(order, latent_ref, *refs):
    *out_refs, points, stage = refs
    columns = stage.shape[0]
    chans = latent_ref.shape[2]
    block = chans // columns
    column, _ = column_and_side()
    group_points(latent_ref, points)
    own = points[...]
    for target in range(columns):
        turned = pltpu.roll(own, chans - target * block, 1) if target else own
        stage[target] = fold(turned[:, : lanes_of(block)], block)
    for apart, ref in zip(order, out_refs):
        ref[...] = stage[column ^ apart]


def cut_kernel(raw_ref, out_ref, points):
    chans = raw_ref.shape[2]
    block = chans // (lax.axis_size("lon") // 2)
    column, _ = column_and_side()
    group_points(raw_ref, points)
    turned = pltpu.roll(points[...], (chans - column * block) % chans, 1)
    out_ref[...] = fold(turned[:, : lanes_of(block)], block)


def column_kernel(order, *refs):
    *in_refs, out_ref = refs
    column, _ = column_and_side()
    for apart, ref in zip(order, in_refs):
        out_ref[column ^ apart] = ref[...]


def apart_kernel(width, step, out_ref):
    lons = out_ref.shape[0]
    side = lax.axis_index("lon") % 2
    source = lax.broadcasted_iota(jnp.int32, out_ref.shape, 0)
    place = lax.broadcasted_iota(jnp.int32, out_ref.shape, 1)
    within = place % step
    apart = source + (place // step) * width + within + (lons - side * width)
    for _ in range(3):
        apart = jnp.where(apart >= lons, apart - lons, apart)
    out_ref[...] = jnp.where(within < width, apart, -1)


def tables_kernel(width, filter_ref, band_ref, apart_ref, table_ref, first):
    bases, lons = filter_ref.shape
    taps, rows, _ = band_ref.shape
    step, places = first.shape[1:]
    columns = places // (2 * step)
    lat = lax.axis_index("lat")
    below = (lat > 0).astype(F32)
    above = (lat < lax.axis_size("lat") - 1).astype(F32)
    inside = [[below, below, 1.0], [1.0, above, above]]
    slots = [[0, 1, 2], [2, 0, 1]]
    profile = filter_ref[...]
    band = band_ref[...].astype(F32)
    apart = apart_ref[...]
    first[...] = jnp.zeros_like(first)
    for lon in range(width):
        pick = (apart == lon).astype(F32).astype(BF16)
        first[:, lon, :] = jnp.dot(profile, pick, preferred_element_type=F32)
    upper = lax.broadcasted_iota(jnp.int32, (SUBLANES, places), 0) < SUBLANES // 2
    count = columns * width
    for basis in range(bases):
        circle = first[basis]
        turned = [
            pltpu.roll(circle, column * 2 * step, 1) if column else circle
            for column in range(columns)
        ]
        last = [block[SUBLANES:] for block in turned]
        pairs = [
            jnp.where(upper, one, pltpu.roll(other, SUBLANES // 2, 0))
            for one, other in zip(last[::2], last[1::2])
        ]
        turned = jnp.concatenate([block[:SUBLANES] for block in turned] + pairs, axis=0)
        at = basis * count
        for row in range(rows):
            for tap in range(taps):
                weight = band[tap, row : row + 1, basis : basis + 1] * inside[row][tap]
                to = slots[row][tap] * places
                table_ref[row, at : at + count, to : to + places] = (weight * turned).astype(BF16)


def squares_kernel(own_ref, mate_ref, squares_ref, padded):
    bases, group, half = own_ref.shape
    lanes = squares_ref.shape[1]
    _, side = column_and_side()
    first = side == 0
    own = own_ref[...].astype(F32)
    mate = mate_ref[...].astype(F32)
    padded[...] = jnp.zeros_like(padded)
    padded[0, :, :group, :half] = jnp.where(first, own, mate)
    padded[1, :, :group, :half] = jnp.where(first, mate, own)
    members = padded.shape[2]
    into = lax.broadcasted_iota(jnp.int32, (lanes, members), 0)
    member = lax.broadcasted_iota(jnp.int32, (lanes, members), 1)
    repeat = (into % group == member).astype(F32).astype(BF16)
    row = lax.broadcasted_iota(jnp.int32, (lanes, lanes), 0)
    column = lax.broadcasted_iota(jnp.int32, (lanes, lanes), 1)
    same = (row // group == column // group) & (row < 2 * half) & (column < 2 * half)
    for basis in range(bases):
        weights = padded[0, basis] + pltpu.roll(padded[1, basis], half, 1)
        repeated = jnp.dot(repeat, weights.astype(BF16), preferred_element_type=F32)
        squares_ref[basis * lanes : (basis + 1) * lanes] = jnp.where(same, repeated, 0.0).astype(
            BF16
        )


def rows_of(message, block, rest):
    groups = unfold(message.astype(F32), block)
    last = (groups[2], pltpu.roll(groups[2], SUBLANES - rest, 0))
    return [jnp.concatenate([groups[row], last[row]], axis=0).astype(BF16) for row in range(2)]


def unpack_kernel(block, width, own_ref, out_ref):
    for at in range(own_ref.shape[0]):
        for row, read in enumerate(rows_of(own_ref[at], block, width - SUBLANES)):
            out_ref[row, at] = read


def own_kernel(block, width, mate, own, even, table_ref, part_ref, even_ref, field):
    rows, columns, step, _ = own.shape
    places = field.shape[1]
    side = lax.axis_index("lon") % 2
    for at in range(columns):
        first = pl.multiple_of((2 * at + side) * step, step)
        other = pl.multiple_of((2 * at + 1 - side) * step, step)
        for row, read in enumerate(rows_of(mate[at], block, width - SUBLANES)):
            field[row, pl.ds(first, step)] = own[row, at]
            field[row, pl.ds(other, step)] = read
    for row in range(rows):
        part_ref[row] = jnp.dot(
            table_ref[row, :, 2 * places :], field[row], preferred_element_type=F32
        )
    for at in range(columns):
        for row, read in enumerate(rows_of(even[at], block, width - SUBLANES)):
            even_ref[row, at] = read


def conv_kernel(
    block,
    width,
    odd_mate,
    odd_own,
    even_mate,
    part_ref,
    even_rows,
    table_ref,
    squares_ref,
    *refs,
):
    *out_refs, field, stage = refs
    columns = len(out_refs)
    lanes = squares_ref.shape[1]
    bases = squares_ref.shape[0] // lanes
    rows, _, inner = table_ref.shape
    places = inner // 3
    step = places // (2 * columns)
    half = columns * width
    rest = width - SUBLANES
    column, side = column_and_side()
    odd = lax.axis_index("lat") % 2

    def place(row, at, message):
        for slot, read in enumerate(rows_of(message, block, rest)):
            first = pl.multiple_of(slot * places + at * step, step)
            field[row, pl.ds(first, step)] = read

    for at in range(columns):
        for slot in range(2):
            first = pl.multiple_of(slot * places + (2 * at + side) * step, step)
            field[1 - odd, pl.ds(first, step)] = even_rows[slot, at]
        place(1 - odd, 2 * at + 1 - side, even_mate[at])
        place(odd, 2 * at + side, odd_own[at])
        place(odd, 2 * at + 1 - side, odd_mate[at])
    over = [
        jnp.dot(table_ref[row, :, : 2 * places], field[row], preferred_element_type=F32)
        for row in range(rows)
    ]
    mixed = None
    for basis in range(bases):
        taken = slice(basis * half, (basis + 1) * half)
        both = [(over[row][taken] + part_ref[row, taken]).astype(BF16) for row in range(rows)]
        product = jnp.dot(
            jnp.concatenate(both, axis=0)[:, :block],
            squares_ref[basis * lanes : basis * lanes + block],
            preferred_element_type=F32,
        )
        mixed = product if mixed is None else mixed + product
    upper = lax.broadcasted_iota(jnp.int32, (SUBLANES, lanes), 0) < rest
    top, bottom = mixed[:half], mixed[half:]
    for target in range(columns):
        at = target * SUBLANES
        pair = (columns + target // 2) * SUBLANES
        first, second = top[pair : pair + SUBLANES], bottom[pair : pair + SUBLANES]
        if target % 2:
            first = pltpu.roll(first, rest, 0)
        else:
            second = pltpu.roll(second, rest, 0)
        last = jnp.where(upper, first, second)
        points = jnp.concatenate(
            [top[at : at + SUBLANES], bottom[at : at + SUBLANES], last], axis=0
        )
        stage[target] = fold(points, block)
    for apart in range(columns):
        out_refs[apart][...] = stage[column ^ apart]


def summed_block(latent_block, message, block):
    convolved = jnp.concatenate(unfold(message.astype(F32), block), axis=0)
    kept = lax.broadcasted_iota(jnp.int32, convolved.shape, 1) < block
    return jnp.where(kept, latent_block + convolved, 0.0).astype(BF16)


def raised_block(summed, column, block, up_ref):
    count = summed.shape[0]
    ones = jnp.ones((up_to(count, 2 * SUBLANES) - count, block), BF16)
    rows = pl.multiple_of(column * block, block)
    return jnp.dot(
        jnp.concatenate([summed[:, :block], ones], axis=0),
        up_ref[pl.ds(rows, block), :],
        preferred_element_type=F32,
    )


def placed(summed, column, chans, block):
    piece = summed.astype(F32)
    if chans > piece.shape[1]:
        gap = jnp.zeros((piece.shape[0], chans - piece.shape[1]), F32)
        piece = jnp.concatenate([piece, gap], axis=1)
    return pltpu.roll(piece, column * block, 1)


def deviations(summed, mean, block):
    kept = lax.broadcasted_iota(jnp.int32, summed.shape, 1) < block
    return jnp.where(kept, summed.astype(F32) - mean, 0.0)


def over_lanes(values):
    return jnp.sum(values, axis=1, keepdims=True)


def lift_kernel(
    apart,
    own_ref,
    first_ref,
    latent_ref,
    up_ref,
    blocks_ref,
    summed_ref,
    raised_ref,
    stats_ref,
    points,
):
    columns = blocks_ref.shape[0]
    chans = latent_ref.shape[2]
    block = chans // columns
    column, _ = column_and_side()
    group_points(latent_ref, points)
    own = points[...]
    for target in range(columns):
        turned = pltpu.roll(own, chans - target * block, 1) if target else own
        blocks_ref[target] = turned[:, : lanes_of(block)]
    other = column ^ apart
    here = summed_block(blocks_ref[column], own_ref[...], block)
    there = summed_block(blocks_ref[other], first_ref[...], block)
    summed_ref[...] = placed(here, column, chans, block) + placed(there, other, chans, block)
    raised_ref[...] = raised_block(here, column, block, up_ref) + raised_block(
        there, other, block, up_ref
    )
    mean = over_lanes(here.astype(F32) + there.astype(F32)) / (2 * block)
    squares = sum(deviations(summed, mean, block) ** 2 for summed in (here, there))
    stats_ref[0] = jnp.broadcast_to(mean, stats_ref.shape[1:])
    stats_ref[1] = jnp.broadcast_to(over_lanes(squares), stats_ref.shape[1:])


def tail_kernel(order, *refs):
    back_refs = refs[: len(order)]
    blocks_ref, summed_ref, raised_ref, stats_ref, up_ref, down_ref, out_ref = refs[len(order) :]
    width, rows, chans = out_ref.shape
    rest = width - SUBLANES
    block = chans // blocks_ref.shape[0]
    column, _ = column_and_side()
    raised = raised_ref[...]
    early_mean, early_squares = stats_ref[0, :, :1], stats_ref[1, :, :1]
    theirs = []
    away = squares = None
    for apart, ref in zip(order, back_refs):
        other = column ^ apart
        there = summed_block(blocks_ref[other], ref[...], block)
        theirs.append((there, other))
        raised = raised + raised_block(there, other, block, up_ref)
        apart_from = deviations(there, early_mean, block)
        away = apart_from if away is None else away + apart_from
        squares = apart_from**2 if squares is None else squares + apart_from**2
    away, squares = over_lanes(away), over_lanes(squares)
    mean = early_mean + away / chans
    variance = (early_squares + squares - away * away / chans) / chans
    scale = lax.rsqrt(variance + 1e-05)
    count = summed_ref.shape[0]
    hidden = scale * (raised[:count] - mean * raised[count : count + 1])
    hidden = (0.5 * hidden * (1.0 + lax.erf(hidden * 0.5**0.5))).astype(BF16)
    summed = summed_ref[...]
    for there, other in theirs:
        summed = summed + placed(there, other, chans, block)
    result = summed + jnp.dot(hidden, down_ref[...], preferred_element_type=F32)
    for row in range(rows):
        out_ref[:SUBLANES, row, :] = result[row * SUBLANES : (row + 1) * SUBLANES].astype(BF16)
        at = rows * SUBLANES + row * rest
        out_ref[SUBLANES:, row, :] = result[at : at + rest].astype(BF16)


VMEM = pl.BlockSpec(memory_space=pltpu.VMEM)


def call(kernel, name, out_shape, scratch, work, *operands):
    several = isinstance(out_shape, tuple)
    return pl.pallas_call(
        kernel,
        out_shape=out_shape,
        in_specs=[VMEM] * len(operands),
        out_specs=(VMEM,) * len(out_shape) if several else VMEM,
        scratch_shapes=scratch,
        compiler_params=pltpu.CompilerParams(vmem_limit_bytes=24 * 2**20),
        cost_estimate=pl.CostEstimate(flops=work, bytes_accessed=10**6, transcendentals=0),
        name=name,
    )(*operands)


def over_columns(message, count, apart):
    pairs = [(i, ((i // 2) ^ apart) * 2 + i % 2) for i in range(count)]
    return lax.ppermute(message, "lon", pairs) if apart else message


def over_sides(block, count):
    return lax.ppermute(block, "lon", [(i, i ^ 1) for i in range(count)])


def swap(block, count, partner):
    pairs = []
    for lat in range(lax.axis_size("lat")):
        for lon in range(count):
            to_lat, to_lon = partner(lat, lon)
            pairs.append((lat * count + lon, to_lat * count + to_lon))
    return lax.ppermute(block, ("lat", "lon"), pairs)


def odd_pair(lat, lon, other_side, rows):
    to = lat + 1 if lat % 2 else lat - 1
    if 0 <= to < rows:
        return to, lon ^ other_side
    return (lat, lon ^ 1) if other_side else (rows - 1 - lat, lon)


def local(latent, lon_filter, mix_weight, band_weight, offsets, w_up, w_down):
    rows, width, chans = latent.shape
    bases, lons = lon_filter.shape
    half, group = mix_weight.shape[1:]
    taps = band_weight.shape[2]
    count = lons // width
    columns = count // 2
    block = 2 * half
    step = up_to(width, 2 * SUBLANES)
    places = count * step
    lanes = lanes_of(block)
    height = message_rows(block)
    assert rows == 2 and taps == 3 and columns & (columns - 1) == 0
    assert lax.axis_size("lat") % 2 == 0
    assert 2 * width == 3 * SUBLANES and columns * width % (2 * SUBLANES) == 0
    assert 3 * (block % LANES) <= LANES

    far_first = tuple(reversed(range(columns)))
    inward = far_first
    if columns > 3:
        inward = (far_first[1], far_first[0]) + far_first[2:]
    message = jax.ShapeDtypeStruct((height, LANES), BF16)
    messages = (message,) * columns
    stage = pltpu.VMEM((columns, height, LANES), BF16)
    points = pltpu.VMEM((3 * SUBLANES, chans), F32)
    lon_first = jnp.transpose(latent, (1, 0, 2))
    mix_own = jnp.transpose(mix_weight, (0, 2, 1))

    raw = over_columns(lon_first, count, inward[0])
    apart = call(
        functools.partial(apart_kernel, width, step),
        "apart",
        jax.ShapeDtypeStruct((lons, places), jnp.int32),
        [],
        10**9,
    )
    loaded, apart = lax.optimization_barrier((lon_first, apart))
    packed = call(
        functools.partial(pack_kernel, inward[1:]),
        "pack",
        (message,) * (columns - 1),
        [points, stage],
        10**9,
        loaded,
    )
    arrived = [call(cut_kernel, "cut", message, [points], 5 * 10**9, raw)]
    arrived += [over_columns(*pair) for pair in zip(packed, [count] * columns, inward[1:])]
    mix_mate = over_sides(mix_own, count)
    table = call(
        functools.partial(tables_kernel, width),
        "tables",
        jax.ShapeDtypeStruct((rows, bases * columns * width, taps * places), BF16),
        [pltpu.VMEM((bases, step, places), F32)],
        10**6,
        lon_filter,
        jnp.transpose(band_weight, (2, 1, 0)),
        apart,
    )
    gathered = jax.ShapeDtypeStruct((columns, height, LANES), BF16)
    own_side = call(
        functools.partial(column_kernel, inward),
        "join_columns",
        gathered,
        [],
        10**8,
        *arrived,
    )
    lats = lax.axis_size("lat")
    mate_side = swap(own_side, count, lambda lat, lon: (lat, lon ^ 1))
    odd_mate = swap(own_side, count, lambda lat, lon: odd_pair(lat, lon, 1, lats))
    odd_own = swap(own_side, count, lambda lat, lon: odd_pair(lat, lon, 0, lats))
    own_rows = call(
        functools.partial(unpack_kernel, block, width),
        "unpack",
        jax.ShapeDtypeStruct((rows, columns, step, lanes), BF16),
        [],
        10**9,
        own_side,
    )
    even_own = swap(own_side, count, lambda lat, lon: (lat ^ 1, lon))
    even_mate = swap(mate_side, count, lambda lat, lon: (lat ^ 1, lon))
    mix_mate, _ = lax.optimization_barrier((mix_mate, mate_side))
    squares = call(
        squares_kernel,
        "squares",
        jax.ShapeDtypeStruct((bases * lanes, lanes), BF16),
        [pltpu.VMEM((2, bases, up_to(group, 2 * SUBLANES), lanes), F32)],
        3 * 10**8,
        mix_own,
        mix_mate,
    )
    part = call(
        functools.partial(own_kernel, block, width),
        "conv_own",
        (
            jax.ShapeDtypeStruct((rows, bases * columns * width, lanes), F32),
            jax.ShapeDtypeStruct((rows, columns, step, lanes), BF16),
        ),
        [pltpu.VMEM((rows, places, lanes), BF16)],
        3 * 10**8,
        mate_side,
        own_rows,
        even_own,
        table,
    )
    mixed = call(
        functools.partial(conv_kernel, block, width),
        "conv",
        messages,
        [
            pltpu.VMEM((rows, 2 * places, lanes), BF16),
            pltpu.VMEM((columns, height, LANES), BF16),
        ],
        10**10,
        odd_mate,
        odd_own,
        even_mate,
        *part,
        table,
        squares,
    )
    outward = tuple(reversed(far_first[:-1]))
    back = [over_columns(mixed[apart], count, apart) for apart in outward]
    first = outward.index(far_first[0])
    lifted = call(
        functools.partial(lift_kernel, far_first[0]),
        "lift",
        (
            jax.ShapeDtypeStruct((columns, 3 * SUBLANES, lanes), F32),
            jax.ShapeDtypeStruct((3 * SUBLANES, chans), F32),
            jax.ShapeDtypeStruct((up_to(3 * SUBLANES, 2 * SUBLANES), w_up.shape[1]), F32),
            jax.ShapeDtypeStruct((2, 3 * SUBLANES, LANES), F32),
        ),
        [points],
        10**8,
        mixed[0],
        back[first],
        lon_first,
        w_up,
    )
    result = call(
        functools.partial(tail_kernel, outward[:first] + outward[first + 1 :]),
        "tail",
        jax.ShapeDtypeStruct(lon_first.shape, BF16),
        [],
        10**9,
        *back[:first],
        *back[first + 1 :],
        *lifted,
        w_up,
        w_down,
    )
    return jnp.transpose(result, (1, 0, 2))


def solution(mesh):
    return jax.shard_map(
        local,
        mesh=mesh,
        in_specs=(
            P("lat", "lon", None),
            P(),
            P(None, "lon", None),
            P(None, "lat", None),
            P("lat"),
            P(),
            P(),
        ),
        out_specs=P("lat", "lon", None),
        check_vma=False,
    )
```

```python
import functools

import jax
import jax.numpy as jnp
from jax import lax
from jax.experimental import pallas as pl
from jax.experimental.pallas import tpu as pltpu
from jax.sharding import PartitionSpec as P

F32 = jnp.float32
BF16 = jnp.bfloat16
LANES = 128
SUBLANES = 8


def up_to(size, step):
    return -(-size // step) * step


def column_and_side():
    place = lax.axis_index("lon")
    return place // 2, place % 2


def message_rows(block):
    tiles = block // LANES
    return up_to(3 * SUBLANES * tiles + (SUBLANES if block % LANES else 0), 2 * SUBLANES)


def lanes_of(block):
    return up_to(block, LANES)


def fold(points, block):
    whole, rest = divmod(block, LANES)
    parts = [points[:, tile * LANES : (tile + 1) * LANES] for tile in range(whole)]
    if rest:
        odd = points[:, whole * LANES : (whole + 1) * LANES]
        kept = lax.broadcasted_iota(jnp.int32, (SUBLANES, LANES), 1) < rest
        shared = None
        for third in range(3):
            piece = jnp.where(kept, odd[third * SUBLANES : (third + 1) * SUBLANES], 0.0)
            piece = pltpu.roll(piece, third * rest, 1) if third else piece
            shared = piece if shared is None else shared + piece
        parts.append(shared)
    filled = sum(part.shape[0] for part in parts)
    if message_rows(block) > filled:
        parts.append(jnp.zeros((message_rows(block) - filled, LANES), F32))
    return jnp.concatenate(parts, axis=0).astype(BF16)


def unfold(message, block):
    whole, rest = divmod(block, LANES)
    groups = []
    for third in range(3):
        first = third * SUBLANES
        parts = [
            message[tile * 3 * SUBLANES + first : tile * 3 * SUBLANES + first + SUBLANES]
            for tile in range(whole)
        ]
        if rest:
            odd = message[whole * 3 * SUBLANES : whole * 3 * SUBLANES + SUBLANES]
            parts.append(pltpu.roll(odd, LANES - third * rest, 1) if third else odd)
        groups.append(jnp.concatenate(parts, axis=1) if len(parts) > 1 else parts[0])
    return groups


def group_points(latent_ref, points):
    width, rows, _ = latent_ref.shape
    rest = width - SUBLANES
    for row in range(rows):
        points[row * SUBLANES : (row + 1) * SUBLANES] = latent_ref[:SUBLANES, row, :].astype(F32)
        at = rows * SUBLANES + row * rest
        points[at : at + rest] = latent_ref[SUBLANES:, row, :].astype(F32)


def pack_kernel(order, latent_ref, *refs):
    *out_refs, points, stage = refs
    columns = stage.shape[0]
    chans = latent_ref.shape[2]
    block = chans // columns
    column, _ = column_and_side()
    group_points(latent_ref, points)
    own = points[...]
    for target in range(columns):
        turned = pltpu.roll(own, chans - target * block, 1) if target else own
        stage[target] = fold(turned[:, : lanes_of(block)], block)
    for apart, ref in zip(order, out_refs):
        ref[...] = stage[column ^ apart]


def cut_kernel(raw_ref, out_ref, points):
    chans = raw_ref.shape[2]
    block = chans // (lax.axis_size("lon") // 2)
    column, _ = column_and_side()
    group_points(raw_ref, points)
    turned = pltpu.roll(points[...], (chans - column * block) % chans, 1)
    out_ref[...] = fold(turned[:, : lanes_of(block)], block)


def column_kernel(order, *refs):
    *in_refs, out_ref = refs
    column, _ = column_and_side()
    for apart, ref in zip(order, in_refs):
        out_ref[column ^ apart] = ref[...]


def apart_kernel(width, step, out_ref):
    lons = out_ref.shape[0]
    side = lax.axis_index("lon") % 2
    source = lax.broadcasted_iota(jnp.int32, out_ref.shape, 0)
    place = lax.broadcasted_iota(jnp.int32, out_ref.shape, 1)
    within = place % step
    apart = source + (place // step) * width + within + (lons - side * width)
    for _ in range(3):
        apart = jnp.where(apart >= lons, apart - lons, apart)
    out_ref[...] = jnp.where(within < width, apart, -1)


def tables_kernel(width, filter_ref, band_ref, apart_ref, table_ref, first):
    bases, lons = filter_ref.shape
    taps, rows, _ = band_ref.shape
    step, places = first.shape[1:]
    columns = places // (2 * step)
    lat = lax.axis_index("lat")
    below = (lat > 0).astype(F32)
    above = (lat < lax.axis_size("lat") - 1).astype(F32)
    inside = [[below, below, 1.0], [1.0, above, above]]
    slots = [[0, 1, 2], [2, 0, 1]]
    profile = filter_ref[...]
    band = band_ref[...].astype(F32)
    apart = apart_ref[...]
    first[...] = jnp.zeros_like(first)
    for lon in range(width):
        pick = (apart == lon).astype(F32).astype(BF16)
        first[:, lon, :] = jnp.dot(profile, pick, preferred_element_type=F32)
    upper = lax.broadcasted_iota(jnp.int32, (SUBLANES, places), 0) < SUBLANES // 2
    count = columns * width
    for basis in range(bases):
        circle = first[basis]
        turned = [
            pltpu.roll(circle, column * 2 * step, 1) if column else circle
            for column in range(columns)
        ]
        last = [block[SUBLANES:] for block in turned]
        pairs = [
            jnp.where(upper, one, pltpu.roll(other, SUBLANES // 2, 0))
            for one, other in zip(last[::2], last[1::2])
        ]
        turned = jnp.concatenate([block[:SUBLANES] for block in turned] + pairs, axis=0)
        at = basis * count
        for row in range(rows):
            for tap in range(taps):
                weight = band[tap, row : row + 1, basis : basis + 1] * inside[row][tap]
                to = slots[row][tap] * places
                table_ref[row, at : at + count, to : to + places] = (weight * turned).astype(BF16)


def squares_kernel(own_ref, mate_ref, squares_ref, padded):
    bases, group, half = own_ref.shape
    lanes = squares_ref.shape[1]
    _, side = column_and_side()
    first = side == 0
    own = own_ref[...].astype(F32)
    mate = mate_ref[...].astype(F32)
    padded[...] = jnp.zeros_like(padded)
    padded[0, :, :group, :half] = jnp.where(first, own, mate)
    padded[1, :, :group, :half] = jnp.where(first, mate, own)
    members = padded.shape[2]
    into = lax.broadcasted_iota(jnp.int32, (lanes, members), 0)
    member = lax.broadcasted_iota(jnp.int32, (lanes, members), 1)
    repeat = (into % group == member).astype(F32).astype(BF16)
    row = lax.broadcasted_iota(jnp.int32, (lanes, lanes), 0)
    column = lax.broadcasted_iota(jnp.int32, (lanes, lanes), 1)
    same = (row // group == column // group) & (row < 2 * half) & (column < 2 * half)
    for basis in range(bases):
        weights = padded[0, basis] + pltpu.roll(padded[1, basis], half, 1)
        repeated = jnp.dot(repeat, weights.astype(BF16), preferred_element_type=F32)
        squares_ref[basis * lanes : (basis + 1) * lanes] = jnp.where(same, repeated, 0.0).astype(
            BF16
        )


def rows_of(message, block, rest):
    groups = unfold(message.astype(F32), block)
    last = (groups[2], pltpu.roll(groups[2], SUBLANES - rest, 0))
    return [jnp.concatenate([groups[row], last[row]], axis=0).astype(BF16) for row in range(2)]


def unpack_kernel(block, width, own_ref, out_ref):
    for at in range(own_ref.shape[0]):
        for row, read in enumerate(rows_of(own_ref[at], block, width - SUBLANES)):
            out_ref[row, at] = read


def own_kernel(block, width, mate, own, even, table_ref, part_ref, even_ref, field):
    rows, columns, step, _ = own.shape
    places = field.shape[1]
    side = lax.axis_index("lon") % 2
    for at in range(columns):
        first = pl.multiple_of((2 * at + side) * step, step)
        other = pl.multiple_of((2 * at + 1 - side) * step, step)
        for row, read in enumerate(rows_of(mate[at], block, width - SUBLANES)):
            field[row, pl.ds(first, step)] = own[row, at]
            field[row, pl.ds(other, step)] = read
    for row in range(rows):
        part_ref[row] = jnp.dot(
            table_ref[row, :, 2 * places :], field[row], preferred_element_type=F32
        )
    for at in range(columns):
        for row, read in enumerate(rows_of(even[at], block, width - SUBLANES)):
            even_ref[row, at] = read


def conv_kernel(
    block,
    width,
    odd_mate,
    odd_own,
    even_mate,
    part_ref,
    even_rows,
    table_ref,
    squares_ref,
    *refs,
):
    *out_refs, field, stage = refs
    columns = len(out_refs)
    lanes = squares_ref.shape[1]
    bases = squares_ref.shape[0] // lanes
    rows, _, inner = table_ref.shape
    places = inner // 3
    step = places // (2 * columns)
    half = columns * width
    rest = width - SUBLANES
    column, side = column_and_side()
    odd = lax.axis_index("lat") % 2

    def place(row, at, message):
        for slot, read in enumerate(rows_of(message, block, rest)):
            first = pl.multiple_of(slot * places + at * step, step)
            field[row, pl.ds(first, step)] = read

    for at in range(columns):
        for slot in range(2):
            first = pl.multiple_of(slot * places + (2 * at + side) * step, step)
            field[1 - odd, pl.ds(first, step)] = even_rows[slot, at]
        place(1 - odd, 2 * at + 1 - side, even_mate[at])
        place(odd, 2 * at + side, odd_own[at])
        place(odd, 2 * at + 1 - side, odd_mate[at])
    over = [
        jnp.dot(table_ref[row, :, : 2 * places], field[row], preferred_element_type=F32)
        for row in range(rows)
    ]
    mixed = None
    for basis in range(bases):
        taken = slice(basis * half, (basis + 1) * half)
        both = [(over[row][taken] + part_ref[row, taken]).astype(BF16) for row in range(rows)]
        product = jnp.dot(
            jnp.concatenate(both, axis=0)[:, :block],
            squares_ref[basis * lanes : basis * lanes + block],
            preferred_element_type=F32,
        )
        mixed = product if mixed is None else mixed + product
    upper = lax.broadcasted_iota(jnp.int32, (SUBLANES, lanes), 0) < rest
    top, bottom = mixed[:half], mixed[half:]
    for target in range(columns):
        at = target * SUBLANES
        pair = (columns + target // 2) * SUBLANES
        first, second = top[pair : pair + SUBLANES], bottom[pair : pair + SUBLANES]
        if target % 2:
            first = pltpu.roll(first, rest, 0)
        else:
            second = pltpu.roll(second, rest, 0)
        last = jnp.where(upper, first, second)
        points = jnp.concatenate(
            [top[at : at + SUBLANES], bottom[at : at + SUBLANES], last], axis=0
        )
        stage[target] = fold(points, block)
    for apart in range(columns):
        out_refs[apart][...] = stage[column ^ apart]


def summed_block(latent_block, message, block):
    convolved = jnp.concatenate(unfold(message.astype(F32), block), axis=0)
    kept = lax.broadcasted_iota(jnp.int32, convolved.shape, 1) < block
    return jnp.where(kept, latent_block + convolved, 0.0).astype(BF16)


def raised_block(summed, column, block, up_ref):
    count = summed.shape[0]
    ones = jnp.ones((up_to(count, 2 * SUBLANES) - count, block), BF16)
    rows = pl.multiple_of(column * block, block)
    return jnp.dot(
        jnp.concatenate([summed[:, :block], ones], axis=0),
        up_ref[pl.ds(rows, block), :],
        preferred_element_type=F32,
    )


def placed(summed, column, chans, block):
    piece = summed.astype(F32)
    if chans > piece.shape[1]:
        gap = jnp.zeros((piece.shape[0], chans - piece.shape[1]), F32)
        piece = jnp.concatenate([piece, gap], axis=1)
    return pltpu.roll(piece, column * block, 1)


def deviations(summed, mean, block):
    kept = lax.broadcasted_iota(jnp.int32, summed.shape, 1) < block
    return jnp.where(kept, summed.astype(F32) - mean, 0.0)


def over_lanes(values):
    return jnp.sum(values, axis=1, keepdims=True)


def lift_kernel(
    apart,
    own_ref,
    first_ref,
    latent_ref,
    up_ref,
    blocks_ref,
    summed_ref,
    raised_ref,
    stats_ref,
    points,
):
    columns = blocks_ref.shape[0]
    chans = latent_ref.shape[2]
    block = chans // columns
    column, _ = column_and_side()
    group_points(latent_ref, points)
    own = points[...]
    for target in range(columns):
        turned = pltpu.roll(own, chans - target * block, 1) if target else own
        blocks_ref[target] = turned[:, : lanes_of(block)]
    other = column ^ apart
    here = summed_block(blocks_ref[column], own_ref[...], block)
    there = summed_block(blocks_ref[other], first_ref[...], block)
    summed_ref[...] = placed(here, column, chans, block) + placed(there, other, chans, block)
    raised_ref[...] = raised_block(here, column, block, up_ref) + raised_block(
        there, other, block, up_ref
    )
    mean = over_lanes(here.astype(F32) + there.astype(F32)) / (2 * block)
    squares = sum(deviations(summed, mean, block) ** 2 for summed in (here, there))
    stats_ref[0] = jnp.broadcast_to(mean, stats_ref.shape[1:])
    stats_ref[1] = jnp.broadcast_to(over_lanes(squares), stats_ref.shape[1:])


def tail_kernel(order, *refs):
    back_refs = refs[: len(order)]
    blocks_ref, summed_ref, raised_ref, stats_ref, up_ref, down_ref, out_ref = refs[len(order) :]
    width, rows, chans = out_ref.shape
    rest = width - SUBLANES
    block = chans // blocks_ref.shape[0]
    column, _ = column_and_side()
    raised = raised_ref[...]
    early_mean, early_squares = stats_ref[0, :, :1], stats_ref[1, :, :1]
    theirs = []
    away = squares = None
    for apart, ref in zip(order, back_refs):
        other = column ^ apart
        there = summed_block(blocks_ref[other], ref[...], block)
        theirs.append((there, other))
        raised = raised + raised_block(there, other, block, up_ref)
        apart_from = deviations(there, early_mean, block)
        away = apart_from if away is None else away + apart_from
        squares = apart_from**2 if squares is None else squares + apart_from**2
    away, squares = over_lanes(away), over_lanes(squares)
    mean = early_mean + away / chans
    variance = (early_squares + squares - away * away / chans) / chans
    scale = lax.rsqrt(variance + 1e-05)
    count = summed_ref.shape[0]
    product = None
    units = raised.shape[1]
    for start in range(0, units, 2 * LANES):
        taken = slice(start, min(start + 2 * LANES, units))
        hidden = scale * (raised[:count, taken] - mean * raised[count : count + 1, taken])
        hidden = (0.5 * hidden * (1.0 + lax.erf(hidden * 0.5**0.5))).astype(BF16)
        part = jnp.dot(hidden, down_ref[taken], preferred_element_type=F32)
        product = part if product is None else product + part
    summed = summed_ref[...]
    for there, other in theirs:
        summed = summed + placed(there, other, chans, block)
    result = summed + product
    for row in range(rows):
        out_ref[:SUBLANES, row, :] = result[row * SUBLANES : (row + 1) * SUBLANES].astype(BF16)
        at = rows * SUBLANES + row * rest
        out_ref[SUBLANES:, row, :] = result[at : at + rest].astype(BF16)


VMEM = pl.BlockSpec(memory_space=pltpu.VMEM)


def call(kernel, name, out_shape, scratch, work, *operands):
    several = isinstance(out_shape, tuple)
    return pl.pallas_call(
        kernel,
        out_shape=out_shape,
        in_specs=[VMEM] * len(operands),
        out_specs=(VMEM,) * len(out_shape) if several else VMEM,
        scratch_shapes=scratch,
        compiler_params=pltpu.CompilerParams(vmem_limit_bytes=24 * 2**20),
        cost_estimate=pl.CostEstimate(flops=work, bytes_accessed=10**6, transcendentals=0),
        name=name,
    )(*operands)


def over_columns(message, count, apart):
    pairs = [(i, ((i // 2) ^ apart) * 2 + i % 2) for i in range(count)]
    return lax.ppermute(message, "lon", pairs) if apart else message


def over_sides(block, count):
    return lax.ppermute(block, "lon", [(i, i ^ 1) for i in range(count)])


def swap(block, count, partner):
    pairs = []
    for lat in range(lax.axis_size("lat")):
        for lon in range(count):
            to_lat, to_lon = partner(lat, lon)
            pairs.append((lat * count + lon, to_lat * count + to_lon))
    return lax.ppermute(block, ("lat", "lon"), pairs)


def odd_pair(lat, lon, other_side, rows):
    to = lat + 1 if lat % 2 else lat - 1
    if 0 <= to < rows:
        return to, lon ^ other_side
    return (lat, lon ^ 1) if other_side else (rows - 1 - lat, lon)


def local(latent, lon_filter, mix_weight, band_weight, offsets, w_up, w_down):
    rows, width, chans = latent.shape
    bases, lons = lon_filter.shape
    half, group = mix_weight.shape[1:]
    taps = band_weight.shape[2]
    count = lons // width
    columns = count // 2
    block = 2 * half
    step = up_to(width, 2 * SUBLANES)
    places = count * step
    lanes = lanes_of(block)
    height = message_rows(block)
    assert rows == 2 and taps == 3 and columns & (columns - 1) == 0
    assert lax.axis_size("lat") % 2 == 0
    assert 2 * width == 3 * SUBLANES and columns * width % (2 * SUBLANES) == 0
    assert 3 * (block % LANES) <= LANES

    far_first = tuple(reversed(range(columns)))
    inward = far_first
    if columns > 3:
        inward = (far_first[1], far_first[0]) + far_first[2:]
    message = jax.ShapeDtypeStruct((height, LANES), BF16)
    messages = (message,) * columns
    stage = pltpu.VMEM((columns, height, LANES), BF16)
    points = pltpu.VMEM((3 * SUBLANES, chans), F32)
    lon_first = jnp.transpose(latent, (1, 0, 2))
    mix_own = jnp.transpose(mix_weight, (0, 2, 1))

    raw = over_columns(lon_first, count, inward[0])
    apart = call(
        functools.partial(apart_kernel, width, step),
        "apart",
        jax.ShapeDtypeStruct((lons, places), jnp.int32),
        [],
        10**9,
    )
    loaded, apart = lax.optimization_barrier((lon_first, apart))
    packed = call(
        functools.partial(pack_kernel, inward[1:]),
        "pack",
        (message,) * (columns - 1),
        [points, stage],
        10**9,
        loaded,
    )
    arrived = [call(cut_kernel, "cut", message, [points], 5 * 10**9, raw)]
    arrived += [over_columns(*pair) for pair in zip(packed, [count] * columns, inward[1:])]
    mix_mate = over_sides(mix_own, count)
    table = call(
        functools.partial(tables_kernel, width),
        "tables",
        jax.ShapeDtypeStruct((rows, bases * columns * width, taps * places), BF16),
        [pltpu.VMEM((bases, step, places), F32)],
        10**6,
        lon_filter,
        jnp.transpose(band_weight, (2, 1, 0)),
        apart,
    )
    gathered = jax.ShapeDtypeStruct((columns, height, LANES), BF16)
    own_side = call(
        functools.partial(column_kernel, inward),
        "join_columns",
        gathered,
        [],
        10**8,
        *arrived,
    )
    lats = lax.axis_size("lat")
    mate_side = swap(own_side, count, lambda lat, lon: (lat, lon ^ 1))
    odd_mate = swap(own_side, count, lambda lat, lon: odd_pair(lat, lon, 1, lats))
    odd_own = swap(own_side, count, lambda lat, lon: odd_pair(lat, lon, 0, lats))
    own_rows = call(
        functools.partial(unpack_kernel, block, width),
        "unpack",
        jax.ShapeDtypeStruct((rows, columns, step, lanes), BF16),
        [],
        10**9,
        own_side,
    )
    even_own = swap(own_side, count, lambda lat, lon: (lat ^ 1, lon))
    even_mate = swap(mate_side, count, lambda lat, lon: (lat ^ 1, lon))
    mix_mate, _ = lax.optimization_barrier((mix_mate, mate_side))
    squares = call(
        squares_kernel,
        "squares",
        jax.ShapeDtypeStruct((bases * lanes, lanes), BF16),
        [pltpu.VMEM((2, bases, up_to(group, 2 * SUBLANES), lanes), F32)],
        3 * 10**8,
        mix_own,
        mix_mate,
    )
    part = call(
        functools.partial(own_kernel, block, width),
        "conv_own",
        (
            jax.ShapeDtypeStruct((rows, bases * columns * width, lanes), F32),
            jax.ShapeDtypeStruct((rows, columns, step, lanes), BF16),
        ),
        [pltpu.VMEM((rows, places, lanes), BF16)],
        3 * 10**8,
        mate_side,
        own_rows,
        even_own,
        table,
    )
    mixed = call(
        functools.partial(conv_kernel, block, width),
        "conv",
        messages,
        [
            pltpu.VMEM((rows, 2 * places, lanes), BF16),
            pltpu.VMEM((columns, height, LANES), BF16),
        ],
        10**10,
        odd_mate,
        odd_own,
        even_mate,
        *part,
        table,
        squares,
    )
    outward = tuple(reversed(far_first[:-1]))
    back = [over_columns(mixed[apart], count, apart) for apart in outward]
    first = outward.index(far_first[0])
    lifted = call(
        functools.partial(lift_kernel, far_first[0]),
        "lift",
        (
            jax.ShapeDtypeStruct((columns, 3 * SUBLANES, lanes), F32),
            jax.ShapeDtypeStruct((3 * SUBLANES, chans), F32),
            jax.ShapeDtypeStruct((up_to(3 * SUBLANES, 2 * SUBLANES), w_up.shape[1]), F32),
            jax.ShapeDtypeStruct((2, 3 * SUBLANES, LANES), F32),
        ),
        [points],
        10**8,
        mixed[0],
        back[first],
        lon_first,
        w_up,
    )
    result = call(
        functools.partial(tail_kernel, outward[:first] + outward[first + 1 :]),
        "tail",
        jax.ShapeDtypeStruct(lon_first.shape, BF16),
        [],
        10**9,
        *back[:first],
        *back[first + 1 :],
        *lifted,
        w_up,
        w_down,
    )
    return jnp.transpose(result, (1, 0, 2))


def solution(mesh):
    return jax.shard_map(
        local,
        mesh=mesh,
        in_specs=(
            P("lat", "lon", None),
            P(),
            P(None, "lon", None),
            P(None, "lat", None),
            P("lat"),
            P(),
            P(),
        ),
        out_specs=P("lat", "lon", None),
        check_vma=False,
    )
```

```python
import functools

import jax
import jax.numpy as jnp
from jax import lax
from jax.experimental import pallas as pl
from jax.experimental.pallas import tpu as pltpu
from jax.sharding import PartitionSpec as P

F32 = jnp.float32
BF16 = jnp.bfloat16
LANES = 128
SUBLANES = 8


def up_to(size, step):
    return -(-size // step) * step


def column_and_side():
    place = lax.axis_index("lon")
    return place // 2, place % 2


def message_rows(block):
    tiles = block // LANES
    return up_to(3 * SUBLANES * tiles + (SUBLANES if block % LANES else 0), 2 * SUBLANES)


def lanes_of(block):
    return up_to(block, LANES)


def fold(points, block):
    whole, rest = divmod(block, LANES)
    parts = [points[:, tile * LANES : (tile + 1) * LANES] for tile in range(whole)]
    if rest:
        odd = points[:, whole * LANES : (whole + 1) * LANES]
        kept = lax.broadcasted_iota(jnp.int32, (SUBLANES, LANES), 1) < rest
        shared = None
        for third in range(3):
            piece = jnp.where(kept, odd[third * SUBLANES : (third + 1) * SUBLANES], 0.0)
            piece = pltpu.roll(piece, third * rest, 1) if third else piece
            shared = piece if shared is None else shared + piece
        parts.append(shared)
    filled = sum(part.shape[0] for part in parts)
    if message_rows(block) > filled:
        parts.append(jnp.zeros((message_rows(block) - filled, LANES), F32))
    return jnp.concatenate(parts, axis=0).astype(BF16)


def unfold(message, block):
    whole, rest = divmod(block, LANES)
    groups = []
    for third in range(3):
        first = third * SUBLANES
        parts = [
            message[tile * 3 * SUBLANES + first : tile * 3 * SUBLANES + first + SUBLANES]
            for tile in range(whole)
        ]
        if rest:
            odd = message[whole * 3 * SUBLANES : whole * 3 * SUBLANES + SUBLANES]
            parts.append(pltpu.roll(odd, LANES - third * rest, 1) if third else odd)
        groups.append(jnp.concatenate(parts, axis=1) if len(parts) > 1 else parts[0])
    return groups


def group_points(latent_ref, points):
    width, rows, _ = latent_ref.shape
    rest = width - SUBLANES
    for row in range(rows):
        points[row * SUBLANES : (row + 1) * SUBLANES] = latent_ref[:SUBLANES, row, :].astype(F32)
        at = rows * SUBLANES + row * rest
        points[at : at + rest] = latent_ref[SUBLANES:, row, :].astype(F32)


def pack_kernel(order, latent_ref, *refs):
    *out_refs, points, stage = refs
    columns = stage.shape[0]
    chans = latent_ref.shape[2]
    block = chans // columns
    column, _ = column_and_side()
    group_points(latent_ref, points)
    own = points[...]
    for target in range(columns):
        turned = pltpu.roll(own, chans - target * block, 1) if target else own
        stage[target] = fold(turned[:, : lanes_of(block)], block)
    for apart, ref in zip(order, out_refs):
        ref[...] = stage[column ^ apart]


def cut_kernel(raw_ref, out_ref, points):
    chans = raw_ref.shape[2]
    block = chans // (lax.axis_size("lon") // 2)
    column, _ = column_and_side()
    group_points(raw_ref, points)
    turned = pltpu.roll(points[...], (chans - column * block) % chans, 1)
    out_ref[...] = fold(turned[:, : lanes_of(block)], block)


def column_kernel(order, *refs):
    *in_refs, out_ref = refs
    column, _ = column_and_side()
    for apart, ref in zip(order, in_refs):
        out_ref[column ^ apart] = ref[...]


def apart_kernel(width, step, out_ref):
    lons = out_ref.shape[0]
    side = lax.axis_index("lon") % 2
    source = lax.broadcasted_iota(jnp.int32, out_ref.shape, 0)
    place = lax.broadcasted_iota(jnp.int32, out_ref.shape, 1)
    within = place % step
    apart = source + (place // step) * width + within + (lons - side * width)
    for _ in range(3):
        apart = jnp.where(apart >= lons, apart - lons, apart)
    out_ref[...] = jnp.where(within < width, apart, -1)


def tables_kernel(width, filter_ref, band_ref, apart_ref, table_ref, first):
    bases, lons = filter_ref.shape
    taps, rows, _ = band_ref.shape
    step, places = first.shape[1:]
    columns = places // (2 * step)
    lat = lax.axis_index("lat")
    below = (lat > 0).astype(F32)
    above = (lat < lax.axis_size("lat") - 1).astype(F32)
    inside = [[below, below, 1.0], [1.0, above, above]]
    slots = [[0, 1, 2], [2, 0, 1]]
    profile = filter_ref[...]
    band = band_ref[...].astype(F32)
    apart = apart_ref[...]
    first[...] = jnp.zeros_like(first)
    for lon in range(width):
        pick = (apart == lon).astype(F32).astype(BF16)
        first[:, lon, :] = jnp.dot(profile, pick, preferred_element_type=F32)
    upper = lax.broadcasted_iota(jnp.int32, (SUBLANES, places), 0) < SUBLANES // 2
    count = columns * width
    for basis in range(bases):
        circle = first[basis]
        turned = [
            pltpu.roll(circle, column * 2 * step, 1) if column else circle
            for column in range(columns)
        ]
        last = [block[SUBLANES:] for block in turned]
        pairs = [
            jnp.where(upper, one, pltpu.roll(other, SUBLANES // 2, 0))
            for one, other in zip(last[::2], last[1::2])
        ]
        turned = jnp.concatenate([block[:SUBLANES] for block in turned] + pairs, axis=0)
        at = basis * count
        for row in range(rows):
            for tap in range(taps):
                weight = band[tap, row : row + 1, basis : basis + 1] * inside[row][tap]
                to = slots[row][tap] * places
                table_ref[row, at : at + count, to : to + places] = (weight * turned).astype(BF16)


def squares_kernel(own_ref, mate_ref, squares_ref, padded):
    bases, group, half = own_ref.shape
    lanes = squares_ref.shape[1]
    _, side = column_and_side()
    first = side == 0
    own = own_ref[...].astype(F32)
    mate = mate_ref[...].astype(F32)
    padded[...] = jnp.zeros_like(padded)
    padded[0, :, :group, :half] = jnp.where(first, own, mate)
    padded[1, :, :group, :half] = jnp.where(first, mate, own)
    members = padded.shape[2]
    into = lax.broadcasted_iota(jnp.int32, (lanes, members), 0)
    member = lax.broadcasted_iota(jnp.int32, (lanes, members), 1)
    repeat = (into % group == member).astype(F32).astype(BF16)
    row = lax.broadcasted_iota(jnp.int32, (lanes, lanes), 0)
    column = lax.broadcasted_iota(jnp.int32, (lanes, lanes), 1)
    same = (row // group == column // group) & (row < 2 * half) & (column < 2 * half)
    for basis in range(bases):
        weights = padded[0, basis] + pltpu.roll(padded[1, basis], half, 1)
        repeated = jnp.dot(repeat, weights.astype(BF16), preferred_element_type=F32)
        squares_ref[basis * lanes : (basis + 1) * lanes] = jnp.where(same, repeated, 0.0).astype(
            BF16
        )


def rows_of(message, block, rest):
    groups = unfold(message.astype(F32), block)
    last = (groups[2], pltpu.roll(groups[2], SUBLANES - rest, 0))
    return [jnp.concatenate([groups[row], last[row]], axis=0).astype(BF16) for row in range(2)]


def unpack_kernel(block, width, own_ref, out_ref):
    for at in range(own_ref.shape[0]):
        for row, read in enumerate(rows_of(own_ref[at], block, width - SUBLANES)):
            out_ref[row, at] = read


def own_kernel(block, width, mate, own, even, table_ref, part_ref, even_ref, field):
    rows, columns, step, _ = own.shape
    places = field.shape[1]
    side = lax.axis_index("lon") % 2
    for at in range(columns):
        first = pl.multiple_of((2 * at + side) * step, step)
        other = pl.multiple_of((2 * at + 1 - side) * step, step)
        for row, read in enumerate(rows_of(mate[at], block, width - SUBLANES)):
            field[row, pl.ds(first, step)] = own[row, at]
            field[row, pl.ds(other, step)] = read
    for row in range(rows):
        part_ref[row] = jnp.dot(
            table_ref[row, :, 2 * places :], field[row], preferred_element_type=F32
        )
    for at in range(columns):
        for row, read in enumerate(rows_of(even[at], block, width - SUBLANES)):
            even_ref[row, at] = read


def conv_kernel(
    block,
    width,
    odd_mate,
    odd_own,
    even_mate,
    part_ref,
    even_rows,
    table_ref,
    squares_ref,
    *refs,
):
    *out_refs, field, stage = refs
    columns = len(out_refs)
    lanes = squares_ref.shape[1]
    bases = squares_ref.shape[0] // lanes
    rows, _, inner = table_ref.shape
    places = inner // 3
    step = places // (2 * columns)
    half = columns * width
    rest = width - SUBLANES
    column, side = column_and_side()
    odd = lax.axis_index("lat") % 2

    def place(row, at, message):
        for slot, read in enumerate(rows_of(message, block, rest)):
            first = pl.multiple_of(slot * places + at * step, step)
            field[row, pl.ds(first, step)] = read

    for at in range(columns):
        for slot in range(2):
            first = pl.multiple_of(slot * places + (2 * at + side) * step, step)
            field[1 - odd, pl.ds(first, step)] = even_rows[slot, at]
        place(1 - odd, 2 * at + 1 - side, even_mate[at])
        place(odd, 2 * at + side, odd_own[at])
        place(odd, 2 * at + 1 - side, odd_mate[at])
    over = [
        jnp.dot(table_ref[row, :, : 2 * places], field[row], preferred_element_type=F32)
        for row in range(rows)
    ]
    mixed = None
    for basis in range(bases):
        taken = slice(basis * half, (basis + 1) * half)
        both = [(over[row][taken] + part_ref[row, taken]).astype(BF16) for row in range(rows)]
        product = jnp.dot(
            jnp.concatenate(both, axis=0)[:, :block],
            squares_ref[basis * lanes : basis * lanes + block],
            preferred_element_type=F32,
        )
        mixed = product if mixed is None else mixed + product
    upper = lax.broadcasted_iota(jnp.int32, (SUBLANES, lanes), 0) < rest
    top, bottom = mixed[:half], mixed[half:]
    for target in range(columns):
        at = target * SUBLANES
        pair = (columns + target // 2) * SUBLANES
        first, second = top[pair : pair + SUBLANES], bottom[pair : pair + SUBLANES]
        if target % 2:
            first = pltpu.roll(first, rest, 0)
        else:
            second = pltpu.roll(second, rest, 0)
        last = jnp.where(upper, first, second)
        points = jnp.concatenate(
            [top[at : at + SUBLANES], bottom[at : at + SUBLANES], last], axis=0
        )
        stage[target] = fold(points, block)
    for apart in range(columns):
        out_refs[apart][...] = stage[column ^ apart]


def summed_block(latent_block, message, block):
    convolved = jnp.concatenate(unfold(message.astype(F32), block), axis=0)
    kept = lax.broadcasted_iota(jnp.int32, convolved.shape, 1) < block
    return jnp.where(kept, latent_block + convolved, 0.0).astype(BF16)


def raised_block(summed, column, block, up_ref, taken=slice(None)):
    count = summed.shape[0]
    ones = jnp.ones((up_to(count, 2 * SUBLANES) - count, block), BF16)
    rows = pl.multiple_of(column * block, block)
    return jnp.dot(
        jnp.concatenate([summed[:, :block], ones], axis=0),
        up_ref[pl.ds(rows, block), taken],
        preferred_element_type=F32,
    )


def placed(summed, column, chans, block):
    piece = summed.astype(F32)
    if chans > piece.shape[1]:
        gap = jnp.zeros((piece.shape[0], chans - piece.shape[1]), F32)
        piece = jnp.concatenate([piece, gap], axis=1)
    return pltpu.roll(piece, column * block, 1)


def deviations(summed, mean, block):
    kept = lax.broadcasted_iota(jnp.int32, summed.shape, 1) < block
    return jnp.where(kept, summed.astype(F32) - mean, 0.0)


def over_lanes(values):
    return jnp.sum(values, axis=1, keepdims=True)


def lift_kernel(
    apart,
    own_ref,
    first_ref,
    latent_ref,
    up_ref,
    blocks_ref,
    summed_ref,
    raised_ref,
    stats_ref,
    points,
):
    columns = blocks_ref.shape[0]
    chans = latent_ref.shape[2]
    block = chans // columns
    column, _ = column_and_side()
    group_points(latent_ref, points)
    own = points[...]
    for target in range(columns):
        turned = pltpu.roll(own, chans - target * block, 1) if target else own
        blocks_ref[target] = turned[:, : lanes_of(block)]
    other = column ^ apart
    here = summed_block(blocks_ref[column], own_ref[...], block)
    there = summed_block(blocks_ref[other], first_ref[...], block)
    summed_ref[...] = placed(here, column, chans, block) + placed(there, other, chans, block)
    raised_ref[...] = raised_block(here, column, block, up_ref) + raised_block(
        there, other, block, up_ref
    )
    mean = over_lanes(here.astype(F32) + there.astype(F32)) / (2 * block)
    squares = sum(deviations(summed, mean, block) ** 2 for summed in (here, there))
    stats_ref[0] = jnp.broadcast_to(mean, stats_ref.shape[1:])
    stats_ref[1] = jnp.broadcast_to(over_lanes(squares), stats_ref.shape[1:])


def tail_kernel(order, *refs):
    back_refs = refs[: len(order)]
    blocks_ref, summed_ref, raised_ref, stats_ref, up_ref, down_ref, out_ref = refs[len(order) :]
    width, rows, chans = out_ref.shape
    rest = width - SUBLANES
    block = chans // blocks_ref.shape[0]
    column, _ = column_and_side()
    early_mean, early_squares = stats_ref[0, :, :1], stats_ref[1, :, :1]
    theirs = []
    away = squares = None
    for apart, ref in zip(order, back_refs):
        other = column ^ apart
        there = summed_block(blocks_ref[other], ref[...], block)
        theirs.append((there, other))
        apart_from = deviations(there, early_mean, block)
        away = apart_from if away is None else away + apart_from
        squares = apart_from**2 if squares is None else squares + apart_from**2
    away, squares = over_lanes(away), over_lanes(squares)
    mean = early_mean + away / chans
    variance = (early_squares + squares - away * away / chans) / chans
    scale = lax.rsqrt(variance + 1e-05)
    count = summed_ref.shape[0]
    product = None
    units = raised_ref.shape[1]
    for start in range(0, units, 2 * LANES):
        taken = slice(start, min(start + 2 * LANES, units))
        raised = raised_ref[:, taken]
        for there, other in theirs:
            raised = raised + raised_block(there, other, block, up_ref, taken)
        hidden = scale * (raised[:count] - mean * raised[count : count + 1])
        hidden = (0.5 * hidden * (1.0 + lax.erf(hidden * 0.5**0.5))).astype(BF16)
        part = jnp.dot(hidden, down_ref[taken], preferred_element_type=F32)
        product = part if product is None else product + part
    summed = summed_ref[...]
    for there, other in theirs:
        summed = summed + placed(there, other, chans, block)
    result = summed + product
    for row in range(rows):
        out_ref[:SUBLANES, row, :] = result[row * SUBLANES : (row + 1) * SUBLANES].astype(BF16)
        at = rows * SUBLANES + row * rest
        out_ref[SUBLANES:, row, :] = result[at : at + rest].astype(BF16)


VMEM = pl.BlockSpec(memory_space=pltpu.VMEM)


def call(kernel, name, out_shape, scratch, work, *operands):
    several = isinstance(out_shape, tuple)
    return pl.pallas_call(
        kernel,
        out_shape=out_shape,
        in_specs=[VMEM] * len(operands),
        out_specs=(VMEM,) * len(out_shape) if several else VMEM,
        scratch_shapes=scratch,
        compiler_params=pltpu.CompilerParams(vmem_limit_bytes=24 * 2**20),
        cost_estimate=pl.CostEstimate(flops=work, bytes_accessed=10**6, transcendentals=0),
        name=name,
    )(*operands)


def over_columns(message, count, apart):
    pairs = [(i, ((i // 2) ^ apart) * 2 + i % 2) for i in range(count)]
    return lax.ppermute(message, "lon", pairs) if apart else message


def over_sides(block, count):
    return lax.ppermute(block, "lon", [(i, i ^ 1) for i in range(count)])


def swap(block, count, partner):
    pairs = []
    for lat in range(lax.axis_size("lat")):
        for lon in range(count):
            to_lat, to_lon = partner(lat, lon)
            pairs.append((lat * count + lon, to_lat * count + to_lon))
    return lax.ppermute(block, ("lat", "lon"), pairs)


def odd_pair(lat, lon, other_side, rows):
    to = lat + 1 if lat % 2 else lat - 1
    if 0 <= to < rows:
        return to, lon ^ other_side
    return (lat, lon ^ 1) if other_side else (rows - 1 - lat, lon)


def local(latent, lon_filter, mix_weight, band_weight, offsets, w_up, w_down):
    rows, width, chans = latent.shape
    bases, lons = lon_filter.shape
    half, group = mix_weight.shape[1:]
    taps = band_weight.shape[2]
    count = lons // width
    columns = count // 2
    block = 2 * half
    step = up_to(width, 2 * SUBLANES)
    places = count * step
    lanes = lanes_of(block)
    height = message_rows(block)
    assert rows == 2 and taps == 3 and columns & (columns - 1) == 0
    assert lax.axis_size("lat") % 2 == 0
    assert 2 * width == 3 * SUBLANES and columns * width % (2 * SUBLANES) == 0
    assert 3 * (block % LANES) <= LANES

    far_first = tuple(reversed(range(columns)))
    inward = far_first
    if columns > 3:
        inward = (far_first[1], far_first[0]) + far_first[2:]
    message = jax.ShapeDtypeStruct((height, LANES), BF16)
    messages = (message,) * columns
    stage = pltpu.VMEM((columns, height, LANES), BF16)
    points = pltpu.VMEM((3 * SUBLANES, chans), F32)
    lon_first = jnp.transpose(latent, (1, 0, 2))
    mix_own = jnp.transpose(mix_weight, (0, 2, 1))

    raw = over_columns(lon_first, count, inward[0])
    apart = call(
        functools.partial(apart_kernel, width, step),
        "apart",
        jax.ShapeDtypeStruct((lons, places), jnp.int32),
        [],
        10**9,
    )
    loaded, apart = lax.optimization_barrier((lon_first, apart))
    packed = call(
        functools.partial(pack_kernel, inward[1:]),
        "pack",
        (message,) * (columns - 1),
        [points, stage],
        10**9,
        loaded,
    )
    arrived = [call(cut_kernel, "cut", message, [points], 5 * 10**9, raw)]
    arrived += [over_columns(*pair) for pair in zip(packed, [count] * columns, inward[1:])]
    mix_mate = over_sides(mix_own, count)
    table = call(
        functools.partial(tables_kernel, width),
        "tables",
        jax.ShapeDtypeStruct((rows, bases * columns * width, taps * places), BF16),
        [pltpu.VMEM((bases, step, places), F32)],
        10**6,
        lon_filter,
        jnp.transpose(band_weight, (2, 1, 0)),
        apart,
    )
    gathered = jax.ShapeDtypeStruct((columns, height, LANES), BF16)
    own_side = call(
        functools.partial(column_kernel, inward),
        "join_columns",
        gathered,
        [],
        10**8,
        *arrived,
    )
    lats = lax.axis_size("lat")
    mate_side = swap(own_side, count, lambda lat, lon: (lat, lon ^ 1))
    odd_mate = swap(own_side, count, lambda lat, lon: odd_pair(lat, lon, 1, lats))
    odd_own = swap(own_side, count, lambda lat, lon: odd_pair(lat, lon, 0, lats))
    own_rows = call(
        functools.partial(unpack_kernel, block, width),
        "unpack",
        jax.ShapeDtypeStruct((rows, columns, step, lanes), BF16),
        [],
        10**9,
        own_side,
    )
    even_own = swap(own_side, count, lambda lat, lon: (lat ^ 1, lon))
    even_mate = swap(mate_side, count, lambda lat, lon: (lat ^ 1, lon))
    mix_mate, _ = lax.optimization_barrier((mix_mate, mate_side))
    squares = call(
        squares_kernel,
        "squares",
        jax.ShapeDtypeStruct((bases * lanes, lanes), BF16),
        [pltpu.VMEM((2, bases, up_to(group, 2 * SUBLANES), lanes), F32)],
        3 * 10**8,
        mix_own,
        mix_mate,
    )
    part = call(
        functools.partial(own_kernel, block, width),
        "conv_own",
        (
            jax.ShapeDtypeStruct((rows, bases * columns * width, lanes), F32),
            jax.ShapeDtypeStruct((rows, columns, step, lanes), BF16),
        ),
        [pltpu.VMEM((rows, places, lanes), BF16)],
        3 * 10**8,
        mate_side,
        own_rows,
        even_own,
        table,
    )
    mixed = call(
        functools.partial(conv_kernel, block, width),
        "conv",
        messages,
        [
            pltpu.VMEM((rows, 2 * places, lanes), BF16),
            pltpu.VMEM((columns, height, LANES), BF16),
        ],
        10**10,
        odd_mate,
        odd_own,
        even_mate,
        *part,
        table,
        squares,
    )
    outward = tuple(reversed(far_first[:-1]))
    back = [over_columns(mixed[apart], count, apart) for apart in outward]
    first = outward.index(far_first[0])
    lifted = call(
        functools.partial(lift_kernel, far_first[0]),
        "lift",
        (
            jax.ShapeDtypeStruct((columns, 3 * SUBLANES, lanes), F32),
            jax.ShapeDtypeStruct((3 * SUBLANES, chans), F32),
            jax.ShapeDtypeStruct((up_to(3 * SUBLANES, 2 * SUBLANES), w_up.shape[1]), F32),
            jax.ShapeDtypeStruct((2, 3 * SUBLANES, LANES), F32),
        ),
        [points],
        10**8,
        mixed[0],
        back[first],
        lon_first,
        w_up,
    )
    result = call(
        functools.partial(tail_kernel, outward[:first] + outward[first + 1 :]),
        "tail",
        jax.ShapeDtypeStruct(lon_first.shape, BF16),
        [],
        10**9,
        *back[:first],
        *back[first + 1 :],
        *lifted,
        w_up,
        w_down,
    )
    return jnp.transpose(result, (1, 0, 2))


def solution(mesh):
    return jax.shard_map(
        local,
        mesh=mesh,
        in_specs=(
            P("lat", "lon", None),
            P(),
            P(None, "lon", None),
            P(None, "lat", None),
            P("lat"),
            P(),
            P(),
        ),
        out_specs=P("lat", "lon", None),
        check_vma=False,
    )
```

```python
import functools

import jax
import jax.numpy as jnp
from jax import lax
from jax.experimental import pallas as pl
from jax.experimental.pallas import tpu as pltpu
from jax.sharding import PartitionSpec as P

F32 = jnp.float32
BF16 = jnp.bfloat16
LANES = 128
SUBLANES = 8


def up_to(size, step):
    return -(-size // step) * step


def column_and_side():
    place = lax.axis_index("lon")
    return place // 2, place % 2


def message_rows(block):
    tiles = block // LANES
    return up_to(3 * SUBLANES * tiles + (SUBLANES if block % LANES else 0), 2 * SUBLANES)


def lanes_of(block):
    return up_to(block, LANES)


def fold(points, block):
    whole, rest = divmod(block, LANES)
    parts = [points[:, tile * LANES : (tile + 1) * LANES] for tile in range(whole)]
    if rest:
        odd = points[:, whole * LANES : (whole + 1) * LANES]
        kept = lax.broadcasted_iota(jnp.int32, (SUBLANES, LANES), 1) < rest
        shared = None
        for third in range(3):
            piece = jnp.where(kept, odd[third * SUBLANES : (third + 1) * SUBLANES], 0.0)
            piece = pltpu.roll(piece, third * rest, 1) if third else piece
            shared = piece if shared is None else shared + piece
        parts.append(shared)
    filled = sum(part.shape[0] for part in parts)
    if message_rows(block) > filled:
        parts.append(jnp.zeros((message_rows(block) - filled, LANES), F32))
    return jnp.concatenate(parts, axis=0).astype(BF16)


def unfold(message, block):
    whole, rest = divmod(block, LANES)
    groups = []
    for third in range(3):
        first = third * SUBLANES
        parts = [
            message[tile * 3 * SUBLANES + first : tile * 3 * SUBLANES + first + SUBLANES]
            for tile in range(whole)
        ]
        if rest:
            odd = message[whole * 3 * SUBLANES : whole * 3 * SUBLANES + SUBLANES]
            parts.append(pltpu.roll(odd, LANES - third * rest, 1) if third else odd)
        groups.append(jnp.concatenate(parts, axis=1) if len(parts) > 1 else parts[0])
    return groups


def group_points(latent_ref, points):
    width, rows, _ = latent_ref.shape
    rest = width - SUBLANES
    for row in range(rows):
        points[row * SUBLANES : (row + 1) * SUBLANES] = latent_ref[:SUBLANES, row, :].astype(F32)
        at = rows * SUBLANES + row * rest
        points[at : at + rest] = latent_ref[SUBLANES:, row, :].astype(F32)


def pack_kernel(order, latent_ref, *refs):
    *out_refs, points, stage = refs
    columns = stage.shape[0]
    chans = latent_ref.shape[2]
    block = chans // columns
    column, _ = column_and_side()
    group_points(latent_ref, points)
    own = points[...]
    for target in range(columns):
        turned = pltpu.roll(own, chans - target * block, 1) if target else own
        stage[target] = fold(turned[:, : lanes_of(block)], block)
    for apart, ref in zip(order, out_refs):
        ref[...] = stage[column ^ apart]


def cut_kernel(raw_ref, out_ref, points):
    chans = raw_ref.shape[2]
    block = chans // (lax.axis_size("lon") // 2)
    column, _ = column_and_side()
    group_points(raw_ref, points)
    turned = pltpu.roll(points[...], (chans - column * block) % chans, 1)
    out_ref[...] = fold(turned[:, : lanes_of(block)], block)


def column_kernel(order, *refs):
    *in_refs, out_ref = refs
    column, _ = column_and_side()
    for apart, ref in zip(order, in_refs):
        out_ref[column ^ apart] = ref[...]


def apart_kernel(width, step, out_ref):
    lons = out_ref.shape[0]
    side = lax.axis_index("lon") % 2
    source = lax.broadcasted_iota(jnp.int32, out_ref.shape, 0)
    place = lax.broadcasted_iota(jnp.int32, out_ref.shape, 1)
    within = place % step
    apart = source + (place // step) * width + within + (lons - side * width)
    for _ in range(3):
        apart = jnp.where(apart >= lons, apart - lons, apart)
    out_ref[...] = jnp.where(within < width, apart, -1)


def tables_kernel(width, filter_ref, band_ref, apart_ref, table_ref, first):
    bases, lons = filter_ref.shape
    taps, rows, _ = band_ref.shape
    step, places = first.shape[1:]
    columns = places // (2 * step)
    lat = lax.axis_index("lat")
    below = (lat > 0).astype(F32)
    above = (lat < lax.axis_size("lat") - 1).astype(F32)
    inside = [[below, below, 1.0], [1.0, above, above]]
    slots = [[0, 1, 2], [2, 0, 1]]
    profile = filter_ref[...]
    band = band_ref[...].astype(F32)
    apart = apart_ref[...]
    first[...] = jnp.zeros_like(first)
    for lon in range(width):
        pick = (apart == lon).astype(F32).astype(BF16)
        first[:, lon, :] = jnp.dot(profile, pick, preferred_element_type=F32)
    upper = lax.broadcasted_iota(jnp.int32, (SUBLANES, places), 0) < SUBLANES // 2
    count = columns * width
    for basis in range(bases):
        circle = first[basis]
        turned = [
            pltpu.roll(circle, column * 2 * step, 1) if column else circle
            for column in range(columns)
        ]
        last = [block[SUBLANES:] for block in turned]
        pairs = [
            jnp.where(upper, one, pltpu.roll(other, SUBLANES // 2, 0))
            for one, other in zip(last[::2], last[1::2])
        ]
        turned = jnp.concatenate([block[:SUBLANES] for block in turned] + pairs, axis=0)
        at = basis * count
        for row in range(rows):
            for tap in range(taps):
                weight = band[tap, row : row + 1, basis : basis + 1] * inside[row][tap]
                to = slots[row][tap] * places
                table_ref[row, at : at + count, to : to + places] = (weight * turned).astype(BF16)


def squares_kernel(own_ref, mate_ref, squares_ref, padded):
    bases, group, half = own_ref.shape
    lanes = squares_ref.shape[1]
    _, side = column_and_side()
    first = side == 0
    own = own_ref[...].astype(F32)
    mate = mate_ref[...].astype(F32)
    padded[...] = jnp.zeros_like(padded)
    padded[0, :, :group, :half] = jnp.where(first, own, mate)
    padded[1, :, :group, :half] = jnp.where(first, mate, own)
    members = padded.shape[2]
    into = lax.broadcasted_iota(jnp.int32, (lanes, members), 0)
    member = lax.broadcasted_iota(jnp.int32, (lanes, members), 1)
    repeat = (into % group == member).astype(F32).astype(BF16)
    row = lax.broadcasted_iota(jnp.int32, (lanes, lanes), 0)
    column = lax.broadcasted_iota(jnp.int32, (lanes, lanes), 1)
    same = (row // group == column // group) & (row < 2 * half) & (column < 2 * half)
    for basis in range(bases):
        weights = padded[0, basis] + pltpu.roll(padded[1, basis], half, 1)
        repeated = jnp.dot(repeat, weights.astype(BF16), preferred_element_type=F32)
        squares_ref[basis * lanes : (basis + 1) * lanes] = jnp.where(same, repeated, 0.0).astype(
            BF16
        )


def rows_of(message, block, rest):
    groups = unfold(message.astype(F32), block)
    last = (groups[2], pltpu.roll(groups[2], SUBLANES - rest, 0))
    return [jnp.concatenate([groups[row], last[row]], axis=0).astype(BF16) for row in range(2)]


def unpack_kernel(block, width, own_ref, out_ref):
    for at in range(own_ref.shape[0]):
        for row, read in enumerate(rows_of(own_ref[at], block, width - SUBLANES)):
            out_ref[row, at] = read


def own_kernel(block, width, mate, own, even, table_ref, part_ref, even_ref, field):
    rows, columns, step, _ = own.shape
    places = field.shape[1]
    side = lax.axis_index("lon") % 2
    for at in range(columns):
        first = pl.multiple_of((2 * at + side) * step, step)
        other = pl.multiple_of((2 * at + 1 - side) * step, step)
        for row, read in enumerate(rows_of(mate[at], block, width - SUBLANES)):
            field[row, pl.ds(first, step)] = own[row, at]
            field[row, pl.ds(other, step)] = read
    for row in range(rows):
        part_ref[row] = jnp.dot(
            table_ref[row, :, 2 * places :], field[row], preferred_element_type=F32
        )
    for at in range(columns):
        for row, read in enumerate(rows_of(even[at], block, width - SUBLANES)):
            even_ref[row, at] = read


def conv_kernel(
    block,
    width,
    odd_mate,
    odd_own,
    even_mate,
    part_ref,
    even_rows,
    table_ref,
    squares_ref,
    *refs,
):
    *out_refs, field, stage = refs
    columns = len(out_refs)
    lanes = squares_ref.shape[1]
    bases = squares_ref.shape[0] // lanes
    rows, _, inner = table_ref.shape
    places = inner // 3
    step = places // (2 * columns)
    half = columns * width
    rest = width - SUBLANES
    column, side = column_and_side()
    odd = lax.axis_index("lat") % 2

    def place(row, at, message):
        for slot, read in enumerate(rows_of(message, block, rest)):
            first = pl.multiple_of(slot * places + at * step, step)
            field[row, pl.ds(first, step)] = read

    for at in range(columns):
        for slot in range(2):
            first = pl.multiple_of(slot * places + (2 * at + side) * step, step)
            field[1 - odd, pl.ds(first, step)] = even_rows[slot, at]
        place(1 - odd, 2 * at + 1 - side, even_mate[at])
        place(odd, 2 * at + side, odd_own[at])
        place(odd, 2 * at + 1 - side, odd_mate[at])
    over = [
        jnp.dot(table_ref[row, :, : 2 * places], field[row], preferred_element_type=F32)
        for row in range(rows)
    ]
    mixed = None
    for basis in range(bases):
        taken = slice(basis * half, (basis + 1) * half)
        both = [(over[row][taken] + part_ref[row, taken]).astype(BF16) for row in range(rows)]
        product = jnp.dot(
            jnp.concatenate(both, axis=0)[:, :block],
            squares_ref[basis * lanes : basis * lanes + block],
            preferred_element_type=F32,
        )
        mixed = product if mixed is None else mixed + product
    upper = lax.broadcasted_iota(jnp.int32, (SUBLANES, lanes), 0) < rest
    top, bottom = mixed[:half], mixed[half:]
    for target in range(columns):
        at = target * SUBLANES
        pair = (columns + target // 2) * SUBLANES
        first, second = top[pair : pair + SUBLANES], bottom[pair : pair + SUBLANES]
        if target % 2:
            first = pltpu.roll(first, rest, 0)
        else:
            second = pltpu.roll(second, rest, 0)
        last = jnp.where(upper, first, second)
        points = jnp.concatenate(
            [top[at : at + SUBLANES], bottom[at : at + SUBLANES], last], axis=0
        )
        stage[target] = fold(points, block)
    for apart in range(columns):
        out_refs[apart][...] = stage[column ^ apart]


def summed_block(latent_block, message, block):
    convolved = jnp.concatenate(unfold(message.astype(F32), block), axis=0)
    kept = lax.broadcasted_iota(jnp.int32, convolved.shape, 1) < block
    return jnp.where(kept, latent_block + convolved, 0.0).astype(BF16)


def raised_block(summed, column, block, up_ref):
    count = summed.shape[0]
    ones = jnp.ones((up_to(count, 2 * SUBLANES) - count, block), BF16)
    rows = pl.multiple_of(column * block, block)
    return jnp.dot(
        jnp.concatenate([summed[:, :block], ones], axis=0),
        up_ref[pl.ds(rows, block), :],
        preferred_element_type=F32,
    )


def placed(summed, column, chans, block):
    piece = summed.astype(F32)
    if chans > piece.shape[1]:
        gap = jnp.zeros((piece.shape[0], chans - piece.shape[1]), F32)
        piece = jnp.concatenate([piece, gap], axis=1)
    return pltpu.roll(piece, column * block, 1)


def deviations(summed, mean, block):
    kept = lax.broadcasted_iota(jnp.int32, summed.shape, 1) < block
    return jnp.where(kept, summed.astype(F32) - mean, 0.0)


def over_lanes(values):
    return jnp.sum(values, axis=1, keepdims=True)


def lift_kernel(
    apart,
    own_ref,
    first_ref,
    latent_ref,
    up_ref,
    blocks_ref,
    summed_ref,
    raised_ref,
    stats_ref,
    points,
):
    columns = blocks_ref.shape[0]
    chans = latent_ref.shape[2]
    block = chans // columns
    column, _ = column_and_side()
    group_points(latent_ref, points)
    own = points[...]
    for target in range(columns):
        turned = pltpu.roll(own, chans - target * block, 1) if target else own
        blocks_ref[target] = turned[:, : lanes_of(block)]
    other = column ^ apart
    here = summed_block(blocks_ref[column], own_ref[...], block)
    there = summed_block(blocks_ref[other], first_ref[...], block)
    summed_ref[...] = placed(here, column, chans, block) + placed(there, other, chans, block)
    raised_ref[...] = raised_block(here, column, block, up_ref) + raised_block(
        there, other, block, up_ref
    )
    mean = over_lanes(here.astype(F32) + there.astype(F32)) / (2 * block)
    squares = sum(deviations(summed, mean, block) ** 2 for summed in (here, there))
    stats_ref[0] = jnp.broadcast_to(mean, stats_ref.shape[1:])
    stats_ref[1] = jnp.broadcast_to(over_lanes(squares), stats_ref.shape[1:])


def tail_kernel(order, *refs):
    back_refs = refs[: len(order)]
    blocks_ref, summed_ref, raised_ref, stats_ref, up_ref, down_ref, out_ref = refs[len(order) :]
    width, rows, chans = out_ref.shape
    rest = width - SUBLANES
    block = chans // blocks_ref.shape[0]
    column, _ = column_and_side()
    raised = raised_ref[...]
    early_mean, early_squares = stats_ref[0, :, :1], stats_ref[1, :, :1]
    theirs = []
    away = squares = None
    for apart, ref in zip(order, back_refs):
        other = column ^ apart
        there = summed_block(blocks_ref[other], ref[...], block)
        theirs.append((there, other))
        raised = raised + raised_block(there, other, block, up_ref)
        apart_from = deviations(there, early_mean, block)
        away = apart_from if away is None else away + apart_from
        squares = apart_from**2 if squares is None else squares + apart_from**2
    away, squares = over_lanes(away), over_lanes(squares)
    mean = early_mean + away / chans
    variance = (early_squares + squares - away * away / chans) / chans
    scale = lax.rsqrt(variance + 1e-05)
    count = summed_ref.shape[0]
    product = None
    units = raised.shape[1]
    for start in range(0, units, 4 * LANES):
        taken = slice(start, min(start + 4 * LANES, units))
        hidden = scale * (raised[:count, taken] - mean * raised[count : count + 1, taken])
        hidden = (0.5 * hidden * (1.0 + lax.erf(hidden * 0.5**0.5))).astype(BF16)
        part = jnp.dot(hidden, down_ref[taken], preferred_element_type=F32)
        product = part if product is None else product + part
    summed = summed_ref[...]
    for there, other in theirs:
        summed = summed + placed(there, other, chans, block)
    result = summed + product
    for row in range(rows):
        out_ref[:SUBLANES, row, :] = result[row * SUBLANES : (row + 1) * SUBLANES].astype(BF16)
        at = rows * SUBLANES + row * rest
        out_ref[SUBLANES:, row, :] = result[at : at + rest].astype(BF16)


VMEM = pl.BlockSpec(memory_space=pltpu.VMEM)


def call(kernel, name, out_shape, scratch, work, *operands):
    several = isinstance(out_shape, tuple)
    return pl.pallas_call(
        kernel,
        out_shape=out_shape,
        in_specs=[VMEM] * len(operands),
        out_specs=(VMEM,) * len(out_shape) if several else VMEM,
        scratch_shapes=scratch,
        compiler_params=pltpu.CompilerParams(vmem_limit_bytes=24 * 2**20),
        cost_estimate=pl.CostEstimate(flops=work, bytes_accessed=10**6, transcendentals=0),
        name=name,
    )(*operands)


def over_columns(message, count, apart):
    pairs = [(i, ((i // 2) ^ apart) * 2 + i % 2) for i in range(count)]
    return lax.ppermute(message, "lon", pairs) if apart else message


def over_sides(block, count):
    return lax.ppermute(block, "lon", [(i, i ^ 1) for i in range(count)])


def swap(block, count, partner):
    pairs = []
    for lat in range(lax.axis_size("lat")):
        for lon in range(count):
            to_lat, to_lon = partner(lat, lon)
            pairs.append((lat * count + lon, to_lat * count + to_lon))
    return lax.ppermute(block, ("lat", "lon"), pairs)


def odd_pair(lat, lon, other_side, rows):
    to = lat + 1 if lat % 2 else lat - 1
    if 0 <= to < rows:
        return to, lon ^ other_side
    return (lat, lon ^ 1) if other_side else (rows - 1 - lat, lon)


def local(latent, lon_filter, mix_weight, band_weight, offsets, w_up, w_down):
    rows, width, chans = latent.shape
    bases, lons = lon_filter.shape
    half, group = mix_weight.shape[1:]
    taps = band_weight.shape[2]
    count = lons // width
    columns = count // 2
    block = 2 * half
    step = up_to(width, 2 * SUBLANES)
    places = count * step
    lanes = lanes_of(block)
    height = message_rows(block)
    assert rows == 2 and taps == 3 and columns & (columns - 1) == 0
    assert lax.axis_size("lat") % 2 == 0
    assert 2 * width == 3 * SUBLANES and columns * width % (2 * SUBLANES) == 0
    assert 3 * (block % LANES) <= LANES

    far_first = tuple(reversed(range(columns)))
    inward = far_first
    if columns > 3:
        inward = (far_first[1], far_first[0]) + far_first[2:]
    message = jax.ShapeDtypeStruct((height, LANES), BF16)
    messages = (message,) * columns
    stage = pltpu.VMEM((columns, height, LANES), BF16)
    points = pltpu.VMEM((3 * SUBLANES, chans), F32)
    lon_first = jnp.transpose(latent, (1, 0, 2))
    mix_own = jnp.transpose(mix_weight, (0, 2, 1))

    raw = over_columns(lon_first, count, inward[0])
    apart = call(
        functools.partial(apart_kernel, width, step),
        "apart",
        jax.ShapeDtypeStruct((lons, places), jnp.int32),
        [],
        10**9,
    )
    loaded, apart = lax.optimization_barrier((lon_first, apart))
    packed = call(
        functools.partial(pack_kernel, inward[1:]),
        "pack",
        (message,) * (columns - 1),
        [points, stage],
        10**9,
        loaded,
    )
    arrived = [call(cut_kernel, "cut", message, [points], 5 * 10**9, raw)]
    arrived += [over_columns(*pair) for pair in zip(packed, [count] * columns, inward[1:])]
    mix_mate = over_sides(mix_own, count)
    table = call(
        functools.partial(tables_kernel, width),
        "tables",
        jax.ShapeDtypeStruct((rows, bases * columns * width, taps * places), BF16),
        [pltpu.VMEM((bases, step, places), F32)],
        10**6,
        lon_filter,
        jnp.transpose(band_weight, (2, 1, 0)),
        apart,
    )
    gathered = jax.ShapeDtypeStruct((columns, height, LANES), BF16)
    own_side = call(
        functools.partial(column_kernel, inward),
        "join_columns",
        gathered,
        [],
        10**8,
        *arrived,
    )
    lats = lax.axis_size("lat")
    mate_side = swap(own_side, count, lambda lat, lon: (lat, lon ^ 1))
    odd_mate = swap(own_side, count, lambda lat, lon: odd_pair(lat, lon, 1, lats))
    odd_own = swap(own_side, count, lambda lat, lon: odd_pair(lat, lon, 0, lats))
    own_rows = call(
        functools.partial(unpack_kernel, block, width),
        "unpack",
        jax.ShapeDtypeStruct((rows, columns, step, lanes), BF16),
        [],
        10**9,
        own_side,
    )
    even_own = swap(own_side, count, lambda lat, lon: (lat ^ 1, lon))
    even_mate = swap(mate_side, count, lambda lat, lon: (lat ^ 1, lon))
    mix_mate, _ = lax.optimization_barrier((mix_mate, mate_side))
    squares = call(
        squares_kernel,
        "squares",
        jax.ShapeDtypeStruct((bases * lanes, lanes), BF16),
        [pltpu.VMEM((2, bases, up_to(group, 2 * SUBLANES), lanes), F32)],
        3 * 10**8,
        mix_own,
        mix_mate,
    )
    part = call(
        functools.partial(own_kernel, block, width),
        "conv_own",
        (
            jax.ShapeDtypeStruct((rows, bases * columns * width, lanes), F32),
            jax.ShapeDtypeStruct((rows, columns, step, lanes), BF16),
        ),
        [pltpu.VMEM((rows, places, lanes), BF16)],
        3 * 10**8,
        mate_side,
        own_rows,
        even_own,
        table,
    )
    mixed = call(
        functools.partial(conv_kernel, block, width),
        "conv",
        messages,
        [
            pltpu.VMEM((rows, 2 * places, lanes), BF16),
            pltpu.VMEM((columns, height, LANES), BF16),
        ],
        10**10,
        odd_mate,
        odd_own,
        even_mate,
        *part,
        table,
        squares,
    )
    outward = tuple(reversed(far_first[:-1]))
    back = [over_columns(mixed[apart], count, apart) for apart in outward]
    first = outward.index(far_first[0])
    lifted = call(
        functools.partial(lift_kernel, far_first[0]),
        "lift",
        (
            jax.ShapeDtypeStruct((columns, 3 * SUBLANES, lanes), F32),
            jax.ShapeDtypeStruct((3 * SUBLANES, chans), F32),
            jax.ShapeDtypeStruct((up_to(3 * SUBLANES, 2 * SUBLANES), w_up.shape[1]), F32),
            jax.ShapeDtypeStruct((2, 3 * SUBLANES, LANES), F32),
        ),
        [points],
        10**8,
        mixed[0],
        back[first],
        lon_first,
        w_up,
    )
    result = call(
        functools.partial(tail_kernel, outward[:first] + outward[first + 1 :]),
        "tail",
        jax.ShapeDtypeStruct(lon_first.shape, BF16),
        [],
        10**9,
        *back[:first],
        *back[first + 1 :],
        *lifted,
        w_up,
        w_down,
    )
    return jnp.transpose(result, (1, 0, 2))


def solution(mesh):
    return jax.shard_map(
        local,
        mesh=mesh,
        in_specs=(
            P("lat", "lon", None),
            P(),
            P(None, "lon", None),
            P(None, "lat", None),
            P("lat"),
            P(),
            P(),
        ),
        out_specs=P("lat", "lon", None),
        check_vma=False,
    )
```

```python
import functools

import jax
import jax.numpy as jnp
from jax import lax
from jax.experimental import pallas as pl
from jax.experimental.pallas import tpu as pltpu
from jax.sharding import PartitionSpec as P

F32 = jnp.float32
BF16 = jnp.bfloat16
LANES = 128
SUBLANES = 8


def up_to(size, step):
    return -(-size // step) * step


def column_and_side():
    place = lax.axis_index("lon")
    return place // 2, place % 2


def message_rows(block):
    tiles = block // LANES
    return up_to(3 * SUBLANES * tiles + (SUBLANES if block % LANES else 0), 2 * SUBLANES)


def lanes_of(block):
    return up_to(block, LANES)


def fold(points, block):
    whole, rest = divmod(block, LANES)
    parts = [points[:, tile * LANES : (tile + 1) * LANES] for tile in range(whole)]
    if rest:
        odd = points[:, whole * LANES : (whole + 1) * LANES]
        kept = lax.broadcasted_iota(jnp.int32, (SUBLANES, LANES), 1) < rest
        shared = None
        for third in range(3):
            piece = jnp.where(kept, odd[third * SUBLANES : (third + 1) * SUBLANES], 0.0)
            piece = pltpu.roll(piece, third * rest, 1) if third else piece
            shared = piece if shared is None else shared + piece
        parts.append(shared)
    filled = sum(part.shape[0] for part in parts)
    if message_rows(block) > filled:
        parts.append(jnp.zeros((message_rows(block) - filled, LANES), F32))
    return jnp.concatenate(parts, axis=0).astype(BF16)


def unfold(message, block):
    whole, rest = divmod(block, LANES)
    groups = []
    for third in range(3):
        first = third * SUBLANES
        parts = [
            message[tile * 3 * SUBLANES + first : tile * 3 * SUBLANES + first + SUBLANES]
            for tile in range(whole)
        ]
        if rest:
            odd = message[whole * 3 * SUBLANES : whole * 3 * SUBLANES + SUBLANES]
            parts.append(pltpu.roll(odd, LANES - third * rest, 1) if third else odd)
        groups.append(jnp.concatenate(parts, axis=1) if len(parts) > 1 else parts[0])
    return groups


def group_points(latent_ref, points):
    width, rows, _ = latent_ref.shape
    rest = width - SUBLANES
    for row in range(rows):
        points[row * SUBLANES : (row + 1) * SUBLANES] = latent_ref[:SUBLANES, row, :].astype(F32)
        at = rows * SUBLANES + row * rest
        points[at : at + rest] = latent_ref[SUBLANES:, row, :].astype(F32)


def pack_kernel(order, latent_ref, *refs):
    *out_refs, points, stage = refs
    columns = stage.shape[0]
    chans = latent_ref.shape[2]
    block = chans // columns
    column, _ = column_and_side()
    group_points(latent_ref, points)
    own = points[...]
    for target in range(columns):
        turned = pltpu.roll(own, chans - target * block, 1) if target else own
        stage[target] = fold(turned[:, : lanes_of(block)], block)
    for apart, ref in zip(order, out_refs):
        ref[...] = stage[column ^ apart]


def cut_kernel(raw_ref, out_ref, points):
    chans = raw_ref.shape[2]
    block = chans // (lax.axis_size("lon") // 2)
    column, _ = column_and_side()
    group_points(raw_ref, points)
    turned = pltpu.roll(points[...], (chans - column * block) % chans, 1)
    out_ref[...] = fold(turned[:, : lanes_of(block)], block)


def column_kernel(order, *refs):
    *in_refs, out_ref = refs
    column, _ = column_and_side()
    for apart, ref in zip(order, in_refs):
        out_ref[column ^ apart] = ref[...]


def apart_kernel(width, step, out_ref):
    lons = out_ref.shape[0]
    side = lax.axis_index("lon") % 2
    source = lax.broadcasted_iota(jnp.int32, out_ref.shape, 0)
    place = lax.broadcasted_iota(jnp.int32, out_ref.shape, 1)
    within = place % step
    apart = source + (place // step) * width + within + (lons - side * width)
    for _ in range(3):
        apart = jnp.where(apart >= lons, apart - lons, apart)
    out_ref[...] = jnp.where(within < width, apart, -1)


def tables_kernel(width, filter_ref, band_ref, apart_ref, table_ref, first):
    bases, lons = filter_ref.shape
    taps, rows, _ = band_ref.shape
    step, places = first.shape[1:]
    columns = places // (2 * step)
    lat = lax.axis_index("lat")
    below = (lat > 0).astype(F32)
    above = (lat < lax.axis_size("lat") - 1).astype(F32)
    inside = [[below, below, 1.0], [1.0, above, above]]
    slots = [[0, 1, 2], [2, 0, 1]]
    profile = filter_ref[...]
    band = band_ref[...].astype(F32)
    apart = apart_ref[...]
    first[...] = jnp.zeros_like(first)
    for lon in range(width):
        pick = (apart == lon).astype(F32).astype(BF16)
        first[:, lon, :] = jnp.dot(profile, pick, preferred_element_type=F32)
    upper = lax.broadcasted_iota(jnp.int32, (SUBLANES, places), 0) < SUBLANES // 2
    count = columns * width
    for basis in range(bases):
        circle = first[basis]
        turned = [
            pltpu.roll(circle, column * 2 * step, 1) if column else circle
            for column in range(columns)
        ]
        last = [block[SUBLANES:] for block in turned]
        pairs = [
            jnp.where(upper, one, pltpu.roll(other, SUBLANES // 2, 0))
            for one, other in zip(last[::2], last[1::2])
        ]
        turned = jnp.concatenate([block[:SUBLANES] for block in turned] + pairs, axis=0)
        at = basis * count
        for row in range(rows):
            for tap in range(taps):
                weight = band[tap, row : row + 1, basis : basis + 1] * inside[row][tap]
                to = slots[row][tap] * places
                table_ref[row, at : at + count, to : to + places] = (weight * turned).astype(BF16)


def squares_kernel(own_ref, mate_ref, squares_ref, padded):
    bases, group, half = own_ref.shape
    lanes = squares_ref.shape[1]
    _, side = column_and_side()
    first = side == 0
    own = own_ref[...].astype(F32)
    mate = mate_ref[...].astype(F32)
    padded[...] = jnp.zeros_like(padded)
    padded[0, :, :group, :half] = jnp.where(first, own, mate)
    padded[1, :, :group, :half] = jnp.where(first, mate, own)
    members = padded.shape[2]
    into = lax.broadcasted_iota(jnp.int32, (lanes, members), 0)
    member = lax.broadcasted_iota(jnp.int32, (lanes, members), 1)
    repeat = (into % group == member).astype(F32).astype(BF16)
    row = lax.broadcasted_iota(jnp.int32, (lanes, lanes), 0)
    column = lax.broadcasted_iota(jnp.int32, (lanes, lanes), 1)
    same = (row // group == column // group) & (row < 2 * half) & (column < 2 * half)
    for basis in range(bases):
        weights = padded[0, basis] + pltpu.roll(padded[1, basis], half, 1)
        repeated = jnp.dot(repeat, weights.astype(BF16), preferred_element_type=F32)
        squares_ref[basis * lanes : (basis + 1) * lanes] = jnp.where(same, repeated, 0.0).astype(
            BF16
        )


def rows_of(message, block, rest):
    groups = unfold(message.astype(F32), block)
    last = (groups[2], pltpu.roll(groups[2], SUBLANES - rest, 0))
    return [jnp.concatenate([groups[row], last[row]], axis=0).astype(BF16) for row in range(2)]


def unpack_kernel(block, width, own_ref, out_ref):
    for at in range(own_ref.shape[0]):
        for row, read in enumerate(rows_of(own_ref[at], block, width - SUBLANES)):
            out_ref[row, at] = read


def own_kernel(block, width, mate, own, even, table_ref, part_ref, even_ref, field):
    rows, columns, step, _ = own.shape
    places = field.shape[1]
    side = lax.axis_index("lon") % 2
    for at in range(columns):
        first = pl.multiple_of((2 * at + side) * step, step)
        other = pl.multiple_of((2 * at + 1 - side) * step, step)
        for row, read in enumerate(rows_of(mate[at], block, width - SUBLANES)):
            field[row, pl.ds(first, step)] = own[row, at]
            field[row, pl.ds(other, step)] = read
    for row in range(rows):
        part_ref[row] = jnp.dot(
            table_ref[row, :, 2 * places :], field[row], preferred_element_type=F32
        )
    for at in range(columns):
        for row, read in enumerate(rows_of(even[at], block, width - SUBLANES)):
            even_ref[row, at] = read


def conv_kernel(
    block,
    width,
    odd_mate,
    odd_own,
    even_mate,
    part_ref,
    even_rows,
    table_ref,
    squares_ref,
    *refs,
):
    *out_refs, field, stage = refs
    columns = len(out_refs)
    lanes = squares_ref.shape[1]
    bases = squares_ref.shape[0] // lanes
    rows, _, inner = table_ref.shape
    places = inner // 3
    step = places // (2 * columns)
    half = columns * width
    rest = width - SUBLANES
    column, side = column_and_side()
    odd = lax.axis_index("lat") % 2

    def place(row, at, message):
        for slot, read in enumerate(rows_of(message, block, rest)):
            first = pl.multiple_of(slot * places + at * step, step)
            field[row, pl.ds(first, step)] = read

    for at in range(columns):
        for slot in range(2):
            first = pl.multiple_of(slot * places + (2 * at + side) * step, step)
            field[1 - odd, pl.ds(first, step)] = even_rows[slot, at]
        place(1 - odd, 2 * at + 1 - side, even_mate[at])
        place(odd, 2 * at + side, odd_own[at])
        place(odd, 2 * at + 1 - side, odd_mate[at])
    over = [
        jnp.dot(table_ref[row, :, : 2 * places], field[row], preferred_element_type=F32)
        for row in range(rows)
    ]
    mixed = None
    for basis in range(bases):
        taken = slice(basis * half, (basis + 1) * half)
        both = [(over[row][taken] + part_ref[row, taken]).astype(BF16) for row in range(rows)]
        product = jnp.dot(
            jnp.concatenate(both, axis=0)[:, :block],
            squares_ref[basis * lanes : basis * lanes + block],
            preferred_element_type=F32,
        )
        mixed = product if mixed is None else mixed + product
    upper = lax.broadcasted_iota(jnp.int32, (SUBLANES, lanes), 0) < rest
    top, bottom = mixed[:half], mixed[half:]
    for target in range(columns):
        at = target * SUBLANES
        pair = (columns + target // 2) * SUBLANES
        first, second = top[pair : pair + SUBLANES], bottom[pair : pair + SUBLANES]
        if target % 2:
            first = pltpu.roll(first, rest, 0)
        else:
            second = pltpu.roll(second, rest, 0)
        last = jnp.where(upper, first, second)
        points = jnp.concatenate(
            [top[at : at + SUBLANES], bottom[at : at + SUBLANES], last], axis=0
        )
        stage[target] = fold(points, block)
    for apart in range(columns):
        out_refs[apart][...] = stage[column ^ apart]


def summed_block(latent_block, message, block):
    convolved = jnp.concatenate(unfold(message.astype(F32), block), axis=0)
    kept = lax.broadcasted_iota(jnp.int32, convolved.shape, 1) < block
    return jnp.where(kept, latent_block + convolved, 0.0).astype(BF16)


def raised_block(summed, column, block, up_ref):
    count = summed.shape[0]
    ones = jnp.ones((up_to(count, 2 * SUBLANES) - count, block), BF16)
    rows = pl.multiple_of(column * block, block)
    return jnp.dot(
        jnp.concatenate([summed[:, :block], ones], axis=0),
        up_ref[pl.ds(rows, block), :],
        preferred_element_type=F32,
    )


def placed(summed, column, chans, block):
    piece = summed.astype(F32)
    if chans > piece.shape[1]:
        gap = jnp.zeros((piece.shape[0], chans - piece.shape[1]), F32)
        piece = jnp.concatenate([piece, gap], axis=1)
    return pltpu.roll(piece, column * block, 1)


def deviations(summed, mean, block):
    kept = lax.broadcasted_iota(jnp.int32, summed.shape, 1) < block
    return jnp.where(kept, summed.astype(F32) - mean, 0.0)


def over_lanes(values):
    return jnp.sum(values, axis=1, keepdims=True)


def lift_kernel(
    apart,
    own_ref,
    first_ref,
    latent_ref,
    up_ref,
    blocks_ref,
    summed_ref,
    raised_ref,
    stats_ref,
    points,
):
    columns = blocks_ref.shape[0]
    chans = latent_ref.shape[2]
    block = chans // columns
    column, _ = column_and_side()
    group_points(latent_ref, points)
    own = points[...]
    for target in range(columns):
        turned = pltpu.roll(own, chans - target * block, 1) if target else own
        blocks_ref[target] = turned[:, : lanes_of(block)]
    other = column ^ apart
    here = summed_block(blocks_ref[column], own_ref[...], block)
    there = summed_block(blocks_ref[other], first_ref[...], block)
    summed_ref[...] = placed(here, column, chans, block) + placed(there, other, chans, block)
    raised_ref[...] = raised_block(here, column, block, up_ref) + raised_block(
        there, other, block, up_ref
    )
    mean = over_lanes(here.astype(F32) + there.astype(F32)) / (2 * block)
    squares = sum(deviations(summed, mean, block) ** 2 for summed in (here, there))
    stats_ref[0] = jnp.broadcast_to(mean, stats_ref.shape[1:])
    stats_ref[1] = jnp.broadcast_to(over_lanes(squares), stats_ref.shape[1:])


def tail_kernel(order, *refs):
    back_refs = refs[: len(order)]
    blocks_ref, summed_ref, raised_ref, stats_ref, up_ref, down_ref, out_ref = refs[len(order) :]
    width, rows, chans = out_ref.shape
    rest = width - SUBLANES
    block = chans // blocks_ref.shape[0]
    column, _ = column_and_side()
    raised = raised_ref[...]
    early_mean, early_squares = stats_ref[0, :, :1], stats_ref[1, :, :1]
    theirs = []
    away = squares = None
    for apart, ref in zip(order, back_refs):
        other = column ^ apart
        there = summed_block(blocks_ref[other], ref[...], block)
        theirs.append((there, other))
        raised = raised + raised_block(there, other, block, up_ref)
        apart_from = deviations(there, early_mean, block)
        away = apart_from if away is None else away + apart_from
        squares = apart_from**2 if squares is None else squares + apart_from**2
    away, squares = over_lanes(away), over_lanes(squares)
    mean = early_mean + away / chans
    variance = (early_squares + squares - away * away / chans) / chans
    scale = lax.rsqrt(variance + 1e-05)
    count = summed_ref.shape[0]
    product = None
    units = raised.shape[1]
    for start in range(0, units, LANES):
        taken = slice(start, min(start + LANES, units))
        hidden = scale * (raised[:count, taken] - mean * raised[count : count + 1, taken])
        hidden = (0.5 * hidden * (1.0 + lax.erf(hidden * 0.5**0.5))).astype(BF16)
        part = jnp.dot(hidden, down_ref[taken], preferred_element_type=F32)
        product = part if product is None else product + part
    summed = summed_ref[...]
    for there, other in theirs:
        summed = summed + placed(there, other, chans, block)
    result = summed + product
    for row in range(rows):
        out_ref[:SUBLANES, row, :] = result[row * SUBLANES : (row + 1) * SUBLANES].astype(BF16)
        at = rows * SUBLANES + row * rest
        out_ref[SUBLANES:, row, :] = result[at : at + rest].astype(BF16)


VMEM = pl.BlockSpec(memory_space=pltpu.VMEM)


def call(kernel, name, out_shape, scratch, work, *operands):
    several = isinstance(out_shape, tuple)
    return pl.pallas_call(
        kernel,
        out_shape=out_shape,
        in_specs=[VMEM] * len(operands),
        out_specs=(VMEM,) * len(out_shape) if several else VMEM,
        scratch_shapes=scratch,
        compiler_params=pltpu.CompilerParams(vmem_limit_bytes=24 * 2**20),
        cost_estimate=pl.CostEstimate(flops=work, bytes_accessed=10**6, transcendentals=0),
        name=name,
    )(*operands)


def over_columns(message, count, apart):
    pairs = [(i, ((i // 2) ^ apart) * 2 + i % 2) for i in range(count)]
    return lax.ppermute(message, "lon", pairs) if apart else message


def over_sides(block, count):
    return lax.ppermute(block, "lon", [(i, i ^ 1) for i in range(count)])


def swap(block, count, partner):
    pairs = []
    for lat in range(lax.axis_size("lat")):
        for lon in range(count):
            to_lat, to_lon = partner(lat, lon)
            pairs.append((lat * count + lon, to_lat * count + to_lon))
    return lax.ppermute(block, ("lat", "lon"), pairs)


def odd_pair(lat, lon, other_side, rows):
    to = lat + 1 if lat % 2 else lat - 1
    if 0 <= to < rows:
        return to, lon ^ other_side
    return (lat, lon ^ 1) if other_side else (rows - 1 - lat, lon)


def local(latent, lon_filter, mix_weight, band_weight, offsets, w_up, w_down):
    rows, width, chans = latent.shape
    bases, lons = lon_filter.shape
    half, group = mix_weight.shape[1:]
    taps = band_weight.shape[2]
    count = lons // width
    columns = count // 2
    block = 2 * half
    step = up_to(width, 2 * SUBLANES)
    places = count * step
    lanes = lanes_of(block)
    height = message_rows(block)
    assert rows == 2 and taps == 3 and columns & (columns - 1) == 0
    assert lax.axis_size("lat") % 2 == 0
    assert 2 * width == 3 * SUBLANES and columns * width % (2 * SUBLANES) == 0
    assert 3 * (block % LANES) <= LANES

    far_first = tuple(reversed(range(columns)))
    inward = far_first
    if columns > 3:
        inward = (far_first[1], far_first[0]) + far_first[2:]
    message = jax.ShapeDtypeStruct((height, LANES), BF16)
    messages = (message,) * columns
    stage = pltpu.VMEM((columns, height, LANES), BF16)
    points = pltpu.VMEM((3 * SUBLANES, chans), F32)
    lon_first = jnp.transpose(latent, (1, 0, 2))
    mix_own = jnp.transpose(mix_weight, (0, 2, 1))

    raw = over_columns(lon_first, count, inward[0])
    apart = call(
        functools.partial(apart_kernel, width, step),
        "apart",
        jax.ShapeDtypeStruct((lons, places), jnp.int32),
        [],
        10**9,
    )
    loaded, apart = lax.optimization_barrier((lon_first, apart))
    packed = call(
        functools.partial(pack_kernel, inward[1:]),
        "pack",
        (message,) * (columns - 1),
        [points, stage],
        10**9,
        loaded,
    )
    arrived = [call(cut_kernel, "cut", message, [points], 5 * 10**9, raw)]
    arrived += [over_columns(*pair) for pair in zip(packed, [count] * columns, inward[1:])]
    mix_mate = over_sides(mix_own, count)
    table = call(
        functools.partial(tables_kernel, width),
        "tables",
        jax.ShapeDtypeStruct((rows, bases * columns * width, taps * places), BF16),
        [pltpu.VMEM((bases, step, places), F32)],
        10**6,
        lon_filter,
        jnp.transpose(band_weight, (2, 1, 0)),
        apart,
    )
    gathered = jax.ShapeDtypeStruct((columns, height, LANES), BF16)
    own_side = call(
        functools.partial(column_kernel, inward),
        "join_columns",
        gathered,
        [],
        10**8,
        *arrived,
    )
    lats = lax.axis_size("lat")
    mate_side = swap(own_side, count, lambda lat, lon: (lat, lon ^ 1))
    odd_mate = swap(own_side, count, lambda lat, lon: odd_pair(lat, lon, 1, lats))
    odd_own = swap(own_side, count, lambda lat, lon: odd_pair(lat, lon, 0, lats))
    own_rows = call(
        functools.partial(unpack_kernel, block, width),
        "unpack",
        jax.ShapeDtypeStruct((rows, columns, step, lanes), BF16),
        [],
        10**9,
        own_side,
    )
    even_own = swap(own_side, count, lambda lat, lon: (lat ^ 1, lon))
    even_mate = swap(mate_side, count, lambda lat, lon: (lat ^ 1, lon))
    mix_mate, _ = lax.optimization_barrier((mix_mate, mate_side))
    squares = call(
        squares_kernel,
        "squares",
        jax.ShapeDtypeStruct((bases * lanes, lanes), BF16),
        [pltpu.VMEM((2, bases, up_to(group, 2 * SUBLANES), lanes), F32)],
        3 * 10**8,
        mix_own,
        mix_mate,
    )
    part = call(
        functools.partial(own_kernel, block, width),
        "conv_own",
        (
            jax.ShapeDtypeStruct((rows, bases * columns * width, lanes), F32),
            jax.ShapeDtypeStruct((rows, columns, step, lanes), BF16),
        ),
        [pltpu.VMEM((rows, places, lanes), BF16)],
        3 * 10**8,
        mate_side,
        own_rows,
        even_own,
        table,
    )
    mixed = call(
        functools.partial(conv_kernel, block, width),
        "conv",
        messages,
        [
            pltpu.VMEM((rows, 2 * places, lanes), BF16),
            pltpu.VMEM((columns, height, LANES), BF16),
        ],
        10**10,
        odd_mate,
        odd_own,
        even_mate,
        *part,
        table,
        squares,
    )
    outward = tuple(reversed(far_first[:-1]))
    back = [over_columns(mixed[apart], count, apart) for apart in outward]
    first = outward.index(far_first[0])
    lifted = call(
        functools.partial(lift_kernel, far_first[0]),
        "lift",
        (
            jax.ShapeDtypeStruct((columns, 3 * SUBLANES, lanes), F32),
            jax.ShapeDtypeStruct((3 * SUBLANES, chans), F32),
            jax.ShapeDtypeStruct((up_to(3 * SUBLANES, 2 * SUBLANES), w_up.shape[1]), F32),
            jax.ShapeDtypeStruct((2, 3 * SUBLANES, LANES), F32),
        ),
        [points],
        10**8,
        mixed[0],
        back[first],
        lon_first,
        w_up,
    )
    result = call(
        functools.partial(tail_kernel, outward[:first] + outward[first + 1 :]),
        "tail",
        jax.ShapeDtypeStruct(lon_first.shape, BF16),
        [],
        10**9,
        *back[:first],
        *back[first + 1 :],
        *lifted,
        w_up,
        w_down,
    )
    return jnp.transpose(result, (1, 0, 2))


def solution(mesh):
    return jax.shard_map(
        local,
        mesh=mesh,
        in_specs=(
            P("lat", "lon", None),
            P(),
            P(None, "lon", None),
            P(None, "lat", None),
            P("lat"),
            P(),
            P(),
        ),
        out_specs=P("lat", "lon", None),
        check_vma=False,
    )
```
